32 devices in a mesh: groups: 2 (over x), rows: 16 (over z, y, core).
Axes of the slice: x: 2, y: 2, z: 4, core: 2. Of those that a mesh axis runs over, the one named last changes fastest.
Arguments:
- right_sides: float32 [16, 65536], P('groups', 'rows'), parts along dimension 0, may hold values from -108 to 108
- near_blocks: bfloat16 [512, 8, 128, 128], P('rows'), may hold values from -0.125 to 0.125
- near_cols: int32 [512, 8], P('rows'), may hold values from 0 to 511, as said below
- near_counts: int32 [512], P('rows'), may hold values from 3 to 8, as said below
- basis_in: bfloat16 [512, 16, 128], P('rows'), may hold values from -0.5 to 0.5
- target_basis: bfloat16 [512, 16, 128], P('rows'), may hold values from -1.5 to 1.5
- coupling: float32 [512, 8, 16, 16], P('rows'), may hold values from -0.375 to 0.375
- far_cols: int32 [512, 8], P('rows'), may hold values from 0 to 511
Outputs:
- solution: float32 [16, 65536], P('groups', 'rows'), parts along dimension 0
- next_basis: float32 [16, 65536], P('groups', 'rows'), parts along dimension 0
The draws below stay inside these ranges and needn't reach their ends.
There are 2 independent parts, one for each index of `groups`. The reference program is written for one: setup_inputs(seed, part) draws one part's arguments, and reference() takes and returns one part's arrays. A program takes and returns all parts, laid end to end along the dimension named above; an argument that names none is the same for every part. Nothing has to cross between parts.
Inputs may be any that keep to these rules, and one draw needn't show every extreme that they name: near_cols[i, k] = (i + o) mod 512 with -64 <= o <= 64; slot 0 is i itself; in the first of each device's 32 rows slot 1 has o = 64 and slot 2 has o = -64. The live slots of row i are its first near_counts[i] slots.
All inputs are finite; a program needn't handle non-finite values.
Results may differ from the reference program's by a relative error of at most 0.0053.
Values may be sent and summed in bfloat16 or wider, within the bound.
No kernel may reach another device: no remote copies, remote signals or barrier semaphores. Data moves between devices by JAX's collectives and lax.ppermute only.
A program may use at most 128 MiB of HBM per device.

```python
import math
from functools import partial
import jax
import jax.numpy as jnp
from jax import lax

UNKNOWNS_EACH = 128
R = 16
RIGHT_SIDE_COUNT = 8
NB = 8
FA = 8
CL_DEV = 32
CLUSTER_COUNT = 512


def draw_right_sides(key, part):
    key = jax.random.fold_in(key, 7)
    key_one, key_two, key_three = jax.random.split(key, 3)
    position = (jnp.arange(CLUSTER_COUNT * UNKNOWNS_EACH, dtype=jnp.int32) // UNKNOWNS_EACH).astype(jnp.float32) / CLUSTER_COUNT
    rising = 1.0 + 2.0 * position
    cluster_scale = jnp.exp(jax.random.uniform(key_one, (CLUSTER_COUNT,), jnp.float32, math.log(0.3), math.log(3.0)))
    row_scale = jnp.repeat(cluster_scale, UNKNOWNS_EACH) * rising
    column_scale = jnp.exp(jax.random.uniform(key_two, (RIGHT_SIDE_COUNT, 1), jnp.float32, math.log(0.3), math.log(3.0)))
    base_values = jnp.clip(jax.random.normal(key_three, (RIGHT_SIDE_COUNT, CLUSTER_COUNT * UNKNOWNS_EACH), jnp.float32), -4.0, 4.0)
    return (base_values * column_scale * row_scale[None, :]).astype(jnp.float32)


def draw_near_cols(key, part):
    key = jax.random.fold_in(key, 11)
    reach_len = 2 * CL_DEV
    row_index = jnp.arange(CLUSTER_COUNT, dtype=jnp.int32)
    offsets = jax.random.randint(key, (CLUSTER_COUNT, NB), -reach_len, reach_len + 1, dtype=jnp.int32)
    first_row = row_index % CL_DEV == 0
    offsets = offsets.at[:, 0].set(0)
    offsets = offsets.at[:, 1].set(jnp.where(first_row, reach_len, offsets[:, 1]))
    offsets = offsets.at[:, 2].set(jnp.where(first_row, -reach_len, offsets[:, 2]))
    return ((row_index[:, None] + offsets) % CLUSTER_COUNT).astype(jnp.int32)


def draw_near_counts(key, part):
    key = jax.random.fold_in(key, 23)
    key_one, key_two, key_three = jax.random.split(key, 3)
    slab_count = CLUSTER_COUNT // CL_DEV
    heaviness = jax.random.randint(key_one, (slab_count,), 0, 4, dtype=jnp.int32)
    chosen = jax.random.randint(key_two, (), 0, slab_count, dtype=jnp.int32)
    heaviness = jnp.where(jnp.arange(slab_count, dtype=jnp.int32) == chosen, 3, heaviness)
    ceiling = 4 + heaviness * (NB - 4) // 3
    ceiling_rows = jnp.repeat(ceiling, CL_DEV)
    counts = jax.random.randint(key_three, (CLUSTER_COUNT,), 3, ceiling_rows + 1, dtype=jnp.int32)
    position = jnp.arange(CLUSTER_COUNT, dtype=jnp.int32) % CL_DEV
    counts = jnp.where(position == 0, ceiling_rows, jnp.where(position == 1, 3, counts))
    return counts.astype(jnp.int32)


def set_ends(values, stream_key, least, largest):
    longest = values.shape.index(max(values.shape))
    spots = []
    for shift in (0, 1):
        where = [jax.random.randint(jax.random.fold_in(stream_key, axis), (), 0, length) for axis, length in enumerate(values.shape)]
        where[longest] = (where[longest] + shift) % values.shape[longest]
        spots.append(tuple(where))
    return values.at[spots[0]].set(least).at[spots[1]].set(largest)


def levels(own_key, extent, shards, low, largest):
    loudness = 1.0
    for dim, blocks in shards:
        steps = jax.random.uniform(jax.random.fold_in(jax.random.fold_in(own_key, 6), dim), (blocks,), jnp.float32, low / len(shards), largest / len(shards))
        loudness = loudness * jnp.repeat(jnp.exp(steps), extent[dim] // blocks).reshape((-1,) + (1,) * (len(extent) - 1 - dim))
    return loudness


def noise(rng, extent, width, reach, pieces=(), held_as=jnp.bfloat16):
    loudness = levels(rng, extent, pieces, -0.22, 0.18) if pieces else 1.0
    values = jax.random.normal(rng, extent, jnp.float32) * width * loudness
    return jnp.minimum(jnp.maximum(values, -reach), reach).astype(held_as)


def setup_inputs(seed: int = 0, part: int = 0) -> dict:
    keys = jax.random.split(jax.random.key(seed), 9)
    part_splits = jax.random.split(jax.random.fold_in(keys[8], part), 9)
    return {
        "right_sides": draw_right_sides(jax.random.fold_in(jax.random.fold_in(keys[8], part), 71), part),
        "near_blocks": noise(keys[1], (CLUSTER_COUNT, NB, UNKNOWNS_EACH, UNKNOWNS_EACH), (2 * NB * UNKNOWNS_EACH) ** -0.5, 0.125, ((0, 16),)),
        "near_cols": draw_near_cols(jax.random.fold_in(keys[8], 71), part),
        "near_counts": draw_near_counts(jax.random.fold_in(keys[8], 71), part),
        "basis_in": noise(keys[4], (CLUSTER_COUNT, R, UNKNOWNS_EACH), UNKNOWNS_EACH ** -0.5, 0.5, ((0, 16),)),
        "target_basis": noise(keys[5], (CLUSTER_COUNT, R, UNKNOWNS_EACH), R ** -0.5, 1.5, ((0, 16),)),
        "coupling": noise(keys[6], (CLUSTER_COUNT, FA, R, R), (2 * FA * R) ** -0.5, 0.375, ((0, 16),), jnp.float32),
        "far_cols": set_ends(jax.random.randint(keys[7], (CLUSTER_COUNT, FA), 0, CLUSTER_COUNT), jax.random.fold_in(keys[7], 1), 0, CLUSTER_COUNT - 1).astype(jnp.int32),
    }


epsilon = 1e-06
highest_precision = lax.Precision.HIGHEST

def slab_near(lowered, near_blocks, near_cols, near_counts, slab_index):
    offset_row = (slab_index * CL_DEV).astype(jnp.int32)
    blocks = lax.dynamic_slice_in_dim(near_blocks, offset_row, CL_DEV, 0)
    columns = lax.dynamic_slice_in_dim(near_cols, offset_row, CL_DEV, 0)
    counts = lax.dynamic_slice_in_dim(near_counts, offset_row, CL_DEV, 0)
    source = jnp.take(lowered, columns, axis=1).astype(jnp.float32)
    live_mask = (jnp.arange(NB, dtype=jnp.int32)[None, :] < counts[:, None]).astype(jnp.float32)
    source = source * live_mask[None, :, :, None]
    return jnp.einsum('ckab,rckb->rca', blocks.astype(jnp.float32), source, precision=highest_precision)

def apply_operator(vector, near_blocks, near_cols, near_counts, basis_in, target_basis, coupling, far_cols):
    lowered = lax.optimization_barrier(vector.astype(jnp.bfloat16)).reshape(RIGHT_SIDE_COUNT, CLUSTER_COUNT, UNKNOWNS_EACH)
    slab_count = CLUSTER_COUNT // CL_DEV
    near_part = lax.map(partial(slab_near, lowered, near_blocks, near_cols, near_counts), jnp.arange(slab_count, dtype=jnp.int32))
    near_part = jnp.transpose(near_part, (1, 0, 2, 3)).reshape(RIGHT_SIDE_COUNT, CLUSTER_COUNT * UNKNOWNS_EACH)
    compressed = jnp.einsum('cqb,rcb->rqc', basis_in.astype(jnp.float32), lowered.astype(jnp.float32), precision=highest_precision)
    picked = jnp.take(compressed, far_cols, axis=2)
    coupled_matrix = lax.optimization_barrier(jnp.einsum('ckpq,rqck->rcp', coupling, picked, precision=highest_precision).astype(jnp.bfloat16))
    far_field_part = jnp.einsum('feq,kfe->kfq', target_basis.astype(jnp.float32), coupled_matrix.astype(jnp.float32), precision=highest_precision).reshape(RIGHT_SIDE_COUNT, CLUSTER_COUNT * UNKNOWNS_EACH)
    return 0.5 * vector + (near_part + far_field_part)

def inner_mean(first_vec, second_vec):
    return lax.optimization_barrier(jnp.sum(first_vec * second_vec, axis=1)) / (CLUSTER_COUNT * UNKNOWNS_EACH)

def reference(right_sides, near_blocks, near_cols, near_counts, basis_in, target_basis, coupling, far_cols):
    start_norm = jnp.sqrt(inner_mean(right_sides, right_sides) + epsilon)
    krylov = [right_sides / start_norm[:, None]]
    columns = []
    for iteration in range(2):
        candidate = apply_operator(krylov[iteration], near_blocks, near_cols, near_counts, basis_in, target_basis, coupling, far_cols)
        entries = [inner_mean(earlier, candidate) for earlier in krylov]
        for weight_k, earlier in zip(entries, krylov):
            candidate = candidate - weight_k[:, None] * earlier
        length = jnp.sqrt(inner_mean(candidate, candidate) + epsilon)
        krylov.append(candidate / length[:, None])
        columns.append(entries + [length])
    first_diag, first_sub = columns[0]
    second_top, second_diag, second_sub = columns[1]
    gram_first = first_diag * first_diag + first_sub * first_sub
    gram_cross = first_diag * second_top + first_sub * second_diag
    gram_second = second_top * second_top + second_diag * second_diag + second_sub * second_sub
    target_first = start_norm * first_diag
    target_second = start_norm * second_top
    determinant = gram_first * gram_second - gram_cross * gram_cross
    coef_first = (gram_second * target_first - gram_cross * target_second) / determinant
    coef_second = (gram_first * target_second - gram_cross * target_first) / determinant
    solution = coef_first[:, None] * krylov[0] + coef_second[:, None] * krylov[1]
    return (solution, krylov[2])
```

```python
import jax
import jax.numpy as jnp
from jax import lax
from jax.sharding import PartitionSpec as P

epsilon = 1e-06


def shifted(block, distance):
    size = lax.axis_size("rows")
    route = [((i - distance) % size, i) for i in range(size)]
    return lax.ppermute(block, "rows", route)


def gather_exchange(payload):
    size = lax.axis_size("rows")
    spread = jnp.broadcast_to(payload[None], (size,) + payload.shape)
    return lax.all_to_all(spread, "rows", 0, 0)


def digits():
    rest, stride, found = lax.axis_size("rows") // 2, 2, []
    while rest > 1:
        length = 4 if rest % 4 == 0 and rest % 8 != 0 else 2
        found.append((stride, length))
        stride, rest = stride * length, rest // length
    return found + [(1, 2)]


def digit_shift(block, stride, length, step):
    size = lax.axis_size("rows")

    def target(i):
        d = (i // stride) % length
        return i + ((d + step) % length - d) * stride

    return lax.ppermute(block, "rows", [(i, target(i)) for i in range(size)])


def gather_by_digits(payload):
    size = lax.axis_size("rows")
    me = lax.axis_index("rows")
    held = payload[None]
    places = me[None]
    for stride, length in digits():
        parts, spots = [held], [places]
        for step in range(1, length):
            parts.append(digit_shift(held, stride, length, step))
            d = (places // stride) % length
            spots.append(places + ((d - step) % length - d) * stride)
        held, places = jnp.concatenate(parts), jnp.concatenate(spots)
    return held, places


def sum_by_digits(values):
    size = lax.axis_size("rows")
    for stride, length in digits():
        groups = [
            [base + d * stride for d in range(length)]
            for base in range(size)
            if (base // stride) % length == 0
        ]
        values = lax.psum(values, "rows", axis_index_groups=groups)
    return values


def operator(field, lowered, near_sources, near_blocks, compressed, coupling, far_cols, target_basis, scale):
    window, placed, live = near_sources
    rhs_count, local_width = field.shape
    source = jnp.take(window, placed, axis=1) * live[None, :, :, None]
    near = jnp.einsum("ckab,rckb->rca", near_blocks, source, preferred_element_type=jnp.float32)
    picked = jnp.take(compressed, far_cols, axis=2)
    coupled = jnp.einsum(
        "ckpq,rqck->rcp", coupling, picked, precision=lax.Precision.HIGHEST,
        preferred_element_type=jnp.float32,
    )
    coupled = (coupled * scale[:, None, None]).astype(jnp.bfloat16)
    far = jnp.einsum("feq,kfe->kfq", target_basis, coupled, preferred_element_type=jnp.float32)
    near = near * scale[:, None, None]
    return 0.5 * field * scale[:, None] + (near + far).reshape(rhs_count, local_width)


def on_device(
    right_sides, near_blocks, near_cols, near_counts, basis_in, target_basis, coupling, far_cols
):
    rhs_count, local_width = right_sides.shape
    clusters, slot_count = near_cols.shape
    cluster_size = near_blocks.shape[2]
    rank = basis_in.shape[1]
    size = lax.axis_size("rows")
    every = clusters * size
    unknowns = float(local_width * size)

    here = lax.axis_index("rows") * clusters + jnp.arange(clusters, dtype=jnp.int32)
    reach = 2 * clusters
    relative = (near_cols - here[:, None] + reach) % every - reach
    placed = relative + reach + jnp.arange(clusters, dtype=jnp.int32)[:, None]
    live = (jnp.arange(slot_count, dtype=jnp.int32)[None, :] < near_counts[:, None]).astype(jnp.bfloat16)

    def send(field, sums, way):
        lowered = field.astype(jnp.bfloat16).reshape(rhs_count, clusters, cluster_size)
        compressed = jnp.einsum(
            "cqb,rcb->rqc", basis_in.astype(jnp.float32), field.reshape(lowered.shape),
            precision=lax.Precision.HIGHEST,
        ).reshape(clusters, rhs_count * rank)
        tail = jnp.zeros((8, rhs_count * rank), jnp.float32).at[: len(sums), :rhs_count].set(jnp.stack(sums))
        payload = jnp.concatenate([compressed, tail])
        slabs = {d: shifted(lowered, d) for d in (2, 1, -1, -2)}
        if way == "exchange":
            got = gather_exchange(payload)
        else:
            got, places = gather_by_digits(payload)
            order = jnp.zeros((size,), jnp.int32).at[places].set(jnp.arange(size, dtype=jnp.int32))
            got = got[order]
        window = jnp.concatenate([slabs[2], slabs[1], lowered, slabs[-1], slabs[-2]], axis=1)
        totals = jnp.sum(got[:, clusters : clusters + len(sums), :rhs_count], axis=0) / unknowns
        whole = got[:, :clusters].reshape(size, rhs_count, rank, clusters)
        whole = jnp.moveaxis(whole, 0, 2).reshape(rhs_count, rank, every)
        return (window, placed, live), whole, totals

    def dots(*pairs):
        return [jnp.sum(f * g, axis=1) for f, g in pairs]

    sources, whole, totals = send(right_sides, dots((right_sides, right_sides)), "exchange")
    start_square = totals[0] + epsilon
    start_norm = jnp.sqrt(start_square)
    first = right_sides / start_norm[:, None]
    image = operator(
        right_sides, None, sources, near_blocks, whole, coupling, far_cols, target_basis, 1.0 / start_norm
    )
    sources, whole, totals2 = send(image, dots((first, image), (image, image)), "digits")
    h11 = totals2[0]
    v11 = totals[0] / start_square
    uu = jnp.maximum(totals2[1] - 2.0 * h11 * h11 + h11 * h11 * v11, 0.0)
    h21 = jnp.sqrt(uu + epsilon)
    second = (image - h11[:, None] * first) / h21[:, None]
    twice = operator(
        image, None, sources, near_blocks, whole, coupling, far_cols, target_basis, jnp.ones_like(h11)
    )
    candidate = (twice - h11[:, None] * image) / h21[:, None]
    v22 = uu / (uu + epsilon)
    v12 = h11 * (1.0 - v11) / h21
    totals3 = sum_by_digits(jnp.stack(dots((first, candidate), (second, candidate), (candidate, candidate)))) / unknowns
    h12, h22 = totals3[0], totals3[1]
    uu2 = (
        totals3[2] - 2.0 * (h12 * h12 + h22 * h22)
        + h12 * h12 * v11 + h22 * h22 * v22 + 2.0 * h12 * h22 * v12
    )
    h32 = jnp.sqrt(jnp.maximum(uu2, 0.0) + epsilon)
    third = (candidate - h12[:, None] * first - h22[:, None] * second) / h32[:, None]
    g11 = h11 * h11 + h21 * h21
    g12 = h11 * h12 + h21 * h22
    g22 = h12 * h12 + h22 * h22 + h32 * h32
    t1, t2 = start_norm * h11, start_norm * h12
    det = g11 * g22 - g12 * g12
    y1 = (g22 * t1 - g12 * t2) / det
    y2 = (g11 * t2 - g12 * t1) / det
    return y1[:, None] * first + y2[:, None] * second, third


def solution(mesh):
    return jax.shard_map(
        on_device,
        mesh=mesh,
        in_specs=(
            P("groups", "rows"),
            P("rows", None, None, None),
            P("rows", None),
            P("rows"),
            P("rows", None, None),
            P("rows", None, None),
            P("rows", None, None, None),
            P("rows", None),
        ),
        out_specs=(P("groups", "rows"), P("groups", "rows")),
        check_vma=False,
    )
```

```python
import functools

import jax
import jax.numpy as jnp
from jax import lax
from jax.experimental import pallas as pl
from jax.experimental.pallas import tpu as pltpu
from jax.sharding import PartitionSpec as P

epsilon = 1e-06
f32, bf16 = jnp.float32, jnp.bfloat16
VMEM = pl.BlockSpec(memory_space=pltpu.VMEM)
SMEM = pl.BlockSpec(memory_space=pltpu.SMEM)
ANY = pl.BlockSpec(memory_space=pl.ANY)
R = 8
LANES = 128
SUM_SLOTS = 8
TAIL = 16
PARAMS = pltpu.CompilerParams(vmem_limit_bytes=40 * 1024 * 1024)


def lane_ids(rows=R):
    return lax.broadcasted_iota(jnp.int32, (rows, LANES), 1)


def rows_of(ref, j):
    return ref[pl.ds(j * R, R), :]


def dot(a, b, contract=(1, 0)):
    return lax.dot_general(a, b, (((contract[0],), (contract[1],)), ((), ())), preferred_element_type=f32)


def sums_tile(sums):
    lane = lane_ids()
    tile = jnp.zeros((R, LANES), f32)
    for t, partial in enumerate(sums):
        total = jnp.sum(partial, axis=1, keepdims=True)
        high = total.astype(bf16).astype(f32)
        middle = (total - high).astype(bf16).astype(f32)
        low = total - high - middle
        for part, value in enumerate((high, middle, low)):
            tile = jnp.where(lane == part * SUM_SLOTS + t, value, tile)
    return jnp.concatenate([tile, jnp.zeros((TAIL - R, LANES), f32)], axis=0).astype(bf16)


def read_sums(got, first_row, count, unknowns):
    total = jnp.zeros((R, LANES), f32)
    for device in range(got.shape[0]):
        total = total + got[device, pl.ds(first_row, TAIL), :].astype(f32)[:R]
    return [
        sum(total[:, p * SUM_SLOTS + t : p * SUM_SLOTS + t + 1] for p in range(3)) * (1.0 / unknowns)
        for t in range(count)
    ]


def compress(tiles, basis, group):
    stacked = jnp.concatenate(tiles, axis=0)
    high = stacked.astype(bf16)
    low = (stacked - high.astype(f32)).astype(bf16)
    both = dot(jnp.concatenate([high, low], axis=0), basis[pl.ds(group * LANES, LANES), :], (1, 1))
    rows = len(tiles) * R
    both = both[:rows] + both[rows:]
    lane = lane_ids()
    rank = LANES // len(tiles)
    tile = jnp.zeros((R, LANES), f32)
    for m in range(len(tiles)):
        tile = jnp.where(lane // rank == m, both[m * R : (m + 1) * R], tile)
    return tile


def write_payload(payload, tiles, basis, sums, per_group):
    groups = len(tiles) // per_group
    parts = [compress(tiles[g * per_group : (g + 1) * per_group], basis, g) for g in range(groups)]
    block = jnp.concatenate([jnp.concatenate(parts, axis=0).astype(bf16), sums_tile(sums)], axis=0)
    for device in range(payload.shape[0]):
        payload[device] = block


def start_kernel(per_group, b, basis, lowered, payload):
    clusters = b.shape[1] // LANES
    tiles = [b[:, j * LANES : (j + 1) * LANES] for j in range(clusters)]
    lowered[...] = jnp.concatenate(tiles, axis=0).astype(bf16)
    square = sum(t * t for t in tiles)
    write_payload(payload, tiles, basis, [square], per_group)


def prepare_kernel(coupling, target, high_out, low_out, target_out):
    slots, rank, _, clusters = coupling.shape
    per_tile = LANES // clusters
    for s in range(rank // per_tile):
        pieces = [
            coupling[:, s * per_tile + p].reshape(slots * rank, clusters) for p in range(per_tile)
        ]
        tile = jnp.concatenate(pieces, axis=1)
        high = tile.astype(bf16)
        high_out[:, s * LANES : (s + 1) * LANES] = high
        low_out[:, s * LANES : (s + 1) * LANES] = (tile - high.astype(f32)).astype(bf16)
    size = rank * clusters
    row = lax.broadcasted_iota(jnp.int32, (size, size), 0)
    column = lax.broadcasted_iota(jnp.int32, (size, size), 1)
    wanted = (row % clusters) * rank + row // clusters
    target_out[...] = dot((column == wanted).astype(bf16), target[...]).astype(bf16)


def far_field(got, far_cols, high, low, target, table, clusters, rank, far):
    slots = far_cols.shape[0]
    per_group = LANES // rank
    groups = clusters // per_group
    head = groups * R
    for device in range(got.shape[0]):
        table[pl.ds(device * head, head), :] = got[device, pl.ds(0, head), :].astype(f32)
    lane = lane_ids()
    picked = []
    for i in range(clusters):
        tile = jnp.zeros((R, LANES), f32)
        for k in range(slots):
            j = far_cols[k, i]
            found = table[pl.ds(pl.multiple_of(lax.div(j, per_group) * R, R), R), :]
            shift = ((k - j) * rank) & (LANES - 1)
            tile = jnp.where(lane // rank == k, pltpu.roll(found, shift, 1), tile)
        picked.append(tile)
    picked = jnp.concatenate(picked, axis=0).astype(bf16)
    crossed = dot(picked, high[...]) + dot(picked, low[...])
    expanded_high, expanded_low = [], []
    for s in range(rank * clusters // LANES):
        tile = jnp.zeros((R, LANES), f32)
        for i in range(clusters):
            part = crossed[i * R : (i + 1) * R, s * LANES : (s + 1) * LANES]
            tile = jnp.where(lane % clusters == i, part, tile)
        tile_high = tile.astype(bf16).astype(f32)
        tile_low = tile - tile_high
        for source, kept in ((tile_high, expanded_high), (tile_low, expanded_low)):
            spread = [jnp.where(lane % clusters == i, source, 0.0) for i in range(clusters)]
            kept.append(jnp.concatenate(spread, axis=0).astype(bf16))
    far[...] = dot(jnp.concatenate(expanded_high, axis=1), target[...]) + dot(
        jnp.concatenate(expanded_low, axis=1), target[...]
    )


def near_field(slabs, placed, blocks, window, near, copies):
    rows = slabs[0].shape[0]
    for at, slab in enumerate(slabs):
        window[pl.ds(at * rows, rows), :] = slab[...].astype(f32)
    window[pl.ds(len(slabs) * rows, R), :] = jnp.zeros((R, LANES), f32)
    slots, clusters = placed.shape
    chunks = copies.chunks
    per_chunk = clusters // chunks

    def body(chunk, carry):
        copies.wait(chunk)
        for inner in range(per_chunk):
            i = chunk * per_chunk + inner
            total = jnp.zeros((R, LANES), f32)
            for k in range(slots):
                source = window[pl.ds(pl.multiple_of(placed[k, i] * R, R), R), :].astype(bf16)
                total = total + dot(source, blocks[i * slots + k], (1, 1))
            near[pl.ds(pl.multiple_of(i * R, R), R), :] = total
        return carry

    lax.fori_loop(0, chunks, body, 0)


class BlockCopies:
    chunks = 8

    def __init__(self, source, target, sems):
        self.source, self.target, self.sems = source, target, sems
        self.rows = source.shape[0] // self.chunks

    def copy(self, chunk):
        span = pl.ds(chunk * self.rows, self.rows)
        return pltpu.make_async_copy(self.source.at[span], self.target.at[span], self.sems.at[chunk])

    def start(self):
        for chunk in range(self.chunks):
            self.copy(chunk).start()

    def wait(self, chunk):
        self.copy(chunk).wait()


def norm_parts(sums):
    square = sums[0]
    whole = square + epsilon
    return jnp.sqrt(whole), square / whole


def first_kernel(
    per_group, unknowns, b, slab_a, slab_b, slab_c, slab_d, slab_e, got, placed, far_cols, blocks_hbm,
    basis, high, low, target, image, lowered, payload, blocks, window, table, near, far, sems,
):
    copies = BlockCopies(blocks_hbm, blocks, sems)
    copies.start()
    slots, clusters = placed.shape
    head = clusters // per_group * R
    far_field(got, far_cols, high, low, target, table, clusters, LANES // per_group, far)
    near_field((slab_a, slab_b, slab_c, slab_d, slab_e), placed, blocks, window, near, copies)
    start_norm, _ = norm_parts(read_sums(got, head, 1, unknowns))
    scale = 1.0 / start_norm
    cross = jnp.zeros((R, LANES), f32)
    square = jnp.zeros((R, LANES), f32)
    tiles = []
    for j in range(clusters):
        field = b[:, j * LANES : (j + 1) * LANES]
        made = (0.5 * field + (rows_of(near, j) + rows_of(far, j))) * scale
        cross = cross + (field * scale) * made
        square = square + made * made
        image[pl.ds(j * R, R), :] = made
        tiles.append(made)
    lowered[...] = jnp.concatenate(tiles, axis=0).astype(bf16)
    write_payload(payload, tiles, basis, [cross, square], per_group)


def arnoldi_one(sums0, sums1):
    _, v11 = norm_parts(sums0)
    h11 = sums1[0]
    uu = jnp.maximum(sums1[1] - 2.0 * h11 * h11 + h11 * h11 * v11, 0.0)
    h21 = jnp.sqrt(uu + epsilon)
    return h11, h21, v11, uu / (uu + epsilon), h11 * (1.0 - v11) / h21


def second_kernel(
    per_group, unknowns, b, image, slab_a, slab_b, slab_c, slab_d, slab_e, got0, got, placed, far_cols,
    blocks_hbm, high, low, target, candidate, payload, blocks, window, table, near, far, sems,
):
    copies = BlockCopies(blocks_hbm, blocks, sems)
    copies.start()
    slots, clusters = placed.shape
    head = clusters // per_group * R
    far_field(got, far_cols, high, low, target, table, clusters, LANES // per_group, far)
    near_field((slab_a, slab_b, slab_c, slab_d, slab_e), placed, blocks, window, near, copies)
    sums0 = read_sums(got0, head, 1, unknowns)
    scale = 1.0 / norm_parts(sums0)[0]
    h11, h21, _, _, _ = arnoldi_one(sums0, read_sums(got, head, 2, unknowns))
    inverse = 1.0 / h21
    sums = [jnp.zeros((R, LANES), f32) for _ in range(3)]
    for j in range(clusters):
        held = rows_of(image, j)
        first = b[:, j * LANES : (j + 1) * LANES] * scale
        second = (held - h11 * first) * inverse
        made = (0.5 * held + (rows_of(near, j) + rows_of(far, j)) - h11 * held) * inverse
        sums = [s + v * made for s, v in zip(sums, (first, second, made))]
        candidate[pl.ds(j * R, R), :] = made
    block = sums_tile(sums)
    for device in range(payload.shape[0]):
        payload[device] = block


def finish_kernel(per_group, unknowns, b, image, candidate, got0, got1, got2, solution_out, next_out):
    clusters = b.shape[1] // LANES
    head = clusters // per_group * R
    sums0 = read_sums(got0, head, 1, unknowns)
    start_norm, _ = norm_parts(sums0)
    h11, h21, v11, v22, v12 = arnoldi_one(sums0, read_sums(got1, head, 2, unknowns))
    h12, h22, ww = read_sums(got2, 0, 3, unknowns)
    uu = ww - 2.0 * (h12 * h12 + h22 * h22) + h12 * h12 * v11 + h22 * h22 * v22 + 2.0 * h12 * h22 * v12
    h32 = jnp.sqrt(jnp.maximum(uu, 0.0) + epsilon)
    g11 = h11 * h11 + h21 * h21
    g12 = h11 * h12 + h21 * h22
    g22 = h12 * h12 + h22 * h22 + h32 * h32
    t1, t2 = start_norm * h11, start_norm * h12
    det = g11 * g22 - g12 * g12
    y1 = (g22 * t1 - g12 * t2) / det
    y2 = (g11 * t2 - g12 * t1) / det
    scale, inverse, last = 1.0 / start_norm, 1.0 / h21, 1.0 / h32
    for j in range(clusters):
        span = slice(j * LANES, (j + 1) * LANES)
        first = b[:, span] * scale
        second = (rows_of(image, j) - h11 * first) * inverse
        solution_out[:, span] = y1 * first + y2 * second
        next_out[:, span] = (rows_of(candidate, j) - h12 * first - h22 * second) * last


def shifted(block, distance):
    size = lax.axis_size("rows")
    return lax.ppermute(block, "rows", [((i - distance) % size, i) for i in range(size)])


def on_device(
    right_sides, near_blocks, near_cols, near_counts, basis_in, target_basis, coupling, far_cols
):
    width = right_sides.shape[1]
    clusters, slots = near_cols.shape
    rank = basis_in.shape[1]
    per_group = LANES // rank
    head = clusters // per_group * R
    size = lax.axis_size("rows")
    every = clusters * size
    unknowns = float(width * size)
    rows = clusters * R

    def shape(*dims, dtype=f32):
        return jax.ShapeDtypeStruct(dims, dtype)

    basis = basis_in.reshape(clusters * rank, LANES)
    blocks = near_blocks.reshape(clusters * slots, LANES, LANES)
    lowered, payload = pl.pallas_call(
        functools.partial(start_kernel, per_group),
        out_shape=(shape(rows, LANES, dtype=bf16), shape(size, head + TAIL, LANES, dtype=bf16)),
        in_specs=[VMEM] * 2, out_specs=[VMEM] * 2, compiler_params=PARAMS, name="start",
    )(right_sides, basis)

    def exchange(block):
        return lax.all_to_all(block, "rows", 0, 0)

    def slabs_of(block):
        got = {d: shifted(block, d) for d in (2, 1, -1, -2)}
        return [got[2], got[1], block, got[-1], got[-2]]

    got0 = exchange(payload)
    slabs = slabs_of(lowered)

    high, low, target = pl.pallas_call(
        prepare_kernel,
        out_shape=(
            shape(slots * rank, rank * clusters, dtype=bf16),
            shape(slots * rank, rank * clusters, dtype=bf16),
            shape(rank * clusters, LANES, dtype=bf16),
        ),
        in_specs=[VMEM] * 2, out_specs=[VMEM] * 3, compiler_params=PARAMS, name="prepare",
    )(jnp.transpose(coupling, (1, 2, 3, 0)), target_basis.reshape(clusters * rank, LANES))
    reach = 2 * clusters
    start = lax.axis_index("rows") * clusters
    placed = (near_cols.T - start + reach) % every
    live = jnp.arange(slots, dtype=jnp.int32)[:, None] < near_counts[None, :]
    placed = jnp.where(live, placed, 5 * clusters).astype(jnp.int32)
    far_index = far_cols.T

    scratch = [
        pltpu.VMEM((clusters * slots, LANES, LANES), bf16),
        pltpu.VMEM((5 * rows + R, LANES), f32),
        pltpu.VMEM((size * head, LANES), f32),
        pltpu.VMEM((rows, LANES), f32),
        pltpu.VMEM((rows, LANES), f32),
        pltpu.SemaphoreType.DMA((BlockCopies.chunks,)),
    ]
    cost = pl.CostEstimate(flops=2 * 8 * blocks.size, bytes_accessed=2 * blocks.size, transcendentals=0)
    image, lowered, payload = pl.pallas_call(
        functools.partial(first_kernel, per_group, unknowns),
        out_shape=(
            shape(rows, LANES), shape(rows, LANES, dtype=bf16), shape(size, head + TAIL, LANES, dtype=bf16),
        ),
        in_specs=[VMEM] * 7 + [SMEM] * 2 + [ANY] + [VMEM] * 4,
        out_specs=[VMEM] * 3, scratch_shapes=scratch, compiler_params=PARAMS, cost_estimate=cost,
        name="operator_one",
    )(right_sides, *slabs, got0, placed, far_index, blocks, basis, high, low, target)
    got1 = exchange(payload)
    slabs = slabs_of(lowered)
    candidate, payload = pl.pallas_call(
        functools.partial(second_kernel, per_group, unknowns),
        out_shape=(shape(rows, LANES), shape(size, TAIL, LANES, dtype=bf16)),
        in_specs=[VMEM] * 9 + [SMEM] * 2 + [ANY] + [VMEM] * 3,
        out_specs=[VMEM] * 2, scratch_shapes=scratch, compiler_params=PARAMS, cost_estimate=cost,
        name="operator_two",
    )(right_sides, image, *slabs, got0, got1, placed, far_index, blocks, high, low, target)
    got2 = exchange(payload)
    return pl.pallas_call(
        functools.partial(finish_kernel, per_group, unknowns),
        out_shape=(shape(R, width), shape(R, width)),
        in_specs=[VMEM] * 6, out_specs=[VMEM] * 2, compiler_params=PARAMS, name="finish",
    )(right_sides, image, candidate, got0, got1, got2)


def solution(mesh):
    return jax.shard_map(
        on_device,
        mesh=mesh,
        in_specs=(
            P("groups", "rows"),
            P("rows", None, None, None),
            P("rows", None),
            P("rows"),
            P("rows", None, None),
            P("rows", None, None),
            P("rows", None, None, None),
            P("rows", None),
        ),
        out_specs=(P("groups", "rows"), P("groups", "rows")),
        check_vma=False,
    )
```

```python
import functools

import jax
import jax.numpy as jnp
from jax import lax
from jax.experimental import pallas as pl
from jax.experimental.pallas import tpu as pltpu
from jax.sharding import PartitionSpec as P

epsilon = 1e-06
f32, bf16 = jnp.float32, jnp.bfloat16
VMEM = pl.BlockSpec(memory_space=pltpu.VMEM)
SMEM = pl.BlockSpec(memory_space=pltpu.SMEM)
HBM = pl.BlockSpec(memory_space=pltpu.HBM)
R = 8
LANES = 128
SUM_SLOTS = 8
TAIL = 16
PARAMS = pltpu.CompilerParams(vmem_limit_bytes=24 * 1024 * 1024)


def lane_ids(rows=R):
    return lax.broadcasted_iota(jnp.int32, (rows, LANES), 1)


def rows_of(ref, j):
    return ref[pl.ds(j * R, R), :]


def dot(a, b, contract=(1, 0)):
    return lax.dot_general(a, b, (((contract[0],), (contract[1],)), ((), ())), preferred_element_type=f32)


def sums_tile(sums):
    lane = lane_ids()
    tile = jnp.zeros((R, LANES), f32)
    for t, partial in enumerate(sums):
        total = jnp.sum(partial, axis=1, keepdims=True)
        high = total.astype(bf16).astype(f32)
        middle = (total - high).astype(bf16).astype(f32)
        low = total - high - middle
        for part, value in enumerate((high, middle, low)):
            tile = jnp.where(lane == part * SUM_SLOTS + t, value, tile)
    return jnp.concatenate([tile, jnp.zeros((TAIL - R, LANES), f32)], axis=0).astype(bf16)


def read_sums(got, first_row, count, unknowns):
    total = jnp.zeros((R, LANES), f32)
    for device in range(got.shape[0]):
        total = total + got[device, pl.ds(first_row, TAIL), :].astype(f32)[:R]
    return [
        sum(total[:, p * SUM_SLOTS + t : p * SUM_SLOTS + t + 1] for p in range(3)) * (1.0 / unknowns)
        for t in range(count)
    ]


def compress(tiles, basis, group):
    stacked = jnp.concatenate(tiles, axis=0)
    high = stacked.astype(bf16)
    low = (stacked - high.astype(f32)).astype(bf16)
    both = dot(jnp.concatenate([high, low], axis=0), basis[pl.ds(group * LANES, LANES), :], (1, 1))
    rows = len(tiles) * R
    both = both[:rows] + both[rows:]
    lane = lane_ids()
    rank = LANES // len(tiles)
    tile = jnp.zeros((R, LANES), f32)
    for m in range(len(tiles)):
        tile = jnp.where(lane // rank == m, both[m * R : (m + 1) * R], tile)
    return tile


def write_payload(payload, tiles, basis, sums, per_group):
    groups = len(tiles) // per_group
    parts = [compress(tiles[g * per_group : (g + 1) * per_group], basis, g) for g in range(groups)]
    block = jnp.concatenate([jnp.concatenate(parts, axis=0).astype(bf16), sums_tile(sums)], axis=0)
    for device in range(payload.shape[0]):
        payload[device] = block


def start_kernel(per_group, b_hbm, basis_hbm, field, basis, lowered, payload, b, sems):
    copies = [
        pltpu.make_async_copy(b_hbm, b, sems.at[0]),
        pltpu.make_async_copy(basis_hbm, basis, sems.at[1]),
    ]
    for copy in copies:
        copy.start()
    for copy in copies:
        copy.wait()
    clusters = b.shape[1] // LANES
    tiles = [b[:, j * LANES : (j + 1) * LANES] for j in range(clusters)]
    field[...] = jnp.concatenate(tiles, axis=0)
    lowered[...] = jnp.concatenate(tiles, axis=0).astype(bf16)
    square = sum(t * t for t in tiles)
    write_payload(payload, tiles, basis, [square], per_group)


def prepare_kernel(
    coupling_hbm, target_hbm, blocks_hbm, high_out, low_out, target_out, turned, coupling, target, blocks,
    block_sems, sems,
):
    others = [
        pltpu.make_async_copy(coupling_hbm, coupling, sems.at[0]),
        pltpu.make_async_copy(target_hbm, target, sems.at[1]),
    ]
    for copy in others:
        copy.start()
    chunks = block_sems.shape[0]
    rows = blocks.shape[0] // chunks

    def copy_of(chunk):
        span = pl.ds(chunk * rows, rows)
        return pltpu.make_async_copy(blocks_hbm.at[span], blocks.at[span], block_sems.at[chunk])

    for chunk in range(chunks):
        copy_of(chunk).start()
    for copy in others:
        copy.wait()
    slots, rank, _, clusters = coupling.shape
    per_tile = LANES // clusters
    for s in range(rank // per_tile):
        pieces = [
            coupling[:, s * per_tile + p].reshape(slots * rank, clusters) for p in range(per_tile)
        ]
        tile = jnp.concatenate(pieces, axis=1)
        high = tile.astype(bf16)
        high_out[:, s * LANES : (s + 1) * LANES] = high
        low_out[:, s * LANES : (s + 1) * LANES] = (tile - high.astype(f32)).astype(bf16)
    size = rank * clusters
    row = lax.broadcasted_iota(jnp.int32, (size, size), 0)
    column = lax.broadcasted_iota(jnp.int32, (size, size), 1)
    wanted = (row % clusters) * rank + row // clusters
    target_out[...] = dot((column == wanted).astype(bf16), target[...]).astype(bf16)

    pairs_each = rows // (2 * slots)

    def body(chunk, carry):
        copy_of(chunk).wait()
        for inner in range(pairs_each):
            pair = chunk * pairs_each + inner
            for k in range(slots):
                for side in range(2):
                    block = blocks[(2 * pair + side) * slots + k]
                    turned[pair, k * LANES : (k + 1) * LANES, side * LANES : (side + 1) * LANES] = block.T
        return carry

    lax.fori_loop(0, chunks, body, 0)


def far_field(got, far_cols, high, low, target, table, clusters, rank, far):
    slots = far_cols.shape[0]
    per_group = LANES // rank
    groups = clusters // per_group
    head = groups * R
    for device in range(got.shape[0]):
        table[pl.ds(device * head, head), :] = got[device, pl.ds(0, head), :].astype(f32)
    lane = lane_ids()
    picked = []
    for i in range(clusters):
        tile = jnp.zeros((R, LANES), f32)
        for k in range(slots):
            j = far_cols[k, i]
            found = table[pl.ds(pl.multiple_of(lax.div(j, per_group) * R, R), R), :]
            shift = ((k - j) * rank) & (LANES - 1)
            tile = jnp.where(lane // rank == k, pltpu.roll(found, shift, 1), tile)
        picked.append(tile)
    picked = jnp.concatenate(picked, axis=0).astype(bf16)
    crossed = dot(picked, high[...]) + dot(picked, low[...])
    expanded_high, expanded_low = [], []
    for s in range(rank * clusters // LANES):
        tile = jnp.zeros((R, LANES), f32)
        for i in range(clusters):
            part = crossed[i * R : (i + 1) * R, s * LANES : (s + 1) * LANES]
            tile = jnp.where(lane % clusters == i, part, tile)
        tile_high = tile.astype(bf16).astype(f32)
        tile_low = tile - tile_high
        for source, kept in ((tile_high, expanded_high), (tile_low, expanded_low)):
            spread = [jnp.where(lane % clusters == i, source, 0.0) for i in range(clusters)]
            kept.append(jnp.concatenate(spread, axis=0).astype(bf16))
    far[...] = dot(jnp.concatenate(expanded_high, axis=1), target[...]) + dot(
        jnp.concatenate(expanded_low, axis=1), target[...]
    )


def near_field(slabs, placed, turned, window, near):
    rows = slabs[0].shape[0]
    for at, slab in enumerate(slabs):
        window[pl.ds(at * rows, rows), :] = slab[...].astype(f32)
    window[pl.ds(len(slabs) * rows, R), :] = jnp.zeros((R, LANES), f32)
    slots, clusters = placed.shape

    def fetch(k, i):
        return window[pl.ds(pl.multiple_of(placed[k, i] * R, R), R), :]

    for pair in range(clusters // 2):
        sources = [
            jnp.concatenate([fetch(k, 2 * pair), fetch(k, 2 * pair + 1)], axis=0).astype(bf16)
            for k in range(slots)
        ]
        both = dot(jnp.concatenate(sources, axis=1), turned[pair])
        near[pl.ds(2 * pair * R, R), :] = both[:R, :LANES]
        near[pl.ds((2 * pair + 1) * R, R), :] = both[R:, LANES:]


def norm_parts(sums):
    square = sums[0]
    whole = square + epsilon
    return jnp.sqrt(whole), square / whole


def first_kernel(
    per_group, unknowns, b, slab_a, slab_b, slab_c, slab_d, slab_e, got, placed, far_cols, turned,
    basis, high, low, target, image, lowered, payload, window, table, near, far,
):
    slots, clusters = placed.shape
    head = clusters // per_group * R
    far_field(got, far_cols, high, low, target, table, clusters, LANES // per_group, far)
    near_field((slab_a, slab_b, slab_c, slab_d, slab_e), placed, turned, window, near)
    start_norm, _ = norm_parts(read_sums(got, head, 1, unknowns))
    scale = 1.0 / start_norm
    cross = jnp.zeros((R, LANES), f32)
    square = jnp.zeros((R, LANES), f32)
    tiles = []
    for j in range(clusters):
        field = rows_of(b, j)
        made = (0.5 * field + (rows_of(near, j) + rows_of(far, j))) * scale
        cross = cross + (field * scale) * made
        square = square + made * made
        image[pl.ds(j * R, R), :] = made
        tiles.append(made)
    lowered[...] = jnp.concatenate(tiles, axis=0).astype(bf16)
    write_payload(payload, tiles, basis, [cross, square], per_group)


def arnoldi_one(sums0, sums1):
    _, v11 = norm_parts(sums0)
    h11 = sums1[0]
    uu = jnp.maximum(sums1[1] - 2.0 * h11 * h11 + h11 * h11 * v11, 0.0)
    h21 = jnp.sqrt(uu + epsilon)
    return h11, h21, v11, uu / (uu + epsilon), h11 * (1.0 - v11) / h21


def second_kernel(
    per_group, unknowns, b, image, slab_a, slab_b, slab_c, slab_d, slab_e, got0, got, placed, far_cols,
    turned, high, low, target, candidate, sums_out, window, table, near, far,
):
    slots, clusters = placed.shape
    head = clusters // per_group * R
    far_field(got, far_cols, high, low, target, table, clusters, LANES // per_group, far)
    near_field((slab_a, slab_b, slab_c, slab_d, slab_e), placed, turned, window, near)
    sums0 = read_sums(got0, head, 1, unknowns)
    scale = 1.0 / norm_parts(sums0)[0]
    h11, h21, _, _, _ = arnoldi_one(sums0, read_sums(got, head, 2, unknowns))
    inverse = 1.0 / h21
    sums = [jnp.zeros((R, LANES), f32) for _ in range(3)]
    for j in range(clusters):
        held = rows_of(image, j)
        first = rows_of(b, j) * scale
        second = (held - h11 * first) * inverse
        made = (0.5 * held + (rows_of(near, j) + rows_of(far, j)) - h11 * held) * inverse
        sums = [s + v * made for s, v in zip(sums, (first, second, made))]
        candidate[pl.ds(j * R, R), :] = made
    lane = lane_ids()
    tile = jnp.zeros((R, LANES), f32)
    for t, partial in enumerate(sums):
        tile = jnp.where(lane == t, jnp.sum(partial, axis=1, keepdims=True), tile)
    sums_out[...] = tile


def finish_kernel(per_group, unknowns, b, image, candidate, got0, got1, *rest):
    *got2, solution_out, next_out = rest
    clusters = b.shape[0] // R
    head = clusters // per_group * R
    sums0 = read_sums(got0, head, 1, unknowns)
    start_norm, _ = norm_parts(sums0)
    h11, h21, v11, v22, v12 = arnoldi_one(sums0, read_sums(got1, head, 2, unknowns))
    total = sum(part[...] for part in got2)
    h12, h22, ww = [total[:, t : t + 1] * (1.0 / unknowns) for t in range(3)]
    uu = ww - 2.0 * (h12 * h12 + h22 * h22) + h12 * h12 * v11 + h22 * h22 * v22 + 2.0 * h12 * h22 * v12
    h32 = jnp.sqrt(jnp.maximum(uu, 0.0) + epsilon)
    g11 = h11 * h11 + h21 * h21
    g12 = h11 * h12 + h21 * h22
    g22 = h12 * h12 + h22 * h22 + h32 * h32
    t1, t2 = start_norm * h11, start_norm * h12
    det = g11 * g22 - g12 * g12
    y1 = (g22 * t1 - g12 * t2) / det
    y2 = (g11 * t2 - g12 * t1) / det
    scale, inverse, last = 1.0 / start_norm, 1.0 / h21, 1.0 / h32
    for j in range(clusters):
        span = slice(j * LANES, (j + 1) * LANES)
        first = rows_of(b, j) * scale
        second = (rows_of(image, j) - h11 * first) * inverse
        solution_out[:, span] = y1 * first + y2 * second
        next_out[:, span] = (rows_of(candidate, j) - h12 * first - h22 * second) * last


def shifted(block, distance):
    size = lax.axis_size("rows")
    return lax.ppermute(block, "rows", [((i - distance) % size, i) for i in range(size)])


def stages():
    rest, stride, found = lax.axis_size("rows"), 1, []
    while rest > 1:
        length = 4 if rest % 4 == 0 else 2
        found.append((stride, length))
        stride, rest = stride * length, rest // length
    return found


def digit_parts(block, stride, length):
    size = lax.axis_size("rows")
    parts = [block]
    for step in range(1, length):
        parts.append(
            lax.ppermute(block, "rows", [(i, i ^ (step * stride)) for i in range(size)])
        )
    return parts


def on_device(
    right_sides, near_blocks, near_cols, near_counts, basis_in, target_basis, coupling, far_cols
):
    width = right_sides.shape[1]
    clusters, slots = near_cols.shape
    rank = basis_in.shape[1]
    per_group = LANES // rank
    head = clusters // per_group * R
    size = lax.axis_size("rows")
    every = clusters * size
    unknowns = float(width * size)
    rows = clusters * R

    def shape(*dims, dtype=f32):
        return jax.ShapeDtypeStruct(dims, dtype)

    def scratch(*dims, dtype=f32):
        return pltpu.VMEM(dims, dtype)

    basis = basis_in.reshape(clusters * rank, LANES)
    blocks = near_blocks.reshape(clusters * slots, LANES, LANES)
    field, basis, lowered, payload = pl.pallas_call(
        functools.partial(start_kernel, per_group),
        out_shape=(
            shape(rows, LANES), shape(clusters * rank, LANES, dtype=bf16), shape(rows, LANES, dtype=bf16),
            shape(size, head + TAIL, LANES, dtype=bf16),
        ),
        in_specs=[HBM] * 2, out_specs=[VMEM] * 4,
        scratch_shapes=[scratch(R, width), pltpu.SemaphoreType.DMA((2,))],
        compiler_params=PARAMS, name="start",
    )(right_sides, basis)

    def exchange(block):
        return lax.all_to_all(block, "rows", 0, 0)

    def slabs_of(block):
        got = {d: shifted(block, d) for d in (2, 1, -1, -2)}
        return [got[2], got[1], block, got[-1], got[-2]]

    got0 = exchange(payload)
    slabs = slabs_of(lowered)

    turned_shape = (clusters // 2, slots * LANES, 2 * LANES)
    high, low, target, turned = pl.pallas_call(
        prepare_kernel,
        out_shape=(
            shape(slots * rank, rank * clusters, dtype=bf16),
            shape(slots * rank, rank * clusters, dtype=bf16),
            shape(rank * clusters, LANES, dtype=bf16),
            shape(*turned_shape, dtype=bf16),
        ),
        in_specs=[HBM] * 3, out_specs=[VMEM] * 4,
        scratch_shapes=[
            scratch(slots, rank, rank, clusters), scratch(clusters * rank, LANES, dtype=bf16),
            scratch(clusters * slots, LANES, LANES, dtype=bf16),
            pltpu.SemaphoreType.DMA((8,)), pltpu.SemaphoreType.DMA((2,)),
        ],
        compiler_params=PARAMS, name="prepare",
    )(jnp.transpose(coupling, (1, 2, 3, 0)), target_basis.reshape(clusters * rank, LANES), blocks)
    reach = 2 * clusters
    start = lax.axis_index("rows") * clusters
    placed = (near_cols.T - start + reach) % every
    live = jnp.arange(slots, dtype=jnp.int32)[:, None] < near_counts[None, :]
    placed = jnp.where(live, placed, 5 * clusters).astype(jnp.int32)
    far_index = far_cols.T

    kept = [
        scratch(5 * rows + R, LANES), scratch(size * head, LANES), scratch(rows, LANES), scratch(rows, LANES),
    ]
    image, lowered, payload = pl.pallas_call(
        functools.partial(first_kernel, per_group, unknowns),
        out_shape=(
            shape(rows, LANES), shape(rows, LANES, dtype=bf16), shape(size, head + TAIL, LANES, dtype=bf16),
        ),
        in_specs=[VMEM] * 7 + [SMEM] * 2 + [VMEM] * 5,
        out_specs=[VMEM] * 3, scratch_shapes=kept, compiler_params=PARAMS, name="operator_one",
    )(field, *slabs, got0, placed, far_index, turned, basis, high, low, target)
    got1 = exchange(payload)
    slabs = slabs_of(lowered)
    candidate, sums = pl.pallas_call(
        functools.partial(second_kernel, per_group, unknowns),
        out_shape=(shape(rows, LANES), shape(R, LANES)),
        in_specs=[VMEM] * 9 + [SMEM] * 2 + [VMEM] * 4,
        out_specs=[VMEM] * 2, scratch_shapes=kept, compiler_params=PARAMS, name="operator_two",
    )(field, image, *slabs, got0, got1, placed, far_index, turned, high, low, target)
    parts = [sums]
    for stride, length in stages():
        parts = digit_parts(sum(parts), stride, length)
    return pl.pallas_call(
        functools.partial(finish_kernel, per_group, unknowns),
        out_shape=(shape(R, width), shape(R, width)),
        in_specs=[VMEM] * (5 + len(parts)), out_specs=[VMEM] * 2, compiler_params=PARAMS, name="finish",
    )(field, image, candidate, got0, got1, *parts)


def solution(mesh):
    return jax.shard_map(
        on_device,
        mesh=mesh,
        in_specs=(
            P("groups", "rows"),
            P("rows", None, None, None),
            P("rows", None),
            P("rows"),
            P("rows", None, None),
            P("rows", None, None),
            P("rows", None, None, None),
            P("rows", None),
        ),
        out_specs=(P("groups", "rows"), P("groups", "rows")),
        check_vma=False,
    )
```

```python
import functools

import jax
import jax.numpy as jnp
from jax import lax
from jax.experimental import pallas as pl
from jax.experimental.pallas import tpu as pltpu
from jax.sharding import PartitionSpec as P

epsilon = 1e-06
f32, bf16 = jnp.float32, jnp.bfloat16
VMEM = pl.BlockSpec(memory_space=pltpu.VMEM)
SMEM = pl.BlockSpec(memory_space=pltpu.SMEM)
HBM = pl.BlockSpec(memory_space=pltpu.HBM)
R = 8
LANES = 128
SUM_SLOTS = 8
TAIL = 16
PARAMS = pltpu.CompilerParams(vmem_limit_bytes=24 * 1024 * 1024)


def lane_ids(rows=R):
    return lax.broadcasted_iota(jnp.int32, (rows, LANES), 1)


def rows_of(ref, j):
    return ref[pl.ds(j * R, R), :]


def dot(a, b, contract=(1, 0)):
    return lax.dot_general(a, b, (((contract[0],), (contract[1],)), ((), ())), preferred_element_type=f32)


def sums_tile(sums):
    lane = lane_ids()
    tile = jnp.zeros((R, LANES), f32)
    for t, partial in enumerate(sums):
        total = jnp.sum(partial, axis=1, keepdims=True)
        high = total.astype(bf16).astype(f32)
        middle = (total - high).astype(bf16).astype(f32)
        low = total - high - middle
        for part, value in enumerate((high, middle, low)):
            tile = jnp.where(lane == part * SUM_SLOTS + t, value, tile)
    return jnp.concatenate([tile, jnp.zeros((TAIL - R, LANES), f32)], axis=0).astype(bf16)


def read_sums(got, first_row, count, unknowns):
    total = jnp.zeros((R, LANES), f32)
    for device in range(got.shape[0]):
        total = total + got[device, pl.ds(first_row, TAIL), :].astype(f32)[:R]
    return [
        sum(total[:, p * SUM_SLOTS + t : p * SUM_SLOTS + t + 1] for p in range(3)) * (1.0 / unknowns)
        for t in range(count)
    ]


def compress(tiles, basis, group):
    stacked = jnp.concatenate(tiles, axis=0)
    high = stacked.astype(bf16)
    low = (stacked - high.astype(f32)).astype(bf16)
    both = dot(jnp.concatenate([high, low], axis=0), basis[pl.ds(group * LANES, LANES), :], (1, 1))
    rows = len(tiles) * R
    both = both[:rows] + both[rows:]
    lane = lane_ids()
    rank = LANES // len(tiles)
    tile = jnp.zeros((R, LANES), f32)
    for m in range(len(tiles)):
        tile = jnp.where(lane // rank == m, both[m * R : (m + 1) * R], tile)
    return tile


def start_kernel(b_hbm, basis_hbm, field, basis, lowered, b, sems):
    copies = [
        pltpu.make_async_copy(b_hbm, b, sems.at[0]),
        pltpu.make_async_copy(basis_hbm, basis, sems.at[1]),
    ]
    for copy in copies:
        copy.start()
    copies[0].wait()
    clusters = b.shape[1] // LANES
    tiles = jnp.concatenate([b[:, j * LANES : (j + 1) * LANES] for j in range(clusters)], axis=0)
    field[...] = tiles
    lowered[...] = tiles.astype(bf16)
    copies[1].wait()


def compress_kernel(per_group, pairs, *refs):
    *fields, basis, payload = refs
    clusters = fields[0].shape[0] // R
    tiles = [rows_of(fields[-1], j) for j in range(clusters)]
    sums = [
        sum(rows_of(fields[f], j) * rows_of(fields[g], j) for j in range(clusters)) for f, g in pairs
    ]
    groups = clusters // per_group
    parts = [compress(tiles[g * per_group : (g + 1) * per_group], basis, g) for g in range(groups)]
    block = jnp.concatenate([jnp.concatenate(parts, axis=0).astype(bf16), sums_tile(sums)], axis=0)
    for device in range(payload.shape[0]):
        payload[device] = block


def prepare_kernel(
    coupling_hbm, target_hbm, blocks_hbm, high_out, low_out, target_out, turned, coupling, target, blocks,
    block_sems, sems,
):
    others = [
        pltpu.make_async_copy(coupling_hbm, coupling, sems.at[0]),
        pltpu.make_async_copy(target_hbm, target, sems.at[1]),
    ]
    for copy in others:
        copy.start()
    chunks = block_sems.shape[0]
    rows = blocks.shape[0] // chunks

    def copy_of(chunk):
        span = pl.ds(chunk * rows, rows)
        return pltpu.make_async_copy(blocks_hbm.at[span], blocks.at[span], block_sems.at[chunk])

    for chunk in range(chunks):
        copy_of(chunk).start()
    for copy in others:
        copy.wait()
    slots, rank, _, clusters = coupling.shape
    per_tile = LANES // clusters
    for s in range(rank // per_tile):
        pieces = [
            coupling[:, s * per_tile + p].reshape(slots * rank, clusters) for p in range(per_tile)
        ]
        tile = jnp.concatenate(pieces, axis=1)
        high = tile.astype(bf16)
        high_out[:, s * LANES : (s + 1) * LANES] = high
        low_out[:, s * LANES : (s + 1) * LANES] = (tile - high.astype(f32)).astype(bf16)
    size = rank * clusters
    row = lax.broadcasted_iota(jnp.int32, (size, size), 0)
    column = lax.broadcasted_iota(jnp.int32, (size, size), 1)
    wanted = (row % clusters) * rank + row // clusters
    target_out[...] = dot((column == wanted).astype(bf16), target[...]).astype(bf16)

    pairs_each = rows // (2 * slots)

    def body(chunk, carry):
        copy_of(chunk).wait()
        for inner in range(pairs_each):
            pair = chunk * pairs_each + inner
            for k in range(slots):
                for side in range(2):
                    block = blocks[(2 * pair + side) * slots + k]
                    turned[pair, k * LANES : (k + 1) * LANES, side * LANES : (side + 1) * LANES] = block.T
        return carry

    lax.fori_loop(0, chunks, body, 0)


def far_field(got, far_cols, high, low, target, table, clusters, rank, far):
    slots = far_cols.shape[0]
    per_group = LANES // rank
    groups = clusters // per_group
    head = groups * R
    for device in range(got.shape[0]):
        table[pl.ds(device * head, head), :] = got[device, pl.ds(0, head), :].astype(f32)
    lane = lane_ids()
    picked = []
    for i in range(clusters):
        tile = jnp.zeros((R, LANES), f32)
        for k in range(slots):
            j = far_cols[k, i]
            found = table[pl.ds(pl.multiple_of(lax.div(j, per_group) * R, R), R), :]
            shift = ((k - j) * rank) & (LANES - 1)
            tile = jnp.where(lane // rank == k, pltpu.roll(found, shift, 1), tile)
        picked.append(tile)
    picked = jnp.concatenate(picked, axis=0).astype(bf16)
    crossed = dot(picked, high[...]) + dot(picked, low[...])
    expanded_high, expanded_low = [], []
    for s in range(rank * clusters // LANES):
        tile = jnp.zeros((R, LANES), f32)
        for i in range(clusters):
            part = crossed[i * R : (i + 1) * R, s * LANES : (s + 1) * LANES]
            tile = jnp.where(lane % clusters == i, part, tile)
        tile_high = tile.astype(bf16).astype(f32)
        tile_low = tile - tile_high
        for source, kept in ((tile_high, expanded_high), (tile_low, expanded_low)):
            spread = [jnp.where(lane % clusters == i, source, 0.0) for i in range(clusters)]
            kept.append(jnp.concatenate(spread, axis=0).astype(bf16))
    far[...] = dot(jnp.concatenate(expanded_high, axis=1), target[...]) + dot(
        jnp.concatenate(expanded_low, axis=1), target[...]
    )


def near_kernel(*refs):
    *slabs, placed, turned, near, window = refs
    rows = slabs[0].shape[0]
    for at, slab in enumerate(slabs):
        window[pl.ds(at * rows, rows), :] = slab[...].astype(f32)
    window[pl.ds(len(slabs) * rows, R), :] = jnp.zeros((R, LANES), f32)
    slots, clusters = placed.shape

    def fetch(k, i):
        return window[pl.ds(pl.multiple_of(placed[k, i] * R, R), R), :]

    for pair in range(clusters // 2):
        sources = [
            jnp.concatenate([fetch(k, 2 * pair), fetch(k, 2 * pair + 1)], axis=0).astype(bf16)
            for k in range(slots)
        ]
        both = dot(jnp.concatenate(sources, axis=1), turned[pair])
        near[pl.ds(2 * pair * R, R), :] = both[:R, :LANES]
        near[pl.ds((2 * pair + 1) * R, R), :] = both[R:, LANES:]


def norm_parts(sums):
    square = sums[0]
    whole = square + epsilon
    return jnp.sqrt(whole), square / whole


def first_kernel(per_group, unknowns, b, near, got, far_cols, high, low, target, image, lowered, table, far):
    clusters = far_cols.shape[1]
    head = clusters // per_group * R
    far_field(got, far_cols, high, low, target, table, clusters, LANES // per_group, far)
    start_norm, _ = norm_parts(read_sums(got, head, 1, unknowns))
    scale = 1.0 / start_norm
    for j in range(0, clusters, 2):
        made = [
            (0.5 * rows_of(b, i) + (rows_of(near, i) + rows_of(far, i))) * scale for i in (j, j + 1)
        ]
        both = jnp.concatenate(made, axis=0)
        image[pl.ds(j * R, 2 * R), :] = both
        lowered[pl.ds(j * R, 2 * R), :] = both.astype(bf16)


def arnoldi_one(sums0, sums1):
    start_norm, v11 = norm_parts(sums0)
    h11 = sums1[0] * (1.0 / start_norm)
    uu = jnp.maximum(sums1[1] - 2.0 * h11 * h11 + h11 * h11 * v11, 0.0)
    h21 = jnp.sqrt(uu + epsilon)
    return h11, h21, v11, uu / (uu + epsilon), h11 * (1.0 - v11) / h21


def second_kernel(
    per_group, unknowns, b, image, near, got0, got, far_cols, high, low, target, candidate, sums_out, table, far,
):
    clusters = far_cols.shape[1]
    head = clusters // per_group * R
    far_field(got, far_cols, high, low, target, table, clusters, LANES // per_group, far)
    sums0 = read_sums(got0, head, 1, unknowns)
    scale = 1.0 / norm_parts(sums0)[0]
    h11, h21, _, _, _ = arnoldi_one(sums0, read_sums(got, head, 2, unknowns))
    inverse = 1.0 / h21
    sums = [jnp.zeros((R, LANES), f32) for _ in range(3)]
    for j in range(clusters):
        held = rows_of(image, j)
        first = rows_of(b, j) * scale
        second = (held - h11 * first) * inverse
        made = (0.5 * held + (rows_of(near, j) + rows_of(far, j)) - h11 * held) * inverse
        sums = [s + v * made for s, v in zip(sums, (first, second, made))]
        candidate[pl.ds(j * R, R), :] = made
    lane = lane_ids()
    tile = jnp.zeros((R, LANES), f32)
    for t, partial in enumerate(sums):
        tile = jnp.where(lane == t, jnp.sum(partial, axis=1, keepdims=True), tile)
    for device in range(sums_out.shape[0]):
        sums_out[device] = tile


def finish_kernel(per_group, unknowns, b, image, candidate, got0, got1, got2, solution_out, next_out):
    clusters = b.shape[0] // R
    head = clusters // per_group * R
    sums0 = read_sums(got0, head, 1, unknowns)
    start_norm, _ = norm_parts(sums0)
    h11, h21, v11, v22, v12 = arnoldi_one(sums0, read_sums(got1, head, 2, unknowns))
    total = sum(got2[device] for device in range(got2.shape[0]))
    h12, h22, ww = [total[:, t : t + 1] * (1.0 / unknowns) for t in range(3)]
    uu = ww - 2.0 * (h12 * h12 + h22 * h22) + h12 * h12 * v11 + h22 * h22 * v22 + 2.0 * h12 * h22 * v12
    h32 = jnp.sqrt(jnp.maximum(uu, 0.0) + epsilon)
    g11 = h11 * h11 + h21 * h21
    g12 = h11 * h12 + h21 * h22
    g22 = h12 * h12 + h22 * h22 + h32 * h32
    t1, t2 = start_norm * h11, start_norm * h12
    det = g11 * g22 - g12 * g12
    y1 = (g22 * t1 - g12 * t2) / det
    y2 = (g11 * t2 - g12 * t1) / det
    scale, inverse, last = 1.0 / start_norm, 1.0 / h21, 1.0 / h32
    for j in range(clusters):
        span = slice(j * LANES, (j + 1) * LANES)
        first = rows_of(b, j) * scale
        second = (rows_of(image, j) - h11 * first) * inverse
        solution_out[:, span] = y1 * first + y2 * second
        next_out[:, span] = (rows_of(candidate, j) - h12 * first - h22 * second) * last


def swapped(block, partner):
    return lax.ppermute(block, "rows", [(i, partner(i)) for i in range(lax.axis_size("rows"))])


def core_mate(i):
    return i ^ 1


def even_mate(i):
    return i ^ 2


def odd_mate(i):
    chip = i // 2
    other = chip + 1 if chip % 2 else chip - 1
    return 2 * (other % (lax.axis_size("rows") // 2)) + i % 2


def slabs_of(block):
    odd = swapped(block, odd_mate)
    even = swapped(block, even_mate)
    mate = swapped(block, core_mate)
    return [block, mate, even, odd, swapped(even, core_mate), swapped(odd, core_mate)]


def window_place(distance, clusters):
    me = lax.axis_index("rows")
    core, chip = me % 2, me // 2
    before, after = 3 - chip % 2, 2 + chip % 2
    slot = [
        before,
        jnp.where(core == 0, before + 2, 1),
        0,
        jnp.where(core == 0, 1, after + 2),
        after,
    ]
    slab = distance // clusters
    chosen = jnp.zeros_like(distance)
    for s, value in enumerate(slot):
        chosen = jnp.where(slab == s, value, chosen)
    return chosen * clusters + distance % clusters


def on_device(
    right_sides, near_blocks, near_cols, near_counts, basis_in, target_basis, coupling, far_cols
):
    width = right_sides.shape[1]
    clusters, slots = near_cols.shape
    rank = basis_in.shape[1]
    per_group = LANES // rank
    head = clusters // per_group * R
    size = lax.axis_size("rows")
    every = clusters * size
    unknowns = float(width * size)
    rows = clusters * R

    def shape(*dims, dtype=f32):
        return jax.ShapeDtypeStruct(dims, dtype)

    def scratch(*dims, dtype=f32):
        return pltpu.VMEM(dims, dtype)

    def in_hbm(array):
        return pltpu.with_memory_space_constraint(array, pltpu.HBM)

    def call(kernel, name, out, ins, *args, scratch_shapes=()):
        return pl.pallas_call(
            kernel, out_shape=out, in_specs=ins, out_specs=jax.tree.map(lambda _: VMEM, out),
            scratch_shapes=scratch_shapes, compiler_params=PARAMS, name=name,
        )(*args)

    def exchange(block):
        return lax.all_to_all(block, "rows", 0, 0)

    field, basis, lowered = call(
        start_kernel, "start",
        (shape(rows, LANES), shape(clusters * rank, LANES, dtype=bf16), shape(rows, LANES, dtype=bf16)),
        [HBM] * 2, in_hbm(right_sides), in_hbm(basis_in.reshape(clusters * rank, LANES)),
        scratch_shapes=[scratch(R, width), pltpu.SemaphoreType.DMA((2,))],
    )
    slabs = slabs_of(lowered)
    payload_shape = shape(size, head + TAIL, LANES, dtype=bf16)
    payload = call(
        functools.partial(compress_kernel, per_group, [(0, 0)]), "compress_one", payload_shape,
        [VMEM] * 2, field, basis,
    )
    got0 = exchange(payload)

    turned_shape = (clusters // 2, slots * LANES, 2 * LANES)
    high, low, target, turned = pl.pallas_call(
        prepare_kernel,
        out_shape=(
            shape(slots * rank, rank * clusters, dtype=bf16),
            shape(slots * rank, rank * clusters, dtype=bf16),
            shape(rank * clusters, LANES, dtype=bf16),
            pltpu.VMEM(turned_shape, bf16),
        ),
        in_specs=[HBM] * 3, out_specs=[VMEM] * 4,
        scratch_shapes=[
            scratch(slots, rank, rank, clusters), scratch(clusters * rank, LANES, dtype=bf16),
            scratch(clusters * slots, LANES, LANES, dtype=bf16),
            pltpu.SemaphoreType.DMA((8,)), pltpu.SemaphoreType.DMA((2,)),
        ],
        compiler_params=PARAMS, name="prepare",
    )(
        in_hbm(jnp.transpose(coupling, (1, 2, 3, 0))),
        in_hbm(target_basis.reshape(clusters * rank, LANES)),
        in_hbm(near_blocks.reshape(clusters * slots, LANES, LANES)),
    )
    turned = pltpu.with_memory_space_constraint(turned, pltpu.VMEM)
    reach = 2 * clusters
    start = lax.axis_index("rows") * clusters
    distance = (near_cols.T - start + reach) % every
    live = jnp.arange(slots, dtype=jnp.int32)[:, None] < near_counts[None, :]
    placed = jnp.where(live, window_place(distance, clusters), len(slabs) * clusters).astype(jnp.int32)
    far_index = far_cols.T

    def near_of(slabs):
        return call(
            near_kernel, "near", shape(rows, LANES), [VMEM] * len(slabs) + [SMEM, VMEM], *slabs, placed, turned,
            scratch_shapes=[scratch(len(slabs) * rows + R, LANES)],
        )

    kept = [scratch(size * head, LANES), scratch(rows, LANES)]
    near = near_of(slabs)
    image, lowered = call(
        functools.partial(first_kernel, per_group, unknowns), "far_one",
        (shape(rows, LANES), shape(rows, LANES, dtype=bf16)), [VMEM] * 3 + [SMEM] + [VMEM] * 3,
        field, near, got0, far_index, high, low, target, scratch_shapes=kept,
    )
    slabs = slabs_of(lowered)
    payload = call(
        functools.partial(compress_kernel, per_group, [(0, 1), (1, 1)]), "compress_two", payload_shape,
        [VMEM] * 3, field, image, basis,
    )
    got1 = exchange(payload)
    near = near_of(slabs)
    candidate, sums = call(
        functools.partial(second_kernel, per_group, unknowns), "far_two",
        (shape(rows, LANES), shape(size, R, LANES)), [VMEM] * 5 + [SMEM] + [VMEM] * 3,
        field, image, near, got0, got1, far_index, high, low, target, scratch_shapes=kept,
    )
    got2 = exchange(sums)
    return call(
        functools.partial(finish_kernel, per_group, unknowns), "finish", (shape(R, width), shape(R, width)),
        [VMEM] * 6, field, image, candidate, got0, got1, got2,
    )


def solution(mesh):
    return jax.shard_map(
        on_device,
        mesh=mesh,
        in_specs=(
            P("groups", "rows"),
            P("rows", None, None, None),
            P("rows", None),
            P("rows"),
            P("rows", None, None),
            P("rows", None, None),
            P("rows", None, None, None),
            P("rows", None),
        ),
        out_specs=(P("groups", "rows"), P("groups", "rows")),
        check_vma=False,
    )
```

```python
import functools

import jax
import jax.numpy as jnp
from jax import lax
from jax.experimental import pallas as pl
from jax.experimental.pallas import tpu as pltpu
from jax.sharding import PartitionSpec as P

epsilon = 1e-06
f32, bf16 = jnp.float32, jnp.bfloat16
VMEM = pl.BlockSpec(memory_space=pltpu.VMEM)
SMEM = pl.BlockSpec(memory_space=pltpu.SMEM)
HBM = pl.BlockSpec(memory_space=pltpu.HBM)
ANY = pl.BlockSpec(memory_space=pl.ANY)
R = 8
LANES = 128
SUM_SLOTS = 8
TAIL = 16
PARAMS = pltpu.CompilerParams(vmem_limit_bytes=24 * 1024 * 1024)


def lane_ids(rows=R):
    return lax.broadcasted_iota(jnp.int32, (rows, LANES), 1)


def rows_of(ref, j):
    return ref[pl.ds(j * R, R), :]


def dot(a, b, contract=(1, 0)):
    return lax.dot_general(a, b, (((contract[0],), (contract[1],)), ((), ())), preferred_element_type=f32)


def sums_tile(sums):
    lane = lane_ids()
    tile = jnp.zeros((R, LANES), f32)
    for t, partial in enumerate(sums):
        total = jnp.sum(partial, axis=1, keepdims=True)
        high = total.astype(bf16).astype(f32)
        middle = (total - high).astype(bf16).astype(f32)
        low = total - high - middle
        for part, value in enumerate((high, middle, low)):
            tile = jnp.where(lane == part * SUM_SLOTS + t, value, tile)
    return jnp.concatenate([tile, jnp.zeros((TAIL - R, LANES), f32)], axis=0).astype(bf16)


def read_sums(got, first_row, count, unknowns):
    total = jnp.zeros((R, LANES), f32)
    for device in range(got.shape[0]):
        total = total + got[device, pl.ds(first_row, TAIL), :].astype(f32)[:R]
    return [
        sum(total[:, p * SUM_SLOTS + t : p * SUM_SLOTS + t + 1] for p in range(3)) * (1.0 / unknowns)
        for t in range(count)
    ]


def compress(tiles, basis, group):
    stacked = jnp.concatenate(tiles, axis=0)
    high = stacked.astype(bf16)
    low = (stacked - high.astype(f32)).astype(bf16)
    both = dot(jnp.concatenate([high, low], axis=0), basis[pl.ds(group * LANES, LANES), :], (1, 1))
    rows = len(tiles) * R
    both = both[:rows] + both[rows:]
    lane = lane_ids()
    rank = LANES // len(tiles)
    tile = jnp.zeros((R, LANES), f32)
    for m in range(len(tiles)):
        tile = jnp.where(lane // rank == m, both[m * R : (m + 1) * R], tile)
    return tile


def start_kernel(b_hbm, basis_hbm, field, basis, lowered, b, sems):
    copies = [
        pltpu.make_async_copy(b_hbm, b, sems.at[0]),
        pltpu.make_async_copy(basis_hbm, basis, sems.at[1]),
    ]
    for copy in copies:
        copy.start()
    copies[0].wait()
    clusters = b.shape[1] // LANES
    tiles = jnp.concatenate([b[:, j * LANES : (j + 1) * LANES] for j in range(clusters)], axis=0)
    field[...] = tiles
    lowered[...] = tiles.astype(bf16)
    copies[1].wait()


def compress_kernel(per_group, pairs, *refs):
    *fields, basis, _, payload = refs
    clusters = fields[0].shape[0] // R
    tiles = [rows_of(fields[-1], j) for j in range(clusters)]
    sums = [
        sum(rows_of(fields[f], j) * rows_of(fields[g], j) for j in range(clusters)) for f, g in pairs
    ]
    groups = clusters // per_group
    parts = [compress(tiles[g * per_group : (g + 1) * per_group], basis, g) for g in range(groups)]
    block = jnp.concatenate([jnp.concatenate(parts, axis=0).astype(bf16), sums_tile(sums)], axis=0)
    for device in range(payload.shape[0]):
        payload[device] = block


def prepare_kernel(
    coupling_hbm, target_hbm, blocks_hbm, _, high_out, low_out, target_out, turned_hbm, coupling, target, blocks,
    turned, block_sems, turned_sems, sems,
):
    others = [
        pltpu.make_async_copy(coupling_hbm, coupling, sems.at[0]),
        pltpu.make_async_copy(target_hbm, target, sems.at[1]),
    ]
    for copy in others:
        copy.start()
    chunks = block_sems.shape[0]
    rows = blocks.shape[0] // chunks

    def copy_of(chunk):
        span = pl.ds(chunk * rows, rows)
        return pltpu.make_async_copy(blocks_hbm.at[span], blocks.at[span], block_sems.at[chunk])

    for chunk in range(chunks):
        copy_of(chunk).start()
    for copy in others:
        copy.wait()
    slots, rank, _, clusters = coupling.shape
    per_tile = LANES // clusters
    for s in range(rank // per_tile):
        pieces = [
            coupling[:, s * per_tile + p].reshape(slots * rank, clusters) for p in range(per_tile)
        ]
        tile = jnp.concatenate(pieces, axis=1)
        high = tile.astype(bf16)
        high_out[:, s * LANES : (s + 1) * LANES] = high
        low_out[:, s * LANES : (s + 1) * LANES] = (tile - high.astype(f32)).astype(bf16)
    size = rank * clusters
    row = lax.broadcasted_iota(jnp.int32, (size, size), 0)
    column = lax.broadcasted_iota(jnp.int32, (size, size), 1)
    wanted = (row % clusters) * rank + row // clusters
    target_out[...] = dot((column == wanted).astype(bf16), target[...]).astype(bf16)

    pairs_each = rows // (2 * slots)

    def copy_out(chunk):
        span = pl.ds(chunk * pairs_each, pairs_each)
        return pltpu.make_async_copy(turned.at[span], turned_hbm.at[span], turned_sems.at[chunk])

    def body(chunk, carry):
        copy_of(chunk).wait()
        for inner in range(pairs_each):
            pair = chunk * pairs_each + inner
            for k in range(slots):
                for side in range(2):
                    block = blocks[(2 * pair + side) * slots + k]
                    turned[pair, k * LANES : (k + 1) * LANES, side * LANES : (side + 1) * LANES] = block.T
        copy_out(chunk).start()
        return carry

    lax.fori_loop(0, chunks, body, 0)
    for chunk in range(chunks):
        copy_out(chunk).wait()


def far_field(got, far_cols, high, low, target, table, clusters, rank, far):
    slots = far_cols.shape[0]
    per_group = LANES // rank
    groups = clusters // per_group
    head = groups * R
    for device in range(got.shape[0]):
        table[pl.ds(device * head, head), :] = got[device, pl.ds(0, head), :].astype(f32)
    lane = lane_ids()
    picked = []
    for i in range(clusters):
        tile = jnp.zeros((R, LANES), f32)
        for k in range(slots):
            j = far_cols[k, i]
            found = table[pl.ds(pl.multiple_of(lax.div(j, per_group) * R, R), R), :]
            shift = ((k - j) * rank) & (LANES - 1)
            tile = jnp.where(lane // rank == k, pltpu.roll(found, shift, 1), tile)
        picked.append(tile)
    picked = jnp.concatenate(picked, axis=0).astype(bf16)
    crossed = dot(picked, high[...]) + dot(picked, low[...])
    expanded_high, expanded_low = [], []
    for s in range(rank * clusters // LANES):
        tile = jnp.zeros((R, LANES), f32)
        for i in range(clusters):
            part = crossed[i * R : (i + 1) * R, s * LANES : (s + 1) * LANES]
            tile = jnp.where(lane % clusters == i, part, tile)
        tile_high = tile.astype(bf16).astype(f32)
        tile_low = tile - tile_high
        for source, kept in ((tile_high, expanded_high), (tile_low, expanded_low)):
            spread = [jnp.where(lane % clusters == i, source, 0.0) for i in range(clusters)]
            kept.append(jnp.concatenate(spread, axis=0).astype(bf16))
    far[...] = dot(jnp.concatenate(expanded_high, axis=1), target[...]) + dot(
        jnp.concatenate(expanded_low, axis=1), target[...]
    )


def relay_kernel(even, odd, _, both):
    rows = even.shape[0]
    both[pl.ds(0, rows), :] = even[...]
    both[pl.ds(rows, rows), :] = odd[...]


def near_kernel(*refs):
    *slabs, placed, turned_hbm, near, window, turned, sems = refs
    slots, clusters = placed.shape
    chunks = sems.shape[0]
    pairs_each = turned.shape[0] // chunks

    def copy_of(chunk):
        span = pl.ds(chunk * pairs_each, pairs_each)
        return pltpu.make_async_copy(turned_hbm.at[span], turned.at[span], sems.at[chunk])

    for chunk in range(chunks):
        copy_of(chunk).start()
    at = 0
    for slab in slabs:
        window[pl.ds(at, slab.shape[0]), :] = slab[...].astype(f32)
        at += slab.shape[0]
    window[pl.ds(at, R), :] = jnp.zeros((R, LANES), f32)

    def fetch(k, i):
        return window[pl.ds(pl.multiple_of(placed[k, i] * R, R), R), :]

    for pair in range(clusters // 2):
        if pair % pairs_each == 0:
            copy_of(pair // pairs_each).wait()
        sources = [
            jnp.concatenate([fetch(k, 2 * pair), fetch(k, 2 * pair + 1)], axis=0).astype(bf16)
            for k in range(slots)
        ]
        both = dot(jnp.concatenate(sources, axis=1), turned[pair])
        near[pl.ds(2 * pair * R, R), :] = both[:R, :LANES]
        near[pl.ds((2 * pair + 1) * R, R), :] = both[R:, LANES:]


def norm_parts(sums):
    square = sums[0]
    whole = square + epsilon
    return jnp.sqrt(whole), square / whole


def first_kernel(per_group, unknowns, b, near, got, far_cols, high, low, target, image, lowered, table, far):
    clusters = far_cols.shape[1]
    head = clusters // per_group * R
    far_field(got, far_cols, high, low, target, table, clusters, LANES // per_group, far)
    start_norm, _ = norm_parts(read_sums(got, head, 1, unknowns))
    scale = 1.0 / start_norm
    for j in range(0, clusters, 2):
        made = [
            (0.5 * rows_of(b, i) + (rows_of(near, i) + rows_of(far, i))) * scale for i in (j, j + 1)
        ]
        both = jnp.concatenate(made, axis=0)
        image[pl.ds(j * R, 2 * R), :] = both
        lowered[pl.ds(j * R, 2 * R), :] = both.astype(bf16)


def arnoldi_one(sums0, sums1):
    start_norm, v11 = norm_parts(sums0)
    h11 = sums1[0] * (1.0 / start_norm)
    uu = jnp.maximum(sums1[1] - 2.0 * h11 * h11 + h11 * h11 * v11, 0.0)
    h21 = jnp.sqrt(uu + epsilon)
    return h11, h21, v11, uu / (uu + epsilon), h11 * (1.0 - v11) / h21


def second_kernel(
    per_group, unknowns, b, image, near, got0, got, far_cols, high, low, target, candidate, sums_out, table, far,
):
    clusters = far_cols.shape[1]
    head = clusters // per_group * R
    far_field(got, far_cols, high, low, target, table, clusters, LANES // per_group, far)
    sums0 = read_sums(got0, head, 1, unknowns)
    scale = 1.0 / norm_parts(sums0)[0]
    h11, h21, _, _, _ = arnoldi_one(sums0, read_sums(got, head, 2, unknowns))
    inverse = 1.0 / h21
    sums = [jnp.zeros((R, LANES), f32) for _ in range(3)]
    for j in range(clusters):
        held = rows_of(image, j)
        first = rows_of(b, j) * scale
        second = (held - h11 * first) * inverse
        made = (0.5 * held + (rows_of(near, j) + rows_of(far, j)) - h11 * held) * inverse
        sums = [s + v * made for s, v in zip(sums, (first, second, made))]
        candidate[pl.ds(j * R, R), :] = made
    lane = lane_ids()
    tile = jnp.zeros((R, LANES), f32)
    for t, partial in enumerate(sums):
        tile = jnp.where(lane == t, jnp.sum(partial, axis=1, keepdims=True), tile)
    for device in range(sums_out.shape[0]):
        sums_out[device] = tile


def finish_kernel(per_group, unknowns, b, image, candidate, got0, got1, got2, solution_out, next_out):
    clusters = b.shape[0] // R
    head = clusters // per_group * R
    sums0 = read_sums(got0, head, 1, unknowns)
    start_norm, _ = norm_parts(sums0)
    h11, h21, v11, v22, v12 = arnoldi_one(sums0, read_sums(got1, head, 2, unknowns))
    total = sum(got2[device] for device in range(got2.shape[0]))
    h12, h22, ww = [total[:, t : t + 1] * (1.0 / unknowns) for t in range(3)]
    uu = ww - 2.0 * (h12 * h12 + h22 * h22) + h12 * h12 * v11 + h22 * h22 * v22 + 2.0 * h12 * h22 * v12
    h32 = jnp.sqrt(jnp.maximum(uu, 0.0) + epsilon)
    g11 = h11 * h11 + h21 * h21
    g12 = h11 * h12 + h21 * h22
    g22 = h12 * h12 + h22 * h22 + h32 * h32
    t1, t2 = start_norm * h11, start_norm * h12
    det = g11 * g22 - g12 * g12
    y1 = (g22 * t1 - g12 * t2) / det
    y2 = (g11 * t2 - g12 * t1) / det
    scale, inverse, last = 1.0 / start_norm, 1.0 / h21, 1.0 / h32
    for j in range(clusters):
        span = slice(j * LANES, (j + 1) * LANES)
        first = rows_of(b, j) * scale
        second = (rows_of(image, j) - h11 * first) * inverse
        solution_out[:, span] = y1 * first + y2 * second
        next_out[:, span] = (rows_of(candidate, j) - h12 * first - h22 * second) * last


def swapped(block, partner):
    return lax.ppermute(block, "rows", [(i, partner(i)) for i in range(lax.axis_size("rows"))])


def core_mate(i):
    return i ^ 1


def even_mate(i):
    return i ^ 2


def odd_mate(i):
    chip = i // 2
    other = chip + 1 if chip % 2 else chip - 1
    return 2 * (other % (lax.axis_size("rows") // 2)) + i % 2


def sends_of(block):
    return [block] + [swapped(block, partner) for partner in (core_mate, even_mate, odd_mate)]


def window_place(distance, clusters):
    me = lax.axis_index("rows")
    core, chip = me % 2, me // 2
    before, after = 3 - chip % 2, 2 + chip % 2
    slot = [
        before,
        jnp.where(core == 0, before + 2, 1),
        0,
        jnp.where(core == 0, 1, after + 2),
        after,
    ]
    slab = distance // clusters
    chosen = jnp.zeros_like(distance)
    for s, value in enumerate(slot):
        chosen = jnp.where(slab == s, value, chosen)
    return chosen * clusters + distance % clusters


def on_device(
    right_sides, near_blocks, near_cols, near_counts, basis_in, target_basis, coupling, far_cols
):
    width = right_sides.shape[1]
    clusters, slots = near_cols.shape
    rank = basis_in.shape[1]
    per_group = LANES // rank
    head = clusters // per_group * R
    size = lax.axis_size("rows")
    every = clusters * size
    unknowns = float(width * size)
    rows = clusters * R

    def shape(*dims, dtype=f32):
        return jax.ShapeDtypeStruct(dims, dtype)

    def scratch(*dims, dtype=f32):
        return pltpu.VMEM(dims, dtype)

    def in_hbm(array):
        return pltpu.with_memory_space_constraint(array, pltpu.HBM)

    def call(kernel, name, out, ins, *args, scratch_shapes=(), cost_estimate=None):
        return pl.pallas_call(
            kernel, out_shape=out, in_specs=ins, out_specs=jax.tree.map(lambda _: VMEM, out),
            scratch_shapes=scratch_shapes, compiler_params=PARAMS, name=name,
            cost_estimate=cost_estimate,
        )(*args)

    def exchange(block):
        return lax.all_to_all(block, "rows", 0, 0)

    field, basis, lowered = call(
        start_kernel, "start",
        (shape(rows, LANES), shape(clusters * rank, LANES, dtype=bf16), shape(rows, LANES, dtype=bf16)),
        [HBM] * 2, in_hbm(right_sides), in_hbm(basis_in.reshape(clusters * rank, LANES)),
        scratch_shapes=[scratch(R, width), pltpu.SemaphoreType.DMA((2,))],
    )
    held = sends_of(lowered)
    payload_shape = shape(size, head + TAIL, LANES, dtype=bf16)
    payload = call(
        functools.partial(compress_kernel, per_group, [(0, 0)]), "compress_one", payload_shape,
        [VMEM] * 2 + [ANY], field, basis, held[1],
    )
    got0 = exchange(payload)

    def relayed(held, payload):
        both = call(
            relay_kernel, "relay", shape(2 * rows, LANES, dtype=bf16), [VMEM] * 2 + [ANY], *held[2:], payload
        )
        return swapped(both, core_mate)

    turned_shape = (clusters // 2, slots * LANES, 2 * LANES)
    high, low, target, turned = pl.pallas_call(
        prepare_kernel,
        out_shape=(
            shape(slots * rank, rank * clusters, dtype=bf16),
            shape(slots * rank, rank * clusters, dtype=bf16),
            shape(rank * clusters, LANES, dtype=bf16),
            pltpu.HBM(turned_shape, bf16),
        ),
        in_specs=[HBM] * 3 + [ANY], out_specs=[VMEM] * 3 + [HBM],
        scratch_shapes=[
            scratch(slots, rank, rank, clusters), scratch(clusters * rank, LANES, dtype=bf16),
            scratch(clusters * slots, LANES, LANES, dtype=bf16), scratch(*turned_shape, dtype=bf16),
            pltpu.SemaphoreType.DMA((8,)), pltpu.SemaphoreType.DMA((8,)), pltpu.SemaphoreType.DMA((2,)),
        ],
        compiler_params=PARAMS, name="prepare",
        cost_estimate=pl.CostEstimate(flops=0, bytes_accessed=4 * near_blocks.size, transcendentals=0),
    )(
        in_hbm(jnp.transpose(coupling, (1, 2, 3, 0))),
        in_hbm(target_basis.reshape(clusters * rank, LANES)),
        in_hbm(near_blocks.reshape(clusters * slots, LANES, LANES)),
        payload,
    )
    turned = in_hbm(turned)
    reach = 2 * clusters
    start = lax.axis_index("rows") * clusters
    distance = (near_cols.T - start + reach) % every
    live = jnp.arange(slots, dtype=jnp.int32)[:, None] < near_counts[None, :]
    placed = jnp.where(live, window_place(distance, clusters), 6 * clusters).astype(jnp.int32)
    far_index = far_cols.T

    def near_of(slabs):
        return call(
            near_kernel, "near", shape(rows, LANES), [VMEM] * len(slabs) + [SMEM, HBM], *slabs, placed, turned,
            scratch_shapes=[
                scratch(6 * rows + R, LANES), scratch(*turned_shape, dtype=bf16),
                pltpu.SemaphoreType.DMA((8,)),
            ],
            cost_estimate=pl.CostEstimate(
                flops=32 * near_blocks.size, bytes_accessed=2 * near_blocks.size, transcendentals=0
            ),
        )

    kept = [scratch(size * head, LANES), scratch(rows, LANES)]
    near = near_of(held + [relayed(held, payload)])
    image, lowered = call(
        functools.partial(first_kernel, per_group, unknowns), "far_one",
        (shape(rows, LANES), shape(rows, LANES, dtype=bf16)), [VMEM] * 3 + [SMEM] + [VMEM] * 3,
        field, near, got0, far_index, high, low, target, scratch_shapes=kept,
    )
    held = sends_of(lowered)
    payload = call(
        functools.partial(compress_kernel, per_group, [(0, 1), (1, 1)]), "compress_two", payload_shape,
        [VMEM] * 3 + [ANY], field, image, basis, held[1],
    )
    got1 = exchange(payload)
    near = near_of(held + [relayed(held, payload)])
    candidate, sums = call(
        functools.partial(second_kernel, per_group, unknowns), "far_two",
        (shape(rows, LANES), shape(size, R, LANES)), [VMEM] * 5 + [SMEM] + [VMEM] * 3,
        field, image, near, got0, got1, far_index, high, low, target, scratch_shapes=kept,
    )
    got2 = exchange(sums)
    return call(
        functools.partial(finish_kernel, per_group, unknowns), "finish", (shape(R, width), shape(R, width)),
        [VMEM] * 6, field, image, candidate, got0, got1, got2,
    )


def solution(mesh):
    return jax.shard_map(
        on_device,
        mesh=mesh,
        in_specs=(
            P("groups", "rows"),
            P("rows", None, None, None),
            P("rows", None),
            P("rows"),
            P("rows", None, None),
            P("rows", None, None),
            P("rows", None, None, None),
            P("rows", None),
        ),
        out_specs=(P("groups", "rows"), P("groups", "rows")),
        check_vma=False,
    )
```

```python
import functools

import jax
import jax.numpy as jnp
from jax import lax
from jax.experimental import pallas as pl
from jax.experimental.pallas import tpu as pltpu
from jax.sharding import PartitionSpec as P

epsilon = 1e-06
f32, bf16 = jnp.float32, jnp.bfloat16
VMEM = pl.BlockSpec(memory_space=pltpu.VMEM)
SMEM = pl.BlockSpec(memory_space=pltpu.SMEM)
HBM = pl.BlockSpec(memory_space=pltpu.HBM)
ANY = pl.BlockSpec(memory_space=pl.ANY)
R = 8
LANES = 128
SUM_SLOTS = 8
TAIL = 16
PARAMS = pltpu.CompilerParams(vmem_limit_bytes=24 * 1024 * 1024)


def lane_ids(rows=R):
    return lax.broadcasted_iota(jnp.int32, (rows, LANES), 1)


def rows_of(ref, j):
    return ref[pl.ds(j * R, R), :]


def dot(a, b, contract=(1, 0)):
    return lax.dot_general(a, b, (((contract[0],), (contract[1],)), ((), ())), preferred_element_type=f32)


def sums_tile(sums):
    lane = lane_ids()
    tile = jnp.zeros((R, LANES), f32)
    for t, partial in enumerate(sums):
        total = jnp.sum(partial, axis=1, keepdims=True)
        high = total.astype(bf16).astype(f32)
        middle = (total - high).astype(bf16).astype(f32)
        low = total - high - middle
        for part, value in enumerate((high, middle, low)):
            tile = jnp.where(lane == part * SUM_SLOTS + t, value, tile)
    return jnp.concatenate([tile, jnp.zeros((TAIL - R, LANES), f32)], axis=0).astype(bf16)


def read_sums(got, first_row, count, unknowns):
    total = jnp.zeros((R, LANES), f32)
    for device in range(got.shape[0]):
        total = total + got[device, pl.ds(first_row, TAIL), :].astype(f32)[:R]
    return [
        sum(total[:, p * SUM_SLOTS + t : p * SUM_SLOTS + t + 1] for p in range(3)) * (1.0 / unknowns)
        for t in range(count)
    ]


def compress(tiles, basis, group):
    stacked = jnp.concatenate(tiles, axis=0)
    high = stacked.astype(bf16)
    low = (stacked - high.astype(f32)).astype(bf16)
    both = dot(jnp.concatenate([high, low], axis=0), basis[pl.ds(group * LANES, LANES), :], (1, 1))
    rows = len(tiles) * R
    both = both[:rows] + both[rows:]
    lane = lane_ids()
    rank = LANES // len(tiles)
    tile = jnp.zeros((R, LANES), f32)
    for m in range(len(tiles)):
        tile = jnp.where(lane // rank == m, both[m * R : (m + 1) * R], tile)
    return tile


def start_kernel(b_hbm, basis_hbm, field, basis, lowered, b, sems):
    copies = [
        pltpu.make_async_copy(b_hbm, b, sems.at[0]),
        pltpu.make_async_copy(basis_hbm, basis, sems.at[1]),
    ]
    for copy in copies:
        copy.start()
    copies[0].wait()
    clusters = b.shape[1] // LANES
    tiles = jnp.concatenate([b[:, j * LANES : (j + 1) * LANES] for j in range(clusters)], axis=0)
    field[...] = tiles
    lowered[...] = tiles.astype(bf16)
    copies[1].wait()


def compress_kernel(per_group, pairs, *refs):
    *fields, basis, payload = refs
    clusters = fields[0].shape[0] // R
    tiles = [rows_of(fields[-1], j) for j in range(clusters)]
    sums = [
        sum(rows_of(fields[f], j) * rows_of(fields[g], j) for j in range(clusters)) for f, g in pairs
    ]
    groups = clusters // per_group
    parts = [compress(tiles[g * per_group : (g + 1) * per_group], basis, g) for g in range(groups)]
    block = jnp.concatenate([jnp.concatenate(parts, axis=0).astype(bf16), sums_tile(sums)], axis=0)
    for device in range(payload.shape[0]):
        payload[device] = block


def prepare_kernel(
    coupling_hbm, target_hbm, blocks_hbm, _, high_out, low_out, target_out, turned_hbm, coupling, target, blocks,
    turned, block_sems, turned_sems, sems,
):
    others = [
        pltpu.make_async_copy(coupling_hbm, coupling, sems.at[0]),
        pltpu.make_async_copy(target_hbm, target, sems.at[1]),
    ]
    for copy in others:
        copy.start()
    chunks = block_sems.shape[0]
    rows = blocks.shape[0] // chunks

    def copy_of(chunk):
        span = pl.ds(chunk * rows, rows)
        return pltpu.make_async_copy(blocks_hbm.at[span], blocks.at[span], block_sems.at[chunk])

    for chunk in range(chunks):
        copy_of(chunk).start()
    for copy in others:
        copy.wait()
    slots, rank, _, clusters = coupling.shape
    per_tile = LANES // clusters
    for s in range(rank // per_tile):
        pieces = [
            coupling[:, s * per_tile + p].reshape(slots * rank, clusters) for p in range(per_tile)
        ]
        tile = jnp.concatenate(pieces, axis=1)
        high = tile.astype(bf16)
        high_out[:, s * LANES : (s + 1) * LANES] = high
        low_out[:, s * LANES : (s + 1) * LANES] = (tile - high.astype(f32)).astype(bf16)
    size = rank * clusters
    row = lax.broadcasted_iota(jnp.int32, (size, size), 0)
    column = lax.broadcasted_iota(jnp.int32, (size, size), 1)
    wanted = (row % clusters) * rank + row // clusters
    target_out[...] = dot((column == wanted).astype(bf16), target[...]).astype(bf16)

    pairs_each = rows // (2 * slots)

    def copy_out(chunk):
        span = pl.ds(chunk * pairs_each, pairs_each)
        return pltpu.make_async_copy(turned.at[span], turned_hbm.at[span], turned_sems.at[chunk])

    def body(chunk, carry):
        copy_of(chunk).wait()
        for inner in range(pairs_each):
            pair = chunk * pairs_each + inner
            for k in range(slots):
                for side in range(2):
                    block = blocks[(2 * pair + side) * slots + k]
                    turned[pair, k * LANES : (k + 1) * LANES, side * LANES : (side + 1) * LANES] = block.T
        copy_out(chunk).start()
        return carry

    lax.fori_loop(0, chunks, body, 0)
    for chunk in range(chunks):
        copy_out(chunk).wait()


def far_field(got, far_cols, high, low, target, table, clusters, rank, far):
    slots = far_cols.shape[0]
    per_group = LANES // rank
    groups = clusters // per_group
    head = groups * R
    for device in range(got.shape[0]):
        table[pl.ds(device * head, head), :] = got[device, pl.ds(0, head), :].astype(f32)
    lane = lane_ids()
    picked = []
    for i in range(clusters):
        tile = jnp.zeros((R, LANES), f32)
        for k in range(slots):
            j = far_cols[k, i]
            found = table[pl.ds(pl.multiple_of(lax.div(j, per_group) * R, R), R), :]
            shift = ((k - j) * rank) & (LANES - 1)
            tile = jnp.where(lane // rank == k, pltpu.roll(found, shift, 1), tile)
        picked.append(tile)
    picked = jnp.concatenate(picked, axis=0).astype(bf16)
    crossed = dot(picked, high[...]) + dot(picked, low[...])
    expanded_high, expanded_low = [], []
    for s in range(rank * clusters // LANES):
        tile = jnp.zeros((R, LANES), f32)
        for i in range(clusters):
            part = crossed[i * R : (i + 1) * R, s * LANES : (s + 1) * LANES]
            tile = jnp.where(lane % clusters == i, part, tile)
        tile_high = tile.astype(bf16).astype(f32)
        tile_low = tile - tile_high
        for source, kept in ((tile_high, expanded_high), (tile_low, expanded_low)):
            spread = [jnp.where(lane % clusters == i, source, 0.0) for i in range(clusters)]
            kept.append(jnp.concatenate(spread, axis=0).astype(bf16))
    far[...] = dot(jnp.concatenate(expanded_high, axis=1), target[...]) + dot(
        jnp.concatenate(expanded_low, axis=1), target[...]
    )


def relay_kernel(even, odd, _, both):
    rows = even.shape[0]
    both[pl.ds(0, rows), :] = even[...]
    both[pl.ds(rows, rows), :] = odd[...]


def near_kernel(*refs):
    *slabs, placed, turned_hbm, near, window, turned, sems = refs
    slots, clusters = placed.shape
    chunks = sems.shape[0]
    pairs_each = turned.shape[0] // chunks

    def copy_of(chunk):
        span = pl.ds(chunk * pairs_each, pairs_each)
        return pltpu.make_async_copy(turned_hbm.at[span], turned.at[span], sems.at[chunk])

    for chunk in range(chunks):
        copy_of(chunk).start()
    at = 0
    for slab in slabs:
        window[pl.ds(at, slab.shape[0]), :] = slab[...].astype(f32)
        at += slab.shape[0]
    window[pl.ds(at, R), :] = jnp.zeros((R, LANES), f32)

    def fetch(k, i):
        return window[pl.ds(pl.multiple_of(placed[k, i] * R, R), R), :]

    for pair in range(clusters // 2):
        if pair % pairs_each == 0:
            copy_of(pair // pairs_each).wait()
        sources = [
            jnp.concatenate([fetch(k, 2 * pair), fetch(k, 2 * pair + 1)], axis=0).astype(bf16)
            for k in range(slots)
        ]
        both = dot(jnp.concatenate(sources, axis=1), turned[pair])
        near[pl.ds(2 * pair * R, R), :] = both[:R, :LANES]
        near[pl.ds((2 * pair + 1) * R, R), :] = both[R:, LANES:]


def norm_parts(sums):
    square = sums[0]
    whole = square + epsilon
    return jnp.sqrt(whole), square / whole


def first_kernel(per_group, unknowns, b, near, got, far_cols, high, low, target, image, lowered, table, far):
    clusters = far_cols.shape[1]
    head = clusters // per_group * R
    far_field(got, far_cols, high, low, target, table, clusters, LANES // per_group, far)
    start_norm, _ = norm_parts(read_sums(got, head, 1, unknowns))
    scale = 1.0 / start_norm
    for j in range(0, clusters, 2):
        made = [
            (0.5 * rows_of(b, i) + (rows_of(near, i) + rows_of(far, i))) * scale for i in (j, j + 1)
        ]
        both = jnp.concatenate(made, axis=0)
        image[pl.ds(j * R, 2 * R), :] = both
        lowered[pl.ds(j * R, 2 * R), :] = both.astype(bf16)


def arnoldi_one(sums0, sums1):
    start_norm, v11 = norm_parts(sums0)
    h11 = sums1[0] * (1.0 / start_norm)
    uu = jnp.maximum(sums1[1] - 2.0 * h11 * h11 + h11 * h11 * v11, 0.0)
    h21 = jnp.sqrt(uu + epsilon)
    return h11, h21, v11, uu / (uu + epsilon), h11 * (1.0 - v11) / h21


def second_kernel(
    per_group, unknowns, b, image, near, got0, got, far_cols, high, low, target, candidate, sums_out, table, far,
):
    clusters = far_cols.shape[1]
    head = clusters // per_group * R
    far_field(got, far_cols, high, low, target, table, clusters, LANES // per_group, far)
    sums0 = read_sums(got0, head, 1, unknowns)
    scale = 1.0 / norm_parts(sums0)[0]
    h11, h21, _, _, _ = arnoldi_one(sums0, read_sums(got, head, 2, unknowns))
    inverse = 1.0 / h21
    sums = [jnp.zeros((R, LANES), f32) for _ in range(3)]
    for j in range(clusters):
        held = rows_of(image, j)
        first = rows_of(b, j) * scale
        second = (held - h11 * first) * inverse
        made = (0.5 * held + (rows_of(near, j) + rows_of(far, j)) - h11 * held) * inverse
        sums = [s + v * made for s, v in zip(sums, (first, second, made))]
        candidate[pl.ds(j * R, R), :] = made
    lane = lane_ids()
    tile = jnp.zeros((R, LANES), f32)
    for t, partial in enumerate(sums):
        tile = jnp.where(lane == t, jnp.sum(partial, axis=1, keepdims=True), tile)
    for device in range(sums_out.shape[0]):
        sums_out[device] = tile


def finish_kernel(per_group, unknowns, b, image, candidate, got0, got1, got2, solution_out, next_out):
    clusters = b.shape[0] // R
    head = clusters // per_group * R
    sums0 = read_sums(got0, head, 1, unknowns)
    start_norm, _ = norm_parts(sums0)
    h11, h21, v11, v22, v12 = arnoldi_one(sums0, read_sums(got1, head, 2, unknowns))
    total = sum(got2[device] for device in range(got2.shape[0]))
    h12, h22, ww = [total[:, t : t + 1] * (1.0 / unknowns) for t in range(3)]
    uu = ww - 2.0 * (h12 * h12 + h22 * h22) + h12 * h12 * v11 + h22 * h22 * v22 + 2.0 * h12 * h22 * v12
    h32 = jnp.sqrt(jnp.maximum(uu, 0.0) + epsilon)
    g11 = h11 * h11 + h21 * h21
    g12 = h11 * h12 + h21 * h22
    g22 = h12 * h12 + h22 * h22 + h32 * h32
    t1, t2 = start_norm * h11, start_norm * h12
    det = g11 * g22 - g12 * g12
    y1 = (g22 * t1 - g12 * t2) / det
    y2 = (g11 * t2 - g12 * t1) / det
    scale, inverse, last = 1.0 / start_norm, 1.0 / h21, 1.0 / h32
    for j in range(clusters):
        span = slice(j * LANES, (j + 1) * LANES)
        first = rows_of(b, j) * scale
        second = (rows_of(image, j) - h11 * first) * inverse
        solution_out[:, span] = y1 * first + y2 * second
        next_out[:, span] = (rows_of(candidate, j) - h12 * first - h22 * second) * last


def swapped(block, partner):
    return lax.ppermute(block, "rows", [(i, partner(i)) for i in range(lax.axis_size("rows"))])


def core_mate(i):
    return i ^ 1


def even_mate(i):
    return i ^ 2


def odd_mate(i):
    chip = i // 2
    other = chip + 1 if chip % 2 else chip - 1
    return 2 * (other % (lax.axis_size("rows") // 2)) + i % 2


def sends_of(block):
    return [block] + [swapped(block, partner) for partner in (core_mate, even_mate, odd_mate)]


def window_place(distance, clusters):
    me = lax.axis_index("rows")
    core, chip = me % 2, me // 2
    before, after = 3 - chip % 2, 2 + chip % 2
    slot = [
        before,
        jnp.where(core == 0, before + 2, 1),
        0,
        jnp.where(core == 0, 1, after + 2),
        after,
    ]
    slab = distance // clusters
    chosen = jnp.zeros_like(distance)
    for s, value in enumerate(slot):
        chosen = jnp.where(slab == s, value, chosen)
    return chosen * clusters + distance % clusters


def on_device(
    right_sides, near_blocks, near_cols, near_counts, basis_in, target_basis, coupling, far_cols
):
    width = right_sides.shape[1]
    clusters, slots = near_cols.shape
    rank = basis_in.shape[1]
    per_group = LANES // rank
    head = clusters // per_group * R
    size = lax.axis_size("rows")
    every = clusters * size
    unknowns = float(width * size)
    rows = clusters * R

    def shape(*dims, dtype=f32):
        return jax.ShapeDtypeStruct(dims, dtype)

    def scratch(*dims, dtype=f32):
        return pltpu.VMEM(dims, dtype)

    def in_hbm(array):
        return pltpu.with_memory_space_constraint(array, pltpu.HBM)

    def call(kernel, name, out, ins, *args, scratch_shapes=(), cost_estimate=None):
        return pl.pallas_call(
            kernel, out_shape=out, in_specs=ins, out_specs=jax.tree.map(lambda _: VMEM, out),
            scratch_shapes=scratch_shapes, compiler_params=PARAMS, name=name,
            cost_estimate=cost_estimate,
        )(*args)

    def exchange(block):
        return lax.all_to_all(block, "rows", 0, 0)

    field, basis, lowered = call(
        start_kernel, "start",
        (shape(rows, LANES), shape(clusters * rank, LANES, dtype=bf16), shape(rows, LANES, dtype=bf16)),
        [HBM] * 2, in_hbm(right_sides), in_hbm(basis_in.reshape(clusters * rank, LANES)),
        scratch_shapes=[scratch(R, width), pltpu.SemaphoreType.DMA((2,))],
    )
    held = sends_of(lowered)
    payload_shape = shape(size, head + TAIL, LANES, dtype=bf16)
    payload = call(
        functools.partial(compress_kernel, per_group, [(0, 0)]), "compress_one", payload_shape,
        [VMEM] * 2, field, basis,
    )
    got0 = exchange(payload)

    def relayed(held, payload):
        both = call(
            relay_kernel, "relay", shape(2 * rows, LANES, dtype=bf16), [VMEM] * 2 + [ANY], *held[2:], payload
        )
        return swapped(both, core_mate)

    turned_shape = (clusters // 2, slots * LANES, 2 * LANES)
    high, low, target, turned = pl.pallas_call(
        prepare_kernel,
        out_shape=(
            shape(slots * rank, rank * clusters, dtype=bf16),
            shape(slots * rank, rank * clusters, dtype=bf16),
            shape(rank * clusters, LANES, dtype=bf16),
            pltpu.HBM(turned_shape, bf16),
        ),
        in_specs=[HBM] * 3 + [ANY], out_specs=[VMEM] * 3 + [HBM],
        scratch_shapes=[
            scratch(slots, rank, rank, clusters), scratch(clusters * rank, LANES, dtype=bf16),
            scratch(clusters * slots, LANES, LANES, dtype=bf16), scratch(*turned_shape, dtype=bf16),
            pltpu.SemaphoreType.DMA((8,)), pltpu.SemaphoreType.DMA((8,)), pltpu.SemaphoreType.DMA((2,)),
        ],
        compiler_params=PARAMS, name="prepare",
        cost_estimate=pl.CostEstimate(flops=0, bytes_accessed=4 * near_blocks.size, transcendentals=0),
    )(
        in_hbm(jnp.transpose(coupling, (1, 2, 3, 0))),
        in_hbm(target_basis.reshape(clusters * rank, LANES)),
        in_hbm(near_blocks.reshape(clusters * slots, LANES, LANES)),
        payload,
    )
    turned = in_hbm(turned)
    reach = 2 * clusters
    start = lax.axis_index("rows") * clusters
    distance = (near_cols.T - start + reach) % every
    live = jnp.arange(slots, dtype=jnp.int32)[:, None] < near_counts[None, :]
    placed = jnp.where(live, window_place(distance, clusters), 6 * clusters).astype(jnp.int32)
    far_index = far_cols.T

    near_cost = pl.CostEstimate(flops=32 * near_blocks.size, bytes_accessed=32 * near_blocks.size, transcendentals=0)

    def near_of(slabs):
        return call(
            near_kernel, "near", shape(rows, LANES), [VMEM] * len(slabs) + [SMEM, HBM], *slabs, placed, turned,
            scratch_shapes=[
                scratch(6 * rows + R, LANES), scratch(*turned_shape, dtype=bf16),
                pltpu.SemaphoreType.DMA((8,)),
            ],
            cost_estimate=near_cost,
        )

    kept = [scratch(size * head, LANES), scratch(rows, LANES)]
    near = near_of(held + [relayed(held, payload)])
    image, lowered = call(
        functools.partial(first_kernel, per_group, unknowns), "far_one",
        (shape(rows, LANES), shape(rows, LANES, dtype=bf16)), [VMEM] * 3 + [SMEM] + [VMEM] * 3,
        field, near, got0, far_index, high, low, target, scratch_shapes=kept,
    )
    held = sends_of(lowered)
    payload = call(
        functools.partial(compress_kernel, per_group, [(0, 1), (1, 1)]), "compress_two", payload_shape,
        [VMEM] * 3, field, image, basis,
    )
    got1 = exchange(payload)
    near = near_of(held + [relayed(held, payload)])
    candidate, sums = call(
        functools.partial(second_kernel, per_group, unknowns), "far_two",
        (shape(rows, LANES), shape(size, R, LANES)), [VMEM] * 5 + [SMEM] + [VMEM] * 3,
        field, image, near, got0, got1, far_index, high, low, target, scratch_shapes=kept,
    )
    got2 = exchange(sums)
    return call(
        functools.partial(finish_kernel, per_group, unknowns), "finish", (shape(R, width), shape(R, width)),
        [VMEM] * 6, field, image, candidate, got0, got1, got2,
    )


def solution(mesh):
    return jax.shard_map(
        on_device,
        mesh=mesh,
        in_specs=(
            P("groups", "rows"),
            P("rows", None, None, None),
            P("rows", None),
            P("rows"),
            P("rows", None, None),
            P("rows", None, None),
            P("rows", None, None, None),
            P("rows", None),
        ),
        out_specs=(P("groups", "rows"), P("groups", "rows")),
        check_vma=False,
    )
```

```python
import functools

import jax
import jax.numpy as jnp
from jax import lax
from jax.experimental import pallas as pl
from jax.experimental.pallas import tpu as pltpu
from jax.sharding import PartitionSpec as P

epsilon = 1e-06
f32, bf16 = jnp.float32, jnp.bfloat16
VMEM = pl.BlockSpec(memory_space=pltpu.VMEM)
SMEM = pl.BlockSpec(memory_space=pltpu.SMEM)
HBM = pl.BlockSpec(memory_space=pltpu.HBM)
ANY = pl.BlockSpec(memory_space=pl.ANY)
R = 8
LANES = 128
SUM_SLOTS = 8
TAIL = 16
PARAMS = pltpu.CompilerParams(vmem_limit_bytes=24 * 1024 * 1024)


def lane_ids(rows=R):
    return lax.broadcasted_iota(jnp.int32, (rows, LANES), 1)


def rows_of(ref, j):
    return ref[pl.ds(j * R, R), :]


def dot(a, b, contract=(1, 0)):
    return lax.dot_general(a, b, (((contract[0],), (contract[1],)), ((), ())), preferred_element_type=f32)


def sums_tile(sums):
    lane = lane_ids()
    tile = jnp.zeros((R, LANES), f32)
    for t, partial in enumerate(sums):
        total = jnp.sum(partial, axis=1, keepdims=True)
        high = total.astype(bf16).astype(f32)
        middle = (total - high).astype(bf16).astype(f32)
        low = total - high - middle
        for part, value in enumerate((high, middle, low)):
            tile = jnp.where(lane == part * SUM_SLOTS + t, value, tile)
    return jnp.concatenate([tile, jnp.zeros((TAIL - R, LANES), f32)], axis=0).astype(bf16)


def read_sums(got, first_row, count, unknowns):
    total = jnp.zeros((R, LANES), f32)
    for device in range(got.shape[0]):
        total = total + got[device, pl.ds(first_row, TAIL), :].astype(f32)[:R]
    return [
        sum(total[:, p * SUM_SLOTS + t : p * SUM_SLOTS + t + 1] for p in range(3)) * (1.0 / unknowns)
        for t in range(count)
    ]


def compress(tiles, basis, group):
    stacked = jnp.concatenate(tiles, axis=0)
    high = stacked.astype(bf16)
    low = (stacked - high.astype(f32)).astype(bf16)
    both = dot(jnp.concatenate([high, low], axis=0), basis[pl.ds(group * LANES, LANES), :], (1, 1))
    rows = len(tiles) * R
    both = both[:rows] + both[rows:]
    lane = lane_ids()
    rank = LANES // len(tiles)
    tile = jnp.zeros((R, LANES), f32)
    for m in range(len(tiles)):
        tile = jnp.where(lane // rank == m, both[m * R : (m + 1) * R], tile)
    return tile


def start_kernel(b_hbm, basis_hbm, field, basis, lowered, b, sems):
    copies = [
        pltpu.make_async_copy(b_hbm, b, sems.at[0]),
        pltpu.make_async_copy(basis_hbm, basis, sems.at[1]),
    ]
    for copy in copies:
        copy.start()
    copies[0].wait()
    clusters = b.shape[1] // LANES
    tiles = jnp.concatenate([b[:, j * LANES : (j + 1) * LANES] for j in range(clusters)], axis=0)
    field[...] = tiles
    lowered[...] = tiles.astype(bf16)
    copies[1].wait()


def compress_kernel(per_group, pairs, *refs):
    *fields, basis, payload = refs
    clusters = fields[0].shape[0] // R
    tiles = [rows_of(fields[-1], j) for j in range(clusters)]
    sums = [
        sum(rows_of(fields[f], j) * rows_of(fields[g], j) for j in range(clusters)) for f, g in pairs
    ]
    groups = clusters // per_group
    parts = [compress(tiles[g * per_group : (g + 1) * per_group], basis, g) for g in range(groups)]
    block = jnp.concatenate([jnp.concatenate(parts, axis=0).astype(bf16), sums_tile(sums)], axis=0)
    for device in range(payload.shape[0]):
        payload[device] = block


def prepare_kernel(coupling_hbm, target_hbm, _, high_out, low_out, target_out, coupling, target, sems):
    copies = [
        pltpu.make_async_copy(coupling_hbm, coupling, sems.at[0]),
        pltpu.make_async_copy(target_hbm, target, sems.at[1]),
    ]
    for copy in copies:
        copy.start()
    for copy in copies:
        copy.wait()
    slots, rank, _, clusters = coupling.shape
    per_tile = LANES // clusters
    for s in range(rank // per_tile):
        pieces = [
            coupling[:, s * per_tile + p].reshape(slots * rank, clusters) for p in range(per_tile)
        ]
        tile = jnp.concatenate(pieces, axis=1)
        high = tile.astype(bf16)
        high_out[:, s * LANES : (s + 1) * LANES] = high
        low_out[:, s * LANES : (s + 1) * LANES] = (tile - high.astype(f32)).astype(bf16)
    size = rank * clusters
    row = lax.broadcasted_iota(jnp.int32, (size, size), 0)
    column = lax.broadcasted_iota(jnp.int32, (size, size), 1)
    wanted = (row % clusters) * rank + row // clusters
    target_out[...] = dot((column == wanted).astype(bf16), target[...]).astype(bf16)


def far_field(got, far_cols, high, low, target, table, clusters, rank, far):
    slots = far_cols.shape[0]
    per_group = LANES // rank
    groups = clusters // per_group
    head = groups * R
    for device in range(got.shape[0]):
        table[pl.ds(device * head, head), :] = got[device, pl.ds(0, head), :].astype(f32)
    lane = lane_ids()
    picked = []
    for i in range(clusters):
        tile = jnp.zeros((R, LANES), f32)
        for k in range(slots):
            j = far_cols[k, i]
            found = table[pl.ds(pl.multiple_of(lax.div(j, per_group) * R, R), R), :]
            shift = ((k - j) * rank) & (LANES - 1)
            tile = jnp.where(lane // rank == k, pltpu.roll(found, shift, 1), tile)
        picked.append(tile)
    picked = jnp.concatenate(picked, axis=0).astype(bf16)
    crossed = dot(picked, high[...]) + dot(picked, low[...])
    expanded_high, expanded_low = [], []
    for s in range(rank * clusters // LANES):
        tile = jnp.zeros((R, LANES), f32)
        for i in range(clusters):
            part = crossed[i * R : (i + 1) * R, s * LANES : (s + 1) * LANES]
            tile = jnp.where(lane % clusters == i, part, tile)
        tile_high = tile.astype(bf16).astype(f32)
        tile_low = tile - tile_high
        for source, kept in ((tile_high, expanded_high), (tile_low, expanded_low)):
            spread = [jnp.where(lane % clusters == i, source, 0.0) for i in range(clusters)]
            kept.append(jnp.concatenate(spread, axis=0).astype(bf16))
    far[...] = dot(jnp.concatenate(expanded_high, axis=1), target[...]) + dot(
        jnp.concatenate(expanded_low, axis=1), target[...]
    )


def relay_kernel(even, odd, _, both):
    rows = even.shape[0]
    both[pl.ds(0, rows), :] = even[...]
    both[pl.ds(rows, rows), :] = odd[...]


def near_kernel(*refs):
    *slabs, placed, blocks_hbm, near, window, blocks, sems = refs
    slots, clusters = placed.shape
    chunks = sems.shape[0]
    each = clusters // chunks

    def copy_of(chunk):
        span = pl.ds(chunk * each * slots, each * slots)
        return pltpu.make_async_copy(blocks_hbm.at[span], blocks.at[span], sems.at[chunk])

    for chunk in range(chunks):
        copy_of(chunk).start()
    at = 0
    for slab in slabs:
        window[pl.ds(at, slab.shape[0]), :] = slab[...].astype(f32)
        at += slab.shape[0]
    window[pl.ds(at, R), :] = jnp.zeros((R, LANES), f32)

    def fetch(k, i):
        return window[pl.ds(pl.multiple_of(placed[k, i] * R, R), R), :]

    def block(k, i):
        return blocks[i * slots + k]

    for i in range(0, clusters, 2):
        if i % each == 0:
            copy_of(i // each).wait()
        both = jnp.zeros((2 * R, 2 * LANES), f32)
        for k in range(0, slots, 2):
            sources = jnp.concatenate(
                [jnp.concatenate([fetch(k + n, i), fetch(k + n, i + 1)], axis=0) for n in range(2)], axis=1
            )
            weights = jnp.concatenate(
                [jnp.concatenate([block(k + n, i), block(k + n, i + 1)], axis=0) for n in range(2)], axis=1
            )
            both = both + dot(sources.astype(bf16), weights, (1, 1))
        near[pl.ds(i * R, R), :] = both[:R, :LANES]
        near[pl.ds((i + 1) * R, R), :] = both[R:, LANES:]


def norm_parts(sums):
    square = sums[0]
    whole = square + epsilon
    return jnp.sqrt(whole), square / whole


def first_kernel(per_group, unknowns, b, near, got, far_cols, high, low, target, image, lowered, table, far):
    clusters = far_cols.shape[1]
    head = clusters // per_group * R
    far_field(got, far_cols, high, low, target, table, clusters, LANES // per_group, far)
    start_norm, _ = norm_parts(read_sums(got, head, 1, unknowns))
    scale = 1.0 / start_norm
    for j in range(0, clusters, 2):
        made = [
            (0.5 * rows_of(b, i) + (rows_of(near, i) + rows_of(far, i))) * scale for i in (j, j + 1)
        ]
        both = jnp.concatenate(made, axis=0)
        image[pl.ds(j * R, 2 * R), :] = both
        lowered[pl.ds(j * R, 2 * R), :] = both.astype(bf16)


def arnoldi_one(sums0, sums1):
    start_norm, v11 = norm_parts(sums0)
    h11 = sums1[0] * (1.0 / start_norm)
    uu = jnp.maximum(sums1[1] - 2.0 * h11 * h11 + h11 * h11 * v11, 0.0)
    h21 = jnp.sqrt(uu + epsilon)
    return h11, h21, v11, uu / (uu + epsilon), h11 * (1.0 - v11) / h21


def second_kernel(
    per_group, unknowns, b, image, near, got0, got, far_cols, high, low, target, candidate, sums_out, table, far,
):
    clusters = far_cols.shape[1]
    head = clusters // per_group * R
    far_field(got, far_cols, high, low, target, table, clusters, LANES // per_group, far)
    sums0 = read_sums(got0, head, 1, unknowns)
    scale = 1.0 / norm_parts(sums0)[0]
    h11, h21, _, _, _ = arnoldi_one(sums0, read_sums(got, head, 2, unknowns))
    inverse = 1.0 / h21
    sums = [jnp.zeros((R, LANES), f32) for _ in range(3)]
    for j in range(clusters):
        held = rows_of(image, j)
        first = rows_of(b, j) * scale
        second = (held - h11 * first) * inverse
        made = (0.5 * held + (rows_of(near, j) + rows_of(far, j)) - h11 * held) * inverse
        sums = [s + v * made for s, v in zip(sums, (first, second, made))]
        candidate[pl.ds(j * R, R), :] = made
    lane = lane_ids()
    tile = jnp.zeros((R, LANES), f32)
    for t, partial in enumerate(sums):
        tile = jnp.where(lane == t, jnp.sum(partial, axis=1, keepdims=True), tile)
    for device in range(sums_out.shape[0]):
        sums_out[device] = tile


def finish_kernel(per_group, unknowns, b, image, candidate, got0, got1, got2, solution_out, next_out):
    clusters = b.shape[0] // R
    head = clusters // per_group * R
    sums0 = read_sums(got0, head, 1, unknowns)
    start_norm, _ = norm_parts(sums0)
    h11, h21, v11, v22, v12 = arnoldi_one(sums0, read_sums(got1, head, 2, unknowns))
    total = sum(got2[device] for device in range(got2.shape[0]))
    h12, h22, ww = [total[:, t : t + 1] * (1.0 / unknowns) for t in range(3)]
    uu = ww - 2.0 * (h12 * h12 + h22 * h22) + h12 * h12 * v11 + h22 * h22 * v22 + 2.0 * h12 * h22 * v12
    h32 = jnp.sqrt(jnp.maximum(uu, 0.0) + epsilon)
    g11 = h11 * h11 + h21 * h21
    g12 = h11 * h12 + h21 * h22
    g22 = h12 * h12 + h22 * h22 + h32 * h32
    t1, t2 = start_norm * h11, start_norm * h12
    det = g11 * g22 - g12 * g12
    y1 = (g22 * t1 - g12 * t2) / det
    y2 = (g11 * t2 - g12 * t1) / det
    scale, inverse, last = 1.0 / start_norm, 1.0 / h21, 1.0 / h32
    for j in range(clusters):
        span = slice(j * LANES, (j + 1) * LANES)
        first = rows_of(b, j) * scale
        second = (rows_of(image, j) - h11 * first) * inverse
        solution_out[:, span] = y1 * first + y2 * second
        next_out[:, span] = (rows_of(candidate, j) - h12 * first - h22 * second) * last


def swapped(block, partner):
    return lax.ppermute(block, "rows", [(i, partner(i)) for i in range(lax.axis_size("rows"))])


def core_mate(i):
    return i ^ 1


def even_mate(i):
    return i ^ 2


def odd_mate(i):
    chip = i // 2
    other = chip + 1 if chip % 2 else chip - 1
    return 2 * (other % (lax.axis_size("rows") // 2)) + i % 2


def sends_of(block):
    return [block] + [swapped(block, partner) for partner in (core_mate, even_mate, odd_mate)]


def window_place(distance, clusters):
    me = lax.axis_index("rows")
    core, chip = me % 2, me // 2
    before, after = 3 - chip % 2, 2 + chip % 2
    slot = [
        before,
        jnp.where(core == 0, before + 2, 1),
        0,
        jnp.where(core == 0, 1, after + 2),
        after,
    ]
    slab = distance // clusters
    chosen = jnp.zeros_like(distance)
    for s, value in enumerate(slot):
        chosen = jnp.where(slab == s, value, chosen)
    return chosen * clusters + distance % clusters


def on_device(
    right_sides, near_blocks, near_cols, near_counts, basis_in, target_basis, coupling, far_cols
):
    width = right_sides.shape[1]
    clusters, slots = near_cols.shape
    rank = basis_in.shape[1]
    per_group = LANES // rank
    head = clusters // per_group * R
    size = lax.axis_size("rows")
    every = clusters * size
    unknowns = float(width * size)
    rows = clusters * R

    def shape(*dims, dtype=f32):
        return jax.ShapeDtypeStruct(dims, dtype)

    def scratch(*dims, dtype=f32):
        return pltpu.VMEM(dims, dtype)

    def in_hbm(array):
        return pltpu.with_memory_space_constraint(array, pltpu.HBM)

    def call(kernel, name, out, ins, *args, scratch_shapes=(), cost_estimate=None):
        return pl.pallas_call(
            kernel, out_shape=out, in_specs=ins, out_specs=jax.tree.map(lambda _: VMEM, out),
            scratch_shapes=scratch_shapes, compiler_params=PARAMS, name=name,
            cost_estimate=cost_estimate,
        )(*args)

    def exchange(block):
        return lax.all_to_all(block, "rows", 0, 0)

    field, basis, lowered = call(
        start_kernel, "start",
        (shape(rows, LANES), shape(clusters * rank, LANES, dtype=bf16), shape(rows, LANES, dtype=bf16)),
        [HBM] * 2, in_hbm(right_sides), in_hbm(basis_in.reshape(clusters * rank, LANES)),
        scratch_shapes=[scratch(R, width), pltpu.SemaphoreType.DMA((2,))],
    )
    held = sends_of(lowered)
    compress_cost = pl.CostEstimate(flops=0, bytes_accessed=64 * basis.size * rank, transcendentals=0)
    payload_shape = shape(size, head + TAIL, LANES, dtype=bf16)
    payload = call(
        functools.partial(compress_kernel, per_group, [(0, 0)]), "compress_one", payload_shape,
        [VMEM] * 2, field, basis, cost_estimate=compress_cost,
    )
    got0 = exchange(payload)

    def relayed(held, payload):
        both = call(
            relay_kernel, "relay", shape(2 * rows, LANES, dtype=bf16), [VMEM] * 2 + [ANY], *held[2:], payload
        )
        return swapped(both, core_mate)

    high, low, target = call(
        prepare_kernel, "prepare",
        (
            shape(slots * rank, rank * clusters, dtype=bf16),
            shape(slots * rank, rank * clusters, dtype=bf16),
            shape(rank * clusters, LANES, dtype=bf16),
        ),
        [HBM] * 2 + [ANY],
        in_hbm(jnp.transpose(coupling, (1, 2, 3, 0))), in_hbm(target_basis.reshape(clusters * rank, LANES)), payload,
        scratch_shapes=[
            scratch(slots, rank, rank, clusters), scratch(clusters * rank, LANES, dtype=bf16),
            pltpu.SemaphoreType.DMA((2,)),
        ],
    )
    blocks = in_hbm(near_blocks.reshape(clusters * slots, LANES, LANES))
    reach = 2 * clusters
    start = lax.axis_index("rows") * clusters
    distance = (near_cols.T - start + reach) % every
    live = jnp.arange(slots, dtype=jnp.int32)[:, None] < near_counts[None, :]
    placed = jnp.where(live, window_place(distance, clusters), 6 * clusters).astype(jnp.int32)
    far_index = far_cols.T

    near_cost = pl.CostEstimate(flops=32 * near_blocks.size, bytes_accessed=32 * near_blocks.size, transcendentals=0)

    def near_of(slabs):
        return call(
            near_kernel, "near", shape(rows, LANES), [VMEM] * len(slabs) + [SMEM, HBM], *slabs, placed, blocks,
            scratch_shapes=[
                scratch(6 * rows + R, LANES), scratch(*blocks.shape, dtype=bf16),
                pltpu.SemaphoreType.DMA((8,)),
            ],
            cost_estimate=near_cost,
        )

    kept = [scratch(size * head, LANES), scratch(rows, LANES)]
    near = near_of(held + [relayed(held, payload)])
    image, lowered = call(
        functools.partial(first_kernel, per_group, unknowns), "far_one",
        (shape(rows, LANES), shape(rows, LANES, dtype=bf16)), [VMEM] * 3 + [SMEM] + [VMEM] * 3,
        field, near, got0, far_index, high, low, target, scratch_shapes=kept,
    )
    held = sends_of(lowered)
    payload = call(
        functools.partial(compress_kernel, per_group, [(0, 1), (1, 1)]), "compress_two", payload_shape,
        [VMEM] * 3, field, image, basis, cost_estimate=compress_cost,
    )
    got1 = exchange(payload)
    near = near_of(held + [relayed(held, payload)])
    candidate, sums = call(
        functools.partial(second_kernel, per_group, unknowns), "far_two",
        (shape(rows, LANES), shape(size, R, LANES)), [VMEM] * 5 + [SMEM] + [VMEM] * 3,
        field, image, near, got0, got1, far_index, high, low, target, scratch_shapes=kept,
    )
    got2 = exchange(sums)
    return call(
        functools.partial(finish_kernel, per_group, unknowns), "finish", (shape(R, width), shape(R, width)),
        [VMEM] * 6, field, image, candidate, got0, got1, got2,
    )


def solution(mesh):
    return jax.shard_map(
        on_device,
        mesh=mesh,
        in_specs=(
            P("groups", "rows"),
            P("rows", None, None, None),
            P("rows", None),
            P("rows"),
            P("rows", None, None),
            P("rows", None, None),
            P("rows", None, None, None),
            P("rows", None),
        ),
        out_specs=(P("groups", "rows"), P("groups", "rows")),
        check_vma=False,
    )
```

```python
import functools

import jax
import jax.numpy as jnp
from jax import lax
from jax.experimental import pallas as pl
from jax.experimental.pallas import tpu as pltpu
from jax.sharding import PartitionSpec as P

epsilon = 1e-06
f32, bf16 = jnp.float32, jnp.bfloat16
VMEM = pl.BlockSpec(memory_space=pltpu.VMEM)
SMEM = pl.BlockSpec(memory_space=pltpu.SMEM)
HBM = pl.BlockSpec(memory_space=pltpu.HBM)
ANY = pl.BlockSpec(memory_space=pl.ANY)
R = 8
LANES = 128
SUM_SLOTS = 8
TAIL = 16
PARAMS = pltpu.CompilerParams(vmem_limit_bytes=24 * 1024 * 1024)


def lane_ids(rows=R):
    return lax.broadcasted_iota(jnp.int32, (rows, LANES), 1)


def rows_of(ref, j):
    return ref[pl.ds(j * R, R), :]


def dot(a, b, contract=(1, 0)):
    return lax.dot_general(a, b, (((contract[0],), (contract[1],)), ((), ())), preferred_element_type=f32)


def sums_tile(sums):
    lane = lane_ids()
    tile = jnp.zeros((R, LANES), f32)
    for t, partial in enumerate(sums):
        total = jnp.sum(partial, axis=1, keepdims=True)
        high = total.astype(bf16).astype(f32)
        middle = (total - high).astype(bf16).astype(f32)
        low = total - high - middle
        for part, value in enumerate((high, middle, low)):
            tile = jnp.where(lane == part * SUM_SLOTS + t, value, tile)
    return jnp.concatenate([tile, jnp.zeros((TAIL - R, LANES), f32)], axis=0).astype(bf16)


def read_sums(got, first_row, count, unknowns):
    total = jnp.zeros((R, LANES), f32)
    for device in range(got.shape[0]):
        total = total + got[device, pl.ds(first_row, TAIL), :].astype(f32)[:R]
    return [
        sum(total[:, p * SUM_SLOTS + t : p * SUM_SLOTS + t + 1] for p in range(3)) * (1.0 / unknowns)
        for t in range(count)
    ]


def compress(tiles, basis, group):
    stacked = jnp.concatenate(tiles, axis=0)
    high = stacked.astype(bf16)
    low = (stacked - high.astype(f32)).astype(bf16)
    both = dot(jnp.concatenate([high, low], axis=0), basis[pl.ds(group * LANES, LANES), :], (1, 1))
    rows = len(tiles) * R
    both = both[:rows] + both[rows:]
    lane = lane_ids()
    rank = LANES // len(tiles)
    tile = jnp.zeros((R, LANES), f32)
    for m in range(len(tiles)):
        tile = jnp.where(lane // rank == m, both[m * R : (m + 1) * R], tile)
    return tile


def write_payload(payload, tiles, sums, basis, per_group):
    groups = len(tiles) // per_group
    parts = [compress(tiles[g * per_group : (g + 1) * per_group], basis, g) for g in range(groups)]
    block = jnp.concatenate([jnp.concatenate(parts, axis=0).astype(bf16), sums_tile(sums)], axis=0)
    for device in range(payload.shape[0]):
        payload[device] = block


def start_kernel(per_group, b_hbm, basis_hbm, field, basis, lowered, payload, b, sems):
    copies = [
        pltpu.make_async_copy(b_hbm, b, sems.at[0]),
        pltpu.make_async_copy(basis_hbm, basis, sems.at[1]),
    ]
    for copy in copies:
        copy.start()
    for copy in copies:
        copy.wait()
    clusters = b.shape[1] // LANES
    tiles = [b[:, j * LANES : (j + 1) * LANES] for j in range(clusters)]
    field[...] = jnp.concatenate(tiles, axis=0)
    lowered[...] = jnp.concatenate(tiles, axis=0).astype(bf16)
    write_payload(payload, tiles, [sum(t * t for t in tiles)], basis, per_group)


def prepare_kernel(coupling_hbm, target_hbm, _, __, high_out, low_out, target_out, coupling, target, sems):
    copies = [
        pltpu.make_async_copy(coupling_hbm, coupling, sems.at[0]),
        pltpu.make_async_copy(target_hbm, target, sems.at[1]),
    ]
    for copy in copies:
        copy.start()
    for copy in copies:
        copy.wait()
    slots, rank, _, clusters = coupling.shape
    per_tile = LANES // clusters
    for s in range(rank // per_tile):
        pieces = [
            coupling[:, s * per_tile + p].reshape(slots * rank, clusters) for p in range(per_tile)
        ]
        tile = jnp.concatenate(pieces, axis=1)
        high = tile.astype(bf16)
        high_out[:, s * LANES : (s + 1) * LANES] = high
        low_out[:, s * LANES : (s + 1) * LANES] = (tile - high.astype(f32)).astype(bf16)
    size = rank * clusters
    row = lax.broadcasted_iota(jnp.int32, (size, size), 0)
    column = lax.broadcasted_iota(jnp.int32, (size, size), 1)
    wanted = (row % clusters) * rank + row // clusters
    target_out[...] = dot((column == wanted).astype(bf16), target[...]).astype(bf16)


def far_kernel(per_group, got, far_cols, high, low, target, far, table):
    slots, clusters = far_cols.shape
    rank = LANES // per_group
    groups = clusters // per_group
    head = groups * R
    for device in range(got.shape[0]):
        table[pl.ds(device * head, head), :] = got[device, pl.ds(0, head), :].astype(f32)
    lane = lane_ids()
    picked = []
    for i in range(clusters):
        tile = jnp.zeros((R, LANES), f32)
        for k in range(slots):
            j = far_cols[k, i]
            found = table[pl.ds(pl.multiple_of(lax.div(j, per_group) * R, R), R), :]
            shift = ((k - j) * rank) & (LANES - 1)
            tile = jnp.where(lane // rank == k, pltpu.roll(found, shift, 1), tile)
        picked.append(tile)
    picked = jnp.concatenate(picked, axis=0).astype(bf16)
    crossed = dot(picked, high[...]) + dot(picked, low[...])
    expanded_high, expanded_low = [], []
    for s in range(rank * clusters // LANES):
        tile = jnp.zeros((R, LANES), f32)
        for i in range(clusters):
            part = crossed[i * R : (i + 1) * R, s * LANES : (s + 1) * LANES]
            tile = jnp.where(lane % clusters == i, part, tile)
        tile_high = tile.astype(bf16).astype(f32)
        tile_low = tile - tile_high
        for source, kept in ((tile_high, expanded_high), (tile_low, expanded_low)):
            spread = [jnp.where(lane % clusters == i, source, 0.0) for i in range(clusters)]
            kept.append(jnp.concatenate(spread, axis=0).astype(bf16))
    far[...] = dot(jnp.concatenate(expanded_high, axis=1), target[...]) + dot(
        jnp.concatenate(expanded_low, axis=1), target[...]
    )


def relay_kernel(even, odd, _, both):
    rows = even.shape[0]
    both[pl.ds(0, rows), :] = even[...]
    both[pl.ds(rows, rows), :] = odd[...]


def near_field(slabs, placed, blocks, near, window):
    slots, clusters = placed.shape
    at = 0
    for slab in slabs:
        window[pl.ds(at, slab.shape[0]), :] = slab[...].astype(f32)
        at += slab.shape[0]
    window[pl.ds(at, R), :] = jnp.zeros((R, LANES), f32)

    def fetch(k, i):
        return window[pl.ds(pl.multiple_of(placed[k, i] * R, R), R), :]

    def block(k, i):
        return blocks[i * slots + k]

    for i in range(0, clusters, 2):
        both = jnp.zeros((2 * R, 2 * LANES), f32)
        for k in range(0, slots, 2):
            sources = jnp.concatenate(
                [jnp.concatenate([fetch(k + n, i), fetch(k + n, i + 1)], axis=0) for n in range(2)], axis=1
            )
            weights = jnp.concatenate(
                [jnp.concatenate([block(k + n, i), block(k + n, i + 1)], axis=0) for n in range(2)], axis=1
            )
            both = both + dot(sources.astype(bf16), weights, (1, 1))
        near[pl.ds(i * R, R), :] = both[:R, :LANES]
        near[pl.ds((i + 1) * R, R), :] = both[R:, LANES:]


def norm_parts(sums):
    square = sums[0]
    whole = square + epsilon
    return jnp.sqrt(whole), square / whole


def first_kernel(
    per_group, unknowns, own, mate, even, odd, relayed, placed, blocks, b, far, got, basis,
    image, lowered, payload, near, window,
):
    near_field((own, mate, even, odd, relayed), placed, blocks, near, window)
    clusters = placed.shape[1]
    head = clusters // per_group * R
    start_norm, _ = norm_parts(read_sums(got, head, 1, unknowns))
    scale = 1.0 / start_norm
    tiles = []
    cross, square = jnp.zeros((R, LANES), f32), jnp.zeros((R, LANES), f32)
    for i in range(clusters):
        field = rows_of(b, i)
        made = (0.5 * field + (rows_of(near, i) + rows_of(far, i))) * scale
        cross = cross + field * made
        square = square + made * made
        tiles.append(made)
    for i in range(0, clusters, 2):
        both = jnp.concatenate(tiles[i : i + 2], axis=0)
        image[pl.ds(i * R, 2 * R), :] = both
        lowered[pl.ds(i * R, 2 * R), :] = both.astype(bf16)
    write_payload(payload, tiles, [cross, square], basis, per_group)


def arnoldi_one(sums0, sums1):
    start_norm, v11 = norm_parts(sums0)
    h11 = sums1[0] * (1.0 / start_norm)
    uu = jnp.maximum(sums1[1] - 2.0 * h11 * h11 + h11 * h11 * v11, 0.0)
    h21 = jnp.sqrt(uu + epsilon)
    return h11, h21, v11, uu / (uu + epsilon), h11 * (1.0 - v11) / h21


def second_kernel(
    per_group, unknowns, own, mate, even, odd, relayed, placed, blocks, b, image, far, got0, got,
    candidate, sums_out, near, window,
):
    near_field((own, mate, even, odd, relayed), placed, blocks, near, window)
    clusters = placed.shape[1]
    head = clusters // per_group * R
    sums0 = read_sums(got0, head, 1, unknowns)
    scale = 1.0 / norm_parts(sums0)[0]
    h11, h21, _, _, _ = arnoldi_one(sums0, read_sums(got, head, 2, unknowns))
    inverse = 1.0 / h21
    sums = [jnp.zeros((R, LANES), f32) for _ in range(3)]
    for j in range(clusters):
        held = rows_of(image, j)
        first = rows_of(b, j) * scale
        second = (held - h11 * first) * inverse
        made = (0.5 * held + (rows_of(near, j) + rows_of(far, j)) - h11 * held) * inverse
        sums = [s + v * made for s, v in zip(sums, (first, second, made))]
        candidate[pl.ds(j * R, R), :] = made
    lane = lane_ids()
    tile = jnp.zeros((R, LANES), f32)
    for t, partial in enumerate(sums):
        tile = jnp.where(lane == t, jnp.sum(partial, axis=1, keepdims=True), tile)
    for device in range(sums_out.shape[0]):
        sums_out[device] = tile


def finish_kernel(per_group, unknowns, b, image, candidate, got0, got1, got2, solution_out, next_out):
    clusters = b.shape[0] // R
    head = clusters // per_group * R
    sums0 = read_sums(got0, head, 1, unknowns)
    start_norm, _ = norm_parts(sums0)
    h11, h21, v11, v22, v12 = arnoldi_one(sums0, read_sums(got1, head, 2, unknowns))
    total = sum(got2[device] for device in range(got2.shape[0]))
    h12, h22, ww = [total[:, t : t + 1] * (1.0 / unknowns) for t in range(3)]
    uu = ww - 2.0 * (h12 * h12 + h22 * h22) + h12 * h12 * v11 + h22 * h22 * v22 + 2.0 * h12 * h22 * v12
    h32 = jnp.sqrt(jnp.maximum(uu, 0.0) + epsilon)
    g11 = h11 * h11 + h21 * h21
    g12 = h11 * h12 + h21 * h22
    g22 = h12 * h12 + h22 * h22 + h32 * h32
    t1, t2 = start_norm * h11, start_norm * h12
    det = g11 * g22 - g12 * g12
    y1 = (g22 * t1 - g12 * t2) / det
    y2 = (g11 * t2 - g12 * t1) / det
    scale, inverse, last = 1.0 / start_norm, 1.0 / h21, 1.0 / h32
    for j in range(clusters):
        span = slice(j * LANES, (j + 1) * LANES)
        first = rows_of(b, j) * scale
        second = (rows_of(image, j) - h11 * first) * inverse
        solution_out[:, span] = y1 * first + y2 * second
        next_out[:, span] = (rows_of(candidate, j) - h12 * first - h22 * second) * last


def swapped(block, partner):
    return lax.ppermute(block, "rows", [(i, partner(i)) for i in range(lax.axis_size("rows"))])


def core_mate(i):
    return i ^ 1


def even_mate(i):
    return i ^ 2


def odd_mate(i):
    chip = i // 2
    other = chip + 1 if chip % 2 else chip - 1
    return 2 * (other % (lax.axis_size("rows") // 2)) + i % 2


def sends_of(block):
    return [block] + [swapped(block, partner) for partner in (core_mate, even_mate, odd_mate)]


def window_place(distance, clusters):
    me = lax.axis_index("rows")
    core, chip = me % 2, me // 2
    before, after = 3 - chip % 2, 2 + chip % 2
    slot = [
        before,
        jnp.where(core == 0, before + 2, 1),
        0,
        jnp.where(core == 0, 1, after + 2),
        after,
    ]
    slab = distance // clusters
    chosen = jnp.zeros_like(distance)
    for s, value in enumerate(slot):
        chosen = jnp.where(slab == s, value, chosen)
    return chosen * clusters + distance % clusters


def on_device(
    right_sides, near_blocks, near_cols, near_counts, basis_in, target_basis, coupling, far_cols
):
    width = right_sides.shape[1]
    clusters, slots = near_cols.shape
    rank = basis_in.shape[1]
    per_group = LANES // rank
    head = clusters // per_group * R
    size = lax.axis_size("rows")
    every = clusters * size
    unknowns = float(width * size)
    rows = clusters * R

    def shape(*dims, dtype=f32):
        return jax.ShapeDtypeStruct(dims, dtype)

    def scratch(*dims, dtype=f32):
        return pltpu.VMEM(dims, dtype)

    def in_hbm(array):
        return pltpu.with_memory_space_constraint(array, pltpu.HBM)

    def call(kernel, name, out, ins, *args, scratch_shapes=()):
        return pl.pallas_call(
            kernel, out_shape=out, in_specs=ins, out_specs=jax.tree.map(lambda _: VMEM, out),
            scratch_shapes=scratch_shapes, compiler_params=PARAMS, name=name,
        )(*args)

    def exchange(block):
        return lax.all_to_all(block, "rows", 0, 0)

    payload_shape = shape(size, head + TAIL, LANES, dtype=bf16)
    field, basis, lowered, payload = call(
        functools.partial(start_kernel, per_group), "start",
        (
            shape(rows, LANES), shape(clusters * rank, LANES, dtype=bf16), shape(rows, LANES, dtype=bf16),
            payload_shape,
        ),
        [HBM] * 2, in_hbm(right_sides), in_hbm(basis_in.reshape(clusters * rank, LANES)),
        scratch_shapes=[scratch(R, width), pltpu.SemaphoreType.DMA((2,))],
    )
    got0 = exchange(payload)
    held = sends_of(lowered)

    reach = 2 * clusters
    start = lax.axis_index("rows") * clusters
    distance = (near_cols.T - start + reach) % every
    live = jnp.arange(slots, dtype=jnp.int32)[:, None] < near_counts[None, :]
    placed = jnp.where(live, window_place(distance, clusters), 6 * clusters).astype(jnp.int32)
    far_index = far_cols.T
    high, low, target = call(
        prepare_kernel, "prepare",
        (
            shape(slots * rank, rank * clusters, dtype=bf16),
            shape(slots * rank, rank * clusters, dtype=bf16),
            shape(rank * clusters, LANES, dtype=bf16),
        ),
        [HBM] * 2 + [ANY] * 2,
        in_hbm(jnp.transpose(coupling, (1, 2, 3, 0))), in_hbm(target_basis.reshape(clusters * rank, LANES)),
        payload, placed,
        scratch_shapes=[
            scratch(slots, rank, rank, clusters), scratch(clusters * rank, LANES, dtype=bf16),
            pltpu.SemaphoreType.DMA((2,)),
        ],
    )
    blocks = pltpu.with_memory_space_constraint(
        near_blocks.reshape(clusters * slots, LANES, LANES), pltpu.VMEM
    )

    def far_of(got):
        return call(
            functools.partial(far_kernel, per_group), "far", shape(rows, LANES), [VMEM, SMEM] + [VMEM] * 3,
            got, far_index, high, low, target, scratch_shapes=[scratch(size * head, LANES)],
        )

    def relayed(held, far):
        both = call(
            relay_kernel, "relay", shape(2 * rows, LANES, dtype=bf16), [VMEM] * 2 + [ANY], *held[2:], far
        )
        return swapped(both, core_mate)

    kept = [scratch(rows, LANES), scratch(6 * rows + R, LANES)]
    far = far_of(got0)
    image, lowered, payload = call(
        functools.partial(first_kernel, per_group, unknowns), "near_one",
        (shape(rows, LANES), shape(rows, LANES, dtype=bf16), payload_shape),
        [VMEM] * 5 + [SMEM] + [VMEM] * 5,
        *held, relayed(held, far), placed, blocks, field, far, got0, basis, scratch_shapes=kept,
    )
    got1 = exchange(payload)
    held = sends_of(lowered)
    far = far_of(got1)
    candidate, sums = call(
        functools.partial(second_kernel, per_group, unknowns), "near_two",
        (shape(rows, LANES), shape(size, R, LANES)), [VMEM] * 5 + [SMEM] + [VMEM] * 6,
        *held, relayed(held, far), placed, blocks, field, image, far, got0, got1, scratch_shapes=kept,
    )
    got2 = exchange(sums)
    return call(
        functools.partial(finish_kernel, per_group, unknowns), "finish", (shape(R, width), shape(R, width)),
        [VMEM] * 6, field, image, candidate, got0, got1, got2,
    )


def solution(mesh):
    return jax.shard_map(
        on_device,
        mesh=mesh,
        in_specs=(
            P("groups", "rows"),
            P("rows", None, None, None),
            P("rows", None),
            P("rows"),
            P("rows", None, None),
            P("rows", None, None),
            P("rows", None, None, None),
            P("rows", None),
        ),
        out_specs=(P("groups", "rows"), P("groups", "rows")),
        check_vma=False,
    )
```

```python
import functools

import jax
import jax.numpy as jnp
from jax import lax
from jax.experimental import pallas as pl
from jax.experimental.pallas import tpu as pltpu
from jax.sharding import PartitionSpec as P

epsilon = 1e-06
f32, bf16 = jnp.float32, jnp.bfloat16
VMEM = pl.BlockSpec(memory_space=pltpu.VMEM)
SMEM = pl.BlockSpec(memory_space=pltpu.SMEM)
HBM = pl.BlockSpec(memory_space=pltpu.HBM)
ANY = pl.BlockSpec(memory_space=pl.ANY)
R = 8
LANES = 128
SUM_SLOTS = 8
TAIL = 16
PARAMS = pltpu.CompilerParams(vmem_limit_bytes=24 * 1024 * 1024)


def lane_ids(rows=R):
    return lax.broadcasted_iota(jnp.int32, (rows, LANES), 1)


def rows_of(ref, j):
    return ref[pl.ds(j * R, R), :]


def dot(a, b, contract=(1, 0)):
    return lax.dot_general(a, b, (((contract[0],), (contract[1],)), ((), ())), preferred_element_type=f32)


def sums_tile(sums):
    lane = lane_ids()
    tile = jnp.zeros((R, LANES), f32)
    for t, partial in enumerate(sums):
        total = jnp.sum(partial, axis=1, keepdims=True)
        high = total.astype(bf16).astype(f32)
        middle = (total - high).astype(bf16).astype(f32)
        low = total - high - middle
        for part, value in enumerate((high, middle, low)):
            tile = jnp.where(lane == part * SUM_SLOTS + t, value, tile)
    return tile


def read_sums(gathered, first_row, rows, count, unknowns):
    total = jnp.zeros((R, LANES), f32)
    for got in gathered:
        for device in range(got.shape[0]):
            total = total + got[device, pl.ds(first_row, rows), :].astype(f32)[:R]
    return [
        sum(total[:, p * SUM_SLOTS + t : p * SUM_SLOTS + t + 1] for p in range(3)) * (1.0 / unknowns)
        for t in range(count)
    ]


def compress(tiles, basis, group):
    stacked = jnp.concatenate(tiles, axis=0)
    high = stacked.astype(bf16)
    low = (stacked - high.astype(f32)).astype(bf16)
    both = dot(jnp.concatenate([high, low], axis=0), basis[pl.ds(group * LANES, LANES), :], (1, 1))
    rows = len(tiles) * R
    both = both[:rows] + both[rows:]
    lane = lane_ids()
    rank = LANES // len(tiles)
    tile = jnp.zeros((R, LANES), f32)
    for m in range(len(tiles)):
        tile = jnp.where(lane // rank == m, both[m * R : (m + 1) * R], tile)
    return tile


def write_payload(payload, tiles, sums, basis, per_group):
    groups = len(tiles) // per_group
    parts = [compress(tiles[g * per_group : (g + 1) * per_group], basis, g) for g in range(groups)]
    if sums:
        parts += [sums_tile(sums), jnp.zeros((TAIL - R, LANES), f32)]
    block = jnp.concatenate(parts, axis=0).astype(bf16)
    for device in range(payload.shape[0]):
        payload[device] = block


def start_kernel(per_group, b_hbm, basis_hbm, field, basis, lowered, payload, b, sems):
    copies = [
        pltpu.make_async_copy(b_hbm, b, sems.at[0]),
        pltpu.make_async_copy(basis_hbm, basis, sems.at[1]),
    ]
    for copy in copies:
        copy.start()
    for copy in copies:
        copy.wait()
    clusters = b.shape[1] // LANES
    tiles = [b[:, j * LANES : (j + 1) * LANES] for j in range(clusters)]
    field[...] = jnp.concatenate(tiles, axis=0)
    lowered[...] = jnp.concatenate(tiles, axis=0).astype(bf16)
    write_payload(payload, tiles, [], basis, per_group)


def prepare_kernel(coupling_hbm, target_hbm, _, __, ___, high_out, low_out, target_out, coupling, target, sems):
    copies = [
        pltpu.make_async_copy(coupling_hbm, coupling, sems.at[0]),
        pltpu.make_async_copy(target_hbm, target, sems.at[1]),
    ]
    for copy in copies:
        copy.start()
    for copy in copies:
        copy.wait()
    slots, rank, _, clusters = coupling.shape
    per_tile = LANES // clusters
    for s in range(rank // per_tile):
        pieces = [
            coupling[:, s * per_tile + p].reshape(slots * rank, clusters) for p in range(per_tile)
        ]
        tile = jnp.concatenate(pieces, axis=1)
        high = tile.astype(bf16)
        high_out[:, s * LANES : (s + 1) * LANES] = high
        low_out[:, s * LANES : (s + 1) * LANES] = (tile - high.astype(f32)).astype(bf16)
    size = rank * clusters
    row = lax.broadcasted_iota(jnp.int32, (size, size), 0)
    column = lax.broadcasted_iota(jnp.int32, (size, size), 1)
    wanted = (row % clusters) * rank + row // clusters
    target_out[...] = dot((column == wanted).astype(bf16), target[...]).astype(bf16)


def far_kernel(
    per_group, got, got_mate, far_cols, high, low, target, blocks_hbm, _, far, blocks, table, sems,
):
    chunks = sems.shape[0]
    each = blocks.shape[0] // chunks
    copies = [
        pltpu.make_async_copy(
            blocks_hbm.at[pl.ds(c * each, each)], blocks.at[pl.ds(c * each, each)], sems.at[c]
        )
        for c in range(chunks)
    ]
    for copy in copies:
        copy.start()
    slots, clusters = far_cols.shape
    rank = LANES // per_group
    groups = clusters // per_group
    head = groups * R
    for part, values in enumerate((got, got_mate)):
        for device in range(values.shape[0]):
            at = (part * values.shape[0] + device) * head
            table[pl.ds(at, head), :] = values[device, pl.ds(0, head), :].astype(f32)
    lane = lane_ids()
    picked = []
    for i in range(clusters):
        tile = jnp.zeros((R, LANES), f32)
        for k in range(slots):
            j = far_cols[k, i]
            found = table[pl.ds(pl.multiple_of(lax.div(j, per_group) * R, R), R), :]
            shift = ((k - j) * rank) & (LANES - 1)
            tile = jnp.where(lane // rank == k, pltpu.roll(found, shift, 1), tile)
        picked.append(tile)
    picked = jnp.concatenate(picked, axis=0).astype(bf16)
    crossed = dot(picked, high[...]) + dot(picked, low[...])
    expanded_high, expanded_low = [], []
    for s in range(rank * clusters // LANES):
        tile = jnp.zeros((R, LANES), f32)
        for i in range(clusters):
            part = crossed[i * R : (i + 1) * R, s * LANES : (s + 1) * LANES]
            tile = jnp.where(lane % clusters == i, part, tile)
        tile_high = tile.astype(bf16).astype(f32)
        tile_low = tile - tile_high
        for source, kept in ((tile_high, expanded_high), (tile_low, expanded_low)):
            spread = [jnp.where(lane % clusters == i, source, 0.0) for i in range(clusters)]
            kept.append(jnp.concatenate(spread, axis=0).astype(bf16))
    far[...] = dot(jnp.concatenate(expanded_high, axis=1), target[...]) + dot(
        jnp.concatenate(expanded_low, axis=1), target[...]
    )
    for copy in copies:
        copy.wait()


def relay_kernel(even, odd, both):
    rows = even.shape[0]
    both[pl.ds(0, rows), :] = even[...]
    both[pl.ds(rows, rows), :] = odd[...]


def near_field(slabs, placed, blocks, near, window):
    slots, clusters = placed.shape
    at = 0
    for slab in slabs:
        window[pl.ds(at, slab.shape[0]), :] = slab[...].astype(f32)
        at += slab.shape[0]
    window[pl.ds(at, R), :] = jnp.zeros((R, LANES), f32)

    def fetch(k, i):
        return window[pl.ds(pl.multiple_of(placed[k, i] * R, R), R), :]

    def block(k, i):
        return blocks[i * slots + k]

    for i in range(0, clusters, 2):
        both = jnp.zeros((2 * R, 2 * LANES), f32)
        for k in range(0, slots, 2):
            sources = jnp.concatenate(
                [jnp.concatenate([fetch(k + n, i), fetch(k + n, i + 1)], axis=0) for n in range(2)], axis=1
            )
            weights = jnp.concatenate(
                [jnp.concatenate([block(k + n, i), block(k + n, i + 1)], axis=0) for n in range(2)], axis=1
            )
            both = both + dot(sources.astype(bf16), weights, (1, 1))
        near[pl.ds(i * R, R), :] = both[:R, :LANES]
        near[pl.ds((i + 1) * R, R), :] = both[R:, LANES:]


def first_kernel(
    per_group, own, mate, even, odd, relayed, placed, blocks, b, far, basis, image, lowered, payload, near, window,
):
    near_field((own, mate, even, odd, relayed), placed, blocks, near, window)
    clusters = placed.shape[1]
    tiles = []
    sums = [jnp.zeros((R, LANES), f32) for _ in range(3)]
    for i in range(clusters):
        field = rows_of(b, i)
        made = 0.5 * field + (rows_of(near, i) + rows_of(far, i))
        sums = [s + f * g for s, f, g in zip(sums, (field, field, made), (field, made, made))]
        tiles.append(made)
    for i in range(0, clusters, 2):
        both = jnp.concatenate(tiles[i : i + 2], axis=0)
        image[pl.ds(i * R, 2 * R), :] = both
        lowered[pl.ds(i * R, 2 * R), :] = both.astype(bf16)
    write_payload(payload, tiles, sums, basis, per_group)


def arnoldi_one(bb, bw, ww):
    whole = bb + epsilon
    start_norm = jnp.sqrt(whole)
    scale = 1.0 / start_norm
    v11 = bb / whole
    h11 = (bw * scale) * scale
    uu = jnp.maximum((ww * scale) * scale - 2.0 * h11 * h11 + h11 * h11 * v11, 0.0)
    h21 = jnp.sqrt(uu + epsilon)
    return start_norm, h11, h21, v11, uu / (uu + epsilon), h11 * (1.0 - v11) / h21


def second_kernel(
    per_group, unknowns, own, mate, even, odd, relayed, placed, blocks, b, image, far, got, got_mate,
    candidate, sums_out, near, window,
):
    near_field((own, mate, even, odd, relayed), placed, blocks, near, window)
    clusters = placed.shape[1]
    head = clusters // per_group * R
    start_norm, h11, h21, _, _, _ = arnoldi_one(*read_sums((got, got_mate), head, TAIL, 3, unknowns))
    scale = 1.0 / start_norm
    inverse = 1.0 / h21
    sums = [jnp.zeros((R, LANES), f32) for _ in range(3)]
    for j in range(clusters):
        held = rows_of(image, j) * scale
        first = rows_of(b, j) * scale
        second = (held - h11 * first) * inverse
        made = (0.5 * held + (rows_of(near, j) + rows_of(far, j)) * scale - h11 * held) * inverse
        sums = [s + v * made for s, v in zip(sums, (first, second, made))]
        candidate[pl.ds(j * R, R), :] = made
    tile = sums_tile(sums).astype(bf16)
    for device in range(sums_out.shape[0]):
        sums_out[device] = tile


def finish_kernel(per_group, unknowns, b, image, candidate, got1, got1_mate, got2, solution_out, next_out):
    clusters = b.shape[0] // R
    head = clusters // per_group * R
    start_norm, h11, h21, v11, v22, v12 = arnoldi_one(*read_sums((got1, got1_mate), head, TAIL, 3, unknowns))
    h12, h22, ww = read_sums((got2,), 0, R, 3, unknowns)
    uu = ww - 2.0 * (h12 * h12 + h22 * h22) + h12 * h12 * v11 + h22 * h22 * v22 + 2.0 * h12 * h22 * v12
    h32 = jnp.sqrt(jnp.maximum(uu, 0.0) + epsilon)
    g11 = h11 * h11 + h21 * h21
    g12 = h11 * h12 + h21 * h22
    g22 = h12 * h12 + h22 * h22 + h32 * h32
    t1, t2 = start_norm * h11, start_norm * h12
    det = g11 * g22 - g12 * g12
    y1 = (g22 * t1 - g12 * t2) / det
    y2 = (g11 * t2 - g12 * t1) / det
    scale, inverse, last = 1.0 / start_norm, 1.0 / h21, 1.0 / h32
    for j in range(clusters):
        span = slice(j * LANES, (j + 1) * LANES)
        first = rows_of(b, j) * scale
        second = (rows_of(image, j) * scale - h11 * first) * inverse
        solution_out[:, span] = y1 * first + y2 * second
        next_out[:, span] = (rows_of(candidate, j) - h12 * first - h22 * second) * last


def swapped(block, partner):
    return lax.ppermute(block, "rows", [(i, partner(i)) for i in range(lax.axis_size("rows"))])


def core_mate(i):
    return i ^ 1


def even_mate(i):
    return i ^ 2


def odd_mate(i):
    chip = i // 2
    other = chip + 1 if chip % 2 else chip - 1
    return 2 * (other % (lax.axis_size("rows") // 2)) + i % 2


def sends_of(block):
    return [block] + [swapped(block, partner) for partner in (core_mate, even_mate, odd_mate)]


def window_place(distance, clusters):
    me = lax.axis_index("rows")
    core, chip = me % 2, me // 2
    before, after = 3 - chip % 2, 2 + chip % 2
    slot = [
        before,
        jnp.where(core == 0, before + 2, 1),
        0,
        jnp.where(core == 0, 1, after + 2),
        after,
    ]
    slab = distance // clusters
    chosen = jnp.zeros_like(distance)
    for s, value in enumerate(slot):
        chosen = jnp.where(slab == s, value, chosen)
    return chosen * clusters + distance % clusters


def on_device(
    right_sides, near_blocks, near_cols, near_counts, basis_in, target_basis, coupling, far_cols
):
    width = right_sides.shape[1]
    clusters, slots = near_cols.shape
    rank = basis_in.shape[1]
    per_group = LANES // rank
    head = clusters // per_group * R
    size = lax.axis_size("rows")
    every = clusters * size
    unknowns = float(width * size)
    rows = clusters * R

    def shape(*dims, dtype=f32):
        return jax.ShapeDtypeStruct(dims, dtype)

    def scratch(*dims, dtype=f32):
        return pltpu.VMEM(dims, dtype)

    def in_hbm(array):
        return pltpu.with_memory_space_constraint(array, pltpu.HBM)

    def call(kernel, name, out, ins, *args, scratch_shapes=()):
        return pl.pallas_call(
            kernel, out_shape=out, in_specs=ins, out_specs=jax.tree.map(lambda _: VMEM, out),
            scratch_shapes=scratch_shapes, compiler_params=PARAMS, name=name,
        )(*args)

    def exchange(block):
        return lax.all_to_all(block, "rows", 0, 0)

    def gathered(block):
        groups = [list(range(core, size, 2)) for core in range(2)]
        got = lax.all_to_all(block, "rows", 0, 0, axis_index_groups=groups)
        return got, swapped(got, core_mate)

    field, basis, lowered, payload = call(
        functools.partial(start_kernel, per_group), "start",
        (
            shape(rows, LANES), shape(clusters * rank, LANES, dtype=bf16), shape(rows, LANES, dtype=bf16),
            shape(size // 2, head, LANES, dtype=bf16),
        ),
        [HBM] * 2, in_hbm(right_sides), in_hbm(basis_in.reshape(clusters * rank, LANES)),
        scratch_shapes=[scratch(R, width), pltpu.SemaphoreType.DMA((2,))],
    )
    got = gathered(payload)
    held = sends_of(lowered)

    reach = 2 * clusters
    start = lax.axis_index("rows") * clusters
    distance = (near_cols.T - start + reach) % every
    live = jnp.arange(slots, dtype=jnp.int32)[:, None] < near_counts[None, :]
    placed = jnp.where(live, window_place(distance, clusters), 6 * clusters).astype(jnp.int32)
    owner = far_cols.T // clusters
    other_core = (owner % 2) ^ (lax.axis_index("rows") % 2)
    far_index = (other_core * (size // 2) + owner // 2) * clusters + far_cols.T % clusters
    high, low, target = call(
        prepare_kernel, "prepare",
        (
            shape(slots * rank, rank * clusters, dtype=bf16),
            shape(slots * rank, rank * clusters, dtype=bf16),
            shape(rank * clusters, LANES, dtype=bf16),
        ),
        [HBM] * 2 + [ANY] * 3,
        in_hbm(jnp.transpose(coupling, (1, 2, 3, 0))), in_hbm(target_basis.reshape(clusters * rank, LANES)),
        payload, placed, far_index,
        scratch_shapes=[
            scratch(slots, rank, rank, clusters), scratch(clusters * rank, LANES, dtype=bf16),
            pltpu.SemaphoreType.DMA((2,)),
        ],
    )
    blocks = in_hbm(near_blocks.reshape(clusters * slots, LANES, LANES))

    def far_of(got, relay):
        far, near = call(
            functools.partial(far_kernel, per_group), "far",
            (shape(rows, LANES), pltpu.VMEM(blocks.shape, bf16)), [VMEM] * 2 + [SMEM] + [VMEM] * 3 + [HBM, ANY],
            *got, far_index, high, low, target, blocks, relay,
            scratch_shapes=[scratch(size * head, LANES), pltpu.SemaphoreType.DMA((8,))],
        )
        return far, pltpu.with_memory_space_constraint(near, pltpu.VMEM)

    def relay_of(held):
        return call(relay_kernel, "relay", shape(2 * rows, LANES, dtype=bf16), [VMEM] * 2, *held[2:])

    kept = [scratch(rows, LANES), scratch(6 * rows + R, LANES)]
    relay = relay_of(held)
    relayed = swapped(relay, core_mate)
    far, near_here = far_of(got, relay)
    image, lowered, payload = call(
        functools.partial(first_kernel, per_group), "near_one",
        (
            shape(rows, LANES), shape(rows, LANES, dtype=bf16),
            shape(size // 2, head + TAIL, LANES, dtype=bf16),
        ),
        [VMEM] * 5 + [SMEM] + [VMEM] * 4,
        *held, relayed, placed, near_here, field, far, basis, scratch_shapes=kept,
    )
    got = gathered(payload)
    held = sends_of(lowered)
    relay = relay_of(held)
    relayed = swapped(relay, core_mate)
    far, near_here = far_of(got, relay)
    candidate, sums = call(
        functools.partial(second_kernel, per_group, unknowns), "near_two",
        (shape(rows, LANES), shape(size, R, LANES, dtype=bf16)), [VMEM] * 5 + [SMEM] + [VMEM] * 6,
        *held, relayed, placed, near_here, field, image, far, *got, scratch_shapes=kept,
    )
    return call(
        functools.partial(finish_kernel, per_group, unknowns), "finish", (shape(R, width), shape(R, width)),
        [VMEM] * 6, field, image, candidate, *got, exchange(sums),
    )


def solution(mesh):
    return jax.shard_map(
        on_device,
        mesh=mesh,
        in_specs=(
            P("groups", "rows"),
            P("rows", None, None, None),
            P("rows", None),
            P("rows"),
            P("rows", None, None),
            P("rows", None, None),
            P("rows", None, None, None),
            P("rows", None),
        ),
        out_specs=(P("groups", "rows"), P("groups", "rows")),
        check_vma=False,
    )
```

```python
import functools

import jax
import jax.numpy as jnp
from jax import lax
from jax.experimental import pallas as pl
from jax.experimental.pallas import tpu as pltpu
from jax.sharding import PartitionSpec as P

epsilon = 1e-06
f32, bf16 = jnp.float32, jnp.bfloat16
VMEM = pl.BlockSpec(memory_space=pltpu.VMEM)
SMEM = pl.BlockSpec(memory_space=pltpu.SMEM)
HBM = pl.BlockSpec(memory_space=pltpu.HBM)
ANY = pl.BlockSpec(memory_space=pl.ANY)
R = 8
LANES = 128
SUM_SLOTS = 8
TAIL = 16
PARAMS = pltpu.CompilerParams(vmem_limit_bytes=24 * 1024 * 1024)


def lane_ids(rows=R):
    return lax.broadcasted_iota(jnp.int32, (rows, LANES), 1)


def rows_of(ref, j):
    return ref[pl.ds(j * R, R), :]


def dot(a, b, contract=(1, 0)):
    return lax.dot_general(a, b, (((contract[0],), (contract[1],)), ((), ())), preferred_element_type=f32)


def sums_tile(sums):
    lane = lane_ids()
    tile = jnp.zeros((R, LANES), f32)
    for t, partial in enumerate(sums):
        total = jnp.sum(partial, axis=1, keepdims=True)
        high = total.astype(bf16).astype(f32)
        middle = (total - high).astype(bf16).astype(f32)
        low = total - high - middle
        for part, value in enumerate((high, middle, low)):
            tile = jnp.where(lane == part * SUM_SLOTS + t, value, tile)
    return tile


def read_sums(gathered, first_row, rows, count, unknowns):
    total = jnp.zeros((R, LANES), f32)
    for got in gathered:
        for device in range(got.shape[0]):
            total = total + got[device, pl.ds(first_row, rows), :].astype(f32)[:R]
    return [
        sum(total[:, p * SUM_SLOTS + t : p * SUM_SLOTS + t + 1] for p in range(3)) * (1.0 / unknowns)
        for t in range(count)
    ]


def compress(tiles, basis, group):
    stacked = jnp.concatenate(tiles, axis=0)
    high = stacked.astype(bf16)
    low = (stacked - high.astype(f32)).astype(bf16)
    both = dot(jnp.concatenate([high, low], axis=0), basis[pl.ds(group * LANES, LANES), :], (1, 1))
    rows = len(tiles) * R
    both = both[:rows] + both[rows:]
    lane = lane_ids()
    rank = LANES // len(tiles)
    tile = jnp.zeros((R, LANES), f32)
    for m in range(len(tiles)):
        tile = jnp.where(lane // rank == m, both[m * R : (m + 1) * R], tile)
    return tile


def write_payload(payload, tiles, sums, basis, per_group):
    groups = len(tiles) // per_group
    parts = [compress(tiles[g * per_group : (g + 1) * per_group], basis, g) for g in range(groups)]
    if sums:
        parts += [sums_tile(sums), jnp.zeros((TAIL - R, LANES), f32)]
    block = jnp.concatenate(parts, axis=0).astype(bf16)
    for device in range(payload.shape[0]):
        payload[device] = block


def start_kernel(per_group, b_hbm, basis_hbm, field, basis, lowered, payload, b, sems):
    copies = [
        pltpu.make_async_copy(b_hbm, b, sems.at[0]),
        pltpu.make_async_copy(basis_hbm, basis, sems.at[1]),
    ]
    for copy in copies:
        copy.start()
    for copy in copies:
        copy.wait()
    clusters = b.shape[1] // LANES
    tiles = [b[:, j * LANES : (j + 1) * LANES] for j in range(clusters)]
    field[...] = jnp.concatenate(tiles, axis=0)
    lowered[...] = jnp.concatenate(tiles, axis=0).astype(bf16)
    write_payload(payload, tiles, [], basis, per_group)


def prepare_kernel(coupling_hbm, target_hbm, _, __, ___, high_out, low_out, target_out, coupling, target, sems):
    copies = [
        pltpu.make_async_copy(coupling_hbm, coupling, sems.at[0]),
        pltpu.make_async_copy(target_hbm, target, sems.at[1]),
    ]
    for copy in copies:
        copy.start()
    for copy in copies:
        copy.wait()
    slots, rank, _, clusters = coupling.shape
    per_tile = LANES // clusters
    for s in range(rank // per_tile):
        pieces = [
            coupling[:, s * per_tile + p].reshape(slots * rank, clusters) for p in range(per_tile)
        ]
        tile = jnp.concatenate(pieces, axis=1)
        high = tile.astype(bf16)
        high_out[:, s * LANES : (s + 1) * LANES] = high
        low_out[:, s * LANES : (s + 1) * LANES] = (tile - high.astype(f32)).astype(bf16)
    size = rank * clusters
    row = lax.broadcasted_iota(jnp.int32, (size, size), 0)
    column = lax.broadcasted_iota(jnp.int32, (size, size), 1)
    wanted = (row % clusters) * rank + row // clusters
    target_out[...] = dot((column == wanted).astype(bf16), target[...]).astype(bf16)


def chunk_copies(source, first, target, sems):
    chunks = sems.shape[0]
    each = target.shape[0] // chunks
    copies = [
        pltpu.make_async_copy(
            source.at[pl.ds(first + c * each, each)], target.at[pl.ds(c * each, each)], sems.at[c]
        )
        for c in range(chunks)
    ]
    for c, copy in enumerate(copies):
        copy.start(priority=c % 2)
    return copies


def far_kernel(per_group, got, got_mate, far_cols, high, low, target, blocks_hbm, far, blocks, table, sems):
    copies = chunk_copies(blocks_hbm, 0, blocks, sems)
    slots, clusters = far_cols.shape
    rank = LANES // per_group
    groups = clusters // per_group
    head = groups * R
    for part, values in enumerate((got, got_mate)):
        for device in range(values.shape[0]):
            at = (part * values.shape[0] + device) * head
            table[pl.ds(at, head), :] = values[device, pl.ds(0, head), :].astype(f32)
    lane = lane_ids()
    picked = []
    for i in range(clusters):
        tile = jnp.zeros((R, LANES), f32)
        for k in range(slots):
            j = far_cols[k, i]
            found = table[pl.ds(pl.multiple_of(lax.div(j, per_group) * R, R), R), :]
            shift = ((k - j) * rank) & (LANES - 1)
            tile = jnp.where(lane // rank == k, pltpu.roll(found, shift, 1), tile)
        picked.append(tile)
    picked = jnp.concatenate(picked, axis=0).astype(bf16)
    crossed = dot(picked, high[...]) + dot(picked, low[...])
    expanded_high, expanded_low = [], []
    for s in range(rank * clusters // LANES):
        tile = jnp.zeros((R, LANES), f32)
        for i in range(clusters):
            part = crossed[i * R : (i + 1) * R, s * LANES : (s + 1) * LANES]
            tile = jnp.where(lane % clusters == i, part, tile)
        tile_high = tile.astype(bf16).astype(f32)
        tile_low = tile - tile_high
        for source, kept in ((tile_high, expanded_high), (tile_low, expanded_low)):
            spread = [jnp.where(lane % clusters == i, source, 0.0) for i in range(clusters)]
            kept.append(jnp.concatenate(spread, axis=0).astype(bf16))
    far[...] = dot(jnp.concatenate(expanded_high, axis=1), target[...]) + dot(
        jnp.concatenate(expanded_low, axis=1), target[...]
    )
    for copy in copies:
        copy.wait()


def behind_kernel(values, _, out):
    out[...] = values[...]


def relay_kernel(even, odd, _, both):
    rows = even.shape[0]
    both[pl.ds(0, rows), :] = even[...]
    both[pl.ds(rows, rows), :] = odd[...]


def near_field(slabs, placed, blocks, blocks_hbm, near, window, later, sems):
    slots, clusters = placed.shape
    copies = chunk_copies(blocks_hbm, blocks.shape[0], later, sems)
    each = later.shape[0] // len(copies)
    at = 0
    for slab in slabs:
        window[pl.ds(at, slab.shape[0]), :] = slab[...].astype(f32)
        at += slab.shape[0]
    window[pl.ds(at, R), :] = jnp.zeros((R, LANES), f32)

    def fetch(k, i):
        return window[pl.ds(pl.multiple_of(placed[k, i] * R, R), R), :]

    def block(k, i):
        at = i * slots + k
        return blocks[at] if at < blocks.shape[0] else later[at - blocks.shape[0]]

    for i in range(0, clusters, 2):
        beyond = i * slots - blocks.shape[0]
        if beyond >= 0 and beyond % each == 0:
            copies[beyond // each].wait()
        both = jnp.zeros((2 * R, 2 * LANES), f32)
        for k in range(0, slots, 2):
            sources = jnp.concatenate(
                [jnp.concatenate([fetch(k + n, i), fetch(k + n, i + 1)], axis=0) for n in range(2)], axis=1
            )
            weights = jnp.concatenate(
                [jnp.concatenate([block(k + n, i), block(k + n, i + 1)], axis=0) for n in range(2)], axis=1
            )
            both = both + dot(sources.astype(bf16), weights, (1, 1))
        near[pl.ds(i * R, R), :] = both[:R, :LANES]
        near[pl.ds((i + 1) * R, R), :] = both[R:, LANES:]


def first_kernel(
    per_group, own, mate, even, odd, relayed, placed, blocks, blocks_hbm, b, far, basis,
    image, lowered, payload, near, window, later, sems,
):
    near_field((own, mate, even, odd, relayed), placed, blocks, blocks_hbm, near, window, later, sems)
    clusters = placed.shape[1]
    tiles = []
    sums = [jnp.zeros((R, LANES), f32) for _ in range(3)]
    for i in range(clusters):
        field = rows_of(b, i)
        made = 0.5 * field + (rows_of(near, i) + rows_of(far, i))
        sums = [s + f * g for s, f, g in zip(sums, (field, field, made), (field, made, made))]
        tiles.append(made)
    for i in range(0, clusters, 2):
        both = jnp.concatenate(tiles[i : i + 2], axis=0)
        image[pl.ds(i * R, 2 * R), :] = both
        lowered[pl.ds(i * R, 2 * R), :] = both.astype(bf16)
    write_payload(payload, tiles, sums, basis, per_group)


def arnoldi_one(bb, bw, ww):
    whole = bb + epsilon
    start_norm = jnp.sqrt(whole)
    scale = 1.0 / start_norm
    v11 = bb / whole
    h11 = (bw * scale) * scale
    uu = jnp.maximum((ww * scale) * scale - 2.0 * h11 * h11 + h11 * h11 * v11, 0.0)
    h21 = jnp.sqrt(uu + epsilon)
    return start_norm, h11, h21, v11, uu / (uu + epsilon), h11 * (1.0 - v11) / h21


def second_kernel(
    per_group, unknowns, own, mate, even, odd, relayed, placed, blocks, blocks_hbm, b, image, far,
    got, got_mate, candidate, sums_out, near, window, later, sems,
):
    near_field((own, mate, even, odd, relayed), placed, blocks, blocks_hbm, near, window, later, sems)
    clusters = placed.shape[1]
    head = clusters // per_group * R
    start_norm, h11, h21, _, _, _ = arnoldi_one(*read_sums((got, got_mate), head, TAIL, 3, unknowns))
    scale = 1.0 / start_norm
    inverse = 1.0 / h21
    sums = [jnp.zeros((R, LANES), f32) for _ in range(3)]
    for j in range(clusters):
        held = rows_of(image, j) * scale
        first = rows_of(b, j) * scale
        second = (held - h11 * first) * inverse
        made = (0.5 * held + (rows_of(near, j) + rows_of(far, j)) * scale - h11 * held) * inverse
        sums = [s + v * made for s, v in zip(sums, (first, second, made))]
        candidate[pl.ds(j * R, R), :] = made
    tile = sums_tile(sums).astype(bf16)
    for device in range(sums_out.shape[0]):
        sums_out[device] = tile


def finish_kernel(per_group, unknowns, b, image, candidate, got1, got1_mate, got2, solution_out, next_out):
    clusters = b.shape[0] // R
    head = clusters // per_group * R
    start_norm, h11, h21, v11, v22, v12 = arnoldi_one(*read_sums((got1, got1_mate), head, TAIL, 3, unknowns))
    h12, h22, ww = read_sums((got2,), 0, R, 3, unknowns)
    uu = ww - 2.0 * (h12 * h12 + h22 * h22) + h12 * h12 * v11 + h22 * h22 * v22 + 2.0 * h12 * h22 * v12
    h32 = jnp.sqrt(jnp.maximum(uu, 0.0) + epsilon)
    g11 = h11 * h11 + h21 * h21
    g12 = h11 * h12 + h21 * h22
    g22 = h12 * h12 + h22 * h22 + h32 * h32
    t1, t2 = start_norm * h11, start_norm * h12
    det = g11 * g22 - g12 * g12
    y1 = (g22 * t1 - g12 * t2) / det
    y2 = (g11 * t2 - g12 * t1) / det
    scale, inverse, last = 1.0 / start_norm, 1.0 / h21, 1.0 / h32
    for j in range(clusters):
        span = slice(j * LANES, (j + 1) * LANES)
        first = rows_of(b, j) * scale
        second = (rows_of(image, j) * scale - h11 * first) * inverse
        solution_out[:, span] = y1 * first + y2 * second
        next_out[:, span] = (rows_of(candidate, j) - h12 * first - h22 * second) * last


def swapped(block, partner):
    return lax.ppermute(block, "rows", [(i, partner(i)) for i in range(lax.axis_size("rows"))])


def core_mate(i):
    return i ^ 1


def even_mate(i):
    return i ^ 2


def odd_mate(i):
    chip = i // 2
    other = chip + 1 if chip % 2 else chip - 1
    return 2 * (other % (lax.axis_size("rows") // 2)) + i % 2


def sends_of(block):
    return [block] + [swapped(block, partner) for partner in (core_mate, even_mate, odd_mate)]


def window_place(distance, clusters):
    me = lax.axis_index("rows")
    core, chip = me % 2, me // 2
    before, after = 3 - chip % 2, 2 + chip % 2
    slot = [
        before,
        jnp.where(core == 0, before + 2, 1),
        0,
        jnp.where(core == 0, 1, after + 2),
        after,
    ]
    slab = distance // clusters
    chosen = jnp.zeros_like(distance)
    for s, value in enumerate(slot):
        chosen = jnp.where(slab == s, value, chosen)
    return chosen * clusters + distance % clusters


def on_device(
    right_sides, near_blocks, near_cols, near_counts, basis_in, target_basis, coupling, far_cols
):
    width = right_sides.shape[1]
    clusters, slots = near_cols.shape
    rank = basis_in.shape[1]
    per_group = LANES // rank
    head = clusters // per_group * R
    size = lax.axis_size("rows")
    every = clusters * size
    unknowns = float(width * size)
    rows = clusters * R

    def shape(*dims, dtype=f32):
        return jax.ShapeDtypeStruct(dims, dtype)

    def scratch(*dims, dtype=f32):
        return pltpu.VMEM(dims, dtype)

    def in_hbm(array):
        return pltpu.with_memory_space_constraint(array, pltpu.HBM)

    def call(kernel, name, out, ins, *args, scratch_shapes=()):
        return pl.pallas_call(
            kernel, out_shape=out, in_specs=ins, out_specs=jax.tree.map(lambda _: VMEM, out),
            scratch_shapes=scratch_shapes, compiler_params=PARAMS, name=name,
        )(*args)

    def exchange(block):
        return lax.all_to_all(block, "rows", 0, 0)

    def gather(block):
        groups = [list(range(core, size, 2)) for core in range(2)]
        return lax.all_to_all(block, "rows", 0, 0, axis_index_groups=groups)

    field, basis, lowered, payload = call(
        functools.partial(start_kernel, per_group), "start",
        (
            shape(rows, LANES), shape(clusters * rank, LANES, dtype=bf16), shape(rows, LANES, dtype=bf16),
            shape(size // 2, head, LANES, dtype=bf16),
        ),
        [HBM] * 2, in_hbm(right_sides), in_hbm(basis_in.reshape(clusters * rank, LANES)),
        scratch_shapes=[scratch(R, width), pltpu.SemaphoreType.DMA((2,))],
    )
    got = gather(payload)
    held = sends_of(lowered)

    reach = 2 * clusters
    start = lax.axis_index("rows") * clusters
    distance = (near_cols.T - start + reach) % every
    live = jnp.arange(slots, dtype=jnp.int32)[:, None] < near_counts[None, :]
    placed = jnp.where(live, window_place(distance, clusters), 6 * clusters).astype(jnp.int32)
    owner = far_cols.T // clusters
    other_core = (owner % 2) ^ (lax.axis_index("rows") % 2)
    far_index = (other_core * (size // 2) + owner // 2) * clusters + far_cols.T % clusters
    high, low, target = call(
        prepare_kernel, "prepare",
        (
            shape(slots * rank, rank * clusters, dtype=bf16),
            shape(slots * rank, rank * clusters, dtype=bf16),
            shape(rank * clusters, LANES, dtype=bf16),
        ),
        [HBM] * 2 + [ANY] * 3,
        in_hbm(jnp.transpose(coupling, (1, 2, 3, 0))), in_hbm(target_basis.reshape(clusters * rank, LANES)),
        payload, placed, far_index,
        scratch_shapes=[
            scratch(slots, rank, rank, clusters), scratch(clusters * rank, LANES, dtype=bf16),
            pltpu.SemaphoreType.DMA((2,)),
        ],
    )
    blocks = in_hbm(near_blocks.reshape(clusters * slots, LANES, LANES))

    here = blocks.shape[0] // 2

    def far_of(got):
        far, first = call(
            functools.partial(far_kernel, per_group), "far",
            (shape(rows, LANES), pltpu.VMEM((here, LANES, LANES), bf16)), [VMEM] * 2 + [SMEM] + [VMEM] * 3 + [HBM],
            *got, far_index, high, low, target, blocks,
            scratch_shapes=[scratch(size * head, LANES), pltpu.SemaphoreType.DMA((4,))],
        )
        return far, pltpu.with_memory_space_constraint(first, pltpu.VMEM)

    def relayed(held, far):
        both = call(
            relay_kernel, "relay", shape(2 * rows, LANES, dtype=bf16), [VMEM] * 2 + [ANY], *held[2:], far
        )
        return swapped(both, core_mate)

    kept = [
        scratch(rows, LANES), scratch(6 * rows + R, LANES),
        scratch(blocks.shape[0] - here, LANES, LANES, dtype=bf16), pltpu.SemaphoreType.DMA((4,)),
    ]
    got = call(behind_kernel, "behind", shape(*got.shape, dtype=bf16), [VMEM, ANY], got, target)
    far, first = far_of((got, swapped(got, core_mate)))
    image, lowered, payload = call(
        functools.partial(first_kernel, per_group), "near_one",
        (
            shape(rows, LANES), shape(rows, LANES, dtype=bf16),
            shape(size // 2, head + TAIL, LANES, dtype=bf16),
        ),
        [VMEM] * 5 + [SMEM, VMEM, HBM] + [VMEM] * 3,
        *held, relayed(held, far), placed, first, blocks, field, far, basis, scratch_shapes=kept,
    )
    got = gather(payload)
    got = (got, swapped(got, core_mate))
    held = sends_of(lowered)
    far, first = far_of(got)
    candidate, sums = call(
        functools.partial(second_kernel, per_group, unknowns), "near_two",
        (shape(rows, LANES), shape(size, R, LANES, dtype=bf16)), [VMEM] * 5 + [SMEM, VMEM, HBM] + [VMEM] * 5,
        *held, relayed(held, far), placed, first, blocks, field, image, far, *got, scratch_shapes=kept,
    )
    return call(
        functools.partial(finish_kernel, per_group, unknowns), "finish", (shape(R, width), shape(R, width)),
        [VMEM] * 6, field, image, candidate, *got, exchange(sums),
    )


def solution(mesh):
    return jax.shard_map(
        on_device,
        mesh=mesh,
        in_specs=(
            P("groups", "rows"),
            P("rows", None, None, None),
            P("rows", None),
            P("rows"),
            P("rows", None, None),
            P("rows", None, None),
            P("rows", None, None, None),
            P("rows", None),
        ),
        out_specs=(P("groups", "rows"), P("groups", "rows")),
        check_vma=False,
    )
```

```python
import functools

import jax
import jax.numpy as jnp
from jax import lax
from jax.experimental import pallas as pl
from jax.experimental.pallas import tpu as pltpu
from jax.sharding import PartitionSpec as P

epsilon = 1e-06
f32, bf16 = jnp.float32, jnp.bfloat16
VMEM = pl.BlockSpec(memory_space=pltpu.VMEM)
SMEM = pl.BlockSpec(memory_space=pltpu.SMEM)
HBM = pl.BlockSpec(memory_space=pltpu.HBM)
ANY = pl.BlockSpec(memory_space=pl.ANY)
R = 8
LANES = 128
SUM_SLOTS = 8
TAIL = 16
PARAMS = pltpu.CompilerParams(vmem_limit_bytes=24 * 1024 * 1024)


def lane_ids(rows=R):
    return lax.broadcasted_iota(jnp.int32, (rows, LANES), 1)


def rows_of(ref, j):
    return ref[pl.ds(j * R, R), :]


def dot(a, b, contract=(1, 0)):
    return lax.dot_general(a, b, (((contract[0],), (contract[1],)), ((), ())), preferred_element_type=f32)


def sums_tile(sums):
    lane = lane_ids()
    tile = jnp.zeros((R, LANES), f32)
    for t, partial in enumerate(sums):
        total = jnp.sum(partial, axis=1, keepdims=True)
        high = total.astype(bf16).astype(f32)
        middle = (total - high).astype(bf16).astype(f32)
        low = total - high - middle
        for part, value in enumerate((high, middle, low)):
            tile = jnp.where(lane == part * SUM_SLOTS + t, value, tile)
    return tile


def read_sums(gathered, first_row, rows, count, unknowns):
    total = jnp.zeros((R, LANES), f32)
    for got in gathered:
        for device in range(got.shape[0]):
            total = total + got[device, pl.ds(first_row, rows), :].astype(f32)[:R]
    return [
        sum(total[:, p * SUM_SLOTS + t : p * SUM_SLOTS + t + 1] for p in range(3)) * (1.0 / unknowns)
        for t in range(count)
    ]


def compress(tiles, basis, group):
    stacked = jnp.concatenate(tiles, axis=0)
    high = stacked.astype(bf16)
    low = (stacked - high.astype(f32)).astype(bf16)
    both = dot(jnp.concatenate([high, low], axis=0), basis[pl.ds(group * LANES, LANES), :], (1, 1))
    rows = len(tiles) * R
    both = both[:rows] + both[rows:]
    lane = lane_ids()
    rank = LANES // len(tiles)
    tile = jnp.zeros((R, LANES), f32)
    for m in range(len(tiles)):
        tile = jnp.where(lane // rank == m, both[m * R : (m + 1) * R], tile)
    return tile


def write_payload(payload, tiles, sums, basis, per_group):
    groups = len(tiles) // per_group
    parts = [compress(tiles[g * per_group : (g + 1) * per_group], basis, g) for g in range(groups)]
    if sums:
        parts += [sums_tile(sums), jnp.zeros((TAIL - R, LANES), f32)]
    block = jnp.concatenate(parts, axis=0).astype(bf16)
    for device in range(payload.shape[0]):
        payload[device] = block


def start_kernel(per_group, b_hbm, basis_hbm, field, basis, lowered, payload, b, sems):
    copies = [
        pltpu.make_async_copy(b_hbm, b, sems.at[0]),
        pltpu.make_async_copy(basis_hbm, basis, sems.at[1]),
    ]
    for copy in copies:
        copy.start()
    for copy in copies:
        copy.wait()
    clusters = b.shape[1] // LANES
    tiles = [b[:, j * LANES : (j + 1) * LANES] for j in range(clusters)]
    field[...] = jnp.concatenate(tiles, axis=0)
    lowered[...] = jnp.concatenate(tiles, axis=0).astype(bf16)
    write_payload(payload, tiles, [], basis, per_group)


def prepare_kernel(coupling_hbm, target_hbm, _, __, ___, high_out, low_out, target_out, coupling, target, sems):
    copies = [
        pltpu.make_async_copy(coupling_hbm, coupling, sems.at[0]),
        pltpu.make_async_copy(target_hbm, target, sems.at[1]),
    ]
    for copy in copies:
        copy.start()
    for copy in copies:
        copy.wait()
    slots, rank, _, clusters = coupling.shape
    per_tile = LANES // clusters
    for s in range(rank // per_tile):
        pieces = [
            coupling[:, s * per_tile + p].reshape(slots * rank, clusters) for p in range(per_tile)
        ]
        tile = jnp.concatenate(pieces, axis=1)
        high = tile.astype(bf16)
        high_out[:, s * LANES : (s + 1) * LANES] = high
        low_out[:, s * LANES : (s + 1) * LANES] = (tile - high.astype(f32)).astype(bf16)
    size = rank * clusters
    row = lax.broadcasted_iota(jnp.int32, (size, size), 0)
    column = lax.broadcasted_iota(jnp.int32, (size, size), 1)
    wanted = (row % clusters) * rank + row // clusters
    target_out[...] = dot((column == wanted).astype(bf16), target[...]).astype(bf16)


def fetch_kernel(blocks_hbm, *refs):
    *_, blocks, token, sems = refs
    chunks = sems.shape[0]
    each = blocks.shape[0] // chunks
    copies = [
        pltpu.make_async_copy(
            blocks_hbm.at[pl.ds(c * each, each)], blocks.at[pl.ds(c * each, each)], sems.at[c]
        )
        for c in range(chunks)
    ]
    for copy in copies:
        copy.start()
    token[...] = jnp.zeros_like(token)
    for copy in copies:
        copy.wait()


def behind_kernel(values, *refs):
    refs[-1][...] = values[...]


def far_kernel(per_group, got, got_mate, far_cols, high, low, target, _, far, table):
    slots, clusters = far_cols.shape
    rank = LANES // per_group
    groups = clusters // per_group
    head = groups * R
    for part, values in enumerate((got, got_mate)):
        for device in range(values.shape[0]):
            at = (part * values.shape[0] + device) * head
            table[pl.ds(at, head), :] = values[device, pl.ds(0, head), :].astype(f32)
    lane = lane_ids()
    picked = []
    for i in range(clusters):
        tile = jnp.zeros((R, LANES), f32)
        for k in range(slots):
            j = far_cols[k, i]
            found = table[pl.ds(pl.multiple_of(lax.div(j, per_group) * R, R), R), :]
            shift = ((k - j) * rank) & (LANES - 1)
            tile = jnp.where(lane // rank == k, pltpu.roll(found, shift, 1), tile)
        picked.append(tile)
    picked = jnp.concatenate(picked, axis=0).astype(bf16)
    crossed = dot(picked, high[...]) + dot(picked, low[...])
    expanded_high, expanded_low = [], []
    for s in range(rank * clusters // LANES):
        tile = jnp.zeros((R, LANES), f32)
        for i in range(clusters):
            part = crossed[i * R : (i + 1) * R, s * LANES : (s + 1) * LANES]
            tile = jnp.where(lane % clusters == i, part, tile)
        tile_high = tile.astype(bf16).astype(f32)
        tile_low = tile - tile_high
        for source, kept in ((tile_high, expanded_high), (tile_low, expanded_low)):
            spread = [jnp.where(lane % clusters == i, source, 0.0) for i in range(clusters)]
            kept.append(jnp.concatenate(spread, axis=0).astype(bf16))
    far[...] = dot(jnp.concatenate(expanded_high, axis=1), target[...]) + dot(
        jnp.concatenate(expanded_low, axis=1), target[...]
    )


def relay_kernel(even, odd, _, both):
    rows = even.shape[0]
    both[pl.ds(0, rows), :] = even[...]
    both[pl.ds(rows, rows), :] = odd[...]


def near_field(slabs, placed, blocks, near, window):
    slots, clusters = placed.shape
    at = 0
    for slab in slabs:
        window[pl.ds(at, slab.shape[0]), :] = slab[...].astype(f32)
        at += slab.shape[0]
    window[pl.ds(at, R), :] = jnp.zeros((R, LANES), f32)

    def fetch(k, i):
        return window[pl.ds(pl.multiple_of(placed[k, i] * R, R), R), :]

    def block(k, i):
        return blocks[i * slots + k]

    for i in range(0, clusters, 2):
        both = jnp.zeros((2 * R, 2 * LANES), f32)
        for k in range(0, slots, 2):
            sources = jnp.concatenate(
                [jnp.concatenate([fetch(k + n, i), fetch(k + n, i + 1)], axis=0) for n in range(2)], axis=1
            )
            weights = jnp.concatenate(
                [jnp.concatenate([block(k + n, i), block(k + n, i + 1)], axis=0) for n in range(2)], axis=1
            )
            both = both + dot(sources.astype(bf16), weights, (1, 1))
        near[pl.ds(i * R, R), :] = both[:R, :LANES]
        near[pl.ds((i + 1) * R, R), :] = both[R:, LANES:]


def first_kernel(
    per_group, own, mate, even, odd, relayed, placed, blocks, b, far, basis, image, lowered, payload, near, window,
):
    near_field((own, mate, even, odd, relayed), placed, blocks, near, window)
    clusters = placed.shape[1]
    tiles = []
    sums = [jnp.zeros((R, LANES), f32) for _ in range(3)]
    for i in range(clusters):
        field = rows_of(b, i)
        made = 0.5 * field + (rows_of(near, i) + rows_of(far, i))
        sums = [s + f * g for s, f, g in zip(sums, (field, field, made), (field, made, made))]
        tiles.append(made)
    for i in range(0, clusters, 2):
        both = jnp.concatenate(tiles[i : i + 2], axis=0)
        image[pl.ds(i * R, 2 * R), :] = both
        lowered[pl.ds(i * R, 2 * R), :] = both.astype(bf16)
    write_payload(payload, tiles, sums, basis, per_group)


def arnoldi_one(bb, bw, ww):
    whole = bb + epsilon
    start_norm = jnp.sqrt(whole)
    scale = 1.0 / start_norm
    v11 = bb / whole
    h11 = (bw * scale) * scale
    uu = jnp.maximum((ww * scale) * scale - 2.0 * h11 * h11 + h11 * h11 * v11, 0.0)
    h21 = jnp.sqrt(uu + epsilon)
    return start_norm, h11, h21, v11, uu / (uu + epsilon), h11 * (1.0 - v11) / h21


def second_kernel(
    per_group, unknowns, own, mate, even, odd, relayed, placed, blocks, b, image, far, got, got_mate,
    candidate, sums_out, near, window,
):
    near_field((own, mate, even, odd, relayed), placed, blocks, near, window)
    clusters = placed.shape[1]
    head = clusters // per_group * R
    start_norm, h11, h21, _, _, _ = arnoldi_one(*read_sums((got, got_mate), head, TAIL, 3, unknowns))
    scale = 1.0 / start_norm
    inverse = 1.0 / h21
    sums = [jnp.zeros((R, LANES), f32) for _ in range(3)]
    for j in range(clusters):
        held = rows_of(image, j) * scale
        first = rows_of(b, j) * scale
        second = (held - h11 * first) * inverse
        made = (0.5 * held + (rows_of(near, j) + rows_of(far, j)) * scale - h11 * held) * inverse
        sums = [s + v * made for s, v in zip(sums, (first, second, made))]
        candidate[pl.ds(j * R, R), :] = made
    tile = sums_tile(sums).astype(bf16)
    for device in range(sums_out.shape[0]):
        sums_out[device] = tile


def finish_kernel(per_group, unknowns, b, image, candidate, got1, got1_mate, got2, solution_out, next_out):
    clusters = b.shape[0] // R
    head = clusters // per_group * R
    start_norm, h11, h21, v11, v22, v12 = arnoldi_one(*read_sums((got1, got1_mate), head, TAIL, 3, unknowns))
    h12, h22, ww = read_sums((got2,), 0, R, 3, unknowns)
    uu = ww - 2.0 * (h12 * h12 + h22 * h22) + h12 * h12 * v11 + h22 * h22 * v22 + 2.0 * h12 * h22 * v12
    h32 = jnp.sqrt(jnp.maximum(uu, 0.0) + epsilon)
    g11 = h11 * h11 + h21 * h21
    g12 = h11 * h12 + h21 * h22
    g22 = h12 * h12 + h22 * h22 + h32 * h32
    t1, t2 = start_norm * h11, start_norm * h12
    det = g11 * g22 - g12 * g12
    y1 = (g22 * t1 - g12 * t2) / det
    y2 = (g11 * t2 - g12 * t1) / det
    scale, inverse, last = 1.0 / start_norm, 1.0 / h21, 1.0 / h32
    for j in range(clusters):
        span = slice(j * LANES, (j + 1) * LANES)
        first = rows_of(b, j) * scale
        second = (rows_of(image, j) * scale - h11 * first) * inverse
        solution_out[:, span] = y1 * first + y2 * second
        next_out[:, span] = (rows_of(candidate, j) - h12 * first - h22 * second) * last


def swapped(block, partner):
    return lax.ppermute(block, "rows", [(i, partner(i)) for i in range(lax.axis_size("rows"))])


def core_mate(i):
    return i ^ 1


def even_mate(i):
    return i ^ 2


def odd_mate(i):
    chip = i // 2
    other = chip + 1 if chip % 2 else chip - 1
    return 2 * (other % (lax.axis_size("rows") // 2)) + i % 2


def sends_of(block):
    return [block] + [swapped(block, partner) for partner in (core_mate, even_mate, odd_mate)]


def window_place(distance, clusters):
    me = lax.axis_index("rows")
    core, chip = me % 2, me // 2
    before, after = 3 - chip % 2, 2 + chip % 2
    slot = [
        before,
        jnp.where(core == 0, before + 2, 1),
        0,
        jnp.where(core == 0, 1, after + 2),
        after,
    ]
    slab = distance // clusters
    chosen = jnp.zeros_like(distance)
    for s, value in enumerate(slot):
        chosen = jnp.where(slab == s, value, chosen)
    return chosen * clusters + distance % clusters


def on_device(
    right_sides, near_blocks, near_cols, near_counts, basis_in, target_basis, coupling, far_cols
):
    width = right_sides.shape[1]
    clusters, slots = near_cols.shape
    rank = basis_in.shape[1]
    per_group = LANES // rank
    head = clusters // per_group * R
    size = lax.axis_size("rows")
    every = clusters * size
    unknowns = float(width * size)
    rows = clusters * R

    def shape(*dims, dtype=f32):
        return jax.ShapeDtypeStruct(dims, dtype)

    def scratch(*dims, dtype=f32):
        return pltpu.VMEM(dims, dtype)

    def in_hbm(array):
        return pltpu.with_memory_space_constraint(array, pltpu.HBM)

    def call(kernel, name, out, ins, *args, scratch_shapes=()):
        return pl.pallas_call(
            kernel, out_shape=out, in_specs=ins, out_specs=jax.tree.map(lambda _: VMEM, out),
            scratch_shapes=scratch_shapes, compiler_params=PARAMS, name=name,
        )(*args)

    def exchange(block):
        return lax.all_to_all(block, "rows", 0, 0)

    def gather(block):
        groups = [list(range(core, size, 2)) for core in range(2)]
        return lax.all_to_all(block, "rows", 0, 0, axis_index_groups=groups)

    field, basis, lowered, payload = call(
        functools.partial(start_kernel, per_group), "start",
        (
            shape(rows, LANES), shape(clusters * rank, LANES, dtype=bf16), shape(rows, LANES, dtype=bf16),
            shape(size // 2, head, LANES, dtype=bf16),
        ),
        [HBM] * 2, in_hbm(right_sides), in_hbm(basis_in.reshape(clusters * rank, LANES)),
        scratch_shapes=[scratch(R, width), pltpu.SemaphoreType.DMA((2,))],
    )
    got = gather(payload)
    held = sends_of(lowered)

    reach = 2 * clusters
    start = lax.axis_index("rows") * clusters
    distance = (near_cols.T - start + reach) % every
    live = jnp.arange(slots, dtype=jnp.int32)[:, None] < near_counts[None, :]
    placed = jnp.where(live, window_place(distance, clusters), 6 * clusters).astype(jnp.int32)
    owner = far_cols.T // clusters
    other_core = (owner % 2) ^ (lax.axis_index("rows") % 2)
    far_index = (other_core * (size // 2) + owner // 2) * clusters + far_cols.T % clusters
    high, low, target = call(
        prepare_kernel, "prepare",
        (
            shape(slots * rank, rank * clusters, dtype=bf16),
            shape(slots * rank, rank * clusters, dtype=bf16),
            shape(rank * clusters, LANES, dtype=bf16),
        ),
        [HBM] * 2 + [ANY] * 3,
        in_hbm(jnp.transpose(coupling, (1, 2, 3, 0))), in_hbm(target_basis.reshape(clusters * rank, LANES)),
        payload, placed, far_index,
        scratch_shapes=[
            scratch(slots, rank, rank, clusters), scratch(clusters * rank, LANES, dtype=bf16),
            pltpu.SemaphoreType.DMA((2,)),
        ],
    )
    blocks = in_hbm(near_blocks.reshape(clusters * slots, LANES, LANES))


    def arrived(got, held, *made):
        near_blocks_here, token = call(
            fetch_kernel, "fetch", (pltpu.VMEM(blocks.shape, bf16), shape(R, LANES)),
            [HBM] + [ANY] * (1 + len(made)), blocks, got, *made,
            scratch_shapes=[pltpu.SemaphoreType.DMA((8,))],
        )
        near_blocks_here = pltpu.with_memory_space_constraint(near_blocks_here, pltpu.VMEM)
        got = call(
            behind_kernel, "behind", shape(*got.shape, dtype=bf16), [VMEM] + [ANY] * 2, got, held[3], token
        )
        got = (got, swapped(got, core_mate))
        relay = call(
            relay_kernel, "relay", shape(2 * rows, LANES, dtype=bf16), [VMEM] * 2 + [ANY], *held[2:], got[0]
        )
        far = call(
            functools.partial(far_kernel, per_group), "far", shape(rows, LANES),
            [VMEM] * 2 + [SMEM] + [VMEM] * 3 + [ANY], *got, far_index, high, low, target, relay,
            scratch_shapes=[scratch(size * head, LANES)],
        )
        return got, near_blocks_here, held + [swapped(relay, core_mate)], far

    kept = [scratch(rows, LANES), scratch(6 * rows + R, LANES)]
    got, near_blocks_here, held, far = arrived(got, held, target)
    image, lowered, payload = call(
        functools.partial(first_kernel, per_group), "near_one",
        (
            shape(rows, LANES), shape(rows, LANES, dtype=bf16),
            shape(size // 2, head + TAIL, LANES, dtype=bf16),
        ),
        [VMEM] * 5 + [SMEM] + [VMEM] * 4,
        *held, placed, near_blocks_here, field, far, basis, scratch_shapes=kept,
    )
    got = gather(payload)
    held = sends_of(lowered)
    got, near_blocks_here, held, far = arrived(got, held)
    candidate, sums = call(
        functools.partial(second_kernel, per_group, unknowns), "near_two",
        (shape(rows, LANES), shape(size, R, LANES, dtype=bf16)), [VMEM] * 5 + [SMEM] + [VMEM] * 6,
        *held, placed, near_blocks_here, field, image, far, *got, scratch_shapes=kept,
    )
    return call(
        functools.partial(finish_kernel, per_group, unknowns), "finish", (shape(R, width), shape(R, width)),
        [VMEM] * 6, field, image, candidate, *got, exchange(sums),
    )


def solution(mesh):
    return jax.shard_map(
        on_device,
        mesh=mesh,
        in_specs=(
            P("groups", "rows"),
            P("rows", None, None, None),
            P("rows", None),
            P("rows"),
            P("rows", None, None),
            P("rows", None, None),
            P("rows", None, None, None),
            P("rows", None),
        ),
        out_specs=(P("groups", "rows"), P("groups", "rows")),
        check_vma=False,
    )
```

```python
import functools

import jax
import jax.numpy as jnp
from jax import lax
from jax.experimental import pallas as pl
from jax.experimental.pallas import tpu as pltpu
from jax.sharding import PartitionSpec as P

epsilon = 1e-06
f32, bf16 = jnp.float32, jnp.bfloat16
VMEM = pl.BlockSpec(memory_space=pltpu.VMEM)
SMEM = pl.BlockSpec(memory_space=pltpu.SMEM)
HBM = pl.BlockSpec(memory_space=pltpu.HBM)
ANY = pl.BlockSpec(memory_space=pl.ANY)
R = 8
LANES = 128
SUM_SLOTS = 8
TAIL = 16
PARAMS = pltpu.CompilerParams(vmem_limit_bytes=24 * 1024 * 1024)


def lane_ids(rows=R):
    return lax.broadcasted_iota(jnp.int32, (rows, LANES), 1)


def rows_of(ref, j):
    return ref[pl.ds(j * R, R), :]


def dot(a, b, contract=(1, 0)):
    return lax.dot_general(a, b, (((contract[0],), (contract[1],)), ((), ())), preferred_element_type=f32)


def sums_tile(sums):
    lane = lane_ids()
    tile = jnp.zeros((R, LANES), f32)
    for t, partial in enumerate(sums):
        total = jnp.sum(partial, axis=1, keepdims=True)
        high = total.astype(bf16).astype(f32)
        middle = (total - high).astype(bf16).astype(f32)
        low = total - high - middle
        for part, value in enumerate((high, middle, low)):
            tile = jnp.where(lane == part * SUM_SLOTS + t, value, tile)
    return tile


def read_sums(gathered, first_row, rows, count, unknowns):
    total = jnp.zeros((R, LANES), f32)
    for got in gathered:
        for device in range(got.shape[0]):
            total = total + got[device, pl.ds(first_row, rows), :].astype(f32)[:R]
    return [
        sum(total[:, p * SUM_SLOTS + t : p * SUM_SLOTS + t + 1] for p in range(3)) * (1.0 / unknowns)
        for t in range(count)
    ]


def compress(tiles, basis, group):
    stacked = jnp.concatenate(tiles, axis=0)
    high = stacked.astype(bf16)
    low = (stacked - high.astype(f32)).astype(bf16)
    both = dot(jnp.concatenate([high, low], axis=0), basis[pl.ds(group * LANES, LANES), :], (1, 1))
    rows = len(tiles) * R
    both = both[:rows] + both[rows:]
    lane = lane_ids()
    rank = LANES // len(tiles)
    tile = jnp.zeros((R, LANES), f32)
    for m in range(len(tiles)):
        tile = jnp.where(lane // rank == m, both[m * R : (m + 1) * R], tile)
    return tile


def write_payload(payload, tiles, sums, basis, per_group):
    groups = len(tiles) // per_group
    parts = [compress(tiles[g * per_group : (g + 1) * per_group], basis, g) for g in range(groups)]
    if sums:
        parts += [sums_tile(sums), jnp.zeros((TAIL - R, LANES), f32)]
    block = jnp.concatenate(parts, axis=0).astype(bf16)
    for device in range(payload.shape[0]):
        payload[device] = block


def start_kernel(per_group, b_hbm, basis_hbm, field, basis, lowered, payload, b, sems):
    copies = [
        pltpu.make_async_copy(b_hbm, b, sems.at[0]),
        pltpu.make_async_copy(basis_hbm, basis, sems.at[1]),
    ]
    for copy in copies:
        copy.start()
    for copy in copies:
        copy.wait()
    clusters = b.shape[1] // LANES
    tiles = [b[:, j * LANES : (j + 1) * LANES] for j in range(clusters)]
    field[...] = jnp.concatenate(tiles, axis=0)
    lowered[...] = jnp.concatenate(tiles, axis=0).astype(bf16)
    write_payload(payload, tiles, [], basis, per_group)


def prepare_kernel(coupling_hbm, target_hbm, _, __, high_out, low_out, target_out, coupling, target, sems):
    copies = [
        pltpu.make_async_copy(coupling_hbm, coupling, sems.at[0]),
        pltpu.make_async_copy(target_hbm, target, sems.at[1]),
    ]
    for copy in copies:
        copy.start()
    for copy in copies:
        copy.wait()
    slots, rank, _, clusters = coupling.shape
    per_tile = LANES // clusters
    for s in range(rank // per_tile):
        pieces = [
            coupling[:, s * per_tile + p].reshape(slots * rank, clusters) for p in range(per_tile)
        ]
        tile = jnp.concatenate(pieces, axis=1)
        high = tile.astype(bf16)
        high_out[:, s * LANES : (s + 1) * LANES] = high
        low_out[:, s * LANES : (s + 1) * LANES] = (tile - high.astype(f32)).astype(bf16)
    size = rank * clusters
    row = lax.broadcasted_iota(jnp.int32, (size, size), 0)
    column = lax.broadcasted_iota(jnp.int32, (size, size), 1)
    wanted = (row % clusters) * rank + row // clusters
    target_out[...] = dot((column == wanted).astype(bf16), target[...]).astype(bf16)


def fetch_kernel(least, blocks_hbm, places, *refs):
    *_, blocks, token, sems = refs
    clusters = sems.shape[0]
    slots = blocks.shape[0] // clusters

    def for_live(i, act):
        count = places[2 * slots, i]
        for live in range(least, slots + 1):
            pl.when(count <= live if live == least else count == live)(functools.partial(act, i, live))

    def copy_of(i, live):
        span = pl.ds(i * slots, live)
        return pltpu.make_async_copy(blocks_hbm.at[span], blocks.at[span], sems.at[i])

    def start(i, live):
        copy_of(i, live).start()
        if live < slots:
            blocks[pl.ds(i * slots + live, slots - live)] = jnp.zeros((slots - live, LANES, LANES), bf16)

    def body(act, i, carry):
        for_live(i, act)
        return carry

    lax.fori_loop(0, clusters, functools.partial(body, start), 0)
    token[...] = jnp.zeros_like(token)
    lax.fori_loop(0, clusters, functools.partial(body, lambda i, live: copy_of(i, live).wait()), 0)


def behind_kernel(values, *refs):
    refs[-1][...] = values[...]


def relay_kernel(even, odd, _, both):
    rows = even.shape[0]
    both[pl.ds(0, rows), :] = even[...]
    both[pl.ds(rows, rows), :] = odd[...]


def apply(per_group, slabs, places, blocks, got, got_mate, high, low, target, near, far, window, table):
    clusters = near.shape[0] // R
    slots = blocks.shape[0] // clusters
    rank = LANES // per_group
    head = clusters // per_group * R
    at = 0
    for slab in slabs:
        window[pl.ds(at, slab.shape[0]), :] = slab[...].astype(f32)
        at += slab.shape[0]
    window[pl.ds(at, R), :] = jnp.zeros((R, LANES), f32)
    for part, values in enumerate((got, got_mate)):
        for device in range(values.shape[0]):
            at = (part * values.shape[0] + device) * head
            table[pl.ds(at, head), :] = values[device, pl.ds(0, head), :].astype(f32)
    lane = lane_ids()

    def fetch(k, i):
        return window[pl.ds(pl.multiple_of(places[k, i] * R, R), R), :]

    def block(k, i):
        return blocks[i * slots + k]

    def pick(i):
        tile = jnp.zeros((R, LANES), f32)
        for k in range(slots):
            j = places[slots + k, i]
            found = table[pl.ds(pl.multiple_of(lax.div(j, per_group) * R, R), R), :]
            shift = ((k - j) * rank) & (LANES - 1)
            tile = jnp.where(lane // rank == k, pltpu.roll(found, shift, 1), tile)
        return tile

    picked = []
    for i in range(0, clusters, 2):
        both = jnp.zeros((2 * R, 2 * LANES), f32)
        for k in range(0, slots, 2):
            sources = jnp.concatenate(
                [jnp.concatenate([fetch(k + n, i), fetch(k + n, i + 1)], axis=0) for n in range(2)], axis=1
            )
            weights = jnp.concatenate(
                [jnp.concatenate([block(k + n, i), block(k + n, i + 1)], axis=0) for n in range(2)], axis=1
            )
            both = both + dot(sources.astype(bf16), weights, (1, 1))
        near[pl.ds(i * R, R), :] = both[:R, :LANES]
        near[pl.ds((i + 1) * R, R), :] = both[R:, LANES:]
        picked += [pick(i), pick(i + 1)]

    picked = jnp.concatenate(picked, axis=0).astype(bf16)
    crossed = dot(picked, high[...]) + dot(picked, low[...])
    expanded_high, expanded_low = [], []
    for s in range(rank * clusters // LANES):
        tile = jnp.zeros((R, LANES), f32)
        for i in range(clusters):
            part = crossed[i * R : (i + 1) * R, s * LANES : (s + 1) * LANES]
            tile = jnp.where(lane % clusters == i, part, tile)
        tile_high = tile.astype(bf16).astype(f32)
        tile_low = tile - tile_high
        for source, kept in ((tile_high, expanded_high), (tile_low, expanded_low)):
            spread = [jnp.where(lane % clusters == i, source, 0.0) for i in range(clusters)]
            kept.append(jnp.concatenate(spread, axis=0).astype(bf16))
    far[...] = dot(jnp.concatenate(expanded_high, axis=1), target[...]) + dot(
        jnp.concatenate(expanded_low, axis=1), target[...]
    )


def first_kernel(
    per_group, own, mate, even, odd, relayed, places, blocks, got, got_mate, high, low, target, b, basis,
    image, lowered, payload, near, far, window, table,
):
    slabs = (own, mate, even, odd, relayed)
    apply(per_group, slabs, places, blocks, got, got_mate, high, low, target, near, far, window, table)
    clusters = near.shape[0] // R
    tiles = []
    sums = [jnp.zeros((R, LANES), f32) for _ in range(3)]
    for i in range(clusters):
        field = rows_of(b, i)
        made = 0.5 * field + (rows_of(near, i) + rows_of(far, i))
        sums = [s + f * g for s, f, g in zip(sums, (field, field, made), (field, made, made))]
        tiles.append(made)
    for i in range(0, clusters, 2):
        both = jnp.concatenate(tiles[i : i + 2], axis=0)
        image[pl.ds(i * R, 2 * R), :] = both
        lowered[pl.ds(i * R, 2 * R), :] = both.astype(bf16)
    write_payload(payload, tiles, sums, basis, per_group)


def arnoldi_one(bb, bw, ww):
    whole = bb + epsilon
    start_norm = jnp.sqrt(whole)
    scale = 1.0 / start_norm
    v11 = bb / whole
    h11 = (bw * scale) * scale
    uu = jnp.maximum((ww * scale) * scale - 2.0 * h11 * h11 + h11 * h11 * v11, 0.0)
    h21 = jnp.sqrt(uu + epsilon)
    return start_norm, h11, h21, v11, uu / (uu + epsilon), h11 * (1.0 - v11) / h21


def second_kernel(
    per_group, unknowns, own, mate, even, odd, relayed, places, blocks, got, got_mate, high, low, target, b, image,
    candidate, sums_out, near, far, window, table,
):
    slabs = (own, mate, even, odd, relayed)
    apply(per_group, slabs, places, blocks, got, got_mate, high, low, target, near, far, window, table)
    clusters = near.shape[0] // R
    head = clusters // per_group * R
    start_norm, h11, h21, _, _, _ = arnoldi_one(*read_sums((got, got_mate), head, TAIL, 3, unknowns))
    scale = 1.0 / start_norm
    inverse = 1.0 / h21
    sums = [jnp.zeros((R, LANES), f32) for _ in range(3)]
    for j in range(clusters):
        held = rows_of(image, j) * scale
        first = rows_of(b, j) * scale
        second = (held - h11 * first) * inverse
        made = (0.5 * held + (rows_of(near, j) + rows_of(far, j)) * scale - h11 * held) * inverse
        sums = [s + v * made for s, v in zip(sums, (first, second, made))]
        candidate[pl.ds(j * R, R), :] = made
    tile = sums_tile(sums).astype(bf16)
    for device in range(sums_out.shape[0]):
        sums_out[device] = tile


def finish_kernel(per_group, unknowns, b, image, candidate, got1, got1_mate, got2, solution_out, next_out):
    clusters = b.shape[0] // R
    head = clusters // per_group * R
    start_norm, h11, h21, v11, v22, v12 = arnoldi_one(*read_sums((got1, got1_mate), head, TAIL, 3, unknowns))
    h12, h22, ww = read_sums((got2,), 0, R, 3, unknowns)
    uu = ww - 2.0 * (h12 * h12 + h22 * h22) + h12 * h12 * v11 + h22 * h22 * v22 + 2.0 * h12 * h22 * v12
    h32 = jnp.sqrt(jnp.maximum(uu, 0.0) + epsilon)
    g11 = h11 * h11 + h21 * h21
    g12 = h11 * h12 + h21 * h22
    g22 = h12 * h12 + h22 * h22 + h32 * h32
    t1, t2 = start_norm * h11, start_norm * h12
    det = g11 * g22 - g12 * g12
    y1 = (g22 * t1 - g12 * t2) / det
    y2 = (g11 * t2 - g12 * t1) / det
    scale, inverse, last = 1.0 / start_norm, 1.0 / h21, 1.0 / h32
    for j in range(clusters):
        span = slice(j * LANES, (j + 1) * LANES)
        first = rows_of(b, j) * scale
        second = (rows_of(image, j) * scale - h11 * first) * inverse
        solution_out[:, span] = y1 * first + y2 * second
        next_out[:, span] = (rows_of(candidate, j) - h12 * first - h22 * second) * last


def swapped(block, partner):
    return lax.ppermute(block, "rows", [(i, partner(i)) for i in range(lax.axis_size("rows"))])


def core_mate(i):
    return i ^ 1


def even_mate(i):
    return i ^ 2


def odd_mate(i):
    chip = i // 2
    other = chip + 1 if chip % 2 else chip - 1
    return 2 * (other % (lax.axis_size("rows") // 2)) + i % 2


def sends_of(block):
    return [block] + [swapped(block, partner) for partner in (core_mate, even_mate, odd_mate)]


def window_place(distance, clusters):
    me = lax.axis_index("rows")
    core, chip = me % 2, me // 2
    before, after = 3 - chip % 2, 2 + chip % 2
    slot = [
        before,
        jnp.where(core == 0, before + 2, 1),
        0,
        jnp.where(core == 0, 1, after + 2),
        after,
    ]
    slab = distance // clusters
    chosen = jnp.zeros_like(distance)
    for s, value in enumerate(slot):
        chosen = jnp.where(slab == s, value, chosen)
    return chosen * clusters + distance % clusters


def on_device(
    right_sides, near_blocks, near_cols, near_counts, basis_in, target_basis, coupling, far_cols
):
    width = right_sides.shape[1]
    clusters, slots = near_cols.shape
    rank = basis_in.shape[1]
    per_group = LANES // rank
    head = clusters // per_group * R
    size = lax.axis_size("rows")
    every = clusters * size
    unknowns = float(width * size)
    rows = clusters * R

    def shape(*dims, dtype=f32):
        return jax.ShapeDtypeStruct(dims, dtype)

    def scratch(*dims, dtype=f32):
        return pltpu.VMEM(dims, dtype)

    def in_hbm(array):
        return pltpu.with_memory_space_constraint(array, pltpu.HBM)

    def call(kernel, name, out, ins, *args, scratch_shapes=()):
        return pl.pallas_call(
            kernel, out_shape=out, in_specs=ins, out_specs=jax.tree.map(lambda _: VMEM, out),
            scratch_shapes=scratch_shapes, compiler_params=PARAMS, name=name,
        )(*args)

    def exchange(block):
        return lax.all_to_all(block, "rows", 0, 0)

    def gather(block):
        groups = [list(range(core, size, 2)) for core in range(2)]
        return lax.all_to_all(block, "rows", 0, 0, axis_index_groups=groups)

    field, basis, lowered, payload = call(
        functools.partial(start_kernel, per_group), "start",
        (
            shape(rows, LANES), shape(clusters * rank, LANES, dtype=bf16), shape(rows, LANES, dtype=bf16),
            shape(size // 2, head, LANES, dtype=bf16),
        ),
        [HBM] * 2, in_hbm(right_sides), in_hbm(basis_in.reshape(clusters * rank, LANES)),
        scratch_shapes=[scratch(R, width), pltpu.SemaphoreType.DMA((2,))],
    )
    got = gather(payload)
    held = sends_of(lowered)

    reach = 2 * clusters
    start = lax.axis_index("rows") * clusters
    distance = (near_cols.T - start + reach) % every
    live = jnp.arange(slots, dtype=jnp.int32)[:, None] < near_counts[None, :]
    placed = jnp.where(live, window_place(distance, clusters), 6 * clusters).astype(jnp.int32)
    owner = far_cols.T // clusters
    other_core = (owner % 2) ^ (lax.axis_index("rows") % 2)
    far_index = (other_core * (size // 2) + owner // 2) * clusters + far_cols.T % clusters
    places = jnp.concatenate([placed, far_index, near_counts[None, :]], axis=0)
    high, low, target = call(
        prepare_kernel, "prepare",
        (
            shape(slots * rank, rank * clusters, dtype=bf16),
            shape(slots * rank, rank * clusters, dtype=bf16),
            shape(rank * clusters, LANES, dtype=bf16),
        ),
        [HBM] * 2 + [ANY] * 2,
        in_hbm(jnp.transpose(coupling, (1, 2, 3, 0))), in_hbm(target_basis.reshape(clusters * rank, LANES)),
        payload, places,
        scratch_shapes=[
            scratch(slots, rank, rank, clusters), scratch(clusters * rank, LANES, dtype=bf16),
            pltpu.SemaphoreType.DMA((2,)),
        ],
    )
    blocks = in_hbm(near_blocks.reshape(clusters * slots, LANES, LANES))


    def arrived(got, held, *made):
        near_blocks_here, token = call(
            functools.partial(fetch_kernel, 3), "fetch", (pltpu.VMEM(blocks.shape, bf16), shape(R, LANES)),
            [HBM, SMEM] + [ANY] * (1 + len(made)), blocks, places, got, *made,
            scratch_shapes=[pltpu.SemaphoreType.DMA((clusters,))],
        )
        near_blocks_here = pltpu.with_memory_space_constraint(near_blocks_here, pltpu.VMEM)
        got = call(
            behind_kernel, "behind", shape(*got.shape, dtype=bf16), [VMEM] + [ANY] * 2, got, held[3], token
        )
        relay = call(
            relay_kernel, "relay", shape(2 * rows, LANES, dtype=bf16), [VMEM] * 2 + [ANY], *held[2:], got
        )
        got = (got, swapped(got, core_mate))
        return (*held, swapped(relay, core_mate)), near_blocks_here, got

    kept = [scratch(rows, LANES), scratch(rows, LANES), scratch(6 * rows + R, LANES), scratch(size * head, LANES)]
    operands = [VMEM] * 5 + [SMEM] + [VMEM] * 8
    slabs, near_blocks_here, got = arrived(got, held, target)
    image, lowered, payload = call(
        functools.partial(first_kernel, per_group), "operator_one",
        (
            shape(rows, LANES), shape(rows, LANES, dtype=bf16),
            shape(size // 2, head + TAIL, LANES, dtype=bf16),
        ),
        operands, *slabs, places, near_blocks_here, *got, high, low, target, field, basis, scratch_shapes=kept,
    )
    got = gather(payload)
    slabs, near_blocks_here, got = arrived(got, sends_of(lowered))
    candidate, sums = call(
        functools.partial(second_kernel, per_group, unknowns), "operator_two",
        (shape(rows, LANES), shape(size, R, LANES, dtype=bf16)),
        operands, *slabs, places, near_blocks_here, *got, high, low, target, field, image, scratch_shapes=kept,
    )
    return call(
        functools.partial(finish_kernel, per_group, unknowns), "finish", (shape(R, width), shape(R, width)),
        [VMEM] * 6, field, image, candidate, *got, exchange(sums),
    )


def solution(mesh):
    return jax.shard_map(
        on_device,
        mesh=mesh,
        in_specs=(
            P("groups", "rows"),
            P("rows", None, None, None),
            P("rows", None),
            P("rows"),
            P("rows", None, None),
            P("rows", None, None),
            P("rows", None, None, None),
            P("rows", None),
        ),
        out_specs=(P("groups", "rows"), P("groups", "rows")),
        check_vma=False,
    )
```

```python
import functools

import jax
import jax.numpy as jnp
from jax import lax
from jax.experimental import pallas as pl
from jax.experimental.pallas import tpu as pltpu
from jax.sharding import PartitionSpec as P

epsilon = 1e-06
f32, bf16 = jnp.float32, jnp.bfloat16
VMEM = pl.BlockSpec(memory_space=pltpu.VMEM)
SMEM = pl.BlockSpec(memory_space=pltpu.SMEM)
HBM = pl.BlockSpec(memory_space=pltpu.HBM)
ANY = pl.BlockSpec(memory_space=pl.ANY)
R = 8
LANES = 128
SUM_SLOTS = 8
TAIL = 16
PARAMS = pltpu.CompilerParams(vmem_limit_bytes=24 * 1024 * 1024)


def lane_ids(rows=R):
    return lax.broadcasted_iota(jnp.int32, (rows, LANES), 1)


def rows_of(ref, j):
    return ref[pl.ds(j * R, R), :]


def dot(a, b, contract=(1, 0)):
    return lax.dot_general(a, b, (((contract[0],), (contract[1],)), ((), ())), preferred_element_type=f32)


def sums_tile(sums):
    lane = lane_ids()
    tile = jnp.zeros((R, LANES), f32)
    for t, partial in enumerate(sums):
        total = jnp.sum(partial, axis=1, keepdims=True)
        high = total.astype(bf16).astype(f32)
        middle = (total - high).astype(bf16).astype(f32)
        low = total - high - middle
        for part, value in enumerate((high, middle, low)):
            tile = jnp.where(lane == part * SUM_SLOTS + t, value, tile)
    return tile


def read_sums(parts, count, unknowns):
    total = jnp.zeros((R, LANES), f32)
    for part in parts:
        total = total + part.astype(f32)[:R]
    return [
        sum(total[:, p * SUM_SLOTS + t : p * SUM_SLOTS + t + 1] for p in range(3)) * (1.0 / unknowns)
        for t in range(count)
    ]


def tails(swaps, rows, head):
    each = head + TAIL
    return [
        values[pl.ds(device * each + head, TAIL), :]
        for values in swaps
        for device in range((values.shape[0] - rows) // each)
    ]


def compress(tiles, basis, group):
    stacked = jnp.concatenate(tiles, axis=0)
    high = stacked.astype(bf16)
    low = (stacked - high.astype(f32)).astype(bf16)
    both = dot(jnp.concatenate([high, low], axis=0), basis[pl.ds(group * LANES, LANES), :], (1, 1))
    rows = len(tiles) * R
    both = both[:rows] + both[rows:]
    lane = lane_ids()
    rank = LANES // len(tiles)
    tile = jnp.zeros((R, LANES), f32)
    for m in range(len(tiles)):
        tile = jnp.where(lane // rank == m, both[m * R : (m + 1) * R], tile)
    return tile


def write_payload(payload, tiles, sums, basis, per_group):
    groups = len(tiles) // per_group
    parts = [compress(tiles[g * per_group : (g + 1) * per_group], basis, g) for g in range(groups)]
    if sums:
        parts += [sums_tile(sums), jnp.zeros((TAIL - R, LANES), f32)]
    block = jnp.concatenate(parts, axis=0).astype(bf16)
    for device in range(payload.shape[0]):
        payload[device] = block


def start_kernel(per_group, b_hbm, basis_hbm, field, basis, lowered, payload, b, sems):
    copies = [
        pltpu.make_async_copy(b_hbm, b, sems.at[0]),
        pltpu.make_async_copy(basis_hbm, basis, sems.at[1]),
    ]
    for copy in copies:
        copy.start()
    for copy in copies:
        copy.wait()
    clusters = b.shape[1] // LANES
    tiles = [b[:, j * LANES : (j + 1) * LANES] for j in range(clusters)]
    field[...] = jnp.concatenate(tiles, axis=0)
    lowered[...] = jnp.concatenate(tiles, axis=0).astype(bf16)
    write_payload(payload, tiles, [], basis, per_group)


def prepare_kernel(coupling_hbm, target_hbm, _, __, high_out, low_out, target_out, coupling, target, sems):
    copies = [
        pltpu.make_async_copy(coupling_hbm, coupling, sems.at[0]),
        pltpu.make_async_copy(target_hbm, target, sems.at[1]),
    ]
    for copy in copies:
        copy.start()
    for copy in copies:
        copy.wait()
    slots, rank, _, clusters = coupling.shape
    per_tile = LANES // clusters
    for s in range(rank // per_tile):
        pieces = [
            coupling[:, s * per_tile + p].reshape(slots * rank, clusters) for p in range(per_tile)
        ]
        tile = jnp.concatenate(pieces, axis=1)
        high = tile.astype(bf16)
        high_out[:, s * LANES : (s + 1) * LANES] = high
        low_out[:, s * LANES : (s + 1) * LANES] = (tile - high.astype(f32)).astype(bf16)
    size = rank * clusters
    row = lax.broadcasted_iota(jnp.int32, (size, size), 0)
    column = lax.broadcasted_iota(jnp.int32, (size, size), 1)
    wanted = (row % clusters) * rank + row // clusters
    target_out[...] = dot((column == wanted).astype(bf16), target[...]).astype(bf16)


def fetch_kernel(first, blocks_hbm, *refs):
    *_, blocks, token, sems = refs
    chunks = sems.shape[0]
    each = blocks.shape[0] // chunks
    copies = [
        pltpu.make_async_copy(
            blocks_hbm.at[pl.ds(first + c * each, each)], blocks.at[pl.ds(c * each, each)], sems.at[c]
        )
        for c in range(chunks)
    ]
    for copy in copies:
        copy.start()
    token[...] = jnp.zeros_like(token)
    for copy in copies:
        copy.wait()


def relay_kernel(axis, got, even, odd, _, out):
    me = lax.axis_index(axis)
    devices, each, _ = got.shape
    for device in range(devices):
        out[pl.ds(device * each, each), :] = got[device]
    wants_even = (me // 2 + me) % 2 == 0
    span = pl.ds(devices * each, even.shape[0])

    @pl.when(wants_even)
    def _():
        out[span, :] = even[...]

    @pl.when(jnp.logical_not(wants_even))
    def _():
        out[span, :] = odd[...]


def apply(per_group, each, slabs, places, ahead, blocks, swaps, high, low, target, near, far, window, table):
    clusters = near.shape[0] // R
    slots = (ahead.shape[0] + blocks.shape[0]) // clusters
    rank = LANES // per_group
    head = clusters // per_group * R
    rows = slabs[0].shape[0]
    devices = (swaps[0].shape[0] - rows) // each
    for at, slab in enumerate(slabs):
        window[pl.ds(at * rows, rows), :] = slab[...].astype(f32)
    window[pl.ds(len(slabs) * rows, rows), :] = swaps[1][pl.ds(devices * each, rows), :].astype(f32)
    window[pl.ds((len(slabs) + 1) * rows, R), :] = jnp.zeros((R, LANES), f32)
    for part, values in enumerate(swaps):
        for device in range(devices):
            at = (part * devices + device) * head
            table[pl.ds(at, head), :] = values[pl.ds(device * each, head), :].astype(f32)
    lane = lane_ids()

    def fetch(k, i):
        return window[pl.ds(pl.multiple_of(places[k, i] * R, R), R), :]

    def block(k, i):
        at = i * slots + k
        return ahead[at] if at < ahead.shape[0] else blocks[at - ahead.shape[0]]

    def pick(i):
        tile = jnp.zeros((R, LANES), f32)
        for k in range(slots):
            j = places[slots + k, i]
            found = table[pl.ds(pl.multiple_of(lax.div(j, per_group) * R, R), R), :]
            shift = ((k - j) * rank) & (LANES - 1)
            tile = jnp.where(lane // rank == k, pltpu.roll(found, shift, 1), tile)
        return tile

    picked = []
    for i in range(0, clusters, 2):
        both = jnp.zeros((2 * R, 2 * LANES), f32)
        for k in range(0, slots, 2):
            sources = jnp.concatenate(
                [jnp.concatenate([fetch(k + n, i), fetch(k + n, i + 1)], axis=0) for n in range(2)], axis=1
            )
            weights = jnp.concatenate(
                [jnp.concatenate([block(k + n, i), block(k + n, i + 1)], axis=0) for n in range(2)], axis=1
            )
            both = both + dot(sources.astype(bf16), weights, (1, 1))
        near[pl.ds(i * R, R), :] = both[:R, :LANES]
        near[pl.ds((i + 1) * R, R), :] = both[R:, LANES:]
        if 2 * i < clusters:
            picked += [pick(n) for n in range(2 * i, 2 * i + 4)]
        if 2 * i == clusters - 4:
            picked = jnp.concatenate(picked, axis=0).astype(bf16)
            crossed = dot(picked, high[...]) + dot(picked, low[...])
            expanded_high, expanded_low = [], []
            for s in range(rank * clusters // LANES):
                tile = jnp.zeros((R, LANES), f32)
                for n in range(clusters):
                    part = crossed[n * R : (n + 1) * R, s * LANES : (s + 1) * LANES]
                    tile = jnp.where(lane % clusters == n, part, tile)
                tile_high = tile.astype(bf16).astype(f32)
                tile_low = tile - tile_high
                for source, kept in ((tile_high, expanded_high), (tile_low, expanded_low)):
                    spread = [jnp.where(lane % clusters == n, source, 0.0) for n in range(clusters)]
                    kept.append(jnp.concatenate(spread, axis=0).astype(bf16))
            far[...] = dot(jnp.concatenate(expanded_high, axis=1), target[...]) + dot(
                jnp.concatenate(expanded_low, axis=1), target[...]
            )


def first_kernel(
    per_group, own, mate, even, odd, places, ahead, blocks, sent, received, high, low, target, b, basis,
    image, lowered, payload, near, far, window, table,
):
    clusters = near.shape[0] // R
    slabs, swaps = (own, mate, even, odd), (sent, received)
    each = clusters // per_group * R
    apply(per_group, each, slabs, places, ahead, blocks, swaps, high, low, target, near, far, window, table)
    tiles = []
    sums = [jnp.zeros((R, LANES), f32) for _ in range(3)]
    for i in range(clusters):
        field = rows_of(b, i)
        made = 0.5 * field + (rows_of(near, i) + rows_of(far, i))
        sums = [s + f * g for s, f, g in zip(sums, (field, field, made), (field, made, made))]
        tiles.append(made)
    for i in range(0, clusters, 2):
        both = jnp.concatenate(tiles[i : i + 2], axis=0)
        image[pl.ds(i * R, 2 * R), :] = both
        lowered[pl.ds(i * R, 2 * R), :] = both.astype(bf16)
    write_payload(payload, tiles, sums, basis, per_group)


def arnoldi_one(bb, bw, ww):
    whole = bb + epsilon
    start_norm = jnp.sqrt(whole)
    scale = 1.0 / start_norm
    v11 = bb / whole
    h11 = (bw * scale) * scale
    uu = jnp.maximum((ww * scale) * scale - 2.0 * h11 * h11 + h11 * h11 * v11, 0.0)
    h21 = jnp.sqrt(uu + epsilon)
    return start_norm, h11, h21, v11, uu / (uu + epsilon), h11 * (1.0 - v11) / h21


def second_kernel(
    per_group, unknowns, own, mate, even, odd, places, ahead, blocks, sent, received, high, low, target, b, image,
    candidate, sums_out, near, far, window, table,
):
    clusters = near.shape[0] // R
    head = clusters // per_group * R
    slabs, swaps = (own, mate, even, odd), (sent, received)
    apply(per_group, head + TAIL, slabs, places, ahead, blocks, swaps, high, low, target, near, far, window, table)
    sums = read_sums(tails(swaps, own.shape[0], head), 3, unknowns)
    start_norm, h11, h21, _, _, _ = arnoldi_one(*sums)
    scale = 1.0 / start_norm
    inverse = 1.0 / h21
    sums = [jnp.zeros((R, LANES), f32) for _ in range(3)]
    for j in range(clusters):
        held = rows_of(image, j) * scale
        first = rows_of(b, j) * scale
        second = (held - h11 * first) * inverse
        made = (0.5 * held + (rows_of(near, j) + rows_of(far, j)) * scale - h11 * held) * inverse
        sums = [s + v * made for s, v in zip(sums, (first, second, made))]
        candidate[pl.ds(j * R, R), :] = made
    tile = sums_tile(sums).astype(bf16)
    for device in range(sums_out.shape[0]):
        sums_out[device] = tile


def finish_kernel(per_group, unknowns, b, image, candidate, sent, received, got, solution_out, next_out):
    clusters = b.shape[0] // R
    sums = read_sums(tails((sent, received), b.shape[0], clusters // per_group * R), 3, unknowns)
    start_norm, h11, h21, v11, v22, v12 = arnoldi_one(*sums)
    h12, h22, ww = read_sums([got[device] for device in range(got.shape[0])], 3, unknowns)
    uu = ww - 2.0 * (h12 * h12 + h22 * h22) + h12 * h12 * v11 + h22 * h22 * v22 + 2.0 * h12 * h22 * v12
    h32 = jnp.sqrt(jnp.maximum(uu, 0.0) + epsilon)
    g11 = h11 * h11 + h21 * h21
    g12 = h11 * h12 + h21 * h22
    g22 = h12 * h12 + h22 * h22 + h32 * h32
    t1, t2 = start_norm * h11, start_norm * h12
    det = g11 * g22 - g12 * g12
    y1 = (g22 * t1 - g12 * t2) / det
    y2 = (g11 * t2 - g12 * t1) / det
    scale, inverse, last = 1.0 / start_norm, 1.0 / h21, 1.0 / h32
    for j in range(clusters):
        span = slice(j * LANES, (j + 1) * LANES)
        first = rows_of(b, j) * scale
        second = (rows_of(image, j) * scale - h11 * first) * inverse
        solution_out[:, span] = y1 * first + y2 * second
        next_out[:, span] = (rows_of(candidate, j) - h12 * first - h22 * second) * last


def swapped(block, partner):
    return lax.ppermute(block, "rows", [(i, partner(i)) for i in range(lax.axis_size("rows"))])


def core_mate(i):
    return i ^ 1


def even_mate(i):
    return i ^ 2


def odd_mate(i):
    chip = i // 2
    other = chip + 1 if chip % 2 else chip - 1
    return 2 * (other % (lax.axis_size("rows") // 2)) + i % 2


def sends_of(block):
    return [block] + [swapped(block, partner) for partner in (core_mate, even_mate, odd_mate)]


def window_place(distance, clusters):
    me = lax.axis_index("rows")
    core, chip = me % 2, me // 2
    before, after = 3 - chip % 2, 2 + chip % 2
    slot = [
        before,
        jnp.where(core == 0, 4, 1),
        0,
        jnp.where(core == 0, 1, 4),
        after,
    ]
    slab = distance // clusters
    chosen = jnp.zeros_like(distance)
    for s, value in enumerate(slot):
        chosen = jnp.where(slab == s, value, chosen)
    return chosen * clusters + distance % clusters


def on_device(
    right_sides, near_blocks, near_cols, near_counts, basis_in, target_basis, coupling, far_cols
):
    width = right_sides.shape[1]
    clusters, slots = near_cols.shape
    rank = basis_in.shape[1]
    per_group = LANES // rank
    head = clusters // per_group * R
    size = lax.axis_size("rows")
    every = clusters * size
    unknowns = float(width * size)
    rows = clusters * R

    def shape(*dims, dtype=f32):
        return jax.ShapeDtypeStruct(dims, dtype)

    def scratch(*dims, dtype=f32):
        return pltpu.VMEM(dims, dtype)

    def in_hbm(array):
        return pltpu.with_memory_space_constraint(array, pltpu.HBM)

    def call(kernel, name, out, ins, *args, scratch_shapes=()):
        return pl.pallas_call(
            kernel, out_shape=out, in_specs=ins, out_specs=jax.tree.map(lambda _: VMEM, out),
            scratch_shapes=scratch_shapes, compiler_params=PARAMS, name=name,
        )(*args)

    def exchange(block):
        return lax.all_to_all(block, "rows", 0, 0)

    def gather(block):
        groups = [list(range(core, size, 2)) for core in range(2)]
        return lax.all_to_all(block, "rows", 0, 0, axis_index_groups=groups)

    field, basis, lowered, payload = call(
        functools.partial(start_kernel, per_group), "start",
        (
            shape(rows, LANES), shape(clusters * rank, LANES, dtype=bf16), shape(rows, LANES, dtype=bf16),
            shape(size // 2, head, LANES, dtype=bf16),
        ),
        [HBM] * 2, in_hbm(right_sides), in_hbm(basis_in.reshape(clusters * rank, LANES)),
        scratch_shapes=[scratch(R, width), pltpu.SemaphoreType.DMA((2,))],
    )
    got = gather(payload)
    held = sends_of(lowered)

    reach = 2 * clusters
    start = lax.axis_index("rows") * clusters
    distance = (near_cols.T - start + reach) % every
    live = jnp.arange(slots, dtype=jnp.int32)[:, None] < near_counts[None, :]
    placed = jnp.where(live, window_place(distance, clusters), 5 * clusters).astype(jnp.int32)
    owner = far_cols.T // clusters
    other_core = (owner % 2) ^ (lax.axis_index("rows") % 2)
    far_index = (other_core * (size // 2) + owner // 2) * clusters + far_cols.T % clusters
    places = jnp.concatenate([placed, far_index], axis=0)
    high, low, target = call(
        prepare_kernel, "prepare",
        (
            shape(slots * rank, rank * clusters, dtype=bf16),
            shape(slots * rank, rank * clusters, dtype=bf16),
            shape(rank * clusters, LANES, dtype=bf16),
        ),
        [HBM] * 2 + [ANY] * 2,
        in_hbm(jnp.transpose(coupling, (1, 2, 3, 0))), in_hbm(target_basis.reshape(clusters * rank, LANES)),
        payload, places,
        scratch_shapes=[
            scratch(slots, rank, rank, clusters), scratch(clusters * rank, LANES, dtype=bf16),
            pltpu.SemaphoreType.DMA((2,)),
        ],
    )
    blocks = in_hbm(near_blocks.reshape(clusters * slots, LANES, LANES))


    early = blocks.shape[0] * 3 // 16

    def fetch(name, first, count, chunks, *behind):
        here, token = call(
            functools.partial(fetch_kernel, first), name, (pltpu.VMEM((count, LANES, LANES), bf16), shape(R, LANES)),
            [HBM] + [ANY] * len(behind), blocks, *behind, scratch_shapes=[pltpu.SemaphoreType.DMA((chunks,))],
        )
        return pltpu.with_memory_space_constraint(here, pltpu.VMEM), token

    def arrived(got, held, made):
        ahead, token = fetch("ahead", 0, early, 2, made)
        near_blocks_here, token = fetch("fetch", early, blocks.shape[0] - early, 8, got, token)
        sent = call(
            functools.partial(relay_kernel, "rows"), "relay",
            shape(got.shape[0] * got.shape[1] + rows, LANES, dtype=bf16), [VMEM] * 3 + [ANY], got, *held[2:], token
        )
        return *held, places, ahead, near_blocks_here, sent, swapped(sent, core_mate), high, low, target

    kept = [scratch(rows, LANES), scratch(rows, LANES), scratch(5 * rows + R, LANES), scratch(size * head, LANES)]
    operands = [VMEM] * 4 + [SMEM] + [VMEM] * 9
    image, lowered, payload = call(
        functools.partial(first_kernel, per_group), "operator_one",
        (
            shape(rows, LANES), shape(rows, LANES, dtype=bf16),
            shape(size // 2, head + TAIL, LANES, dtype=bf16),
        ),
        operands, *arrived(got, held, target), field, basis, scratch_shapes=kept,
    )
    held = sends_of(lowered)
    here = arrived(gather(payload), held, held[2])
    candidate, sums = call(
        functools.partial(second_kernel, per_group, unknowns), "operator_two",
        (shape(rows, LANES), shape(size, R, LANES, dtype=bf16)),
        operands, *here, field, image, scratch_shapes=kept,
    )
    return call(
        functools.partial(finish_kernel, per_group, unknowns), "finish", (shape(R, width), shape(R, width)),
        [VMEM] * 6, field, image, candidate, *here[7:9], exchange(sums),
    )


def solution(mesh):
    return jax.shard_map(
        on_device,
        mesh=mesh,
        in_specs=(
            P("groups", "rows"),
            P("rows", None, None, None),
            P("rows", None),
            P("rows"),
            P("rows", None, None),
            P("rows", None, None),
            P("rows", None, None, None),
            P("rows", None),
        ),
        out_specs=(P("groups", "rows"), P("groups", "rows")),
        check_vma=False,
    )
```

```python
import functools

import jax
import jax.numpy as jnp
from jax import lax
from jax.experimental import pallas as pl
from jax.experimental.pallas import tpu as pltpu
from jax.sharding import PartitionSpec as P

epsilon = 1e-06
f32, bf16 = jnp.float32, jnp.bfloat16
VMEM = pl.BlockSpec(memory_space=pltpu.VMEM)
SMEM = pl.BlockSpec(memory_space=pltpu.SMEM)
HBM = pl.BlockSpec(memory_space=pltpu.HBM)
ANY = pl.BlockSpec(memory_space=pl.ANY)
R = 8
LANES = 128
SUM_SLOTS = 8
TAIL = 16
PARAMS = pltpu.CompilerParams(vmem_limit_bytes=24 * 1024 * 1024)


def lane_ids(rows=R):
    return lax.broadcasted_iota(jnp.int32, (rows, LANES), 1)


def rows_of(ref, j):
    return ref[pl.ds(j * R, R), :]


def dot(a, b, contract=(1, 0)):
    return lax.dot_general(a, b, (((contract[0],), (contract[1],)), ((), ())), preferred_element_type=f32)


def sums_tile(sums):
    lane = lane_ids()
    tile = jnp.zeros((R, LANES), f32)
    for t, partial in enumerate(sums):
        total = jnp.sum(partial, axis=1, keepdims=True)
        high = total.astype(bf16).astype(f32)
        middle = (total - high).astype(bf16).astype(f32)
        low = total - high - middle
        for part, value in enumerate((high, middle, low)):
            tile = jnp.where(lane == part * SUM_SLOTS + t, value, tile)
    return tile


def read_sums(parts, count, unknowns):
    total = jnp.zeros((R, LANES), f32)
    for part in parts:
        total = total + part.astype(f32)[:R]
    return [
        sum(total[:, p * SUM_SLOTS + t : p * SUM_SLOTS + t + 1] for p in range(3)) * (1.0 / unknowns)
        for t in range(count)
    ]


def tails(swaps, rows, head):
    each = head + TAIL
    return [
        values[pl.ds(device * each + head, TAIL), :]
        for values in swaps
        for device in range((values.shape[0] - rows) // each)
    ]


def compress(tiles, basis, group):
    stacked = jnp.concatenate(tiles, axis=0)
    high = stacked.astype(bf16)
    low = (stacked - high.astype(f32)).astype(bf16)
    both = dot(jnp.concatenate([high, low], axis=0), basis[pl.ds(group * LANES, LANES), :], (1, 1))
    rows = len(tiles) * R
    both = both[:rows] + both[rows:]
    lane = lane_ids()
    rank = LANES // len(tiles)
    tile = jnp.zeros((R, LANES), f32)
    for m in range(len(tiles)):
        tile = jnp.where(lane // rank == m, both[m * R : (m + 1) * R], tile)
    return tile


def write_payload(payload, tiles, sums, basis, per_group):
    groups = len(tiles) // per_group
    parts = [compress(tiles[g * per_group : (g + 1) * per_group], basis, g) for g in range(groups)]
    parts += [sums_tile(sums), jnp.zeros((TAIL - R, LANES), f32)]
    block = jnp.concatenate(parts, axis=0).astype(bf16)
    for device in range(payload.shape[0]):
        payload[device] = block


def start_kernel(per_group, b_hbm, basis_hbm, field, basis, lowered, payload, b, sems):
    copies = [
        pltpu.make_async_copy(b_hbm, b, sems.at[0]),
        pltpu.make_async_copy(basis_hbm, basis, sems.at[1]),
    ]
    for copy in copies:
        copy.start()
    for copy in copies:
        copy.wait()
    clusters = b.shape[1] // LANES
    tiles = [b[:, j * LANES : (j + 1) * LANES] for j in range(clusters)]
    field[...] = jnp.concatenate(tiles, axis=0)
    lowered[...] = jnp.concatenate(tiles, axis=0).astype(bf16)
    write_payload(payload, tiles, [], basis, per_group)


def prepare_kernel(
    coupling_hbm, target_hbm, blocks_hbm, _, __, high_out, low_out, target_out, ahead, coupling, target, sems
):
    copies = [
        pltpu.make_async_copy(coupling_hbm, coupling, sems.at[0]),
        pltpu.make_async_copy(target_hbm, target, sems.at[1]),
        pltpu.make_async_copy(blocks_hbm.at[pl.ds(0, ahead.shape[0])], ahead, sems.at[2]),
    ]
    for copy in copies:
        copy.start()
    for copy in copies[:2]:
        copy.wait()
    slots, rank, _, clusters = coupling.shape
    per_tile = LANES // clusters
    for s in range(rank // per_tile):
        pieces = [
            coupling[:, s * per_tile + p].reshape(slots * rank, clusters) for p in range(per_tile)
        ]
        tile = jnp.concatenate(pieces, axis=1)
        high = tile.astype(bf16)
        high_out[:, s * LANES : (s + 1) * LANES] = high
        low_out[:, s * LANES : (s + 1) * LANES] = (tile - high.astype(f32)).astype(bf16)
    size = rank * clusters
    row = lax.broadcasted_iota(jnp.int32, (size, size), 0)
    column = lax.broadcasted_iota(jnp.int32, (size, size), 1)
    wanted = (row % clusters) * rank + row // clusters
    target_out[...] = dot((column == wanted).astype(bf16), target[...]).astype(bf16)
    copies[2].wait()


def fetch_kernel(first, blocks_hbm, *refs):
    *_, blocks, token, sems = refs
    chunks = sems.shape[0]
    each = blocks.shape[0] // chunks
    copies = [
        pltpu.make_async_copy(
            blocks_hbm.at[pl.ds(first + c * each, each)], blocks.at[pl.ds(c * each, each)], sems.at[c]
        )
        for c in range(chunks)
    ]
    for copy in copies:
        copy.start()
    token[...] = jnp.zeros_like(token)
    for copy in copies:
        copy.wait()


def relay_kernel(axis, got, even, odd, _, out):
    me = lax.axis_index(axis)
    devices, each, _ = got.shape
    for device in range(devices):
        out[pl.ds(device * each, each), :] = got[device]
    wants_even = (me // 2 + me) % 2 == 0
    span = pl.ds(devices * each, even.shape[0])

    @pl.when(wants_even)
    def _():
        out[span, :] = even[...]

    @pl.when(jnp.logical_not(wants_even))
    def _():
        out[span, :] = odd[...]


def apply(per_group, each, slabs, places, ahead, blocks, swaps, high, low, target, near, far, window, table):
    clusters = near.shape[0] // R
    slots = (ahead.shape[0] + blocks.shape[0]) // clusters
    rank = LANES // per_group
    head = clusters // per_group * R
    rows = slabs[0].shape[0]
    devices = (swaps[0].shape[0] - rows) // each
    for at, slab in enumerate(slabs):
        window[pl.ds(at * rows, rows), :] = slab[...].astype(f32)
    window[pl.ds(len(slabs) * rows, rows), :] = swaps[1][pl.ds(devices * each, rows), :].astype(f32)
    window[pl.ds((len(slabs) + 1) * rows, R), :] = jnp.zeros((R, LANES), f32)
    for part, values in enumerate(swaps):
        for device in range(devices):
            at = (part * devices + device) * head
            table[pl.ds(at, head), :] = values[pl.ds(device * each, head), :].astype(f32)
    lane = lane_ids()

    def fetch(k, i):
        return window[pl.ds(pl.multiple_of(places[k, i] * R, R), R), :]

    def block(k, i):
        at = i * slots + k
        return ahead[at] if at < ahead.shape[0] else blocks[at - ahead.shape[0]]

    def pick(i):
        tile = jnp.zeros((R, LANES), f32)
        for k in range(slots):
            j = places[slots + k, i]
            found = table[pl.ds(pl.multiple_of(lax.div(j, per_group) * R, R), R), :]
            shift = ((k - j) * rank) & (LANES - 1)
            tile = jnp.where(lane // rank == k, pltpu.roll(found, shift, 1), tile)
        return tile

    picked = []
    for i in range(0, clusters, 2):
        both = jnp.zeros((2 * R, 2 * LANES), f32)
        for k in range(0, slots, 2):
            sources = jnp.concatenate(
                [jnp.concatenate([fetch(k + n, i), fetch(k + n, i + 1)], axis=0) for n in range(2)], axis=1
            )
            weights = jnp.concatenate(
                [jnp.concatenate([block(k + n, i), block(k + n, i + 1)], axis=0) for n in range(2)], axis=1
            )
            both = both + dot(sources.astype(bf16), weights, (1, 1))
        near[pl.ds(i * R, R), :] = both[:R, :LANES]
        near[pl.ds((i + 1) * R, R), :] = both[R:, LANES:]
        if 2 * i < clusters:
            picked += [pick(n) for n in range(2 * i, 2 * i + 4)]
        if 2 * i == clusters - 4:
            picked = jnp.concatenate(picked, axis=0).astype(bf16)
            crossed = dot(picked, high[...]) + dot(picked, low[...])
            expanded_high, expanded_low = [], []
            for s in range(rank * clusters // LANES):
                tile = jnp.zeros((R, LANES), f32)
                for n in range(clusters):
                    part = crossed[n * R : (n + 1) * R, s * LANES : (s + 1) * LANES]
                    tile = jnp.where(lane % clusters == n, part, tile)
                tile_high = tile.astype(bf16).astype(f32)
                tile_low = tile - tile_high
                for source, kept in ((tile_high, expanded_high), (tile_low, expanded_low)):
                    spread = [jnp.where(lane % clusters == n, source, 0.0) for n in range(clusters)]
                    kept.append(jnp.concatenate(spread, axis=0).astype(bf16))
            far[...] = dot(jnp.concatenate(expanded_high, axis=1), target[...]) + dot(
                jnp.concatenate(expanded_low, axis=1), target[...]
            )


def first_kernel(
    per_group, own, mate, even, odd, places, ahead, blocks, sent, received, high, low, target, b, basis,
    image, lowered, payload, near, far, window, table,
):
    clusters = near.shape[0] // R
    slabs, swaps = (own, mate, even, odd), (sent, received)
    each = clusters // per_group * R + TAIL
    apply(per_group, each, slabs, places, ahead, blocks, swaps, high, low, target, near, far, window, table)
    tiles = []
    sums = [jnp.zeros((R, LANES), f32) for _ in range(3)]
    for i in range(clusters):
        field = rows_of(b, i)
        made = 0.5 * field + (rows_of(near, i) + rows_of(far, i))
        sums = [s + f * g for s, f, g in zip(sums, (field, field, made), (field, made, made))]
        tiles.append(made)
    for i in range(0, clusters, 2):
        both = jnp.concatenate(tiles[i : i + 2], axis=0)
        image[pl.ds(i * R, 2 * R), :] = both
        lowered[pl.ds(i * R, 2 * R), :] = both.astype(bf16)
    write_payload(payload, tiles, sums, basis, per_group)


def arnoldi_one(bb, bw, ww):
    whole = bb + epsilon
    start_norm = jnp.sqrt(whole)
    scale = 1.0 / start_norm
    v11 = bb / whole
    h11 = (bw * scale) * scale
    uu = jnp.maximum((ww * scale) * scale - 2.0 * h11 * h11 + h11 * h11 * v11, 0.0)
    h21 = jnp.sqrt(uu + epsilon)
    return start_norm, h11, h21, v11, uu / (uu + epsilon), h11 * (1.0 - v11) / h21


def second_kernel(
    per_group, unknowns, own, mate, even, odd, places, ahead, blocks, sent, received, high, low, target, b, image,
    candidate, sums_out, near, far, window, table,
):
    clusters = near.shape[0] // R
    head = clusters // per_group * R
    slabs, swaps = (own, mate, even, odd), (sent, received)
    apply(per_group, head + TAIL, slabs, places, ahead, blocks, swaps, high, low, target, near, far, window, table)
    sums = read_sums(tails(swaps, own.shape[0], head), 3, unknowns)
    start_norm, h11, h21, _, _, _ = arnoldi_one(*sums)
    scale = 1.0 / start_norm
    inverse = 1.0 / h21
    sums = [jnp.zeros((R, LANES), f32) for _ in range(3)]
    for j in range(clusters):
        held = rows_of(image, j) * scale
        first = rows_of(b, j) * scale
        second = (held - h11 * first) * inverse
        made = (0.5 * held + (rows_of(near, j) + rows_of(far, j)) * scale - h11 * held) * inverse
        sums = [s + v * made for s, v in zip(sums, (first, second, made))]
        candidate[pl.ds(j * R, R), :] = made
    lane = lane_ids()
    tile = jnp.zeros((R, LANES), f32)
    for t, partial in enumerate(sums):
        tile = jnp.where(lane == t, jnp.sum(partial, axis=1, keepdims=True), tile)
    sums_out[...] = tile


def finish_kernel(
    per_group, unknowns, b, image, candidate, sent, received, total, total_mate, solution_out, next_out
):
    clusters = b.shape[0] // R
    sums = read_sums(tails((sent, received), b.shape[0], clusters // per_group * R), 3, unknowns)
    start_norm, h11, h21, v11, v22, v12 = arnoldi_one(*sums)
    totals = total[...] + total_mate[...]
    h12, h22, ww = [totals[:, t : t + 1] * (1.0 / unknowns) for t in range(3)]
    uu = ww - 2.0 * (h12 * h12 + h22 * h22) + h12 * h12 * v11 + h22 * h22 * v22 + 2.0 * h12 * h22 * v12
    h32 = jnp.sqrt(jnp.maximum(uu, 0.0) + epsilon)
    g11 = h11 * h11 + h21 * h21
    g12 = h11 * h12 + h21 * h22
    g22 = h12 * h12 + h22 * h22 + h32 * h32
    t1, t2 = start_norm * h11, start_norm * h12
    det = g11 * g22 - g12 * g12
    y1 = (g22 * t1 - g12 * t2) / det
    y2 = (g11 * t2 - g12 * t1) / det
    scale, inverse, last = 1.0 / start_norm, 1.0 / h21, 1.0 / h32
    for j in range(clusters):
        span = slice(j * LANES, (j + 1) * LANES)
        first = rows_of(b, j) * scale
        second = (rows_of(image, j) * scale - h11 * first) * inverse
        solution_out[:, span] = y1 * first + y2 * second
        next_out[:, span] = (rows_of(candidate, j) - h12 * first - h22 * second) * last


def swapped(block, partner):
    return lax.ppermute(block, "rows", [(i, partner(i)) for i in range(lax.axis_size("rows"))])


def core_mate(i):
    return i ^ 1


def even_mate(i):
    return i ^ 2


def odd_mate(i):
    chip = i // 2
    other = chip + 1 if chip % 2 else chip - 1
    return 2 * (other % (lax.axis_size("rows") // 2)) + i % 2


def sends_of(block):
    return [block] + [swapped(block, partner) for partner in (core_mate, even_mate, odd_mate)]


def window_place(distance, clusters):
    me = lax.axis_index("rows")
    core, chip = me % 2, me // 2
    before, after = 3 - chip % 2, 2 + chip % 2
    slot = [
        before,
        jnp.where(core == 0, 4, 1),
        0,
        jnp.where(core == 0, 1, 4),
        after,
    ]
    slab = distance // clusters
    chosen = jnp.zeros_like(distance)
    for s, value in enumerate(slot):
        chosen = jnp.where(slab == s, value, chosen)
    return chosen * clusters + distance % clusters


def on_device(
    right_sides, near_blocks, near_cols, near_counts, basis_in, target_basis, coupling, far_cols
):
    width = right_sides.shape[1]
    clusters, slots = near_cols.shape
    rank = basis_in.shape[1]
    per_group = LANES // rank
    head = clusters // per_group * R
    size = lax.axis_size("rows")
    every = clusters * size
    unknowns = float(width * size)
    rows = clusters * R

    def shape(*dims, dtype=f32):
        return jax.ShapeDtypeStruct(dims, dtype)

    def scratch(*dims, dtype=f32):
        return pltpu.VMEM(dims, dtype)

    def in_hbm(array):
        return pltpu.with_memory_space_constraint(array, pltpu.HBM)

    def call(kernel, name, out, ins, *args, scratch_shapes=()):
        return pl.pallas_call(
            kernel, out_shape=out, in_specs=ins, out_specs=jax.tree.map(lambda _: VMEM, out),
            scratch_shapes=scratch_shapes, compiler_params=PARAMS, name=name,
        )(*args)

    def gather(block):
        groups = [list(range(core, size, 2)) for core in range(2)]
        return lax.all_to_all(block, "rows", 0, 0, axis_index_groups=groups)

    field, basis, lowered, payload = call(
        functools.partial(start_kernel, per_group), "start",
        (
            shape(rows, LANES), shape(clusters * rank, LANES, dtype=bf16), shape(rows, LANES, dtype=bf16),
            shape(size // 2, head + TAIL, LANES, dtype=bf16),
        ),
        [HBM] * 2, in_hbm(right_sides), in_hbm(basis_in.reshape(clusters * rank, LANES)),
        scratch_shapes=[scratch(R, width), pltpu.SemaphoreType.DMA((2,))],
    )
    got = gather(payload)
    held = sends_of(lowered)

    reach = 2 * clusters
    start = lax.axis_index("rows") * clusters
    distance = (near_cols.T - start + reach) % every
    live = jnp.arange(slots, dtype=jnp.int32)[:, None] < near_counts[None, :]
    placed = jnp.where(live, window_place(distance, clusters), 5 * clusters).astype(jnp.int32)
    owner = far_cols.T // clusters
    other_core = (owner % 2) ^ (lax.axis_index("rows") % 2)
    far_index = (other_core * (size // 2) + owner // 2) * clusters + far_cols.T % clusters
    places = jnp.concatenate([placed, far_index], axis=0)
    blocks = in_hbm(near_blocks.reshape(clusters * slots, LANES, LANES))
    early = blocks.shape[0] // 4
    high, low, target, ahead = call(
        prepare_kernel, "prepare",
        (
            shape(slots * rank, rank * clusters, dtype=bf16),
            shape(slots * rank, rank * clusters, dtype=bf16),
            shape(rank * clusters, LANES, dtype=bf16),
            pltpu.VMEM((early, LANES, LANES), bf16),
        ),
        [HBM] * 3 + [ANY] * 2,
        in_hbm(jnp.transpose(coupling, (1, 2, 3, 0))), in_hbm(target_basis.reshape(clusters * rank, LANES)),
        blocks, payload, places,
        scratch_shapes=[
            scratch(slots, rank, rank, clusters), scratch(clusters * rank, LANES, dtype=bf16),
            pltpu.SemaphoreType.DMA((3,)),
        ],
    )

    def fetch(name, first, count, chunks, *behind):
        here, token = call(
            functools.partial(fetch_kernel, first), name, (pltpu.VMEM((count, LANES, LANES), bf16), shape(R, LANES)),
            [HBM] + [ANY] * len(behind), blocks, *behind, scratch_shapes=[pltpu.SemaphoreType.DMA((chunks,))],
        )
        return pltpu.with_memory_space_constraint(here, pltpu.VMEM), token

    def arrived(got, held, ahead, behind):
        rest, token = fetch("fetch", early, blocks.shape[0] - early, 8, got, behind)
        sent = call(
            functools.partial(relay_kernel, "rows"), "relay",
            shape(got.shape[0] * got.shape[1] + rows, LANES, dtype=bf16), [VMEM] * 3 + [ANY], got, *held[2:], token
        )
        return *held, places, ahead, rest, sent, swapped(sent, core_mate), high, low, target

    ahead = pltpu.with_memory_space_constraint(ahead, pltpu.VMEM)
    kept = [scratch(rows, LANES), scratch(rows, LANES), scratch(5 * rows + R, LANES), scratch(size * head, LANES)]
    operands = [VMEM] * 4 + [SMEM] + [VMEM] * 9
    image, lowered, payload = call(
        functools.partial(first_kernel, per_group), "operator_one",
        (
            shape(rows, LANES), shape(rows, LANES, dtype=bf16),
            shape(size // 2, head + TAIL, LANES, dtype=bf16),
        ),
        operands, *arrived(got, held, ahead, target), field, basis, scratch_shapes=kept,
    )
    got = gather(payload)
    ahead, token = fetch("ahead", 0, early, 2, payload)
    here = arrived(got, sends_of(lowered), ahead, token)
    candidate, sums = call(
        functools.partial(second_kernel, per_group, unknowns), "operator_two",
        (shape(rows, LANES), shape(R, LANES)),
        operands, *here, field, image, scratch_shapes=kept,
    )
    *steps, last = [1 << n for n in range((size - 1).bit_length())]
    for step in steps:
        sums = sums + swapped(sums, lambda i: i ^ step)
    return call(
        functools.partial(finish_kernel, per_group, unknowns), "finish", (shape(R, width), shape(R, width)),
        [VMEM] * 7, field, image, candidate, *here[7:9], sums, swapped(sums, lambda i: i ^ last),
    )


def solution(mesh):
    return jax.shard_map(
        on_device,
        mesh=mesh,
        in_specs=(
            P("groups", "rows"),
            P("rows", None, None, None),
            P("rows", None),
            P("rows"),
            P("rows", None, None),
            P("rows", None, None),
            P("rows", None, None, None),
            P("rows", None),
        ),
        out_specs=(P("groups", "rows"), P("groups", "rows")),
        check_vma=False,
    )
```

```python
import functools

import jax
import jax.numpy as jnp
from jax import lax
from jax.experimental import pallas as pl
from jax.experimental.pallas import tpu as pltpu
from jax.sharding import PartitionSpec as P

epsilon = 1e-06
f32, bf16 = jnp.float32, jnp.bfloat16
VMEM = pl.BlockSpec(memory_space=pltpu.VMEM)
SMEM = pl.BlockSpec(memory_space=pltpu.SMEM)
HBM = pl.BlockSpec(memory_space=pltpu.HBM)
ANY = pl.BlockSpec(memory_space=pl.ANY)
R = 8
LANES = 128
SUM_SLOTS = 8
TAIL = 16
PARAMS = pltpu.CompilerParams(vmem_limit_bytes=24 * 1024 * 1024)


def lane_ids(rows=R):
    return lax.broadcasted_iota(jnp.int32, (rows, LANES), 1)


def rows_of(ref, j):
    return ref[pl.ds(j * R, R), :]


def dot(a, b, contract=(1, 0)):
    return lax.dot_general(a, b, (((contract[0],), (contract[1],)), ((), ())), preferred_element_type=f32)


def sums_tile(sums):
    lane = lane_ids()
    tile = jnp.zeros((R, LANES), f32)
    for t, partial in enumerate(sums):
        total = jnp.sum(partial, axis=1, keepdims=True)
        high = total.astype(bf16).astype(f32)
        middle = (total - high).astype(bf16).astype(f32)
        low = total - high - middle
        for part, value in enumerate((high, middle, low)):
            tile = jnp.where(lane == part * SUM_SLOTS + t, value, tile)
    return tile


def read_sums(parts, count, unknowns):
    total = jnp.zeros((R, LANES), f32)
    for part in parts:
        total = total + part.astype(f32)[:R]
    return [
        sum(total[:, p * SUM_SLOTS + t : p * SUM_SLOTS + t + 1] for p in range(3)) * (1.0 / unknowns)
        for t in range(count)
    ]


def tails(swaps, rows, head):
    each = head + TAIL
    return [
        values[pl.ds(device * each + head, TAIL), :]
        for values in swaps
        for device in range((values.shape[0] - rows) // each)
    ]


def compress(tiles, basis, group):
    stacked = jnp.concatenate(tiles, axis=0)
    high = stacked.astype(bf16)
    low = (stacked - high.astype(f32)).astype(bf16)
    both = dot(jnp.concatenate([high, low], axis=0), basis[pl.ds(group * LANES, LANES), :], (1, 1))
    rows = len(tiles) * R
    both = both[:rows] + both[rows:]
    lane = lane_ids()
    rank = LANES // len(tiles)
    tile = jnp.zeros((R, LANES), f32)
    for m in range(len(tiles)):
        tile = jnp.where(lane // rank == m, both[m * R : (m + 1) * R], tile)
    return tile


def write_payload(payload, tiles, sums, basis, per_group):
    groups = len(tiles) // per_group
    parts = [compress(tiles[g * per_group : (g + 1) * per_group], basis, g) for g in range(groups)]
    parts += [sums_tile(sums), jnp.zeros((TAIL - R, LANES), f32)]
    block = jnp.concatenate(parts, axis=0).astype(bf16)
    for device in range(payload.shape[0]):
        payload[device] = block


def start_kernel(per_group, b_hbm, basis_hbm, field, basis, lowered, payload, b, sems):
    copies = [
        pltpu.make_async_copy(b_hbm, b, sems.at[0]),
        pltpu.make_async_copy(basis_hbm, basis, sems.at[1]),
    ]
    for copy in copies:
        copy.start()
    for copy in copies:
        copy.wait()
    clusters = b.shape[1] // LANES
    tiles = [b[:, j * LANES : (j + 1) * LANES] for j in range(clusters)]
    field[...] = jnp.concatenate(tiles, axis=0)
    lowered[...] = jnp.concatenate(tiles, axis=0).astype(bf16)
    write_payload(payload, tiles, [], basis, per_group)


def window_place(distance, clusters, me):
    core, chip = me % 2, me // 2
    before, after = 3 - chip % 2, 2 + chip % 2
    slot = [before, jnp.where(core == 0, 4, 1), 0, jnp.where(core == 0, 1, 4), after]
    slab = lax.div(distance, clusters)
    chosen = jnp.zeros_like(distance)
    for s, value in enumerate(slot):
        chosen = jnp.where(slab == s, value, chosen)
    return chosen * clusters + lax.rem(distance, clusters)


def prepare_kernel(
    axis, size, near_cols_hbm, near_counts_hbm, far_cols_hbm, coupling_hbm, target_hbm, blocks_hbm, _,
    places, high_out, low_out, target_out, ahead, near_cols, near_counts, far_cols, coupling, target, sems,
):
    pairs = (
        (near_cols_hbm, near_cols), (near_counts_hbm, near_counts), (far_cols_hbm, far_cols),
        (coupling_hbm, coupling), (target_hbm, target), (blocks_hbm.at[pl.ds(0, ahead.shape[0])], ahead),
    )
    copies = [pltpu.make_async_copy(source, to, sems.at[n]) for n, (source, to) in enumerate(pairs)]
    for copy in copies:
        copy.start()
    for copy in copies[:3]:
        copy.wait()
    slots, clusters = near_cols.shape
    me = lax.axis_index(axis)
    every = clusters * size
    distance = near_cols[...] - me * clusters + 2 * clusters
    distance = jnp.where(distance < 0, distance + every, distance)
    distance = jnp.where(distance >= every, distance - every, distance)
    live = lax.broadcasted_iota(jnp.int32, (slots, clusters), 0) < near_counts[...]
    places[:slots, :] = jnp.where(live, window_place(distance, clusters, me), 5 * clusters)
    owner = lax.div(far_cols[...], clusters)
    other_core = (owner ^ me) & 1
    places[slots:, :] = (other_core * (size // 2) + owner // 2) * clusters + lax.rem(far_cols[...], clusters)
    for copy in copies[3:5]:
        copy.wait()
    slots, rank, _, clusters = coupling.shape
    per_tile = LANES // clusters
    for s in range(rank // per_tile):
        pieces = [
            coupling[:, s * per_tile + p].reshape(slots * rank, clusters) for p in range(per_tile)
        ]
        tile = jnp.concatenate(pieces, axis=1)
        high = tile.astype(bf16)
        high_out[:, s * LANES : (s + 1) * LANES] = high
        low_out[:, s * LANES : (s + 1) * LANES] = (tile - high.astype(f32)).astype(bf16)
    size = rank * clusters
    row = lax.broadcasted_iota(jnp.int32, (size, size), 0)
    column = lax.broadcasted_iota(jnp.int32, (size, size), 1)
    wanted = (row % clusters) * rank + row // clusters
    target_out[...] = dot((column == wanted).astype(bf16), target[...]).astype(bf16)
    copies[5].wait()


def fetch_kernel(first, blocks_hbm, *refs):
    *_, blocks, token, sems = refs
    chunks = sems.shape[0]
    each = blocks.shape[0] // chunks
    copies = [
        pltpu.make_async_copy(
            blocks_hbm.at[pl.ds(first + c * each, each)], blocks.at[pl.ds(c * each, each)], sems.at[c]
        )
        for c in range(chunks)
    ]
    for copy in copies:
        copy.start()
    token[...] = jnp.zeros_like(token)
    for copy in copies:
        copy.wait()


def relay_kernel(axis, got, even, odd, _, out):
    me = lax.axis_index(axis)
    devices, each, _ = got.shape
    for device in range(devices):
        out[pl.ds(device * each, each), :] = got[device]
    wants_even = (me // 2 + me) % 2 == 0
    span = pl.ds(devices * each, even.shape[0])

    @pl.when(wants_even)
    def _():
        out[span, :] = even[...]

    @pl.when(jnp.logical_not(wants_even))
    def _():
        out[span, :] = odd[...]


def apply(per_group, each, slabs, places, ahead, blocks, swaps, high, low, target, near, far, window, table):
    clusters = near.shape[0] // R
    slots = (ahead.shape[0] + blocks.shape[0]) // clusters
    rank = LANES // per_group
    head = clusters // per_group * R
    rows = slabs[0].shape[0]
    devices = (swaps[0].shape[0] - rows) // each
    for at, slab in enumerate(slabs):
        window[pl.ds(at * rows, rows), :] = slab[...].astype(f32)
    window[pl.ds(len(slabs) * rows, rows), :] = swaps[1][pl.ds(devices * each, rows), :].astype(f32)
    window[pl.ds((len(slabs) + 1) * rows, R), :] = jnp.zeros((R, LANES), f32)
    for part, values in enumerate(swaps):
        for device in range(devices):
            at = (part * devices + device) * head
            table[pl.ds(at, head), :] = values[pl.ds(device * each, head), :].astype(f32)
    lane = lane_ids()

    def fetch(k, i):
        return window[pl.ds(pl.multiple_of(places[k, i] * R, R), R), :]

    def block(k, i):
        at = i * slots + k
        return ahead[at] if at < ahead.shape[0] else blocks[at - ahead.shape[0]]

    def pick(i):
        tile = jnp.zeros((R, LANES), f32)
        for k in range(slots):
            j = places[slots + k, i]
            found = table[pl.ds(pl.multiple_of(lax.div(j, per_group) * R, R), R), :]
            shift = ((k - j) * rank) & (LANES - 1)
            tile = jnp.where(lane // rank == k, pltpu.roll(found, shift, 1), tile)
        return tile

    picked = []
    for i in range(0, clusters, 2):
        both = jnp.zeros((2 * R, 2 * LANES), f32)
        for k in range(0, slots, 2):
            sources = jnp.concatenate(
                [jnp.concatenate([fetch(k + n, i), fetch(k + n, i + 1)], axis=0) for n in range(2)], axis=1
            )
            weights = jnp.concatenate(
                [jnp.concatenate([block(k + n, i), block(k + n, i + 1)], axis=0) for n in range(2)], axis=1
            )
            both = both + dot(sources.astype(bf16), weights, (1, 1))
        near[pl.ds(i * R, R), :] = both[:R, :LANES]
        near[pl.ds((i + 1) * R, R), :] = both[R:, LANES:]
        if 2 * i < clusters:
            picked += [pick(n) for n in range(2 * i, 2 * i + 4)]
        if 2 * i == clusters - 4:
            picked = jnp.concatenate(picked, axis=0).astype(bf16)
            crossed = dot(picked, high[...]) + dot(picked, low[...])
            expanded_high, expanded_low = [], []
            for s in range(rank * clusters // LANES):
                tile = jnp.zeros((R, LANES), f32)
                for n in range(clusters):
                    part = crossed[n * R : (n + 1) * R, s * LANES : (s + 1) * LANES]
                    tile = jnp.where(lane % clusters == n, part, tile)
                tile_high = tile.astype(bf16).astype(f32)
                tile_low = tile - tile_high
                for source, kept in ((tile_high, expanded_high), (tile_low, expanded_low)):
                    spread = [jnp.where(lane % clusters == n, source, 0.0) for n in range(clusters)]
                    kept.append(jnp.concatenate(spread, axis=0).astype(bf16))
            far[...] = dot(jnp.concatenate(expanded_high, axis=1), target[...]) + dot(
                jnp.concatenate(expanded_low, axis=1), target[...]
            )


def first_kernel(
    per_group, own, mate, even, odd, places, ahead, blocks, sent, received, high, low, target, b, basis,
    image, lowered, payload, near, far, window, table,
):
    clusters = near.shape[0] // R
    slabs, swaps = (own, mate, even, odd), (sent, received)
    each = clusters // per_group * R + TAIL
    apply(per_group, each, slabs, places, ahead, blocks, swaps, high, low, target, near, far, window, table)
    tiles = []
    sums = [jnp.zeros((R, LANES), f32) for _ in range(3)]
    for i in range(clusters):
        field = rows_of(b, i)
        made = 0.5 * field + (rows_of(near, i) + rows_of(far, i))
        sums = [s + f * g for s, f, g in zip(sums, (field, field, made), (field, made, made))]
        tiles.append(made)
    for i in range(0, clusters, 2):
        both = jnp.concatenate(tiles[i : i + 2], axis=0)
        image[pl.ds(i * R, 2 * R), :] = both
        lowered[pl.ds(i * R, 2 * R), :] = both.astype(bf16)
    write_payload(payload, tiles, sums, basis, per_group)


def arnoldi_one(bb, bw, ww):
    whole = bb + epsilon
    start_norm = jnp.sqrt(whole)
    scale = 1.0 / start_norm
    v11 = bb / whole
    h11 = (bw * scale) * scale
    uu = jnp.maximum((ww * scale) * scale - 2.0 * h11 * h11 + h11 * h11 * v11, 0.0)
    h21 = jnp.sqrt(uu + epsilon)
    return start_norm, h11, h21, v11, uu / (uu + epsilon), h11 * (1.0 - v11) / h21


def second_kernel(
    per_group, unknowns, own, mate, even, odd, places, ahead, blocks, sent, received, high, low, target, b, image,
    candidate, sums_out, near, far, window, table,
):
    clusters = near.shape[0] // R
    head = clusters // per_group * R
    slabs, swaps = (own, mate, even, odd), (sent, received)
    apply(per_group, head + TAIL, slabs, places, ahead, blocks, swaps, high, low, target, near, far, window, table)
    sums = read_sums(tails(swaps, own.shape[0], head), 3, unknowns)
    start_norm, h11, h21, _, _, _ = arnoldi_one(*sums)
    scale = 1.0 / start_norm
    inverse = 1.0 / h21
    sums = [jnp.zeros((R, LANES), f32) for _ in range(3)]
    for j in range(clusters):
        held = rows_of(image, j) * scale
        first = rows_of(b, j) * scale
        second = (held - h11 * first) * inverse
        made = (0.5 * held + (rows_of(near, j) + rows_of(far, j)) * scale - h11 * held) * inverse
        sums = [s + v * made for s, v in zip(sums, (first, second, made))]
        candidate[pl.ds(j * R, R), :] = made
    tile = sums_tile(sums).astype(bf16)
    for device in range(sums_out.shape[0]):
        sums_out[device] = tile


def finish_kernel(per_group, unknowns, b, image, candidate, sent, received, got, solution_out, next_out):
    clusters = b.shape[0] // R
    sums = read_sums(tails((sent, received), b.shape[0], clusters // per_group * R), 3, unknowns)
    start_norm, h11, h21, v11, v22, v12 = arnoldi_one(*sums)
    h12, h22, ww = read_sums([got[device] for device in range(got.shape[0])], 3, unknowns)
    uu = ww - 2.0 * (h12 * h12 + h22 * h22) + h12 * h12 * v11 + h22 * h22 * v22 + 2.0 * h12 * h22 * v12
    h32 = jnp.sqrt(jnp.maximum(uu, 0.0) + epsilon)
    g11 = h11 * h11 + h21 * h21
    g12 = h11 * h12 + h21 * h22
    g22 = h12 * h12 + h22 * h22 + h32 * h32
    t1, t2 = start_norm * h11, start_norm * h12
    det = g11 * g22 - g12 * g12
    y1 = (g22 * t1 - g12 * t2) / det
    y2 = (g11 * t2 - g12 * t1) / det
    scale, inverse, last = 1.0 / start_norm, 1.0 / h21, 1.0 / h32
    for j in range(clusters):
        span = slice(j * LANES, (j + 1) * LANES)
        first = rows_of(b, j) * scale
        second = (rows_of(image, j) * scale - h11 * first) * inverse
        solution_out[:, span] = y1 * first + y2 * second
        next_out[:, span] = (rows_of(candidate, j) - h12 * first - h22 * second) * last


def swapped(block, partner):
    return lax.ppermute(block, "rows", [(i, partner(i)) for i in range(lax.axis_size("rows"))])


def core_mate(i):
    return i ^ 1


def even_mate(i):
    return i ^ 2


def odd_mate(i):
    chip = i // 2
    other = chip + 1 if chip % 2 else chip - 1
    return 2 * (other % (lax.axis_size("rows") // 2)) + i % 2


def sends_of(block):
    return [block] + [swapped(block, partner) for partner in (core_mate, even_mate, odd_mate)]


def on_device(
    right_sides, near_blocks, near_cols, near_counts, basis_in, target_basis, coupling, far_cols
):
    width = right_sides.shape[1]
    clusters, slots = near_cols.shape
    rank = basis_in.shape[1]
    per_group = LANES // rank
    head = clusters // per_group * R
    size = lax.axis_size("rows")
    unknowns = float(width * size)
    rows = clusters * R

    def shape(*dims, dtype=f32):
        return jax.ShapeDtypeStruct(dims, dtype)

    def scratch(*dims, dtype=f32):
        return pltpu.VMEM(dims, dtype)

    def in_hbm(array):
        return pltpu.with_memory_space_constraint(array, pltpu.HBM)

    def call(kernel, name, out, ins, *args, scratch_shapes=()):
        return pl.pallas_call(
            kernel, out_shape=out, in_specs=ins, out_specs=jax.tree.map(lambda _: VMEM, out),
            scratch_shapes=scratch_shapes, compiler_params=PARAMS, name=name,
        )(*args)

    def gather(block):
        groups = [list(range(core, size, 2)) for core in range(2)]
        return lax.all_to_all(block, "rows", 0, 0, axis_index_groups=groups)

    field, basis, lowered, payload = call(
        functools.partial(start_kernel, per_group), "start",
        (
            shape(rows, LANES), shape(clusters * rank, LANES, dtype=bf16), shape(rows, LANES, dtype=bf16),
            shape(size // 2, head + TAIL, LANES, dtype=bf16),
        ),
        [HBM] * 2, in_hbm(right_sides), in_hbm(basis_in.reshape(clusters * rank, LANES)),
        scratch_shapes=[scratch(R, width), pltpu.SemaphoreType.DMA((2,))],
    )
    got = gather(payload)
    held = sends_of(lowered)

    blocks = in_hbm(near_blocks.reshape(clusters * slots, LANES, LANES))
    early = blocks.shape[0] // 4
    places, high, low, target, ahead = call(
        functools.partial(prepare_kernel, "rows", size), "prepare",
        (
            shape(2 * slots, clusters, dtype=jnp.int32),
            shape(slots * rank, rank * clusters, dtype=bf16),
            shape(slots * rank, rank * clusters, dtype=bf16),
            shape(rank * clusters, LANES, dtype=bf16),
            pltpu.VMEM((early, LANES, LANES), bf16),
        ),
        [HBM] * 6 + [ANY], in_hbm(near_cols.T), in_hbm(near_counts.reshape(1, clusters)), in_hbm(far_cols.T),
        in_hbm(jnp.transpose(coupling, (1, 2, 3, 0))), in_hbm(target_basis.reshape(clusters * rank, LANES)),
        blocks, held[2],
        scratch_shapes=[
            scratch(slots, clusters, dtype=jnp.int32), scratch(1, clusters, dtype=jnp.int32),
            scratch(slots, clusters, dtype=jnp.int32),
            scratch(slots, rank, rank, clusters), scratch(clusters * rank, LANES, dtype=bf16),
            pltpu.SemaphoreType.DMA((6,)),
        ],
    )

    def fetch(name, first, count, chunks, *behind):
        here, token = call(
            functools.partial(fetch_kernel, first), name, (pltpu.VMEM((count, LANES, LANES), bf16), shape(R, LANES)),
            [HBM] + [ANY] * len(behind), blocks, *behind, scratch_shapes=[pltpu.SemaphoreType.DMA((chunks,))],
        )
        return pltpu.with_memory_space_constraint(here, pltpu.VMEM), token

    def arrived(got, held, ahead, behind):
        rest, token = fetch("fetch", early, blocks.shape[0] - early, 8, got, behind)
        sent = call(
            functools.partial(relay_kernel, "rows"), "relay",
            shape(got.shape[0] * got.shape[1] + rows, LANES, dtype=bf16), [VMEM] * 3 + [ANY], got, *held[2:], token
        )
        return *held, places, ahead, rest, sent, swapped(sent, core_mate), high, low, target

    ahead = pltpu.with_memory_space_constraint(ahead, pltpu.VMEM)
    kept = [scratch(rows, LANES), scratch(rows, LANES), scratch(5 * rows + R, LANES), scratch(size * head, LANES)]
    operands = [VMEM] * 4 + [SMEM] + [VMEM] * 9
    image, lowered, payload = call(
        functools.partial(first_kernel, per_group), "operator_one",
        (
            shape(rows, LANES), shape(rows, LANES, dtype=bf16),
            shape(size // 2, head + TAIL, LANES, dtype=bf16),
        ),
        operands, *arrived(got, held, ahead, target), field, basis, scratch_shapes=kept,
    )
    got = gather(payload)
    ahead, token = fetch("ahead", 0, early, 2, payload)
    here = arrived(got, sends_of(lowered), ahead, token)
    candidate, sums = call(
        functools.partial(second_kernel, per_group, unknowns), "operator_two",
        (shape(rows, LANES), shape(size, R, LANES, dtype=bf16)),
        operands, *here, field, image, scratch_shapes=kept,
    )
    return call(
        functools.partial(finish_kernel, per_group, unknowns), "finish", (shape(R, width), shape(R, width)),
        [VMEM] * 6, field, image, candidate, *here[7:9], lax.all_to_all(sums, "rows", 0, 0),
    )


def solution(mesh):
    return jax.shard_map(
        on_device,
        mesh=mesh,
        in_specs=(
            P("groups", "rows"),
            P("rows", None, None, None),
            P("rows", None),
            P("rows"),
            P("rows", None, None),
            P("rows", None, None),
            P("rows", None, None, None),
            P("rows", None),
        ),
        out_specs=(P("groups", "rows"), P("groups", "rows")),
        check_vma=False,
    )
```

```python
import functools

import jax
import jax.numpy as jnp
from jax import lax
from jax.experimental import pallas as pl
from jax.experimental.pallas import tpu as pltpu
from jax.sharding import PartitionSpec as P

epsilon = 1e-06
f32, bf16 = jnp.float32, jnp.bfloat16
VMEM = pl.BlockSpec(memory_space=pltpu.VMEM)
SMEM = pl.BlockSpec(memory_space=pltpu.SMEM)
HBM = pl.BlockSpec(memory_space=pltpu.HBM)
ANY = pl.BlockSpec(memory_space=pl.ANY)
R = 8
LANES = 128
SUM_SLOTS = 8
TAIL = 16
PARAMS = pltpu.CompilerParams(vmem_limit_bytes=24 * 1024 * 1024)


def lane_ids(rows=R):
    return lax.broadcasted_iota(jnp.int32, (rows, LANES), 1)


def rows_of(ref, j):
    return ref[pl.ds(j * R, R), :]


def dot(a, b, contract=(1, 0)):
    return lax.dot_general(a, b, (((contract[0],), (contract[1],)), ((), ())), preferred_element_type=f32)


def sums_tile(sums):
    lane = lane_ids()
    tile = jnp.zeros((R, LANES), f32)
    for t, partial in enumerate(sums):
        total = jnp.sum(partial, axis=1, keepdims=True)
        high = total.astype(bf16).astype(f32)
        middle = (total - high).astype(bf16).astype(f32)
        low = total - high - middle
        for part, value in enumerate((high, middle, low)):
            tile = jnp.where(lane == part * SUM_SLOTS + t, value, tile)
    return tile


def read_sums(parts, count, unknowns):
    total = jnp.zeros((R, LANES), f32)
    for part in parts:
        total = total + part.astype(f32)[:R]
    return [
        sum(total[:, p * SUM_SLOTS + t : p * SUM_SLOTS + t + 1] for p in range(3)) * (1.0 / unknowns)
        for t in range(count)
    ]


def tails(swaps, rows, head):
    each = head + TAIL
    return [
        values[pl.ds(device * each + head, TAIL), :]
        for values in swaps
        for device in range((values.shape[0] - rows) // each)
    ]


def compress(tiles, basis, group):
    stacked = jnp.concatenate(tiles, axis=0)
    high = stacked.astype(bf16)
    low = (stacked - high.astype(f32)).astype(bf16)
    both = dot(jnp.concatenate([high, low], axis=0), basis[pl.ds(group * LANES, LANES), :], (1, 1))
    rows = len(tiles) * R
    both = both[:rows] + both[rows:]
    lane = lane_ids()
    rank = LANES // len(tiles)
    tile = jnp.zeros((R, LANES), f32)
    for m in range(len(tiles)):
        tile = jnp.where(lane // rank == m, both[m * R : (m + 1) * R], tile)
    return tile


def write_payload(payload, parts, sums):
    if sums:
        parts = parts + [sums_tile(sums), jnp.zeros((TAIL - R, LANES), f32)]
    block = jnp.concatenate(parts, axis=0).astype(bf16)
    for device in range(payload.shape[0]):
        payload[device] = block


def start_kernel(per_group, b_hbm, basis_hbm, field, basis, lowered, payload, b, sems):
    copies = [
        pltpu.make_async_copy(b_hbm, b, sems.at[0]),
        pltpu.make_async_copy(basis_hbm, basis, sems.at[1]),
    ]
    for copy in copies:
        copy.start()
    for copy in copies:
        copy.wait()
    clusters = b.shape[1] // LANES
    tiles = [b[:, j * LANES : (j + 1) * LANES] for j in range(clusters)]
    field[...] = jnp.concatenate(tiles, axis=0)
    lowered[...] = jnp.concatenate(tiles, axis=0).astype(bf16)
    groups = [tiles[g : g + per_group] for g in range(0, clusters, per_group)]
    write_payload(payload, [compress(group, basis, g) for g, group in enumerate(groups)], [])


def window_place(distance, clusters, me):
    core, chip = me % 2, me // 2
    before, after = 3 - chip % 2, 2 + chip % 2
    slot = [before, jnp.where(core == 0, 4, 1), 0, jnp.where(core == 0, 1, 4), after]
    slab = lax.div(distance, clusters)
    chosen = jnp.zeros_like(distance)
    for s, value in enumerate(slot):
        chosen = jnp.where(slab == s, value, chosen)
    return chosen * clusters + lax.rem(distance, clusters)


def prepare_kernel(
    axis, size, near_cols_hbm, near_counts_hbm, far_cols_hbm, coupling_hbm, target_hbm, blocks_hbm, _,
    places, high_out, low_out, target_out, ahead, near_cols, near_counts, far_cols, coupling, target, sems,
):
    pairs = (
        (near_cols_hbm, near_cols), (near_counts_hbm, near_counts), (far_cols_hbm, far_cols),
        (coupling_hbm, coupling), (target_hbm, target), (blocks_hbm.at[pl.ds(0, ahead.shape[0])], ahead),
    )
    copies = [pltpu.make_async_copy(source, to, sems.at[n]) for n, (source, to) in enumerate(pairs)]
    for copy in copies:
        copy.start()
    for copy in copies[:3]:
        copy.wait()
    slots, clusters = near_cols.shape
    me = lax.axis_index(axis)
    every = clusters * size
    distance = near_cols[...] - me * clusters + 2 * clusters
    distance = jnp.where(distance < 0, distance + every, distance)
    distance = jnp.where(distance >= every, distance - every, distance)
    live = lax.broadcasted_iota(jnp.int32, (slots, clusters), 0) < near_counts[...]
    places[:slots, :] = jnp.where(live, window_place(distance, clusters, me), 5 * clusters)
    owner = lax.div(far_cols[...], clusters)
    other_core = (owner ^ me) & 1
    places[slots:, :] = (other_core * (size // 2) + owner // 2) * clusters + lax.rem(far_cols[...], clusters)
    for copy in copies[3:5]:
        copy.wait()
    slots, rank, _, clusters = coupling.shape
    per_tile = LANES // clusters
    for s in range(rank // per_tile):
        pieces = [
            coupling[:, s * per_tile + p].reshape(slots * rank, clusters) for p in range(per_tile)
        ]
        tile = jnp.concatenate(pieces, axis=1)
        high = tile.astype(bf16)
        high_out[:, s * LANES : (s + 1) * LANES] = high
        low_out[:, s * LANES : (s + 1) * LANES] = (tile - high.astype(f32)).astype(bf16)
    size = rank * clusters
    row = lax.broadcasted_iota(jnp.int32, (size, size), 0)
    column = lax.broadcasted_iota(jnp.int32, (size, size), 1)
    wanted = (row % clusters) * rank + row // clusters
    target_out[...] = dot((column == wanted).astype(bf16), target[...]).astype(bf16)
    copies[5].wait()


def fetch_kernel(first, blocks_hbm, *refs):
    *_, blocks, token, sems = refs
    chunks = sems.shape[0]
    each = blocks.shape[0] // chunks
    copies = [
        pltpu.make_async_copy(
            blocks_hbm.at[pl.ds(first + c * each, each)], blocks.at[pl.ds(c * each, each)], sems.at[c]
        )
        for c in range(chunks)
    ]
    for copy in copies:
        copy.start()
    token[...] = jnp.zeros_like(token)
    for copy in copies:
        copy.wait()


def relay_kernel(axis, got, even, odd, _, out):
    me = lax.axis_index(axis)
    devices, each, _ = got.shape
    for device in range(devices):
        out[pl.ds(device * each, each), :] = got[device]
    wants_even = (me // 2 + me) % 2 == 0
    span = pl.ds(devices * each, even.shape[0])

    @pl.when(wants_even)
    def _():
        out[span, :] = even[...]

    @pl.when(jnp.logical_not(wants_even))
    def _():
        out[span, :] = odd[...]


def apply(per_group, each, slabs, places, ahead, blocks, swaps, high, low, target, near, far, window, table, finish):
    clusters = near.shape[0] // R
    slots = (ahead.shape[0] + blocks.shape[0]) // clusters
    rank = LANES // per_group
    head = clusters // per_group * R
    rows = slabs[0].shape[0]
    devices = (swaps[0].shape[0] - rows) // each
    for at, slab in enumerate(slabs):
        window[pl.ds(at * rows, rows), :] = slab[...].astype(f32)
    window[pl.ds(len(slabs) * rows, rows), :] = swaps[1][pl.ds(devices * each, rows), :].astype(f32)
    window[pl.ds((len(slabs) + 1) * rows, R), :] = jnp.zeros((R, LANES), f32)
    for part, values in enumerate(swaps):
        for device in range(devices):
            at = (part * devices + device) * head
            table[pl.ds(at, head), :] = values[pl.ds(device * each, head), :].astype(f32)
    lane = lane_ids()

    def fetch(k, i):
        return window[pl.ds(pl.multiple_of(places[k, i] * R, R), R), :]

    def block(k, i):
        at = i * slots + k
        return ahead[at] if at < ahead.shape[0] else blocks[at - ahead.shape[0]]

    def pick(i):
        tile = jnp.zeros((R, LANES), f32)
        for k in range(slots):
            j = places[slots + k, i]
            found = table[pl.ds(pl.multiple_of(lax.div(j, per_group) * R, R), R), :]
            shift = ((k - j) * rank) & (LANES - 1)
            tile = jnp.where(lane // rank == k, pltpu.roll(found, shift, 1), tile)
        return tile

    picked = []
    for i in range(0, clusters, 2):
        both = jnp.zeros((2 * R, 2 * LANES), f32)
        for k in range(0, slots, 2):
            sources = jnp.concatenate(
                [jnp.concatenate([fetch(k + n, i), fetch(k + n, i + 1)], axis=0) for n in range(2)], axis=1
            )
            weights = jnp.concatenate(
                [jnp.concatenate([block(k + n, i), block(k + n, i + 1)], axis=0) for n in range(2)], axis=1
            )
            both = both + dot(sources.astype(bf16), weights, (1, 1))
        near[pl.ds(i * R, R), :] = both[:R, :LANES]
        near[pl.ds((i + 1) * R, R), :] = both[R:, LANES:]
        if 2 * i < clusters:
            picked += [pick(n) for n in range(2 * i, 2 * i + 4)]
        if 2 * i == clusters - 4:
            picked = jnp.concatenate(picked, axis=0).astype(bf16)
            crossed = dot(picked, high[...]) + dot(picked, low[...])
            expanded_high, expanded_low = [], []
            for s in range(rank * clusters // LANES):
                tile = jnp.zeros((R, LANES), f32)
                for n in range(clusters):
                    part = crossed[n * R : (n + 1) * R, s * LANES : (s + 1) * LANES]
                    tile = jnp.where(lane % clusters == n, part, tile)
                tile_high = tile.astype(bf16).astype(f32)
                tile_low = tile - tile_high
                for source, kept in ((tile_high, expanded_high), (tile_low, expanded_low)):
                    spread = [jnp.where(lane % clusters == n, source, 0.0) for n in range(clusters)]
                    kept.append(jnp.concatenate(spread, axis=0).astype(bf16))
            far[...] = dot(jnp.concatenate(expanded_high, axis=1), target[...]) + dot(
                jnp.concatenate(expanded_low, axis=1), target[...]
            )
        if 2 * i >= clusters:
            for n in range(2 * i - clusters, 2 * i - clusters + 4):
                finish(n)


def first_kernel(
    per_group, own, mate, even, odd, places, ahead, blocks, sent, received, high, low, target, b, basis,
    image, lowered, payload, near, far, window, table,
):
    clusters = near.shape[0] // R
    slabs, swaps = (own, mate, even, odd), (sent, received)
    each = clusters // per_group * R
    tiles, parts = [], []
    sums = [jnp.zeros((R, LANES), f32) for _ in range(3)]

    def finish(i):
        field = rows_of(b, i)
        made = 0.5 * field + (rows_of(near, i) + rows_of(far, i))
        sums[:] = [s + f * g for s, f, g in zip(sums, (field, field, made), (field, made, made))]
        tiles.append(made)
        if i % 2:
            both = jnp.concatenate(tiles[i - 1 :], axis=0)
            image[pl.ds((i - 1) * R, 2 * R), :] = both
            lowered[pl.ds((i - 1) * R, 2 * R), :] = both.astype(bf16)
        if i % per_group == per_group - 1:
            parts.append(compress(tiles[-per_group:], basis, i // per_group))

    apply(per_group, each, slabs, places, ahead, blocks, swaps, high, low, target, near, far, window, table, finish)
    write_payload(payload, parts, sums)


def arnoldi_one(bb, bw, ww):
    whole = bb + epsilon
    start_norm = jnp.sqrt(whole)
    scale = 1.0 / start_norm
    v11 = bb / whole
    h11 = (bw * scale) * scale
    uu = jnp.maximum((ww * scale) * scale - 2.0 * h11 * h11 + h11 * h11 * v11, 0.0)
    h21 = jnp.sqrt(uu + epsilon)
    return start_norm, h11, h21, v11, uu / (uu + epsilon), h11 * (1.0 - v11) / h21


def second_kernel(
    per_group, unknowns, own, mate, even, odd, places, ahead, blocks, sent, received, high, low, target, b, image,
    candidate, sums_out, near, far, window, table,
):
    clusters = near.shape[0] // R
    head = clusters // per_group * R
    slabs, swaps = (own, mate, even, odd), (sent, received)
    means = read_sums(tails(swaps, own.shape[0], head), 3, unknowns)
    start_norm, h11, h21, _, _, _ = arnoldi_one(*means)
    scale = 1.0 / start_norm
    inverse = 1.0 / h21
    sums = [jnp.zeros((R, LANES), f32) for _ in range(3)]

    def finish(j):
        held = rows_of(image, j) * scale
        first = rows_of(b, j) * scale
        second = (held - h11 * first) * inverse
        made = (0.5 * held + (rows_of(near, j) + rows_of(far, j)) * scale - h11 * held) * inverse
        sums[:] = [s + v * made for s, v in zip(sums, (first, second, made))]
        candidate[pl.ds(j * R, R), :] = made

    each = head + TAIL
    apply(per_group, each, slabs, places, ahead, blocks, swaps, high, low, target, near, far, window, table, finish)
    tile = sums_tile(sums).astype(bf16)
    for device in range(sums_out.shape[0]):
        sums_out[device] = tile


def finish_kernel(per_group, unknowns, b, image, candidate, sent, received, got, solution_out, next_out):
    clusters = b.shape[0] // R
    sums = read_sums(tails((sent, received), b.shape[0], clusters // per_group * R), 3, unknowns)
    start_norm, h11, h21, v11, v22, v12 = arnoldi_one(*sums)
    h12, h22, ww = read_sums([got[device] for device in range(got.shape[0])], 3, unknowns)
    uu = ww - 2.0 * (h12 * h12 + h22 * h22) + h12 * h12 * v11 + h22 * h22 * v22 + 2.0 * h12 * h22 * v12
    h32 = jnp.sqrt(jnp.maximum(uu, 0.0) + epsilon)
    g11 = h11 * h11 + h21 * h21
    g12 = h11 * h12 + h21 * h22
    g22 = h12 * h12 + h22 * h22 + h32 * h32
    t1, t2 = start_norm * h11, start_norm * h12
    det = g11 * g22 - g12 * g12
    y1 = (g22 * t1 - g12 * t2) / det
    y2 = (g11 * t2 - g12 * t1) / det
    scale, inverse, last = 1.0 / start_norm, 1.0 / h21, 1.0 / h32
    for j in range(clusters):
        span = slice(j * LANES, (j + 1) * LANES)
        first = rows_of(b, j) * scale
        second = (rows_of(image, j) * scale - h11 * first) * inverse
        solution_out[:, span] = y1 * first + y2 * second
        next_out[:, span] = (rows_of(candidate, j) - h12 * first - h22 * second) * last


def swapped(block, partner):
    return lax.ppermute(block, "rows", [(i, partner(i)) for i in range(lax.axis_size("rows"))])


def core_mate(i):
    return i ^ 1


def even_mate(i):
    return i ^ 2


def odd_mate(i):
    chip = i // 2
    other = chip + 1 if chip % 2 else chip - 1
    return 2 * (other % (lax.axis_size("rows") // 2)) + i % 2


def sends_of(block):
    return [block] + [swapped(block, partner) for partner in (core_mate, even_mate, odd_mate)]


def on_device(
    right_sides, near_blocks, near_cols, near_counts, basis_in, target_basis, coupling, far_cols
):
    width = right_sides.shape[1]
    clusters, slots = near_cols.shape
    rank = basis_in.shape[1]
    per_group = LANES // rank
    head = clusters // per_group * R
    size = lax.axis_size("rows")
    unknowns = float(width * size)
    rows = clusters * R

    def shape(*dims, dtype=f32):
        return jax.ShapeDtypeStruct(dims, dtype)

    def scratch(*dims, dtype=f32):
        return pltpu.VMEM(dims, dtype)

    def in_hbm(array):
        return pltpu.with_memory_space_constraint(array, pltpu.HBM)

    def call(kernel, name, out, ins, *args, scratch_shapes=()):
        return pl.pallas_call(
            kernel, out_shape=out, in_specs=ins, out_specs=jax.tree.map(lambda _: VMEM, out),
            scratch_shapes=scratch_shapes, compiler_params=PARAMS, name=name,
        )(*args)

    def gather(block):
        groups = [list(range(core, size, 2)) for core in range(2)]
        return lax.all_to_all(block, "rows", 0, 0, axis_index_groups=groups)

    field, basis, lowered, payload = call(
        functools.partial(start_kernel, per_group), "start",
        (
            shape(rows, LANES), shape(clusters * rank, LANES, dtype=bf16), shape(rows, LANES, dtype=bf16),
            shape(size // 2, head, LANES, dtype=bf16),
        ),
        [HBM] * 2, in_hbm(right_sides), in_hbm(basis_in.reshape(clusters * rank, LANES)),
        scratch_shapes=[scratch(R, width), pltpu.SemaphoreType.DMA((2,))],
    )
    got = gather(payload)
    held = sends_of(lowered)

    blocks = in_hbm(near_blocks.reshape(clusters * slots, LANES, LANES))
    early = blocks.shape[0] // 4
    places, high, low, target, ahead = call(
        functools.partial(prepare_kernel, "rows", size), "prepare",
        (
            shape(2 * slots, clusters, dtype=jnp.int32),
            shape(slots * rank, rank * clusters, dtype=bf16),
            shape(slots * rank, rank * clusters, dtype=bf16),
            shape(rank * clusters, LANES, dtype=bf16),
            pltpu.VMEM((early, LANES, LANES), bf16),
        ),
        [HBM] * 6 + [ANY], in_hbm(near_cols.T), in_hbm(near_counts.reshape(1, clusters)), in_hbm(far_cols.T),
        in_hbm(jnp.transpose(coupling, (1, 2, 3, 0))), in_hbm(target_basis.reshape(clusters * rank, LANES)),
        blocks, held[1],
        scratch_shapes=[
            scratch(slots, clusters, dtype=jnp.int32), scratch(1, clusters, dtype=jnp.int32),
            scratch(slots, clusters, dtype=jnp.int32),
            scratch(slots, rank, rank, clusters), scratch(clusters * rank, LANES, dtype=bf16),
            pltpu.SemaphoreType.DMA((6,)),
        ],
    )

    def fetch(name, first, count, chunks, *behind):
        here, token = call(
            functools.partial(fetch_kernel, first), name, (pltpu.VMEM((count, LANES, LANES), bf16), shape(R, LANES)),
            [HBM] + [ANY] * len(behind), blocks, *behind, scratch_shapes=[pltpu.SemaphoreType.DMA((chunks,))],
        )
        return pltpu.with_memory_space_constraint(here, pltpu.VMEM), token

    def arrived(got, held, ahead, behind):
        rest, token = fetch("fetch", early, blocks.shape[0] - early, 8, got, behind)
        sent = call(
            functools.partial(relay_kernel, "rows"), "relay",
            shape(got.shape[0] * got.shape[1] + rows, LANES, dtype=bf16), [VMEM] * 3 + [ANY], got, *held[2:], token
        )
        return *held, places, ahead, rest, sent, swapped(sent, core_mate), high, low, target

    ahead = pltpu.with_memory_space_constraint(ahead, pltpu.VMEM)
    kept = [scratch(rows, LANES), scratch(rows, LANES), scratch(5 * rows + R, LANES), scratch(size * head, LANES)]
    operands = [VMEM] * 4 + [SMEM] + [VMEM] * 9
    image, lowered, payload = call(
        functools.partial(first_kernel, per_group), "operator_one",
        (
            shape(rows, LANES), shape(rows, LANES, dtype=bf16),
            shape(size // 2, head + TAIL, LANES, dtype=bf16),
        ),
        operands, *arrived(got, held, ahead, target), field, basis, scratch_shapes=kept,
    )
    got = gather(payload)
    ahead, token = fetch("ahead", 0, early, 2, payload)
    here = arrived(got, sends_of(lowered), ahead, token)
    candidate, sums = call(
        functools.partial(second_kernel, per_group, unknowns), "operator_two",
        (shape(rows, LANES), shape(size, R, LANES, dtype=bf16)),
        operands, *here, field, image, scratch_shapes=kept,
    )
    return call(
        functools.partial(finish_kernel, per_group, unknowns), "finish", (shape(R, width), shape(R, width)),
        [VMEM] * 6, field, image, candidate, *here[7:9], lax.all_to_all(sums, "rows", 0, 0),
    )


def solution(mesh):
    return jax.shard_map(
        on_device,
        mesh=mesh,
        in_specs=(
            P("groups", "rows"),
            P("rows", None, None, None),
            P("rows", None),
            P("rows"),
            P("rows", None, None),
            P("rows", None, None),
            P("rows", None, None, None),
            P("rows", None),
        ),
        out_specs=(P("groups", "rows"), P("groups", "rows")),
        check_vma=False,
    )
```

```python
import functools

import jax
import jax.numpy as jnp
from jax import lax
from jax.experimental import pallas as pl
from jax.experimental.pallas import tpu as pltpu
from jax.sharding import PartitionSpec as P

epsilon = 1e-06
f32, bf16 = jnp.float32, jnp.bfloat16
VMEM = pl.BlockSpec(memory_space=pltpu.VMEM)
SMEM = pl.BlockSpec(memory_space=pltpu.SMEM)
HBM = pl.BlockSpec(memory_space=pltpu.HBM)
ANY = pl.BlockSpec(memory_space=pl.ANY)
R = 8
LANES = 128
SUM_SLOTS = 8
TAIL = 16
PARAMS = pltpu.CompilerParams(vmem_limit_bytes=24 * 1024 * 1024)


def lane_ids(rows=R):
    return lax.broadcasted_iota(jnp.int32, (rows, LANES), 1)


def rows_of(ref, j):
    return ref[pl.ds(j * R, R), :]


def dot(a, b, contract=(1, 0)):
    return lax.dot_general(a, b, (((contract[0],), (contract[1],)), ((), ())), preferred_element_type=f32)


def sums_tile(sums):
    lane = lane_ids()
    tile = jnp.zeros((R, LANES), f32)
    for t, partial in enumerate(sums):
        total = jnp.sum(partial, axis=1, keepdims=True)
        high = total.astype(bf16).astype(f32)
        middle = (total - high).astype(bf16).astype(f32)
        low = total - high - middle
        for part, value in enumerate((high, middle, low)):
            tile = jnp.where(lane == part * SUM_SLOTS + t, value, tile)
    return tile


def read_sums(parts, count, unknowns):
    total = jnp.zeros((R, LANES), f32)
    for part in parts:
        total = total + part.astype(f32)[:R]
    return [
        sum(total[:, p * SUM_SLOTS + t : p * SUM_SLOTS + t + 1] for p in range(3)) * (1.0 / unknowns)
        for t in range(count)
    ]


def tails(swaps, rows, head):
    each = head + TAIL
    return [
        values[pl.ds(device * each + head, TAIL), :]
        for values in swaps
        for device in range((values.shape[0] - rows) // each)
    ]


def compress(tiles, basis, group):
    stacked = jnp.concatenate(tiles, axis=0)
    high = stacked.astype(bf16)
    low = (stacked - high.astype(f32)).astype(bf16)
    both = dot(jnp.concatenate([high, low], axis=0), basis[pl.ds(group * LANES, LANES), :], (1, 1))
    rows = len(tiles) * R
    both = both[:rows] + both[rows:]
    lane = lane_ids()
    rank = LANES // len(tiles)
    tile = jnp.zeros((R, LANES), f32)
    for m in range(len(tiles)):
        tile = jnp.where(lane // rank == m, both[m * R : (m + 1) * R], tile)
    return tile


def write_payload(payload, parts, sums):
    if sums:
        parts = parts + [sums_tile(sums), jnp.zeros((TAIL - R, LANES), f32)]
    block = jnp.concatenate(parts, axis=0).astype(bf16)
    for device in range(payload.shape[0]):
        payload[device] = block


def start_kernel(per_group, b_hbm, basis_hbm, field, basis, lowered, payload, b, sems):
    groups = basis.shape[0] // LANES
    span = per_group * LANES
    copies = [
        pltpu.make_async_copy(
            b_hbm.at[:, pl.ds(g * span, span)], b.at[:, pl.ds(g * span, span)], sems.at[g]
        )
        for g in range(groups)
    ]
    whole_basis = pltpu.make_async_copy(basis_hbm, basis, sems.at[groups])
    for copy in copies:
        copy.start()
    whole_basis.start()
    parts = []
    for g, copy in enumerate(copies):
        copy.wait()
        tiles = [b[:, j * LANES : (j + 1) * LANES] for j in range(g * per_group, (g + 1) * per_group)]
        rows = pl.ds(g * per_group * R, per_group * R)
        field[rows, :] = jnp.concatenate(tiles, axis=0)
        lowered[rows, :] = jnp.concatenate(tiles, axis=0).astype(bf16)
        if g == 0:
            whole_basis.wait()
        parts.append(compress(tiles, basis, g))
    write_payload(payload, parts, [])


def window_place(distance, clusters, me):
    core, chip = me % 2, me // 2
    before, after = 3 - chip % 2, 2 + chip % 2
    slot = [before, jnp.where(core == 0, 4, 1), 0, jnp.where(core == 0, 1, 4), after]
    slab = lax.div(distance, clusters)
    chosen = jnp.zeros_like(distance)
    for s, value in enumerate(slot):
        chosen = jnp.where(slab == s, value, chosen)
    return chosen * clusters + lax.rem(distance, clusters)


def prepare_kernel(
    axis, size, middle, near_cols_hbm, near_counts_hbm, far_cols_hbm, coupling_hbm, target_hbm, blocks_hbm, _,
    places, high_out, low_out, target_out, ahead, near_cols, near_counts, far_cols, coupling, target, sems,
):
    pairs = (
        (near_cols_hbm, near_cols), (near_counts_hbm, near_counts), (far_cols_hbm, far_cols),
        (coupling_hbm, coupling), (target_hbm, target), (blocks_hbm.at[pl.ds(0, ahead.shape[0])], ahead),
    )
    copies = [pltpu.make_async_copy(source, to, sems.at[n]) for n, (source, to) in enumerate(pairs)]
    for copy in copies:
        copy.start()
    for copy in copies[:3]:
        copy.wait()
    slots, clusters = near_cols.shape
    me = lax.axis_index(axis)
    every = clusters * size
    distance = near_cols[...] - me * clusters + 2 * clusters
    distance = jnp.where(distance < 0, distance + every, distance)
    distance = jnp.where(distance >= every, distance - every, distance)
    live = lax.broadcasted_iota(jnp.int32, (slots, clusters), 0) < near_counts[...]
    places[:slots, :] = jnp.where(live, window_place(distance, clusters, me), 5 * clusters)
    owner = lax.div(far_cols[...], clusters)
    other_core = (owner ^ me) & 1
    chips = size // 2
    chip = lax.rem(owner // 2 + (chips - middle), chips)
    places[slots:, :] = (other_core * chips + chip) * clusters + lax.rem(far_cols[...], clusters)
    for copy in copies[3:5]:
        copy.wait()
    slots, rank, _, clusters = coupling.shape
    per_tile = LANES // clusters
    for s in range(rank // per_tile):
        pieces = [
            coupling[:, s * per_tile + p].reshape(slots * rank, clusters) for p in range(per_tile)
        ]
        tile = jnp.concatenate(pieces, axis=1)
        high = tile.astype(bf16)
        high_out[:, s * LANES : (s + 1) * LANES] = high
        low_out[:, s * LANES : (s + 1) * LANES] = (tile - high.astype(f32)).astype(bf16)
    size = rank * clusters
    row = lax.broadcasted_iota(jnp.int32, (size, size), 0)
    column = lax.broadcasted_iota(jnp.int32, (size, size), 1)
    wanted = (row % clusters) * rank + row // clusters
    target_out[...] = dot((column == wanted).astype(bf16), target[...]).astype(bf16)
    copies[5].wait()


def fetch_kernel(first, blocks_hbm, *refs):
    *_, blocks, token, sems = refs
    chunks = sems.shape[0]
    each = blocks.shape[0] // chunks
    copies = [
        pltpu.make_async_copy(
            blocks_hbm.at[pl.ds(first + c * each, each)], blocks.at[pl.ds(c * each, each)], sems.at[c]
        )
        for c in range(chunks)
    ]
    for c, copy in enumerate(copies):
        copy.start(priority=c % 2)
    token[...] = jnp.zeros_like(token)
    for copy in copies:
        copy.wait()


def relay_kernel(axis, got, even, odd, _, out):
    me = lax.axis_index(axis)
    devices, each, _ = got.shape
    for device in range(devices):
        out[pl.ds(device * each, each), :] = got[device]
    wants_even = (me // 2 + me) % 2 == 0
    span = pl.ds(devices * each, even.shape[0])

    @pl.when(wants_even)
    def _():
        out[span, :] = even[...]

    @pl.when(jnp.logical_not(wants_even))
    def _():
        out[span, :] = odd[...]


def apply(per_group, each, slabs, places, ahead, blocks, swaps, high, low, target, near, far, window, table, finish):
    clusters = near.shape[0] // R
    slots = (ahead.shape[0] + blocks.shape[0]) // clusters
    rank = LANES // per_group
    head = clusters // per_group * R
    rows = slabs[0].shape[0]
    devices = (swaps[0].shape[0] - rows) // each
    for at, slab in enumerate(slabs):
        window[pl.ds(at * rows, rows), :] = slab[...].astype(f32)
    window[pl.ds(len(slabs) * rows, rows), :] = swaps[1][pl.ds(devices * each, rows), :].astype(f32)
    window[pl.ds((len(slabs) + 1) * rows, R), :] = jnp.zeros((R, LANES), f32)
    for part, values in enumerate(swaps):
        for device in range(devices):
            at = (part * devices + device) * head
            table[pl.ds(at, head), :] = values[pl.ds(device * each, head), :].astype(f32)
    lane = lane_ids()

    def fetch(k, i):
        return window[pl.ds(pl.multiple_of(places[k, i] * R, R), R), :]

    def block(k, i):
        at = i * slots + k
        return ahead[at] if at < ahead.shape[0] else blocks[at - ahead.shape[0]]

    def pick(i):
        tile = jnp.zeros((R, LANES), f32)
        for k in range(slots):
            j = places[slots + k, i]
            found = table[pl.ds(pl.multiple_of(lax.div(j, per_group) * R, R), R), :]
            shift = ((k - j) * rank) & (LANES - 1)
            tile = jnp.where(lane // rank == k, pltpu.roll(found, shift, 1), tile)
        return tile

    picked = []
    for i in range(0, clusters, 2):
        both = jnp.zeros((2 * R, 2 * LANES), f32)
        for k in range(0, slots, 2):
            sources = jnp.concatenate(
                [jnp.concatenate([fetch(k + n, i), fetch(k + n, i + 1)], axis=0) for n in range(2)], axis=1
            )
            weights = jnp.concatenate(
                [jnp.concatenate([block(k + n, i), block(k + n, i + 1)], axis=0) for n in range(2)], axis=1
            )
            both = both + dot(sources.astype(bf16), weights, (1, 1))
        near[pl.ds(i * R, R), :] = both[:R, :LANES]
        near[pl.ds((i + 1) * R, R), :] = both[R:, LANES:]
        if 2 * i < clusters:
            picked += [pick(n) for n in range(2 * i, 2 * i + 4)]
        if 2 * i == clusters - 4:
            picked = jnp.concatenate(picked, axis=0).astype(bf16)
            crossed = dot(picked, high[...]) + dot(picked, low[...])
            expanded_high, expanded_low = [], []
            for s in range(rank * clusters // LANES):
                tile = jnp.zeros((R, LANES), f32)
                for n in range(clusters):
                    part = crossed[n * R : (n + 1) * R, s * LANES : (s + 1) * LANES]
                    tile = jnp.where(lane % clusters == n, part, tile)
                tile_high = tile.astype(bf16).astype(f32)
                tile_low = tile - tile_high
                for source, kept in ((tile_high, expanded_high), (tile_low, expanded_low)):
                    spread = [jnp.where(lane % clusters == n, source, 0.0) for n in range(clusters)]
                    kept.append(jnp.concatenate(spread, axis=0).astype(bf16))
            far[...] = dot(jnp.concatenate(expanded_high, axis=1), target[...]) + dot(
                jnp.concatenate(expanded_low, axis=1), target[...]
            )
        if 2 * i >= clusters:
            for n in range(2 * i - clusters, 2 * i - clusters + 4):
                finish(n)


def first_kernel(
    per_group, own, mate, even, odd, places, ahead, blocks, sent, received, high, low, target, b, basis,
    image, lowered, payload, near, far, window, table,
):
    clusters = near.shape[0] // R
    slabs, swaps = (own, mate, even, odd), (sent, received)
    each = clusters // per_group * R
    tiles, parts = [], []
    sums = [jnp.zeros((R, LANES), f32) for _ in range(3)]

    def finish(i):
        field = rows_of(b, i)
        made = 0.5 * field + (rows_of(near, i) + rows_of(far, i))
        sums[:] = [s + f * g for s, f, g in zip(sums, (field, field, made), (field, made, made))]
        tiles.append(made)
        if i % 2:
            both = jnp.concatenate(tiles[i - 1 :], axis=0)
            image[pl.ds((i - 1) * R, 2 * R), :] = both
            lowered[pl.ds((i - 1) * R, 2 * R), :] = both.astype(bf16)
        if i % per_group == per_group - 1:
            parts.append(compress(tiles[-per_group:], basis, i // per_group))

    apply(per_group, each, slabs, places, ahead, blocks, swaps, high, low, target, near, far, window, table, finish)
    write_payload(payload, parts, sums)


def arnoldi_one(bb, bw, ww):
    whole = bb + epsilon
    start_norm = jnp.sqrt(whole)
    scale = 1.0 / start_norm
    v11 = bb / whole
    h11 = (bw * scale) * scale
    uu = jnp.maximum((ww * scale) * scale - 2.0 * h11 * h11 + h11 * h11 * v11, 0.0)
    h21 = jnp.sqrt(uu + epsilon)
    return start_norm, h11, h21, v11, uu / (uu + epsilon), h11 * (1.0 - v11) / h21


def second_kernel(
    per_group, unknowns, own, mate, even, odd, places, ahead, blocks, sent, received, high, low, target, b, image,
    candidate, sums_out, near, far, window, table,
):
    clusters = near.shape[0] // R
    head = clusters // per_group * R
    slabs, swaps = (own, mate, even, odd), (sent, received)
    means = read_sums(tails(swaps, own.shape[0], head), 3, unknowns)
    start_norm, h11, h21, _, _, _ = arnoldi_one(*means)
    scale = 1.0 / start_norm
    inverse = 1.0 / h21
    sums = [jnp.zeros((R, LANES), f32) for _ in range(3)]

    def finish(j):
        held = rows_of(image, j) * scale
        first = rows_of(b, j) * scale
        second = (held - h11 * first) * inverse
        made = (0.5 * held + (rows_of(near, j) + rows_of(far, j)) * scale - h11 * held) * inverse
        sums[:] = [s + v * made for s, v in zip(sums, (first, second, made))]
        candidate[pl.ds(j * R, R), :] = made

    each = head + TAIL
    apply(per_group, each, slabs, places, ahead, blocks, swaps, high, low, target, near, far, window, table, finish)
    tile = sums_tile(sums).astype(bf16)
    for device in range(sums_out.shape[0]):
        sums_out[device] = tile


def finish_kernel(
    per_group, unknowns, b, image, candidate, sent, received, got, solution_hbm, next_hbm,
    solution_here, next_here, sems,
):
    clusters = b.shape[0] // R
    sums = read_sums(tails((sent, received), b.shape[0], clusters // per_group * R), 3, unknowns)
    start_norm, h11, h21, v11, v22, v12 = arnoldi_one(*sums)
    h12, h22, ww = read_sums([got[device] for device in range(got.shape[0])], 3, unknowns)
    uu = ww - 2.0 * (h12 * h12 + h22 * h22) + h12 * h12 * v11 + h22 * h22 * v22 + 2.0 * h12 * h22 * v12
    h32 = jnp.sqrt(jnp.maximum(uu, 0.0) + epsilon)
    g11 = h11 * h11 + h21 * h21
    g12 = h11 * h12 + h21 * h22
    g22 = h12 * h12 + h22 * h22 + h32 * h32
    t1, t2 = start_norm * h11, start_norm * h12
    det = g11 * g22 - g12 * g12
    y1 = (g22 * t1 - g12 * t2) / det
    y2 = (g11 * t2 - g12 * t1) / det
    scale, inverse, last = 1.0 / start_norm, 1.0 / h21, 1.0 / h32
    chunks = sems.shape[1]
    each = clusters // chunks
    copies = []
    for c in range(chunks):
        for j in range(c * each, (c + 1) * each):
            span = slice(j * LANES, (j + 1) * LANES)
            first = rows_of(b, j) * scale
            second = (rows_of(image, j) * scale - h11 * first) * inverse
            solution_here[:, span] = y1 * first + y2 * second
            next_here[:, span] = (rows_of(candidate, j) - h12 * first - h22 * second) * last
        span = pl.ds(c * each * LANES, each * LANES)
        for n, (here, there) in enumerate(((solution_here, solution_hbm), (next_here, next_hbm))):
            copies.append(pltpu.make_async_copy(here.at[:, span], there.at[:, span], sems.at[n, c]))
            copies[-1].start()
    for copy in copies:
        copy.wait()


def swapped(block, partner):
    return lax.ppermute(block, "rows", [(i, partner(i)) for i in range(lax.axis_size("rows"))])


def core_mate(i):
    return i ^ 1


def even_mate(i):
    return i ^ 2


def odd_mate(i):
    chip = i // 2
    other = chip + 1 if chip % 2 else chip - 1
    return 2 * (other % (lax.axis_size("rows") // 2)) + i % 2


def sends_of(block):
    return [block] + [swapped(block, partner) for partner in (core_mate, even_mate, odd_mate)]


def on_device(
    right_sides, near_blocks, near_cols, near_counts, basis_in, target_basis, coupling, far_cols
):
    width = right_sides.shape[1]
    clusters, slots = near_cols.shape
    rank = basis_in.shape[1]
    per_group = LANES // rank
    head = clusters // per_group * R
    size = lax.axis_size("rows")
    unknowns = float(width * size)
    rows = clusters * R

    def shape(*dims, dtype=f32):
        return jax.ShapeDtypeStruct(dims, dtype)

    def scratch(*dims, dtype=f32):
        return pltpu.VMEM(dims, dtype)

    def in_hbm(array):
        return pltpu.with_memory_space_constraint(array, pltpu.HBM)

    def call(kernel, name, out, ins, *args, scratch_shapes=()):
        return pl.pallas_call(
            kernel, out_shape=out, in_specs=ins, out_specs=jax.tree.map(lambda _: VMEM, out),
            scratch_shapes=scratch_shapes, compiler_params=PARAMS, name=name,
        )(*args)

    chips = size // 2
    middle = chips // 4
    order = [(middle + n) % chips for n in range(chips)]

    def gather(block):
        groups = [[2 * chip + core for chip in order] for core in range(2)]
        return lax.all_to_all(block, "rows", 0, 0, axis_index_groups=groups)

    def exchange(block):
        group = [2 * chip + core for chip in order for core in range(2)]
        return lax.all_to_all(block, "rows", 0, 0, axis_index_groups=[group])

    field, basis, lowered, payload = call(
        functools.partial(start_kernel, per_group), "start",
        (
            shape(rows, LANES), shape(clusters * rank, LANES, dtype=bf16), shape(rows, LANES, dtype=bf16),
            shape(size // 2, head, LANES, dtype=bf16),
        ),
        [HBM] * 2, in_hbm(right_sides), in_hbm(basis_in.reshape(clusters * rank, LANES)),
        scratch_shapes=[scratch(R, width), pltpu.SemaphoreType.DMA((clusters // per_group + 1,))],
    )
    got = gather(payload)
    held = sends_of(lowered)

    blocks = in_hbm(near_blocks.reshape(clusters * slots, LANES, LANES))
    early = blocks.shape[0] * 9 // 32
    places, high, low, target, ahead = call(
        functools.partial(prepare_kernel, "rows", size, middle), "prepare",
        (
            shape(2 * slots, clusters, dtype=jnp.int32),
            shape(slots * rank, rank * clusters, dtype=bf16),
            shape(slots * rank, rank * clusters, dtype=bf16),
            shape(rank * clusters, LANES, dtype=bf16),
            pltpu.VMEM((early, LANES, LANES), bf16),
        ),
        [HBM] * 6 + [ANY], in_hbm(near_cols.T), in_hbm(near_counts.reshape(1, clusters)), in_hbm(far_cols.T),
        in_hbm(jnp.transpose(coupling, (1, 2, 3, 0))), in_hbm(target_basis.reshape(clusters * rank, LANES)),
        blocks, held[1],
        scratch_shapes=[
            scratch(slots, clusters, dtype=jnp.int32), scratch(1, clusters, dtype=jnp.int32),
            scratch(slots, clusters, dtype=jnp.int32),
            scratch(slots, rank, rank, clusters), scratch(clusters * rank, LANES, dtype=bf16),
            pltpu.SemaphoreType.DMA((6,)),
        ],
    )

    def fetch(name, first, count, chunks, *behind):
        here, token = call(
            functools.partial(fetch_kernel, first), name, (pltpu.VMEM((count, LANES, LANES), bf16), shape(R, LANES)),
            [HBM] + [ANY] * len(behind), blocks, *behind, scratch_shapes=[pltpu.SemaphoreType.DMA((chunks,))],
        )
        return pltpu.with_memory_space_constraint(here, pltpu.VMEM), token

    def arrived(got, held, ahead, behind):
        rest, token = fetch("fetch", early, blocks.shape[0] - early, 8, got, behind)
        sent = call(
            functools.partial(relay_kernel, "rows"), "relay",
            shape(got.shape[0] * got.shape[1] + rows, LANES, dtype=bf16), [VMEM] * 3 + [ANY], got, *held[2:], token
        )
        return *held, places, ahead, rest, sent, swapped(sent, core_mate), high, low, target

    ahead = pltpu.with_memory_space_constraint(ahead, pltpu.VMEM)
    kept = [scratch(rows, LANES), scratch(rows, LANES), scratch(5 * rows + R, LANES), scratch(size * head, LANES)]
    operands = [VMEM] * 4 + [SMEM] + [VMEM] * 9
    image, lowered, payload = call(
        functools.partial(first_kernel, per_group), "operator_one",
        (
            shape(rows, LANES), shape(rows, LANES, dtype=bf16),
            shape(size // 2, head + TAIL, LANES, dtype=bf16),
        ),
        operands, *arrived(got, held, ahead, target), field, basis, scratch_shapes=kept,
    )
    got = gather(payload)
    held = sends_of(lowered)
    ahead, token = fetch("ahead", 0, early, 2, held[1])
    here = arrived(got, held, ahead, token)
    candidate, sums = call(
        functools.partial(second_kernel, per_group, unknowns), "operator_two",
        (shape(rows, LANES), shape(size, R, LANES, dtype=bf16)),
        operands, *here, field, image, scratch_shapes=kept,
    )
    return pl.pallas_call(
        functools.partial(finish_kernel, per_group, unknowns), out_shape=(shape(R, width), shape(R, width)),
        in_specs=[VMEM] * 6, out_specs=[HBM] * 2,
        scratch_shapes=[scratch(R, width), scratch(R, width), pltpu.SemaphoreType.DMA((2, 4))],
        compiler_params=PARAMS, name="finish",
    )(field, image, candidate, *here[7:9], exchange(sums))


def solution(mesh):
    return jax.shard_map(
        on_device,
        mesh=mesh,
        in_specs=(
            P("groups", "rows"),
            P("rows", None, None, None),
            P("rows", None),
            P("rows"),
            P("rows", None, None),
            P("rows", None, None),
            P("rows", None, None, None),
            P("rows", None),
        ),
        out_specs=(P("groups", "rows"), P("groups", "rows")),
        check_vma=False,
    )
```

```python
import functools

import jax
import jax.numpy as jnp
from jax import lax
from jax.experimental import pallas as pl
from jax.experimental.pallas import tpu as pltpu
from jax.sharding import PartitionSpec as P

epsilon = 1e-06
f32, bf16 = jnp.float32, jnp.bfloat16
VMEM = pl.BlockSpec(memory_space=pltpu.VMEM)
SMEM = pl.BlockSpec(memory_space=pltpu.SMEM)
HBM = pl.BlockSpec(memory_space=pltpu.HBM)
ANY = pl.BlockSpec(memory_space=pl.ANY)
R = 8
LANES = 128
SUM_SLOTS = 8
TAIL = 16
PARAMS = pltpu.CompilerParams(vmem_limit_bytes=24 * 1024 * 1024)


def lane_ids(rows=R):
    return lax.broadcasted_iota(jnp.int32, (rows, LANES), 1)


def rows_of(ref, j):
    return ref[pl.ds(j * R, R), :]


def dot(a, b, contract=(1, 0)):
    return lax.dot_general(a, b, (((contract[0],), (contract[1],)), ((), ())), preferred_element_type=f32)


def sums_tile(sums):
    lane = lane_ids()
    tile = jnp.zeros((R, LANES), f32)
    for t, partial in enumerate(sums):
        total = jnp.sum(partial, axis=1, keepdims=True)
        high = total.astype(bf16).astype(f32)
        middle = (total - high).astype(bf16).astype(f32)
        low = total - high - middle
        for part, value in enumerate((high, middle, low)):
            tile = jnp.where(lane == part * SUM_SLOTS + t, value, tile)
    return tile


def read_sums(parts, count, unknowns):
    total = jnp.zeros((R, LANES), f32)
    for part in parts:
        total = total + part.astype(f32)[:R]
    return [
        sum(total[:, p * SUM_SLOTS + t : p * SUM_SLOTS + t + 1] for p in range(3)) * (1.0 / unknowns)
        for t in range(count)
    ]


def tails(swaps, rows, head):
    each = head + TAIL
    return [
        values[pl.ds(device * each + head, TAIL), :]
        for values in swaps
        for device in range((values.shape[0] - rows) // each)
    ]


def compress(tiles, basis, group):
    stacked = jnp.concatenate(tiles, axis=0)
    high = stacked.astype(bf16)
    low = (stacked - high.astype(f32)).astype(bf16)
    both = dot(jnp.concatenate([high, low], axis=0), basis[pl.ds(group * LANES, LANES), :], (1, 1))
    rows = len(tiles) * R
    both = both[:rows] + both[rows:]
    lane = lane_ids()
    rank = LANES // len(tiles)
    tile = jnp.zeros((R, LANES), f32)
    for m in range(len(tiles)):
        tile = jnp.where(lane // rank == m, both[m * R : (m + 1) * R], tile)
    return tile


def write_payload(payload, parts, sums):
    if sums:
        parts = parts + [sums_tile(sums), jnp.zeros((TAIL - R, LANES), f32)]
    block = jnp.concatenate(parts, axis=0).astype(bf16)
    for device in range(payload.shape[0]):
        payload[device] = block


def start_kernel(per_group, b_hbm, basis_hbm, field, basis, lowered, payload, b, sems):
    copies = [
        pltpu.make_async_copy(b_hbm, b, sems.at[0]),
        pltpu.make_async_copy(basis_hbm, basis, sems.at[1]),
    ]
    for copy in copies:
        copy.start()
    for copy in copies:
        copy.wait()
    clusters = b.shape[1] // LANES
    tiles = [b[:, j * LANES : (j + 1) * LANES] for j in range(clusters)]
    field[...] = jnp.concatenate(tiles, axis=0)
    lowered[...] = jnp.concatenate(tiles, axis=0).astype(bf16)
    groups = [tiles[g : g + per_group] for g in range(0, clusters, per_group)]
    write_payload(payload, [compress(group, basis, g) for g, group in enumerate(groups)], [])


def window_place(distance, clusters, me):
    core, chip = me % 2, me // 2
    before, after = 3 - chip % 2, 2 + chip % 2
    slot = [before, jnp.where(core == 0, 4, 1), 0, jnp.where(core == 0, 1, 4), after]
    slab = lax.div(distance, clusters)
    chosen = jnp.zeros_like(distance)
    for s, value in enumerate(slot):
        chosen = jnp.where(slab == s, value, chosen)
    return chosen * clusters + lax.rem(distance, clusters)


def prepare_kernel(
    axis, size, middle, near_cols_hbm, near_counts_hbm, far_cols_hbm, coupling_hbm, target_hbm, blocks_hbm, _,
    places, high_out, low_out, target_out, ahead, near_cols, near_counts, far_cols, coupling, target, sems,
):
    pairs = (
        (near_cols_hbm, near_cols), (near_counts_hbm, near_counts), (far_cols_hbm, far_cols),
        (coupling_hbm, coupling), (target_hbm, target), (blocks_hbm.at[pl.ds(0, ahead.shape[0])], ahead),
    )
    copies = [pltpu.make_async_copy(source, to, sems.at[n]) for n, (source, to) in enumerate(pairs)]
    for copy in copies:
        copy.start()
    for copy in copies[:3]:
        copy.wait()
    slots, clusters = near_cols.shape
    me = lax.axis_index(axis)
    every = clusters * size
    distance = near_cols[...] - me * clusters + 2 * clusters
    distance = jnp.where(distance < 0, distance + every, distance)
    distance = jnp.where(distance >= every, distance - every, distance)
    live = lax.broadcasted_iota(jnp.int32, (slots, clusters), 0) < near_counts[...]
    places[:slots, :] = jnp.where(live, window_place(distance, clusters, me), 5 * clusters)
    owner = lax.div(far_cols[...], clusters)
    other_core = (owner ^ me) & 1
    chips = size // 2
    chip = lax.rem(owner // 2 + (chips - middle), chips)
    places[slots:, :] = (other_core * chips + chip) * clusters + lax.rem(far_cols[...], clusters)
    for copy in copies[3:5]:
        copy.wait()
    slots, rank, _, clusters = coupling.shape
    per_tile = LANES // clusters
    for s in range(rank // per_tile):
        pieces = [
            coupling[:, s * per_tile + p].reshape(slots * rank, clusters) for p in range(per_tile)
        ]
        tile = jnp.concatenate(pieces, axis=1)
        high = tile.astype(bf16)
        high_out[:, s * LANES : (s + 1) * LANES] = high
        low_out[:, s * LANES : (s + 1) * LANES] = (tile - high.astype(f32)).astype(bf16)
    size = rank * clusters
    row = lax.broadcasted_iota(jnp.int32, (size, size), 0)
    column = lax.broadcasted_iota(jnp.int32, (size, size), 1)
    wanted = (row % clusters) * rank + row // clusters
    target_out[...] = dot((column == wanted).astype(bf16), target[...]).astype(bf16)
    copies[5].wait()


def fetch_kernel(first, blocks_hbm, _, __, blocks, token, sems):
    chunks = sems.shape[0]
    each = blocks.shape[0] // chunks
    copies = [
        pltpu.make_async_copy(
            blocks_hbm.at[pl.ds(first + c * each, each)], blocks.at[pl.ds(c * each, each)], sems.at[c]
        )
        for c in range(chunks)
    ]
    for copy in copies:
        copy.start()
    token[...] = jnp.zeros_like(token)
    for copy in copies:
        copy.wait()


def relay_kernel(axis, got, even, odd, _, out):
    me = lax.axis_index(axis)
    devices, each, _ = got.shape
    for device in range(devices):
        out[pl.ds(device * each, each), :] = got[device]
    wants_even = (me // 2 + me) % 2 == 0
    span = pl.ds(devices * each, even.shape[0])

    @pl.when(wants_even)
    def _():
        out[span, :] = even[...]

    @pl.when(jnp.logical_not(wants_even))
    def _():
        out[span, :] = odd[...]


def apply(per_group, each, slabs, places, ahead, blocks, swaps, high, low, target, near, far, window, table, finish):
    clusters = near.shape[0] // R
    slots = (ahead.shape[0] + blocks.shape[0]) // clusters
    rank = LANES // per_group
    head = clusters // per_group * R
    rows = slabs[0].shape[0]
    devices = (swaps[0].shape[0] - rows) // each
    for at, slab in enumerate(slabs):
        window[pl.ds(at * rows, rows), :] = slab[...].astype(f32)
    window[pl.ds(len(slabs) * rows, rows), :] = swaps[1][pl.ds(devices * each, rows), :].astype(f32)
    window[pl.ds((len(slabs) + 1) * rows, R), :] = jnp.zeros((R, LANES), f32)
    for part, values in enumerate(swaps):
        for device in range(devices):
            at = (part * devices + device) * head
            table[pl.ds(at, head), :] = values[pl.ds(device * each, head), :].astype(f32)
    lane = lane_ids()

    def fetch(k, i):
        return window[pl.ds(pl.multiple_of(places[k, i] * R, R), R), :]

    def block(k, i):
        at = i * slots + k
        return ahead[at] if at < ahead.shape[0] else blocks[at - ahead.shape[0]]

    def pick(i):
        tile = jnp.zeros((R, LANES), f32)
        for k in range(slots):
            j = places[slots + k, i]
            found = table[pl.ds(pl.multiple_of(lax.div(j, per_group) * R, R), R), :]
            shift = ((k - j) * rank) & (LANES - 1)
            tile = jnp.where(lane // rank == k, pltpu.roll(found, shift, 1), tile)
        return tile

    picked = []
    for i in range(0, clusters, 2):
        sources = jnp.concatenate(
            [jnp.concatenate([fetch(k, i), fetch(k, i + 1)], axis=0) for k in range(slots)], axis=1
        )
        weights = jnp.concatenate(
            [jnp.concatenate([block(k, i), block(k, i + 1)], axis=0) for k in range(slots)], axis=1
        )
        both = dot(sources.astype(bf16), weights, (1, 1))
        near[pl.ds(i * R, R), :] = both[:R, :LANES]
        near[pl.ds((i + 1) * R, R), :] = both[R:, LANES:]
        if 2 * i < clusters:
            picked += [pick(n) for n in range(2 * i, 2 * i + 4)]
        if 2 * i == clusters - 4:
            picked = jnp.concatenate(picked, axis=0).astype(bf16)
            crossed = dot(picked, high[...]) + dot(picked, low[...])
            expanded_high, expanded_low = [], []
            for s in range(rank * clusters // LANES):
                tile = jnp.zeros((R, LANES), f32)
                for n in range(clusters):
                    part = crossed[n * R : (n + 1) * R, s * LANES : (s + 1) * LANES]
                    tile = jnp.where(lane % clusters == n, part, tile)
                tile_high = tile.astype(bf16).astype(f32)
                tile_low = tile - tile_high
                for source, kept in ((tile_high, expanded_high), (tile_low, expanded_low)):
                    spread = [jnp.where(lane % clusters == n, source, 0.0) for n in range(clusters)]
                    kept.append(jnp.concatenate(spread, axis=0).astype(bf16))
            far[...] = dot(jnp.concatenate(expanded_high, axis=1), target[...]) + dot(
                jnp.concatenate(expanded_low, axis=1), target[...]
            )
        if 2 * i >= clusters:
            for n in range(2 * i - clusters, 2 * i - clusters + 4):
                finish(n)


def first_kernel(
    per_group, own, mate, even, odd, places, ahead, blocks, sent, received, high, low, target, b, basis,
    image, lowered, payload, near, far, window, table,
):
    clusters = near.shape[0] // R
    slabs, swaps = (own, mate, even, odd), (sent, received)
    each = clusters // per_group * R
    tiles, parts = [], []
    sums = [jnp.zeros((R, LANES), f32) for _ in range(3)]

    def finish(i):
        field = rows_of(b, i)
        made = 0.5 * field + (rows_of(near, i) + rows_of(far, i))
        sums[:] = [s + f * g for s, f, g in zip(sums, (field, field, made), (field, made, made))]
        tiles.append(made)
        if i % 2:
            both = jnp.concatenate(tiles[i - 1 :], axis=0)
            image[pl.ds((i - 1) * R, 2 * R), :] = both
            lowered[pl.ds((i - 1) * R, 2 * R), :] = both.astype(bf16)
        if i % per_group == per_group - 1:
            parts.append(compress(tiles[-per_group:], basis, i // per_group))

    apply(per_group, each, slabs, places, ahead, blocks, swaps, high, low, target, near, far, window, table, finish)
    write_payload(payload, parts, sums)


def arnoldi_one(bb, bw, ww):
    whole = bb + epsilon
    start_norm = jnp.sqrt(whole)
    scale = 1.0 / start_norm
    v11 = bb / whole
    h11 = (bw * scale) * scale
    uu = jnp.maximum((ww * scale) * scale - 2.0 * h11 * h11 + h11 * h11 * v11, 0.0)
    h21 = jnp.sqrt(uu + epsilon)
    return start_norm, h11, h21, v11, uu / (uu + epsilon), h11 * (1.0 - v11) / h21


def second_kernel(
    per_group, unknowns, own, mate, even, odd, places, ahead, blocks, sent, received, high, low, target, b, image,
    candidate, sums_out, near, far, window, table,
):
    clusters = near.shape[0] // R
    head = clusters // per_group * R
    slabs, swaps = (own, mate, even, odd), (sent, received)
    means = read_sums(tails(swaps, own.shape[0], head), 3, unknowns)
    start_norm, h11, h21, _, _, _ = arnoldi_one(*means)
    scale = 1.0 / start_norm
    inverse = 1.0 / h21
    sums = [jnp.zeros((R, LANES), f32) for _ in range(3)]

    def finish(j):
        held = rows_of(image, j) * scale
        first = rows_of(b, j) * scale
        second = (held - h11 * first) * inverse
        made = (0.5 * held + (rows_of(near, j) + rows_of(far, j)) * scale - h11 * held) * inverse
        sums[:] = [s + v * made for s, v in zip(sums, (first, second, made))]
        candidate[pl.ds(j * R, R), :] = made

    each = head + TAIL
    apply(per_group, each, slabs, places, ahead, blocks, swaps, high, low, target, near, far, window, table, finish)
    tile = sums_tile(sums).astype(bf16)
    for device in range(sums_out.shape[0]):
        sums_out[device] = tile


def finish_kernel(per_group, unknowns, b, image, candidate, sent, received, got, solution_out, next_out):
    clusters = b.shape[0] // R
    sums = read_sums(tails((sent, received), b.shape[0], clusters // per_group * R), 3, unknowns)
    start_norm, h11, h21, v11, v22, v12 = arnoldi_one(*sums)
    h12, h22, ww = read_sums([got[device] for device in range(got.shape[0])], 3, unknowns)
    uu = ww - 2.0 * (h12 * h12 + h22 * h22) + h12 * h12 * v11 + h22 * h22 * v22 + 2.0 * h12 * h22 * v12
    h32 = jnp.sqrt(jnp.maximum(uu, 0.0) + epsilon)
    g11 = h11 * h11 + h21 * h21
    g12 = h11 * h12 + h21 * h22
    g22 = h12 * h12 + h22 * h22 + h32 * h32
    t1, t2 = start_norm * h11, start_norm * h12
    det = g11 * g22 - g12 * g12
    y1 = (g22 * t1 - g12 * t2) / det
    y2 = (g11 * t2 - g12 * t1) / det
    scale, inverse, last = 1.0 / start_norm, 1.0 / h21, 1.0 / h32
    for j in range(clusters):
        span = slice(j * LANES, (j + 1) * LANES)
        first = rows_of(b, j) * scale
        second = (rows_of(image, j) * scale - h11 * first) * inverse
        solution_out[:, span] = y1 * first + y2 * second
        next_out[:, span] = (rows_of(candidate, j) - h12 * first - h22 * second) * last


def swapped(block, partner):
    return lax.ppermute(block, "rows", [(i, partner(i)) for i in range(lax.axis_size("rows"))])


def core_mate(i):
    return i ^ 1


def even_mate(i):
    return i ^ 2


def odd_mate(i):
    chip = i // 2
    other = chip + 1 if chip % 2 else chip - 1
    return 2 * (other % (lax.axis_size("rows") // 2)) + i % 2


def sends_of(block):
    return [block] + [swapped(block, partner) for partner in (core_mate, even_mate, odd_mate)]


def on_device(
    right_sides, near_blocks, near_cols, near_counts, basis_in, target_basis, coupling, far_cols
):
    width = right_sides.shape[1]
    clusters, slots = near_cols.shape
    rank = basis_in.shape[1]
    per_group = LANES // rank
    head = clusters // per_group * R
    size = lax.axis_size("rows")
    unknowns = float(width * size)
    rows = clusters * R

    def shape(*dims, dtype=f32):
        return jax.ShapeDtypeStruct(dims, dtype)

    def scratch(*dims, dtype=f32):
        return pltpu.VMEM(dims, dtype)

    def in_hbm(array):
        return pltpu.with_memory_space_constraint(array, pltpu.HBM)

    def call(kernel, name, out, ins, *args, scratch_shapes=()):
        return pl.pallas_call(
            kernel, out_shape=out, in_specs=ins, out_specs=jax.tree.map(lambda _: VMEM, out),
            scratch_shapes=scratch_shapes, compiler_params=PARAMS, name=name,
        )(*args)

    chips = size // 2
    middle = chips // 4
    order = [(middle + n) % chips for n in range(chips)]

    def gather(block):
        groups = [[2 * chip + core for chip in order] for core in range(2)]
        return lax.all_to_all(block, "rows", 0, 0, axis_index_groups=groups)

    def exchange(block):
        group = [2 * chip + core for chip in order for core in range(2)]
        return lax.all_to_all(block, "rows", 0, 0, axis_index_groups=[group])

    field, basis, lowered, payload = call(
        functools.partial(start_kernel, per_group), "start",
        (
            shape(rows, LANES), shape(clusters * rank, LANES, dtype=bf16), shape(rows, LANES, dtype=bf16),
            shape(size // 2, head, LANES, dtype=bf16),
        ),
        [HBM] * 2, in_hbm(right_sides), in_hbm(basis_in.reshape(clusters * rank, LANES)),
        scratch_shapes=[scratch(R, width), pltpu.SemaphoreType.DMA((2,))],
    )
    got = gather(payload)
    held = sends_of(lowered)

    blocks = in_hbm(near_blocks.reshape(clusters * slots, LANES, LANES))
    early = blocks.shape[0] // 4
    places, high, low, target, ahead = call(
        functools.partial(prepare_kernel, "rows", size, middle), "prepare",
        (
            shape(2 * slots, clusters, dtype=jnp.int32),
            shape(slots * rank, rank * clusters, dtype=bf16),
            shape(slots * rank, rank * clusters, dtype=bf16),
            shape(rank * clusters, LANES, dtype=bf16),
            pltpu.VMEM((early, LANES, LANES), bf16),
        ),
        [HBM] * 6 + [ANY], in_hbm(near_cols.T), in_hbm(near_counts.reshape(1, clusters)), in_hbm(far_cols.T),
        in_hbm(jnp.transpose(coupling, (1, 2, 3, 0))), in_hbm(target_basis.reshape(clusters * rank, LANES)),
        blocks, held[1],
        scratch_shapes=[
            scratch(slots, clusters, dtype=jnp.int32), scratch(1, clusters, dtype=jnp.int32),
            scratch(slots, clusters, dtype=jnp.int32),
            scratch(slots, rank, rank, clusters), scratch(clusters * rank, LANES, dtype=bf16),
            pltpu.SemaphoreType.DMA((6,)),
        ],
    )

    def arrived(got, held, behind):
        rest, token = call(
            functools.partial(fetch_kernel, early), "fetch",
            (pltpu.VMEM((blocks.shape[0] - early, LANES, LANES), bf16), shape(R, LANES)),
            [HBM] + [ANY] * 2, blocks, got, behind, scratch_shapes=[pltpu.SemaphoreType.DMA((8,))],
        )
        rest = pltpu.with_memory_space_constraint(rest, pltpu.VMEM)
        sent = call(
            functools.partial(relay_kernel, "rows"), "relay",
            shape(got.shape[0] * got.shape[1] + rows, LANES, dtype=bf16), [VMEM] * 3 + [ANY], got, *held[2:], token
        )
        return *held, places, ahead, rest, sent, swapped(sent, core_mate), high, low, target

    ahead = pltpu.with_memory_space_constraint(ahead, pltpu.VMEM)
    kept = [scratch(rows, LANES), scratch(rows, LANES), scratch(5 * rows + R, LANES), scratch(size * head, LANES)]
    operands = [VMEM] * 4 + [SMEM] + [VMEM] * 9
    image, lowered, payload = call(
        functools.partial(first_kernel, per_group), "operator_one",
        (
            shape(rows, LANES), shape(rows, LANES, dtype=bf16),
            shape(size // 2, head + TAIL, LANES, dtype=bf16),
        ),
        operands, *arrived(got, held, target), field, basis, scratch_shapes=kept,
    )
    got = gather(payload)
    held = sends_of(lowered)
    here = arrived(got, held, held[1])
    candidate, sums = call(
        functools.partial(second_kernel, per_group, unknowns), "operator_two",
        (shape(rows, LANES), shape(size, R, LANES, dtype=bf16)),
        operands, *here, field, image, scratch_shapes=kept,
    )
    return call(
        functools.partial(finish_kernel, per_group, unknowns), "finish", (shape(R, width), shape(R, width)),
        [VMEM] * 6, field, image, candidate, *here[7:9], exchange(sums),
    )


def solution(mesh):
    return jax.shard_map(
        on_device,
        mesh=mesh,
        in_specs=(
            P("groups", "rows"),
            P("rows", None, None, None),
            P("rows", None),
            P("rows"),
            P("rows", None, None),
            P("rows", None, None),
            P("rows", None, None, None),
            P("rows", None),
        ),
        out_specs=(P("groups", "rows"), P("groups", "rows")),
        check_vma=False,
    )
```

```python
import functools

import jax
import jax.numpy as jnp
from jax import lax
from jax.experimental import pallas as pl
from jax.experimental.pallas import tpu as pltpu
from jax.sharding import PartitionSpec as P

epsilon = 1e-06
f32, bf16 = jnp.float32, jnp.bfloat16
VMEM = pl.BlockSpec(memory_space=pltpu.VMEM)
SMEM = pl.BlockSpec(memory_space=pltpu.SMEM)
HBM = pl.BlockSpec(memory_space=pltpu.HBM)
ANY = pl.BlockSpec(memory_space=pl.ANY)
R = 8
LANES = 128
SUM_SLOTS = 8
TAIL = 16
PARAMS = pltpu.CompilerParams(vmem_limit_bytes=24 * 1024 * 1024)


def lane_ids(rows=R):
    return lax.broadcasted_iota(jnp.int32, (rows, LANES), 1)


def rows_of(ref, j):
    return ref[pl.ds(j * R, R), :]


def dot(a, b, contract=(1, 0)):
    return lax.dot_general(a, b, (((contract[0],), (contract[1],)), ((), ())), preferred_element_type=f32)


def sums_tile(sums):
    lane = lane_ids()
    tile = jnp.zeros((R, LANES), f32)
    for t, partial in enumerate(sums):
        total = jnp.sum(partial, axis=1, keepdims=True)
        high = total.astype(bf16).astype(f32)
        middle = (total - high).astype(bf16).astype(f32)
        low = total - high - middle
        for part, value in enumerate((high, middle, low)):
            tile = jnp.where(lane == part * SUM_SLOTS + t, value, tile)
    return tile


def read_sums(parts, count, unknowns):
    total = jnp.zeros((R, LANES), f32)
    for part in parts:
        total = total + part.astype(f32)[:R]
    return [
        sum(total[:, p * SUM_SLOTS + t : p * SUM_SLOTS + t + 1] for p in range(3)) * (1.0 / unknowns)
        for t in range(count)
    ]


def tails(swaps, rows, head):
    each = head + TAIL
    return [
        values[pl.ds(device * each + head, TAIL), :]
        for values in swaps
        for device in range((values.shape[0] - rows) // each)
    ]


def compress(tiles, basis, group):
    stacked = jnp.concatenate(tiles, axis=0)
    high = stacked.astype(bf16)
    low = (stacked - high.astype(f32)).astype(bf16)
    both = dot(jnp.concatenate([high, low], axis=0), basis[pl.ds(group * LANES, LANES), :], (1, 1))
    rows = len(tiles) * R
    both = both[:rows] + both[rows:]
    lane = lane_ids()
    rank = LANES // len(tiles)
    tile = jnp.zeros((R, LANES), f32)
    for m in range(len(tiles)):
        tile = jnp.where(lane // rank == m, both[m * R : (m + 1) * R], tile)
    return tile


def write_payload(payload, parts, sums):
    if sums:
        parts = parts + [sums_tile(sums), jnp.zeros((TAIL - R, LANES), f32)]
    block = jnp.concatenate(parts, axis=0).astype(bf16)
    for device in range(payload.shape[0]):
        payload[device] = block


def start_kernel(per_group, b_hbm, basis_hbm, field, basis, lowered, payload, b, sems):
    copies = [
        pltpu.make_async_copy(b_hbm, b, sems.at[0]),
        pltpu.make_async_copy(basis_hbm, basis, sems.at[1]),
    ]
    for copy in copies:
        copy.start()
    for copy in copies:
        copy.wait()
    clusters = b.shape[1] // LANES
    tiles = [b[:, j * LANES : (j + 1) * LANES] for j in range(clusters)]
    field[...] = jnp.concatenate(tiles, axis=0)
    lowered[...] = jnp.concatenate(tiles, axis=0).astype(bf16)
    groups = [tiles[g : g + per_group] for g in range(0, clusters, per_group)]
    write_payload(payload, [compress(group, basis, g) for g, group in enumerate(groups)], [])


def window_place(distance, clusters, me):
    core, chip = me % 2, me // 2
    before, after = 3 - chip % 2, 2 + chip % 2
    slot = [before, jnp.where(core == 0, 4, 1), 0, jnp.where(core == 0, 1, 4), after]
    slab = lax.div(distance, clusters)
    chosen = jnp.zeros_like(distance)
    for s, value in enumerate(slot):
        chosen = jnp.where(slab == s, value, chosen)
    return chosen * clusters + lax.rem(distance, clusters)


def prepare_kernel(
    axis, size, middle, near_cols_hbm, near_counts_hbm, far_cols_hbm, coupling_hbm, target_hbm, _,
    places, high_out, low_out, target_out, near_cols, near_counts, far_cols, coupling, target, sems,
):
    pairs = (
        (near_cols_hbm, near_cols), (near_counts_hbm, near_counts), (far_cols_hbm, far_cols),
        (coupling_hbm, coupling), (target_hbm, target),
    )
    copies = [pltpu.make_async_copy(source, to, sems.at[n]) for n, (source, to) in enumerate(pairs)]
    for copy in copies:
        copy.start()
    for copy in copies[:3]:
        copy.wait()
    slots, clusters = near_cols.shape
    me = lax.axis_index(axis)
    every = clusters * size
    distance = near_cols[...] - me * clusters + 2 * clusters
    distance = jnp.where(distance < 0, distance + every, distance)
    distance = jnp.where(distance >= every, distance - every, distance)
    live = lax.broadcasted_iota(jnp.int32, (slots, clusters), 0) < near_counts[...]
    places[:slots, :] = jnp.where(live, window_place(distance, clusters, me), 5 * clusters) * R
    owner = lax.div(far_cols[...], clusters)
    other_core = (owner ^ me) & 1
    chips = size // 2
    chip = lax.rem(owner // 2 + (chips - middle), chips)
    rank = coupling.shape[1]
    per_group = LANES // rank
    inside = lax.rem(far_cols[...], clusters)
    tile = (other_core * chips + chip) * (clusters // per_group) + lax.div(inside, per_group)
    places[slots : 2 * slots, :] = tile * R
    slot = lax.broadcasted_iota(jnp.int32, (slots, clusters), 0)
    places[2 * slots :, :] = ((slot - inside) * rank) & (LANES - 1)
    for copy in copies[3:5]:
        copy.wait()
    slots, rank, _, clusters = coupling.shape
    per_tile = LANES // clusters
    for s in range(rank // per_tile):
        pieces = [
            coupling[:, s * per_tile + p].reshape(slots * rank, clusters) for p in range(per_tile)
        ]
        tile = jnp.concatenate(pieces, axis=1)
        high = tile.astype(bf16)
        high_out[:, s * LANES : (s + 1) * LANES] = high
        low_out[:, s * LANES : (s + 1) * LANES] = (tile - high.astype(f32)).astype(bf16)
    size = rank * clusters
    row = lax.broadcasted_iota(jnp.int32, (size, size), 0)
    column = lax.broadcasted_iota(jnp.int32, (size, size), 1)
    wanted = (row % clusters) * rank + row // clusters
    target_out[...] = dot((column == wanted).astype(bf16), target[...]).astype(bf16)


def fetch_kernel(first, blocks_hbm, *refs):
    *_, blocks, token, sems = refs
    chunks = sems.shape[0]
    each = blocks.shape[0] // chunks
    copies = [
        pltpu.make_async_copy(
            blocks_hbm.at[pl.ds(first + c * each, each)], blocks.at[pl.ds(c * each, each)], sems.at[c]
        )
        for c in range(chunks)
    ]
    for copy in copies:
        copy.start()
    token[...] = jnp.zeros_like(token)
    for copy in copies:
        copy.wait()


def relay_kernel(axis, got, even, odd, _, out):
    me = lax.axis_index(axis)
    devices, each, _ = got.shape
    for device in range(devices):
        out[pl.ds(device * each, each), :] = got[device]
    wants_even = (me // 2 + me) % 2 == 0
    span = pl.ds(devices * each, even.shape[0])

    @pl.when(wants_even)
    def _():
        out[span, :] = even[...]

    @pl.when(jnp.logical_not(wants_even))
    def _():
        out[span, :] = odd[...]


def apply(per_group, each, slabs, places, ahead, blocks, swaps, high, low, target, near, far, window, table, finish):
    clusters = near.shape[0] // R
    slots = (ahead.shape[0] + blocks.shape[0]) // clusters
    rank = LANES // per_group
    head = clusters // per_group * R
    rows = slabs[0].shape[0]
    devices = (swaps[0].shape[0] - rows) // each
    for at, slab in enumerate(slabs):
        window[pl.ds(at * rows, rows), :] = slab[...].astype(f32)
    window[pl.ds(len(slabs) * rows, rows), :] = swaps[1][pl.ds(devices * each, rows), :].astype(f32)
    window[pl.ds((len(slabs) + 1) * rows, R), :] = jnp.zeros((R, LANES), f32)
    for part, values in enumerate(swaps):
        for device in range(devices):
            at = (part * devices + device) * head
            table[pl.ds(at, head), :] = values[pl.ds(device * each, head), :].astype(f32)
    lane = lane_ids()

    def fetch(k, i):
        return window[pl.ds(pl.multiple_of(places[k, i], R), R), :]

    def block(k, i):
        at = i * slots + k
        return ahead[at] if at < ahead.shape[0] else blocks[at - ahead.shape[0]]

    def pick(i):
        tile = jnp.zeros((R, LANES), f32)
        for k in range(slots):
            found = table[pl.ds(pl.multiple_of(places[slots + k, i], R), R), :]
            tile = jnp.where(lane // rank == k, pltpu.roll(found, places[2 * slots + k, i], 1), tile)
        return tile

    picked = []
    for i in range(0, clusters, 2):
        sources = jnp.concatenate(
            [jnp.concatenate([fetch(k, i), fetch(k, i + 1)], axis=0) for k in range(slots)], axis=1
        )
        weights = jnp.concatenate(
            [jnp.concatenate([block(k, i), block(k, i + 1)], axis=0) for k in range(slots)], axis=1
        )
        both = dot(sources.astype(bf16), weights, (1, 1))
        near[pl.ds(i * R, R), :] = both[:R, :LANES]
        near[pl.ds((i + 1) * R, R), :] = both[R:, LANES:]
        if 2 * i < clusters:
            picked += [pick(n) for n in range(2 * i, 2 * i + 4)]
        if 2 * i == clusters - 4:
            picked = jnp.concatenate(picked, axis=0).astype(bf16)
            crossed = dot(picked, high[...]) + dot(picked, low[...])
            expanded_high, expanded_low = [], []
            for s in range(rank * clusters // LANES):
                tile = jnp.zeros((R, LANES), f32)
                for n in range(clusters):
                    part = crossed[n * R : (n + 1) * R, s * LANES : (s + 1) * LANES]
                    tile = jnp.where(lane % clusters == n, part, tile)
                tile_high = tile.astype(bf16).astype(f32)
                tile_low = tile - tile_high
                for source, kept in ((tile_high, expanded_high), (tile_low, expanded_low)):
                    spread = [jnp.where(lane % clusters == n, source, 0.0) for n in range(clusters)]
                    kept.append(jnp.concatenate(spread, axis=0).astype(bf16))
            far[...] = dot(jnp.concatenate(expanded_high, axis=1), target[...]) + dot(
                jnp.concatenate(expanded_low, axis=1), target[...]
            )
        if 2 * i >= clusters:
            for n in range(2 * i - clusters, 2 * i - clusters + 4):
                finish(n)


def first_kernel(
    per_group, own, mate, even, odd, places, ahead, blocks, sent, received, high, low, target, b, basis,
    image, lowered, payload, near, far, window, table,
):
    clusters = near.shape[0] // R
    slabs, swaps = (own, mate, even, odd), (sent, received)
    each = clusters // per_group * R
    tiles, parts = [], []
    sums = [jnp.zeros((R, LANES), f32) for _ in range(3)]

    def finish(i):
        field = rows_of(b, i)
        made = 0.5 * field + (rows_of(near, i) + rows_of(far, i))
        sums[:] = [s + f * g for s, f, g in zip(sums, (field, field, made), (field, made, made))]
        tiles.append(made)
        if i % 2:
            both = jnp.concatenate(tiles[i - 1 :], axis=0)
            image[pl.ds((i - 1) * R, 2 * R), :] = both
            lowered[pl.ds((i - 1) * R, 2 * R), :] = both.astype(bf16)
        if i % per_group == per_group - 1:
            parts.append(compress(tiles[-per_group:], basis, i // per_group))

    apply(per_group, each, slabs, places, ahead, blocks, swaps, high, low, target, near, far, window, table, finish)
    write_payload(payload, parts, sums)


def arnoldi_one(bb, bw, ww):
    whole = bb + epsilon
    start_norm = jnp.sqrt(whole)
    scale = 1.0 / start_norm
    v11 = bb / whole
    h11 = (bw * scale) * scale
    uu = jnp.maximum((ww * scale) * scale - 2.0 * h11 * h11 + h11 * h11 * v11, 0.0)
    h21 = jnp.sqrt(uu + epsilon)
    return start_norm, h11, h21, v11, uu / (uu + epsilon), h11 * (1.0 - v11) / h21


def second_kernel(
    per_group, unknowns, own, mate, even, odd, places, ahead, blocks, sent, received, high, low, target, b, image,
    candidate, sums_out, near, far, window, table,
):
    clusters = near.shape[0] // R
    head = clusters // per_group * R
    slabs, swaps = (own, mate, even, odd), (sent, received)
    means = read_sums(tails(swaps, own.shape[0], head), 3, unknowns)
    start_norm, h11, h21, _, _, _ = arnoldi_one(*means)
    scale = 1.0 / start_norm
    inverse = 1.0 / h21
    sums = [jnp.zeros((R, LANES), f32) for _ in range(3)]

    def finish(j):
        held = rows_of(image, j) * scale
        first = rows_of(b, j) * scale
        second = (held - h11 * first) * inverse
        made = (0.5 * held + (rows_of(near, j) + rows_of(far, j)) * scale - h11 * held) * inverse
        sums[:] = [s + v * made for s, v in zip(sums, (first, second, made))]
        candidate[pl.ds(j * R, R), :] = made

    each = head + TAIL
    apply(per_group, each, slabs, places, ahead, blocks, swaps, high, low, target, near, far, window, table, finish)
    tile = sums_tile(sums).astype(bf16)
    for device in range(sums_out.shape[0]):
        sums_out[device] = tile


def finish_kernel(per_group, unknowns, b, image, candidate, sent, received, got, solution_out, next_out):
    clusters = b.shape[0] // R
    sums = read_sums(tails((sent, received), b.shape[0], clusters // per_group * R), 3, unknowns)
    start_norm, h11, h21, v11, v22, v12 = arnoldi_one(*sums)
    h12, h22, ww = read_sums([got[device] for device in range(got.shape[0])], 3, unknowns)
    uu = ww - 2.0 * (h12 * h12 + h22 * h22) + h12 * h12 * v11 + h22 * h22 * v22 + 2.0 * h12 * h22 * v12
    h32 = jnp.sqrt(jnp.maximum(uu, 0.0) + epsilon)
    g11 = h11 * h11 + h21 * h21
    g12 = h11 * h12 + h21 * h22
    g22 = h12 * h12 + h22 * h22 + h32 * h32
    t1, t2 = start_norm * h11, start_norm * h12
    det = g11 * g22 - g12 * g12
    y1 = (g22 * t1 - g12 * t2) / det
    y2 = (g11 * t2 - g12 * t1) / det
    scale, inverse, last = 1.0 / start_norm, 1.0 / h21, 1.0 / h32
    for j in range(clusters):
        span = slice(j * LANES, (j + 1) * LANES)
        first = rows_of(b, j) * scale
        second = (rows_of(image, j) * scale - h11 * first) * inverse
        solution_out[:, span] = y1 * first + y2 * second
        next_out[:, span] = (rows_of(candidate, j) - h12 * first - h22 * second) * last


def swapped(block, partner):
    return lax.ppermute(block, "rows", [(i, partner(i)) for i in range(lax.axis_size("rows"))])


def core_mate(i):
    return i ^ 1


def even_mate(i):
    return i ^ 2


def odd_mate(i):
    chip = i // 2
    other = chip + 1 if chip % 2 else chip - 1
    return 2 * (other % (lax.axis_size("rows") // 2)) + i % 2


def sends_of(block):
    return [block] + [swapped(block, partner) for partner in (core_mate, even_mate, odd_mate)]


def on_device(
    right_sides, near_blocks, near_cols, near_counts, basis_in, target_basis, coupling, far_cols
):
    width = right_sides.shape[1]
    clusters, slots = near_cols.shape
    rank = basis_in.shape[1]
    per_group = LANES // rank
    head = clusters // per_group * R
    size = lax.axis_size("rows")
    unknowns = float(width * size)
    rows = clusters * R

    def shape(*dims, dtype=f32):
        return jax.ShapeDtypeStruct(dims, dtype)

    def scratch(*dims, dtype=f32):
        return pltpu.VMEM(dims, dtype)

    def in_hbm(array):
        return pltpu.with_memory_space_constraint(array, pltpu.HBM)

    def call(kernel, name, out, ins, *args, scratch_shapes=()):
        return pl.pallas_call(
            kernel, out_shape=out, in_specs=ins, out_specs=jax.tree.map(lambda _: VMEM, out),
            scratch_shapes=scratch_shapes, compiler_params=PARAMS, name=name,
        )(*args)

    chips = size // 2
    middle = chips // 4
    order = [(middle + n) % chips for n in range(chips)]

    def gather(block):
        groups = [[2 * chip + core for chip in order] for core in range(2)]
        return lax.all_to_all(block, "rows", 0, 0, axis_index_groups=groups)

    def exchange(block):
        group = [2 * chip + core for chip in order for core in range(2)]
        return lax.all_to_all(block, "rows", 0, 0, axis_index_groups=[group])

    field, basis, lowered, payload = call(
        functools.partial(start_kernel, per_group), "start",
        (
            shape(rows, LANES), shape(clusters * rank, LANES, dtype=bf16), shape(rows, LANES, dtype=bf16),
            shape(size // 2, head, LANES, dtype=bf16),
        ),
        [HBM] * 2, in_hbm(right_sides), in_hbm(basis_in.reshape(clusters * rank, LANES)),
        scratch_shapes=[scratch(R, width), pltpu.SemaphoreType.DMA((2,))],
    )
    got = gather(payload)
    held = sends_of(lowered)

    blocks = in_hbm(near_blocks.reshape(clusters * slots, LANES, LANES))
    early = blocks.shape[0] // 4
    def fetch(name, first, count, chunks, *behind):
        here, token = call(
            functools.partial(fetch_kernel, first), name, (pltpu.VMEM((count, LANES, LANES), bf16), shape(R, LANES)),
            [HBM] + [ANY] * len(behind), blocks, *behind, scratch_shapes=[pltpu.SemaphoreType.DMA((chunks,))],
        )
        return pltpu.with_memory_space_constraint(here, pltpu.VMEM), token

    def arrived(got, held, behind):
        rest, token = fetch("fetch", early, blocks.shape[0] - early, 8, got, behind)
        sent = call(
            functools.partial(relay_kernel, "rows"), "relay",
            shape(got.shape[0] * got.shape[1] + rows, LANES, dtype=bf16), [VMEM] * 3 + [ANY], got, *held[2:], token
        )
        return ahead, rest, sent, swapped(sent, core_mate)

    ahead, token = fetch("ahead", 0, early, 2, held[1])
    here = arrived(got, held, token)
    prepared = call(
        functools.partial(prepare_kernel, "rows", size, middle), "prepare",
        (
            shape(3 * slots, clusters, dtype=jnp.int32),
            shape(slots * rank, rank * clusters, dtype=bf16),
            shape(slots * rank, rank * clusters, dtype=bf16),
            shape(rank * clusters, LANES, dtype=bf16),
        ),
        [HBM] * 5 + [ANY], in_hbm(near_cols.T), in_hbm(near_counts.reshape(1, clusters)), in_hbm(far_cols.T),
        in_hbm(jnp.transpose(coupling, (1, 2, 3, 0))), in_hbm(target_basis.reshape(clusters * rank, LANES)), here[2],
        scratch_shapes=[
            scratch(slots, clusters, dtype=jnp.int32), scratch(1, clusters, dtype=jnp.int32),
            scratch(slots, clusters, dtype=jnp.int32),
            scratch(slots, rank, rank, clusters), scratch(clusters * rank, LANES, dtype=bf16),
            pltpu.SemaphoreType.DMA((5,)),
        ],
    )
    places, *made = prepared
    kept = [scratch(rows, LANES), scratch(rows, LANES), scratch(5 * rows + R, LANES), scratch(size * head, LANES)]
    operands = [VMEM] * 4 + [SMEM] + [VMEM] * 9
    image, lowered, payload = call(
        functools.partial(first_kernel, per_group), "operator_one",
        (
            shape(rows, LANES), shape(rows, LANES, dtype=bf16),
            shape(size // 2, head + TAIL, LANES, dtype=bf16),
        ),
        operands, *held, places, *here, *made, field, basis, scratch_shapes=kept,
    )
    got = gather(payload)
    held = sends_of(lowered)
    here = arrived(got, held, held[1])
    candidate, sums = call(
        functools.partial(second_kernel, per_group, unknowns), "operator_two",
        (shape(rows, LANES), shape(size, R, LANES, dtype=bf16)),
        operands, *held, places, *here, *made, field, image, scratch_shapes=kept,
    )
    return call(
        functools.partial(finish_kernel, per_group, unknowns), "finish", (shape(R, width), shape(R, width)),
        [VMEM] * 6, field, image, candidate, *here[2:], exchange(sums),
    )


def solution(mesh):
    return jax.shard_map(
        on_device,
        mesh=mesh,
        in_specs=(
            P("groups", "rows"),
            P("rows", None, None, None),
            P("rows", None),
            P("rows"),
            P("rows", None, None),
            P("rows", None, None),
            P("rows", None, None, None),
            P("rows", None),
        ),
        out_specs=(P("groups", "rows"), P("groups", "rows")),
        check_vma=False,
    )
```

```python
import functools

import jax
import jax.numpy as jnp
from jax import lax
from jax.experimental import pallas as pl
from jax.experimental.pallas import tpu as pltpu
from jax.sharding import PartitionSpec as P

epsilon = 1e-06
f32, bf16 = jnp.float32, jnp.bfloat16
VMEM = pl.BlockSpec(memory_space=pltpu.VMEM)
SMEM = pl.BlockSpec(memory_space=pltpu.SMEM)
HBM = pl.BlockSpec(memory_space=pltpu.HBM)
ANY = pl.BlockSpec(memory_space=pl.ANY)
R = 8
LANES = 128
SUM_SLOTS = 8
TAIL = 16
PARAMS = pltpu.CompilerParams(vmem_limit_bytes=24 * 1024 * 1024)


def lane_ids(rows=R):
    return lax.broadcasted_iota(jnp.int32, (rows, LANES), 1)


def rows_of(ref, j):
    return ref[pl.ds(j * R, R), :]


def dot(a, b, contract=(1, 0)):
    return lax.dot_general(a, b, (((contract[0],), (contract[1],)), ((), ())), preferred_element_type=f32)


def sums_tile(sums):
    lane = lane_ids()
    tile = jnp.zeros((R, LANES), f32)
    for t, partial in enumerate(sums):
        total = jnp.sum(partial, axis=1, keepdims=True)
        high = total.astype(bf16).astype(f32)
        middle = (total - high).astype(bf16).astype(f32)
        low = total - high - middle
        for part, value in enumerate((high, middle, low)):
            tile = jnp.where(lane == part * SUM_SLOTS + t, value, tile)
    return tile


def read_sums(parts, count, unknowns):
    total = jnp.zeros((R, LANES), f32)
    for part in parts:
        total = total + part.astype(f32)[:R]
    return [
        sum(total[:, p * SUM_SLOTS + t : p * SUM_SLOTS + t + 1] for p in range(3)) * (1.0 / unknowns)
        for t in range(count)
    ]


def tails(swaps, rows, head):
    each = head + TAIL
    return [
        values[pl.ds(device * each + head, TAIL), :]
        for values in swaps
        for device in range((values.shape[0] - rows) // each)
    ]


def compress(tiles, basis, group):
    stacked = jnp.concatenate(tiles, axis=0)
    high = stacked.astype(bf16)
    low = (stacked - high.astype(f32)).astype(bf16)
    both = dot(jnp.concatenate([high, low], axis=0), basis[pl.ds(group * LANES, LANES), :], (1, 1))
    rows = len(tiles) * R
    both = both[:rows] + both[rows:]
    lane = lane_ids()
    rank = LANES // len(tiles)
    tile = jnp.zeros((R, LANES), f32)
    for m in range(len(tiles)):
        tile = jnp.where(lane // rank == m, both[m * R : (m + 1) * R], tile)
    return tile


def write_payload(payload, parts, sums):
    if sums:
        parts = parts + [sums_tile(sums), jnp.zeros((TAIL - R, LANES), f32)]
    block = jnp.concatenate(parts, axis=0).astype(bf16)
    for device in range(payload.shape[0]):
        payload[device] = block


def start_kernel(per_group, b_hbm, basis_hbm, field, basis, lowered, payload, b, sems):
    copies = [
        pltpu.make_async_copy(b_hbm, b, sems.at[0]),
        pltpu.make_async_copy(basis_hbm, basis, sems.at[1]),
    ]
    for copy in copies:
        copy.start()
    for copy in copies:
        copy.wait()
    clusters = b.shape[1] // LANES
    tiles = [b[:, j * LANES : (j + 1) * LANES] for j in range(clusters)]
    field[...] = jnp.concatenate(tiles, axis=0)
    lowered[...] = jnp.concatenate(tiles, axis=0).astype(bf16)
    groups = [tiles[g : g + per_group] for g in range(0, clusters, per_group)]
    write_payload(payload, [compress(group, basis, g) for g, group in enumerate(groups)], [])


def window_place(distance, clusters, me):
    core, chip = me % 2, me // 2
    before, after = 3 - chip % 2, 2 + chip % 2
    slot = [before, jnp.where(core == 0, 4, 1), 0, jnp.where(core == 0, 1, 4), after]
    slab = lax.div(distance, clusters)
    chosen = jnp.zeros_like(distance)
    for s, value in enumerate(slot):
        chosen = jnp.where(slab == s, value, chosen)
    return chosen * clusters + lax.rem(distance, clusters)


def prepare_kernel(
    axis, size, middle, near_cols_hbm, near_counts_hbm, far_cols_hbm, coupling_hbm, target_hbm, _,
    places, high_out, low_out, target_out, near_cols, near_counts, far_cols, coupling, target, sems,
):
    pairs = (
        (near_cols_hbm, near_cols), (near_counts_hbm, near_counts), (far_cols_hbm, far_cols),
        (coupling_hbm, coupling), (target_hbm, target),
    )
    copies = [pltpu.make_async_copy(source, to, sems.at[n]) for n, (source, to) in enumerate(pairs)]
    for copy in copies:
        copy.start()
    for copy in copies[:3]:
        copy.wait()
    slots, clusters = near_cols.shape
    me = lax.axis_index(axis)
    every = clusters * size
    distance = near_cols[...] - me * clusters + 2 * clusters
    distance = jnp.where(distance < 0, distance + every, distance)
    distance = jnp.where(distance >= every, distance - every, distance)
    live = lax.broadcasted_iota(jnp.int32, (slots, clusters), 0) < near_counts[...]
    places[:slots, :] = jnp.where(live, window_place(distance, clusters, me), 5 * clusters) * R
    owner = lax.div(far_cols[...], clusters)
    other_core = (owner ^ me) & 1
    chips = size // 2
    chip = lax.rem(owner // 2 + (chips - middle), chips)
    rank = coupling.shape[1]
    per_group = LANES // rank
    inside = lax.rem(far_cols[...], clusters)
    tile = (other_core * chips + chip) * (clusters // per_group) + lax.div(inside, per_group)
    places[slots : 2 * slots, :] = tile * R
    slot = lax.broadcasted_iota(jnp.int32, (slots, clusters), 0)
    places[2 * slots :, :] = ((slot - inside) * rank) & (LANES - 1)
    for copy in copies[3:5]:
        copy.wait()
    slots, rank, _, clusters = coupling.shape
    per_tile = LANES // clusters
    for s in range(rank // per_tile):
        pieces = [
            coupling[:, s * per_tile + p].reshape(slots * rank, clusters) for p in range(per_tile)
        ]
        tile = jnp.concatenate(pieces, axis=1)
        high = tile.astype(bf16)
        high_out[:, s * LANES : (s + 1) * LANES] = high
        low_out[:, s * LANES : (s + 1) * LANES] = (tile - high.astype(f32)).astype(bf16)
    size = rank * clusters
    row = lax.broadcasted_iota(jnp.int32, (size, 1), 0)
    column = lax.broadcasted_iota(jnp.int32, (size, size), 1)
    wanted = lax.rem(row, clusters) * rank + lax.div(row, clusters)
    target_out[...] = dot((column == wanted).astype(bf16), target[...]).astype(bf16)


def fetch_kernel(slots, blocks_hbm, *refs):
    *_, blocks, token, sems = refs
    chunks = sems.shape[1]
    each = blocks.shape[0] // chunks
    copies, at = [], 0
    for n, (first, count) in enumerate(slots):
        for c in range(chunks):
            clusters = pl.ds(c * each, each)
            copies.append(
                pltpu.make_async_copy(
                    blocks_hbm.at[clusters, pl.ds(first, count)], blocks.at[clusters, pl.ds(at, count)], sems.at[n, c]
                )
            )
        at += count
    for copy in copies:
        copy.start()
    token[...] = jnp.zeros_like(token)
    for copy in copies:
        copy.wait()


def own_kernel(blocks_hbm, own, _, near, blocks, sems):
    chunks = sems.shape[0]
    each = blocks.shape[0] // chunks
    copies = [
        pltpu.make_async_copy(
            blocks_hbm.at[pl.ds(c * each, each), pl.ds(0, 1)], blocks.at[pl.ds(c * each, each)], sems.at[c]
        )
        for c in range(chunks)
    ]
    for copy in copies:
        copy.start()
    for c, copy in enumerate(copies):
        copy.wait()
        for i in range(c * each, (c + 1) * each, 2):
            both = dot(own[pl.ds(i * R, 2 * R), :], jnp.concatenate([blocks[i, 0], blocks[i + 1, 0]], axis=0), (1, 1))
            near[pl.ds(i * R, R), :] = both[:R, :LANES]
            near[pl.ds((i + 1) * R, R), :] = both[R:, LANES:]


def relay_kernel(axis, got, even, odd, _, out):
    me = lax.axis_index(axis)
    devices, each, _ = got.shape
    for device in range(devices):
        out[pl.ds(device * each, each), :] = got[device]
    wants_even = (me // 2 + me) % 2 == 0
    span = pl.ds(devices * each, even.shape[0])

    @pl.when(wants_even)
    def _():
        out[span, :] = even[...]

    @pl.when(jnp.logical_not(wants_even))
    def _():
        out[span, :] = odd[...]


def apply(
    per_group, each, slabs, places, ahead, blocks, swaps, high, low, target, near, far, window, table, finish, started
):
    clusters = near.shape[0] // R
    early = ahead.shape[1]
    first = 0 if started is None else 1
    slots = early + blocks.shape[1] + first
    rank = LANES // per_group
    head = clusters // per_group * R
    rows = slabs[0].shape[0]
    devices = (swaps[0].shape[0] - rows) // each
    for at, slab in enumerate(slabs):
        window[pl.ds(at * rows, rows), :] = slab[...].astype(f32)
    window[pl.ds(len(slabs) * rows, rows), :] = swaps[1][pl.ds(devices * each, rows), :].astype(f32)
    window[pl.ds((len(slabs) + 1) * rows, R), :] = jnp.zeros((R, LANES), f32)
    for part, values in enumerate(swaps):
        for device in range(devices):
            at = (part * devices + device) * head
            table[pl.ds(at, head), :] = values[pl.ds(device * each, head), :].astype(f32)
    lane = lane_ids()

    def fetch(k, i):
        return window[pl.ds(pl.multiple_of(places[k, i], R), R), :]

    def block(k, i):
        if 0 < k <= early:
            return ahead[i, k - 1]
        return blocks[i, max(k - early - first, 0)]

    def pick(i):
        tile = jnp.zeros((R, LANES), f32)
        for k in range(slots):
            found = table[pl.ds(pl.multiple_of(places[slots + k, i], R), R), :]
            tile = jnp.where(lane // rank == k, pltpu.roll(found, places[2 * slots + k, i], 1), tile)
        return tile

    picked = []
    for i in range(0, clusters, 2):
        sources = jnp.concatenate(
            [jnp.concatenate([fetch(k, i), fetch(k, i + 1)], axis=0) for k in range(first, slots)], axis=1
        )
        weights = jnp.concatenate(
            [jnp.concatenate([block(k, i), block(k, i + 1)], axis=0) for k in range(first, slots)], axis=1
        )
        both = dot(sources.astype(bf16), weights, (1, 1))
        parts = [both[:R, :LANES], both[R:, LANES:]]
        if started is not None:
            parts = [part + rows_of(started, i + n) for n, part in enumerate(parts)]
        near[pl.ds(i * R, 2 * R), :] = jnp.concatenate(parts, axis=0)
        if 2 * i < clusters:
            picked += [pick(n) for n in range(2 * i, 2 * i + 4)]
        if 2 * i == clusters - 4:
            picked = jnp.concatenate(picked, axis=0).astype(bf16)
            crossed = dot(picked, high[...]) + dot(picked, low[...])
            expanded_high, expanded_low = [], []
            for s in range(rank * clusters // LANES):
                tile = jnp.zeros((R, LANES), f32)
                for n in range(clusters):
                    part = crossed[n * R : (n + 1) * R, s * LANES : (s + 1) * LANES]
                    tile = jnp.where(lane % clusters == n, part, tile)
                tile_high = tile.astype(bf16).astype(f32)
                tile_low = tile - tile_high
                for source, kept in ((tile_high, expanded_high), (tile_low, expanded_low)):
                    spread = [jnp.where(lane % clusters == n, source, 0.0) for n in range(clusters)]
                    kept.append(jnp.concatenate(spread, axis=0).astype(bf16))
            far[...] = dot(jnp.concatenate(expanded_high, axis=1), target[...]) + dot(
                jnp.concatenate(expanded_low, axis=1), target[...]
            )
        if 2 * i >= clusters:
            for n in range(2 * i - clusters, 2 * i - clusters + 4):
                finish(n)


def first_kernel(
    per_group, own, mate, even, odd, places, ahead, blocks, sent, received, high, low, target, b, basis,
    image, lowered, payload, near, far, window, table,
):
    clusters = near.shape[0] // R
    slabs, swaps = (own, mate, even, odd), (sent, received)
    each = clusters // per_group * R
    tiles, parts = [], []
    sums = [jnp.zeros((R, LANES), f32) for _ in range(3)]

    def finish(i):
        field = rows_of(b, i)
        made = 0.5 * field + (rows_of(near, i) + rows_of(far, i))
        sums[:] = [s + f * g for s, f, g in zip(sums, (field, field, made), (field, made, made))]
        tiles.append(made)
        if i % 2:
            both = jnp.concatenate(tiles[i - 1 :], axis=0)
            image[pl.ds((i - 1) * R, 2 * R), :] = both
            lowered[pl.ds((i - 1) * R, 2 * R), :] = both.astype(bf16)
        if i % per_group == per_group - 1:
            parts.append(compress(tiles[-per_group:], basis, i // per_group))

    apply(
        per_group, each, slabs, places, ahead, blocks, swaps, high, low, target, near, far, window, table, finish, None
    )
    write_payload(payload, parts, sums)


def arnoldi_one(bb, bw, ww):
    whole = bb + epsilon
    start_norm = jnp.sqrt(whole)
    scale = 1.0 / start_norm
    v11 = bb / whole
    h11 = (bw * scale) * scale
    uu = jnp.maximum((ww * scale) * scale - 2.0 * h11 * h11 + h11 * h11 * v11, 0.0)
    h21 = jnp.sqrt(uu + epsilon)
    return start_norm, h11, h21, v11, uu / (uu + epsilon), h11 * (1.0 - v11) / h21


def second_kernel(
    per_group, unknowns, own, mate, even, odd, places, ahead, blocks, sent, received, high, low, target, b, image,
    started, candidate, sums_out, near, far, window, table,
):
    clusters = near.shape[0] // R
    head = clusters // per_group * R
    slabs, swaps = (own, mate, even, odd), (sent, received)
    means = read_sums(tails(swaps, own.shape[0], head), 3, unknowns)
    start_norm, h11, h21, _, _, _ = arnoldi_one(*means)
    scale = 1.0 / start_norm
    inverse = 1.0 / h21
    sums = [jnp.zeros((R, LANES), f32) for _ in range(3)]

    def finish(j):
        held = rows_of(image, j) * scale
        first = rows_of(b, j) * scale
        second = (held - h11 * first) * inverse
        made = (0.5 * held + (rows_of(near, j) + rows_of(far, j)) * scale - h11 * held) * inverse
        sums[:] = [s + v * made for s, v in zip(sums, (first, second, made))]
        candidate[pl.ds(j * R, R), :] = made

    each = head + TAIL
    apply(
        per_group, each, slabs, places, ahead, blocks, swaps, high, low, target, near, far, window, table, finish, started
    )
    tile = sums_tile(sums).astype(bf16)
    for device in range(sums_out.shape[0]):
        sums_out[device] = tile


def finish_kernel(per_group, unknowns, b, image, candidate, sent, received, got, solution_out, next_out):
    clusters = b.shape[0] // R
    sums = read_sums(tails((sent, received), b.shape[0], clusters // per_group * R), 3, unknowns)
    start_norm, h11, h21, v11, v22, v12 = arnoldi_one(*sums)
    h12, h22, ww = read_sums([got[device] for device in range(got.shape[0])], 3, unknowns)
    uu = ww - 2.0 * (h12 * h12 + h22 * h22) + h12 * h12 * v11 + h22 * h22 * v22 + 2.0 * h12 * h22 * v12
    h32 = jnp.sqrt(jnp.maximum(uu, 0.0) + epsilon)
    g11 = h11 * h11 + h21 * h21
    g12 = h11 * h12 + h21 * h22
    g22 = h12 * h12 + h22 * h22 + h32 * h32
    t1, t2 = start_norm * h11, start_norm * h12
    det = g11 * g22 - g12 * g12
    y1 = (g22 * t1 - g12 * t2) / det
    y2 = (g11 * t2 - g12 * t1) / det
    scale, inverse, last = 1.0 / start_norm, 1.0 / h21, 1.0 / h32
    for j in range(clusters):
        span = slice(j * LANES, (j + 1) * LANES)
        first = rows_of(b, j) * scale
        second = (rows_of(image, j) * scale - h11 * first) * inverse
        solution_out[:, span] = y1 * first + y2 * second
        next_out[:, span] = (rows_of(candidate, j) - h12 * first - h22 * second) * last


def swapped(block, partner):
    return lax.ppermute(block, "rows", [(i, partner(i)) for i in range(lax.axis_size("rows"))])


def core_mate(i):
    return i ^ 1


def even_mate(i):
    return i ^ 2


def odd_mate(i):
    chip = i // 2
    other = chip + 1 if chip % 2 else chip - 1
    return 2 * (other % (lax.axis_size("rows") // 2)) + i % 2


def sends_of(block):
    return [block] + [swapped(block, partner) for partner in (core_mate, even_mate, odd_mate)]


def on_device(
    right_sides, near_blocks, near_cols, near_counts, basis_in, target_basis, coupling, far_cols
):
    width = right_sides.shape[1]
    clusters, slots = near_cols.shape
    rank = basis_in.shape[1]
    per_group = LANES // rank
    head = clusters // per_group * R
    size = lax.axis_size("rows")
    unknowns = float(width * size)
    rows = clusters * R

    def shape(*dims, dtype=f32):
        return jax.ShapeDtypeStruct(dims, dtype)

    def scratch(*dims, dtype=f32):
        return pltpu.VMEM(dims, dtype)

    def in_hbm(array):
        return pltpu.with_memory_space_constraint(array, pltpu.HBM)

    def call(kernel, name, out, ins, *args, scratch_shapes=()):
        return pl.pallas_call(
            kernel, out_shape=out, in_specs=ins, out_specs=jax.tree.map(lambda _: VMEM, out),
            scratch_shapes=scratch_shapes, compiler_params=PARAMS, name=name,
        )(*args)

    chips = size // 2
    middle = chips // 4
    order = [(middle + n) % chips for n in range(chips)]

    def gather(block):
        groups = [[2 * chip + core for chip in order] for core in range(2)]
        return lax.all_to_all(block, "rows", 0, 0, axis_index_groups=groups)

    def exchange(block):
        group = [2 * chip + core for chip in order for core in range(2)]
        return lax.all_to_all(block, "rows", 0, 0, axis_index_groups=[group])

    field, basis, lowered, payload = call(
        functools.partial(start_kernel, per_group), "start",
        (
            shape(rows, LANES), shape(clusters * rank, LANES, dtype=bf16), shape(rows, LANES, dtype=bf16),
            shape(size // 2, head, LANES, dtype=bf16),
        ),
        [HBM] * 2, in_hbm(right_sides), in_hbm(basis_in.reshape(clusters * rank, LANES)),
        scratch_shapes=[scratch(R, width), pltpu.SemaphoreType.DMA((2,))],
    )
    got = gather(payload)
    held = sends_of(lowered)

    blocks = in_hbm(near_blocks)
    early = 2

    def fetch(name, ranges, chunks, *behind):
        count = sum(count for _, count in ranges)
        here, token = call(
            functools.partial(fetch_kernel, ranges), name,
            (pltpu.VMEM((clusters, count, LANES, LANES), bf16), shape(R, LANES)),
            [HBM] + [ANY] * len(behind), blocks, *behind,
            scratch_shapes=[pltpu.SemaphoreType.DMA((len(ranges), chunks))],
        )
        return pltpu.with_memory_space_constraint(here, pltpu.VMEM), token

    def arrived(got, held, ranges, behind):
        rest, token = fetch("fetch", ranges, 4, got, behind)
        sent = call(
            functools.partial(relay_kernel, "rows"), "relay",
            shape(got.shape[0] * got.shape[1] + rows, LANES, dtype=bf16), [VMEM] * 3 + [ANY], got, *held[2:], token
        )
        return ahead, rest, sent, swapped(sent, core_mate)

    late = (1 + early, slots - 1 - early)
    ahead, token = fetch("ahead", [(1, early)], 2, held[1])
    here = arrived(got, held, [(0, 1), late], token)
    prepared = call(
        functools.partial(prepare_kernel, "rows", size, middle), "prepare",
        (
            shape(3 * slots, clusters, dtype=jnp.int32),
            shape(slots * rank, rank * clusters, dtype=bf16),
            shape(slots * rank, rank * clusters, dtype=bf16),
            shape(rank * clusters, LANES, dtype=bf16),
        ),
        [HBM] * 5 + [ANY], in_hbm(near_cols.T), in_hbm(near_counts.reshape(1, clusters)), in_hbm(far_cols.T),
        in_hbm(jnp.transpose(coupling, (1, 2, 3, 0))), in_hbm(target_basis.reshape(clusters * rank, LANES)), here[2],
        scratch_shapes=[
            scratch(slots, clusters, dtype=jnp.int32), scratch(1, clusters, dtype=jnp.int32),
            scratch(slots, clusters, dtype=jnp.int32),
            scratch(slots, rank, rank, clusters), scratch(clusters * rank, LANES, dtype=bf16),
            pltpu.SemaphoreType.DMA((5,)),
        ],
    )
    places, *made = prepared
    kept = [scratch(rows, LANES), scratch(rows, LANES), scratch(5 * rows + R, LANES), scratch(size * head, LANES)]
    operands = [VMEM] * 4 + [SMEM] + [VMEM] * 9
    image, lowered, payload = call(
        functools.partial(first_kernel, per_group), "operator_one",
        (
            shape(rows, LANES), shape(rows, LANES, dtype=bf16),
            shape(size // 2, head + TAIL, LANES, dtype=bf16),
        ),
        operands, *held, places, *here, *made, field, basis, scratch_shapes=kept,
    )
    got = gather(payload)
    held = sends_of(lowered)
    started = call(
        own_kernel, "own", shape(rows, LANES), [HBM, VMEM, ANY], blocks, lowered, held[1],
        scratch_shapes=[scratch(clusters, 1, LANES, LANES, dtype=bf16), pltpu.SemaphoreType.DMA((4,))],
    )
    here = arrived(got, held, [late], started)
    candidate, sums = call(
        functools.partial(second_kernel, per_group, unknowns), "operator_two",
        (shape(rows, LANES), shape(size, R, LANES, dtype=bf16)),
        operands + [VMEM], *held, places, *here, *made, field, image, started, scratch_shapes=kept,
    )
    return call(
        functools.partial(finish_kernel, per_group, unknowns), "finish", (shape(R, width), shape(R, width)),
        [VMEM] * 6, field, image, candidate, *here[2:], exchange(sums),
    )


def solution(mesh):
    return jax.shard_map(
        on_device,
        mesh=mesh,
        in_specs=(
            P("groups", "rows"),
            P("rows", None, None, None),
            P("rows", None),
            P("rows"),
            P("rows", None, None),
            P("rows", None, None),
            P("rows", None, None, None),
            P("rows", None),
        ),
        out_specs=(P("groups", "rows"), P("groups", "rows")),
        check_vma=False,
    )
```

```python
import functools

import jax
import jax.numpy as jnp
from jax import lax
from jax.experimental import pallas as pl
from jax.experimental.pallas import tpu as pltpu
from jax.sharding import PartitionSpec as P

epsilon = 1e-06
f32, bf16 = jnp.float32, jnp.bfloat16
VMEM = pl.BlockSpec(memory_space=pltpu.VMEM)
SMEM = pl.BlockSpec(memory_space=pltpu.SMEM)
HBM = pl.BlockSpec(memory_space=pltpu.HBM)
ANY = pl.BlockSpec(memory_space=pl.ANY)
R = 8
LANES = 128
SUM_SLOTS = 8
TAIL = 16
PARAMS = pltpu.CompilerParams(vmem_limit_bytes=24 * 1024 * 1024)


def lane_ids(rows=R):
    return lax.broadcasted_iota(jnp.int32, (rows, LANES), 1)


def rows_of(ref, j):
    return ref[pl.ds(j * R, R), :]


def dot(a, b, contract=(1, 0)):
    return lax.dot_general(a, b, (((contract[0],), (contract[1],)), ((), ())), preferred_element_type=f32)


def sums_tile(sums):
    lane = lane_ids()
    tile = jnp.zeros((R, LANES), f32)
    for t, partial in enumerate(sums):
        total = jnp.sum(partial, axis=1, keepdims=True)
        high = total.astype(bf16).astype(f32)
        middle = (total - high).astype(bf16).astype(f32)
        low = total - high - middle
        for part, value in enumerate((high, middle, low)):
            tile = jnp.where(lane == part * SUM_SLOTS + t, value, tile)
    return tile


def read_sums(parts, count, unknowns):
    total = jnp.zeros((R, LANES), f32)
    for part in parts:
        total = total + part.astype(f32)[:R]
    return [
        sum(total[:, p * SUM_SLOTS + t : p * SUM_SLOTS + t + 1] for p in range(3)) * (1.0 / unknowns)
        for t in range(count)
    ]


def tails(swaps, rows, head):
    each = head + TAIL
    return [
        values[pl.ds(device * each + head, TAIL), :]
        for values in swaps
        for device in range((values.shape[0] - rows) // each)
    ]


def compress(tiles, basis, group):
    stacked = jnp.concatenate(tiles, axis=0)
    high = stacked.astype(bf16)
    low = (stacked - high.astype(f32)).astype(bf16)
    return dot(jnp.concatenate([high, low], axis=0), basis[pl.ds(group * LANES, LANES), :], (1, 1))


def collect(products, per_group):
    rows = per_group * R
    both = products[:rows] + products[rows:]
    lane = lane_ids()
    tile = jnp.zeros((R, LANES), f32)
    for m in range(per_group):
        tile = jnp.where(lane // (LANES // per_group) == m, both[m * R : (m + 1) * R], tile)
    return tile


def write_payload(payload, parts, sums):
    if sums:
        parts = parts + [sums_tile(sums), jnp.zeros((TAIL - R, LANES), f32)]
    block = jnp.concatenate(parts, axis=0).astype(bf16)
    for device in range(payload.shape[0]):
        payload[device] = block


def start_kernel(per_group, b_hbm, basis_hbm, field, basis, lowered, payload, b, sems):
    copies = [
        pltpu.make_async_copy(b_hbm, b, sems.at[0]),
        pltpu.make_async_copy(basis_hbm, basis, sems.at[1]),
    ]
    for copy in copies:
        copy.start()
    for copy in copies:
        copy.wait()
    clusters = b.shape[1] // LANES
    tiles = [b[:, j * LANES : (j + 1) * LANES] for j in range(clusters)]
    field[...] = jnp.concatenate(tiles, axis=0)
    lowered[...] = jnp.concatenate(tiles, axis=0).astype(bf16)
    groups = [tiles[g : g + per_group] for g in range(0, clusters, per_group)]
    products = [compress(group, basis, g) for g, group in enumerate(groups)]
    write_payload(payload, [collect(product, per_group) for product in products], [])


def window_place(distance, clusters, me):
    core, chip = me % 2, me // 2
    before, after = 3 - chip % 2, 2 + chip % 2
    slot = [before, jnp.where(core == 0, 4, 1), 0, jnp.where(core == 0, 1, 4), after]
    slab = lax.div(distance, clusters)
    chosen = jnp.zeros_like(distance)
    for s, value in enumerate(slot):
        chosen = jnp.where(slab == s, value, chosen)
    return chosen * clusters + lax.rem(distance, clusters)


def prepare_kernel(
    axis, size, middle, near_cols_hbm, near_counts_hbm, far_cols_hbm, coupling_hbm, target_hbm, _,
    places, high_out, low_out, target_out, near_cols, near_counts, far_cols, coupling, target, sems,
):
    pairs = (
        (near_cols_hbm, near_cols), (near_counts_hbm, near_counts), (far_cols_hbm, far_cols),
        (coupling_hbm, coupling), (target_hbm, target),
    )
    copies = [pltpu.make_async_copy(source, to, sems.at[n]) for n, (source, to) in enumerate(pairs)]
    for copy in copies:
        copy.start()
    for copy in copies[:3]:
        copy.wait()
    slots, clusters = near_cols.shape
    me = lax.axis_index(axis)
    every = clusters * size
    distance = near_cols[...] - me * clusters + 2 * clusters
    distance = jnp.where(distance < 0, distance + every, distance)
    distance = jnp.where(distance >= every, distance - every, distance)
    live = lax.broadcasted_iota(jnp.int32, (slots, clusters), 0) < near_counts[...]
    places[:slots, :] = jnp.where(live, window_place(distance, clusters, me), 5 * clusters) * R
    owner = lax.div(far_cols[...], clusters)
    other_core = (owner ^ me) & 1
    chips = size // 2
    chip = lax.rem(owner // 2 + (chips - middle), chips)
    rank = coupling.shape[1]
    per_group = LANES // rank
    inside = lax.rem(far_cols[...], clusters)
    tile = (other_core * chips + chip) * (clusters // per_group) + lax.div(inside, per_group)
    places[slots : 2 * slots, :] = tile * R
    slot = lax.broadcasted_iota(jnp.int32, (slots, clusters), 0)
    places[2 * slots :, :] = ((slot - inside) * rank) & (LANES - 1)
    for copy in copies[3:5]:
        copy.wait()
    slots, rank, _, clusters = coupling.shape
    per_tile = LANES // clusters
    for s in range(rank // per_tile):
        pieces = [
            coupling[:, s * per_tile + p].reshape(slots * rank, clusters) for p in range(per_tile)
        ]
        tile = jnp.concatenate(pieces, axis=1)
        high = tile.astype(bf16)
        high_out[:, s * LANES : (s + 1) * LANES] = high
        low_out[:, s * LANES : (s + 1) * LANES] = (tile - high.astype(f32)).astype(bf16)
    size = rank * clusters
    row = lax.broadcasted_iota(jnp.int32, (size, 1), 0)
    column = lax.broadcasted_iota(jnp.int32, (size, size), 1)
    wanted = lax.rem(row, clusters) * rank + lax.div(row, clusters)
    target_out[...] = dot((column == wanted).astype(bf16), target[...]).astype(bf16)


def fetch_kernel(slots, blocks_hbm, *refs):
    *_, blocks, token, sems = refs
    chunks = sems.shape[1]
    each = blocks.shape[0] // chunks
    copies, at = [], 0
    for n, (first, count) in enumerate(slots):
        for c in range(chunks):
            clusters = pl.ds(c * each, each)
            copies.append(
                pltpu.make_async_copy(
                    blocks_hbm.at[clusters, pl.ds(first, count)], blocks.at[clusters, pl.ds(at, count)], sems.at[n, c]
                )
            )
        at += count
    for copy in copies:
        copy.start()
    token[...] = jnp.zeros_like(token)
    for copy in copies:
        copy.wait()


def own_kernel(blocks_hbm, own, _, near, blocks, sems):
    chunks = sems.shape[0]
    each = blocks.shape[0] // chunks
    copies = [
        pltpu.make_async_copy(
            blocks_hbm.at[pl.ds(c * each, each), pl.ds(0, 1)], blocks.at[pl.ds(c * each, each)], sems.at[c]
        )
        for c in range(chunks)
    ]
    for copy in copies:
        copy.start()
    for c, copy in enumerate(copies):
        copy.wait()
        for i in range(c * each, (c + 1) * each, 2):
            both = dot(own[pl.ds(i * R, 2 * R), :], jnp.concatenate([blocks[i, 0], blocks[i + 1, 0]], axis=0), (1, 1))
            near[pl.ds(i * R, R), :] = both[:R, :LANES]
            near[pl.ds((i + 1) * R, R), :] = both[R:, LANES:]


def relay_kernel(axis, got, even, odd, _, out):
    me = lax.axis_index(axis)
    devices, each, _ = got.shape
    for device in range(devices):
        out[pl.ds(device * each, each), :] = got[device]
    wants_even = (me // 2 + me) % 2 == 0
    span = pl.ds(devices * each, even.shape[0])

    @pl.when(wants_even)
    def _():
        out[span, :] = even[...]

    @pl.when(jnp.logical_not(wants_even))
    def _():
        out[span, :] = odd[...]


def apply(
    per_group, each, slabs, places, ahead, blocks, swaps, high, low, target, near, far, window, table, finish, started
):
    clusters = near.shape[0] // R
    early = ahead.shape[1]
    first = 0 if started is None else 1
    slots = early + blocks.shape[1] + first
    rank = LANES // per_group
    head = clusters // per_group * R
    rows = slabs[0].shape[0]
    devices = (swaps[0].shape[0] - rows) // each
    for at, slab in enumerate(slabs):
        window[pl.ds(at * rows, rows), :] = slab[...].astype(f32)
    window[pl.ds(len(slabs) * rows, rows), :] = swaps[1][pl.ds(devices * each, rows), :].astype(f32)
    window[pl.ds((len(slabs) + 1) * rows, R), :] = jnp.zeros((R, LANES), f32)
    for part, values in enumerate(swaps):
        for device in range(devices):
            at = (part * devices + device) * head
            table[pl.ds(at, head), :] = values[pl.ds(device * each, head), :].astype(f32)
    lane = lane_ids()

    def fetch(k, i):
        return window[pl.ds(pl.multiple_of(places[k, i], R), R), :]

    def block(k, i):
        if 0 < k <= early:
            return ahead[i, k - 1]
        return blocks[i, max(k - early - first, 0)]

    def pick(i):
        tile = jnp.zeros((R, LANES), f32)
        for k in range(slots):
            found = table[pl.ds(pl.multiple_of(places[slots + k, i], R), R), :]
            tile = jnp.where(lane // rank == k, pltpu.roll(found, places[2 * slots + k, i], 1), tile)
        return tile

    def product(i):
        sources = jnp.concatenate(
            [jnp.concatenate([fetch(k, i), fetch(k, i + 1)], axis=0) for k in range(first, slots)], axis=1
        )
        weights = jnp.concatenate(
            [jnp.concatenate([block(k, i), block(k, i + 1)], axis=0) for k in range(first, slots)], axis=1
        )
        return dot(sources.astype(bf16), weights, (1, 1))

    def settle(i, both):
        parts = [both[:R, :LANES], both[R:, LANES:]]
        if started is not None:
            parts = [part + rows_of(started, i + n) for n, part in enumerate(parts)]
        near[pl.ds(i * R, 2 * R), :] = jnp.concatenate(parts, axis=0)

    def expand(crossed):
        spread = []
        for s in range(rank * clusters // LANES):
            tile = jnp.zeros((R, LANES), f32)
            for n in range(clusters):
                part = crossed[n * R : (n + 1) * R, s * LANES : (s + 1) * LANES]
                tile = jnp.where(lane % clusters == n, part, tile)
            tile_high = tile.astype(bf16).astype(f32)
            for n, source in enumerate((tile_high, tile - tile_high)):
                held = [jnp.where(lane % clusters == c, source, 0.0) for c in range(clusters)]
                spread.append((n, jnp.concatenate(held, axis=0).astype(bf16)))
        return [jnp.concatenate([part for m, part in spread if m == n], axis=1) for n in range(2)]

    pairs = clusters // 2
    middle = pairs // 2
    picked, pending, done = [], None, 0
    for p in range(pairs):
        both = product(2 * p)
        if pending is not None:
            settle(2 * p - 2, pending)
        pending = both
        if p < middle:
            picked += [pick(n) for n in range(4 * p, 4 * p + 4)]
        if p == middle - 1:
            chosen = jnp.concatenate(picked, axis=0).astype(bf16)
            crossed = [dot(chosen, high[...]), dot(chosen, low[...])]
        if p == middle:
            spread = expand(crossed[0] + crossed[1])
            made = [dot(part, target[...]) for part in spread]
        if p == middle + 1:
            far[...] = made[0] + made[1]
        if p > middle + 1:
            ready = min(2 * p, done + 6)
            for n in range(done, ready):
                finish(n)
            done = ready
    settle(clusters - 2, pending)
    for n in range(done, clusters):
        finish(n)


def first_kernel(
    per_group, own, mate, even, odd, places, ahead, blocks, sent, received, high, low, target, b, basis,
    image, lowered, payload, near, far, window, table,
):
    clusters = near.shape[0] // R
    slabs, swaps = (own, mate, even, odd), (sent, received)
    each = clusters // per_group * R
    tiles, products, parts = [], [], []
    sums = [jnp.zeros((R, LANES), f32) for _ in range(3)]

    def finish(i):
        field = rows_of(b, i)
        made = 0.5 * field + (rows_of(near, i) + rows_of(far, i))
        sums[:] = [s + f * g for s, f, g in zip(sums, (field, field, made), (field, made, made))]
        tiles.append(made)
        if i % 2:
            both = jnp.concatenate(tiles[i - 1 :], axis=0)
            image[pl.ds((i - 1) * R, 2 * R), :] = both
            lowered[pl.ds((i - 1) * R, 2 * R), :] = both.astype(bf16)
        if i % per_group == per_group - 1:
            products.append(compress(tiles[-per_group:], basis, i // per_group))
            parts.extend(collect(product, per_group) for product in products[-2:-1])

    apply(
        per_group, each, slabs, places, ahead, blocks, swaps, high, low, target, near, far, window, table, finish, None
    )
    write_payload(payload, parts + [collect(products[-1], per_group)], sums)


def arnoldi_one(bb, bw, ww):
    whole = bb + epsilon
    start_norm = jnp.sqrt(whole)
    scale = 1.0 / start_norm
    v11 = bb / whole
    h11 = (bw * scale) * scale
    uu = jnp.maximum((ww * scale) * scale - 2.0 * h11 * h11 + h11 * h11 * v11, 0.0)
    h21 = jnp.sqrt(uu + epsilon)
    return start_norm, h11, h21, v11, uu / (uu + epsilon), h11 * (1.0 - v11) / h21


def second_kernel(
    per_group, unknowns, own, mate, even, odd, places, ahead, blocks, sent, received, high, low, target, b, image,
    started, candidate, sums_out, near, far, window, table,
):
    clusters = near.shape[0] // R
    head = clusters // per_group * R
    slabs, swaps = (own, mate, even, odd), (sent, received)
    means = read_sums(tails(swaps, own.shape[0], head), 3, unknowns)
    start_norm, h11, h21, _, _, _ = arnoldi_one(*means)
    scale = 1.0 / start_norm
    inverse = 1.0 / h21
    sums = [jnp.zeros((R, LANES), f32) for _ in range(3)]

    def finish(j):
        held = rows_of(image, j) * scale
        first = rows_of(b, j) * scale
        second = (held - h11 * first) * inverse
        made = (0.5 * held + (rows_of(near, j) + rows_of(far, j)) * scale - h11 * held) * inverse
        sums[:] = [s + v * made for s, v in zip(sums, (first, second, made))]
        candidate[pl.ds(j * R, R), :] = made

    each = head + TAIL
    apply(
        per_group, each, slabs, places, ahead, blocks, swaps, high, low, target, near, far, window, table, finish, started
    )
    tile = sums_tile(sums).astype(bf16)
    for device in range(sums_out.shape[0]):
        sums_out[device] = tile


def finish_kernel(per_group, unknowns, b, image, candidate, sent, received, got, solution_out, next_out):
    clusters = b.shape[0] // R
    sums = read_sums(tails((sent, received), b.shape[0], clusters // per_group * R), 3, unknowns)
    start_norm, h11, h21, v11, v22, v12 = arnoldi_one(*sums)
    h12, h22, ww = read_sums([got[device] for device in range(got.shape[0])], 3, unknowns)
    uu = ww - 2.0 * (h12 * h12 + h22 * h22) + h12 * h12 * v11 + h22 * h22 * v22 + 2.0 * h12 * h22 * v12
    h32 = jnp.sqrt(jnp.maximum(uu, 0.0) + epsilon)
    g11 = h11 * h11 + h21 * h21
    g12 = h11 * h12 + h21 * h22
    g22 = h12 * h12 + h22 * h22 + h32 * h32
    t1, t2 = start_norm * h11, start_norm * h12
    det = g11 * g22 - g12 * g12
    y1 = (g22 * t1 - g12 * t2) / det
    y2 = (g11 * t2 - g12 * t1) / det
    scale, inverse, last = 1.0 / start_norm, 1.0 / h21, 1.0 / h32
    for j in range(clusters):
        span = slice(j * LANES, (j + 1) * LANES)
        first = rows_of(b, j) * scale
        second = (rows_of(image, j) * scale - h11 * first) * inverse
        solution_out[:, span] = y1 * first + y2 * second
        next_out[:, span] = (rows_of(candidate, j) - h12 * first - h22 * second) * last


def swapped(block, partner):
    return lax.ppermute(block, "rows", [(i, partner(i)) for i in range(lax.axis_size("rows"))])


def core_mate(i):
    return i ^ 1


def even_mate(i):
    return i ^ 2


def odd_mate(i):
    chip = i // 2
    other = chip + 1 if chip % 2 else chip - 1
    return 2 * (other % (lax.axis_size("rows") // 2)) + i % 2


def sends_of(block):
    return [block] + [swapped(block, partner) for partner in (core_mate, even_mate, odd_mate)]


def on_device(
    right_sides, near_blocks, near_cols, near_counts, basis_in, target_basis, coupling, far_cols
):
    width = right_sides.shape[1]
    clusters, slots = near_cols.shape
    rank = basis_in.shape[1]
    per_group = LANES // rank
    head = clusters // per_group * R
    size = lax.axis_size("rows")
    unknowns = float(width * size)
    rows = clusters * R

    def shape(*dims, dtype=f32):
        return jax.ShapeDtypeStruct(dims, dtype)

    def scratch(*dims, dtype=f32):
        return pltpu.VMEM(dims, dtype)

    def in_hbm(array):
        return pltpu.with_memory_space_constraint(array, pltpu.HBM)

    def call(kernel, name, out, ins, *args, scratch_shapes=()):
        return pl.pallas_call(
            kernel, out_shape=out, in_specs=ins, out_specs=jax.tree.map(lambda _: VMEM, out),
            scratch_shapes=scratch_shapes, compiler_params=PARAMS, name=name,
        )(*args)

    chips = size // 2
    middle = chips // 4
    order = [(middle + n) % chips for n in range(chips)]

    def gather(block):
        groups = [[2 * chip + core for chip in order] for core in range(2)]
        return lax.all_to_all(block, "rows", 0, 0, axis_index_groups=groups)

    def exchange(block):
        group = [2 * chip + core for chip in order for core in range(2)]
        return lax.all_to_all(block, "rows", 0, 0, axis_index_groups=[group])

    field, basis, lowered, payload = call(
        functools.partial(start_kernel, per_group), "start",
        (
            shape(rows, LANES), shape(clusters * rank, LANES, dtype=bf16), shape(rows, LANES, dtype=bf16),
            shape(size // 2, head, LANES, dtype=bf16),
        ),
        [HBM] * 2, in_hbm(right_sides), in_hbm(basis_in.reshape(clusters * rank, LANES)),
        scratch_shapes=[scratch(R, width), pltpu.SemaphoreType.DMA((2,))],
    )
    got = gather(payload)
    held = sends_of(lowered)

    blocks = in_hbm(near_blocks)
    early = 2

    def fetch(name, ranges, chunks, *behind):
        count = sum(count for _, count in ranges)
        here, token = call(
            functools.partial(fetch_kernel, ranges), name,
            (pltpu.VMEM((clusters, count, LANES, LANES), bf16), shape(R, LANES)),
            [HBM] + [ANY] * len(behind), blocks, *behind,
            scratch_shapes=[pltpu.SemaphoreType.DMA((len(ranges), chunks))],
        )
        return pltpu.with_memory_space_constraint(here, pltpu.VMEM), token

    def arrived(got, held, ranges, behind):
        rest, token = fetch("fetch", ranges, 4, got, behind)
        sent = call(
            functools.partial(relay_kernel, "rows"), "relay",
            shape(got.shape[0] * got.shape[1] + rows, LANES, dtype=bf16), [VMEM] * 3 + [ANY], got, *held[2:], token
        )
        return ahead, rest, sent, swapped(sent, core_mate)

    late = (1 + early, slots - 1 - early)
    ahead, token = fetch("ahead", [(1, early)], 2, held[1])
    here = arrived(got, held, [(0, 1), late], token)
    prepared = call(
        functools.partial(prepare_kernel, "rows", size, middle), "prepare",
        (
            shape(3 * slots, clusters, dtype=jnp.int32),
            shape(slots * rank, rank * clusters, dtype=bf16),
            shape(slots * rank, rank * clusters, dtype=bf16),
            shape(rank * clusters, LANES, dtype=bf16),
        ),
        [HBM] * 5 + [ANY], in_hbm(near_cols.T), in_hbm(near_counts.reshape(1, clusters)), in_hbm(far_cols.T),
        in_hbm(jnp.transpose(coupling, (1, 2, 3, 0))), in_hbm(target_basis.reshape(clusters * rank, LANES)), here[2],
        scratch_shapes=[
            scratch(slots, clusters, dtype=jnp.int32), scratch(1, clusters, dtype=jnp.int32),
            scratch(slots, clusters, dtype=jnp.int32),
            scratch(slots, rank, rank, clusters), scratch(clusters * rank, LANES, dtype=bf16),
            pltpu.SemaphoreType.DMA((5,)),
        ],
    )
    places, *made = prepared
    kept = [scratch(rows, LANES), scratch(rows, LANES), scratch(5 * rows + R, LANES), scratch(size * head, LANES)]
    operands = [VMEM] * 4 + [SMEM] + [VMEM] * 9
    image, lowered, payload = call(
        functools.partial(first_kernel, per_group), "operator_one",
        (
            shape(rows, LANES), shape(rows, LANES, dtype=bf16),
            shape(size // 2, head + TAIL, LANES, dtype=bf16),
        ),
        operands, *held, places, *here, *made, field, basis, scratch_shapes=kept,
    )
    got = gather(payload)
    held = sends_of(lowered)
    started = call(
        own_kernel, "own", shape(rows, LANES), [HBM, VMEM, ANY], blocks, lowered, held[1],
        scratch_shapes=[scratch(clusters, 1, LANES, LANES, dtype=bf16), pltpu.SemaphoreType.DMA((4,))],
    )
    here = arrived(got, held, [late], started)
    candidate, sums = call(
        functools.partial(second_kernel, per_group, unknowns), "operator_two",
        (shape(rows, LANES), shape(size, R, LANES, dtype=bf16)),
        operands + [VMEM], *held, places, *here, *made, field, image, started, scratch_shapes=kept,
    )
    return call(
        functools.partial(finish_kernel, per_group, unknowns), "finish", (shape(R, width), shape(R, width)),
        [VMEM] * 6, field, image, candidate, *here[2:], exchange(sums),
    )


def solution(mesh):
    return jax.shard_map(
        on_device,
        mesh=mesh,
        in_specs=(
            P("groups", "rows"),
            P("rows", None, None, None),
            P("rows", None),
            P("rows"),
            P("rows", None, None),
            P("rows", None, None),
            P("rows", None, None, None),
            P("rows", None),
        ),
        out_specs=(P("groups", "rows"), P("groups", "rows")),
        check_vma=False,
    )
```

```python
import functools

import jax
import jax.numpy as jnp
from jax import lax
from jax.experimental import pallas as pl
from jax.experimental.pallas import tpu as pltpu
from jax.sharding import PartitionSpec as P

epsilon = 1e-06
f32, bf16 = jnp.float32, jnp.bfloat16
VMEM = pl.BlockSpec(memory_space=pltpu.VMEM)
SMEM = pl.BlockSpec(memory_space=pltpu.SMEM)
HBM = pl.BlockSpec(memory_space=pltpu.HBM)
ANY = pl.BlockSpec(memory_space=pl.ANY)
R = 8
LANES = 128
SUM_SLOTS = 8
TAIL = 16
PARAMS = pltpu.CompilerParams(vmem_limit_bytes=24 * 1024 * 1024)


def lane_ids(rows=R):
    return lax.broadcasted_iota(jnp.int32, (rows, LANES), 1)


def rows_of(ref, j):
    return ref[pl.ds(j * R, R), :]


def dot(a, b, contract=(1, 0)):
    return lax.dot_general(a, b, (((contract[0],), (contract[1],)), ((), ())), preferred_element_type=f32)


def sums_tile(sums):
    lane = lane_ids()
    tile = jnp.zeros((R, LANES), f32)
    for t, partial in enumerate(sums):
        total = jnp.sum(partial, axis=1, keepdims=True)
        high = total.astype(bf16).astype(f32)
        middle = (total - high).astype(bf16).astype(f32)
        low = total - high - middle
        for part, value in enumerate((high, middle, low)):
            tile = jnp.where(lane == part * SUM_SLOTS + t, value, tile)
    return tile


def read_sums(parts, count, unknowns):
    total = jnp.zeros((R, LANES), f32)
    for part in parts:
        total = total + part.astype(f32)[:R]
    return [
        sum(total[:, p * SUM_SLOTS + t : p * SUM_SLOTS + t + 1] for p in range(3)) * (1.0 / unknowns)
        for t in range(count)
    ]


def tails(swaps, rows, head):
    each = head + TAIL
    return [
        values[pl.ds(device * each + head, TAIL), :]
        for values in swaps
        for device in range((values.shape[0] - rows) // each)
    ]


def compress(tiles, basis, group):
    stacked = jnp.concatenate(tiles, axis=0)
    high = stacked.astype(bf16)
    low = (stacked - high.astype(f32)).astype(bf16)
    return dot(jnp.concatenate([high, low], axis=0), basis[pl.ds(group * LANES, LANES), :], (1, 1))


def collect(products, per_group):
    rows = per_group * R
    both = products[:rows] + products[rows:]
    lane = lane_ids()
    tile = jnp.zeros((R, LANES), f32)
    for m in range(per_group):
        tile = jnp.where(lane // (LANES // per_group) == m, both[m * R : (m + 1) * R], tile)
    return tile


def write_payload(payload, parts, sums):
    if sums:
        parts = parts + [sums_tile(sums), jnp.zeros((TAIL - R, LANES), f32)]
    block = jnp.concatenate(parts, axis=0).astype(bf16)
    for device in range(payload.shape[0]):
        payload[device] = block


def start_kernel(per_group, b_hbm, basis_hbm, field, basis, lowered, payload, b, sems):
    copies = [
        pltpu.make_async_copy(b_hbm, b, sems.at[0]),
        pltpu.make_async_copy(basis_hbm, basis, sems.at[1]),
    ]
    for copy in copies:
        copy.start()
    copies[0].wait()
    clusters = b.shape[1] // LANES
    tiles = [b[:, j * LANES : (j + 1) * LANES] for j in range(clusters)]
    field[...] = jnp.concatenate(tiles, axis=0)
    lowered[...] = jnp.concatenate(tiles, axis=0).astype(bf16)
    copies[1].wait()
    groups = [tiles[g : g + per_group] for g in range(0, clusters, per_group)]
    products = [compress(group, basis, g) for g, group in enumerate(groups)]
    write_payload(payload, [collect(product, per_group) for product in products], [])


def window_place(distance, clusters, me):
    core, chip = me % 2, me // 2
    before, after = 3 - chip % 2, 2 + chip % 2
    slot = [before, jnp.where(core == 0, 4, 1), 0, jnp.where(core == 0, 1, 4), after]
    slab = lax.div(distance, clusters)
    chosen = jnp.zeros_like(distance)
    for s, value in enumerate(slot):
        chosen = jnp.where(slab == s, value, chosen)
    return chosen * clusters + lax.rem(distance, clusters)


def ahead_kernel(
    axis, size, middle, first, rank, near_cols_hbm, near_counts_hbm, far_cols_hbm, blocks_hbm, _,
    places, ahead, token, near_cols, near_counts, far_cols, sems,
):
    half = ahead.shape[0] // 2
    pairs = [(near_cols_hbm, near_cols), (near_counts_hbm, near_counts), (far_cols_hbm, far_cols)]
    for n in range(2):
        span = pl.ds(n * half, half)
        pairs.append((blocks_hbm.at[span, pl.ds(first, ahead.shape[1])], ahead.at[span]))
    copies = [pltpu.make_async_copy(source, to, sems.at[n]) for n, (source, to) in enumerate(pairs)]
    for copy in copies:
        copy.start()
    for copy in copies[:3]:
        copy.wait()
    slots, clusters = near_cols.shape
    me = lax.axis_index(axis)
    every = clusters * size
    distance = near_cols[...] - me * clusters + 2 * clusters
    distance = jnp.where(distance < 0, distance + every, distance)
    distance = jnp.where(distance >= every, distance - every, distance)
    slot = lax.broadcasted_iota(jnp.int32, (slots, clusters), 0)
    live = slot < near_counts[...]
    places[:slots, :] = jnp.where(live, window_place(distance, clusters, me), 5 * clusters) * R
    owner = lax.div(far_cols[...], clusters)
    other_core = (owner ^ me) & 1
    chips = size // 2
    chip = lax.rem(owner // 2 + (chips - middle), chips)
    per_group = LANES // rank
    inside = lax.rem(far_cols[...], clusters)
    tile = (other_core * chips + chip) * (clusters // per_group) + lax.div(inside, per_group)
    places[slots : 2 * slots, :] = tile * R
    places[2 * slots :, :] = ((slot - inside) * rank) & (LANES - 1)
    token[...] = jnp.zeros_like(token)
    for copy in copies[3:]:
        copy.wait()


def prepare_kernel(coupling_hbm, target_hbm, _, high_out, low_out, target_out, coupling, target, sems):
    copies = [
        pltpu.make_async_copy(target_hbm, target, sems.at[0]),
        pltpu.make_async_copy(coupling_hbm, coupling, sems.at[1]),
    ]
    for copy in copies:
        copy.start()
    slots, rank, _, clusters = coupling.shape
    size = rank * clusters
    row = lax.broadcasted_iota(jnp.int32, (size, 1), 0)
    column = lax.broadcasted_iota(jnp.int32, (size, size), 1)
    wanted = lax.rem(row, clusters) * rank + lax.div(row, clusters)
    picks = (column == wanted).astype(bf16)
    copies[0].wait()
    target_out[...] = dot(picks, target[...]).astype(bf16)
    copies[1].wait()
    per_tile = LANES // clusters
    for s in range(rank // per_tile):
        pieces = [
            coupling[:, s * per_tile + p].reshape(slots * rank, clusters) for p in range(per_tile)
        ]
        tile = jnp.concatenate(pieces, axis=1)
        high = tile.astype(bf16)
        high_out[:, s * LANES : (s + 1) * LANES] = high
        low_out[:, s * LANES : (s + 1) * LANES] = (tile - high.astype(f32)).astype(bf16)


def fetch_kernel(slots, blocks_hbm, *refs):
    *_, blocks, token, sems = refs
    chunks = sems.shape[1]
    each = blocks.shape[0] // chunks
    copies, at = [], 0
    for n, (first, count) in enumerate(slots):
        for c in range(chunks):
            clusters = pl.ds(c * each, each)
            copies.append(
                pltpu.make_async_copy(
                    blocks_hbm.at[clusters, pl.ds(first, count)], blocks.at[clusters, pl.ds(at, count)], sems.at[n, c]
                )
            )
        at += count
    for copy in copies:
        copy.start()
    token[...] = jnp.zeros_like(token)
    for copy in copies:
        copy.wait()


def own_kernel(blocks_hbm, own, _, near, blocks, sems):
    chunks = sems.shape[0]
    each = blocks.shape[0] // chunks
    copies = [
        pltpu.make_async_copy(
            blocks_hbm.at[pl.ds(c * each, each), pl.ds(0, 1)], blocks.at[pl.ds(c * each, each)], sems.at[c]
        )
        for c in range(chunks)
    ]
    for copy in copies:
        copy.start()
    for c, copy in enumerate(copies):
        copy.wait()
        for i in range(c * each, (c + 1) * each, 2):
            both = dot(own[pl.ds(i * R, 2 * R), :], jnp.concatenate([blocks[i, 0], blocks[i + 1, 0]], axis=0), (1, 1))
            near[pl.ds(i * R, R), :] = both[:R, :LANES]
            near[pl.ds((i + 1) * R, R), :] = both[R:, LANES:]


def relay_kernel(axis, got, even, odd, _, out):
    me = lax.axis_index(axis)
    devices, each, _ = got.shape
    for device in range(devices):
        out[pl.ds(device * each, each), :] = got[device]
    wants_even = (me // 2 + me) % 2 == 0
    span = pl.ds(devices * each, even.shape[0])

    @pl.when(wants_even)
    def _():
        out[span, :] = even[...]

    @pl.when(jnp.logical_not(wants_even))
    def _():
        out[span, :] = odd[...]


def apply(
    per_group, each, slabs, places, ahead, blocks, swaps, high, low, target, near, far, window, table, finish, started
):
    clusters = near.shape[0] // R
    early = ahead.shape[1]
    first = 0 if started is None else 1
    slots = early + blocks.shape[1] + first
    rank = LANES // per_group
    head = clusters // per_group * R
    rows = slabs[0].shape[0]
    devices = (swaps[0].shape[0] - rows) // each
    for at, slab in enumerate(slabs):
        window[pl.ds(at * rows, rows), :] = slab[...].astype(f32)
    window[pl.ds(len(slabs) * rows, rows), :] = swaps[1][pl.ds(devices * each, rows), :].astype(f32)
    window[pl.ds((len(slabs) + 1) * rows, R), :] = jnp.zeros((R, LANES), f32)
    for part, values in enumerate(swaps):
        for device in range(devices):
            at = (part * devices + device) * head
            table[pl.ds(at, head), :] = values[pl.ds(device * each, head), :].astype(f32)
    lane = lane_ids()

    def fetch(k, i):
        return window[pl.ds(pl.multiple_of(places[k, i], R), R), :]

    def block(k, i):
        if 0 < k <= early:
            return ahead[i, k - 1]
        return blocks[i, max(k - early - first, 0)]

    def pick(i):
        tile = jnp.zeros((R, LANES), f32)
        for k in range(slots):
            found = table[pl.ds(pl.multiple_of(places[slots + k, i], R), R), :]
            tile = jnp.where(lane // rank == k, pltpu.roll(found, places[2 * slots + k, i], 1), tile)
        return tile

    def product(i):
        sources = jnp.concatenate(
            [jnp.concatenate([fetch(k, i), fetch(k, i + 1)], axis=0) for k in range(first, slots)], axis=1
        )
        weights = jnp.concatenate(
            [jnp.concatenate([block(k, i), block(k, i + 1)], axis=0) for k in range(first, slots)], axis=1
        )
        return dot(sources.astype(bf16), weights, (1, 1))

    def settle(i, both):
        parts = [both[:R, :LANES], both[R:, LANES:]]
        if started is not None:
            parts = [part + rows_of(started, i + n) for n, part in enumerate(parts)]
        near[pl.ds(i * R, 2 * R), :] = jnp.concatenate(parts, axis=0)

    def expand(crossed):
        spread = []
        for s in range(rank * clusters // LANES):
            tile = jnp.zeros((R, LANES), f32)
            for n in range(clusters):
                part = crossed[n * R : (n + 1) * R, s * LANES : (s + 1) * LANES]
                tile = jnp.where(lane % clusters == n, part, tile)
            tile_high = tile.astype(bf16).astype(f32)
            for n, source in enumerate((tile_high, tile - tile_high)):
                held = [jnp.where(lane % clusters == c, source, 0.0) for c in range(clusters)]
                spread.append((n, jnp.concatenate(held, axis=0).astype(bf16)))
        return [jnp.concatenate([part for m, part in spread if m == n], axis=1) for n in range(2)]

    pairs = clusters // 2
    middle = pairs // 2
    picked, pending, done = [], None, 0
    for p in range(pairs):
        both = product(2 * p)
        if pending is not None:
            settle(2 * p - 2, pending)
        pending = both
        if p < middle:
            picked += [pick(n) for n in range(4 * p, 4 * p + 4)]
        if p == middle - 1:
            chosen = jnp.concatenate(picked, axis=0).astype(bf16)
            crossed = [dot(chosen, high[...]), dot(chosen, low[...])]
        if p == middle:
            spread = expand(crossed[0] + crossed[1])
            made = [dot(part, target[...]) for part in spread]
        if p == middle + 1:
            far[...] = made[0] + made[1]
        if p > middle + 1:
            ready = min(2 * p, done + 6)
            for n in range(done, ready):
                finish(n)
            done = ready
    settle(clusters - 2, pending)
    for n in range(done, clusters):
        finish(n)


def first_kernel(
    per_group, own, mate, even, odd, places, ahead, blocks, sent, received, high, low, target, b, basis,
    image, lowered, payload, near, far, window, table,
):
    clusters = near.shape[0] // R
    slabs, swaps = (own, mate, even, odd), (sent, received)
    each = clusters // per_group * R
    tiles, products, parts = [], [], []
    sums = [jnp.zeros((R, LANES), f32) for _ in range(3)]

    def finish(i):
        field = rows_of(b, i)
        made = 0.5 * field + (rows_of(near, i) + rows_of(far, i))
        sums[:] = [s + f * g for s, f, g in zip(sums, (field, field, made), (field, made, made))]
        tiles.append(made)
        if i % 2:
            both = jnp.concatenate(tiles[i - 1 :], axis=0)
            image[pl.ds((i - 1) * R, 2 * R), :] = both
            lowered[pl.ds((i - 1) * R, 2 * R), :] = both.astype(bf16)
        if i % per_group == per_group - 1:
            products.append(compress(tiles[-per_group:], basis, i // per_group))
            parts.extend(collect(product, per_group) for product in products[-2:-1])

    apply(
        per_group, each, slabs, places, ahead, blocks, swaps, high, low, target, near, far, window, table, finish, None
    )
    write_payload(payload, parts + [collect(products[-1], per_group)], sums)


def arnoldi_one(bb, bw, ww):
    whole = bb + epsilon
    start_norm = jnp.sqrt(whole)
    scale = 1.0 / start_norm
    v11 = bb / whole
    h11 = (bw * scale) * scale
    uu = jnp.maximum((ww * scale) * scale - 2.0 * h11 * h11 + h11 * h11 * v11, 0.0)
    h21 = jnp.sqrt(uu + epsilon)
    return start_norm, h11, h21, v11, uu / (uu + epsilon), h11 * (1.0 - v11) / h21


def second_kernel(
    per_group, unknowns, own, mate, even, odd, places, ahead, blocks, sent, received, high, low, target, b, image,
    started, candidate, sums_out, near, far, window, table,
):
    clusters = near.shape[0] // R
    head = clusters // per_group * R
    slabs, swaps = (own, mate, even, odd), (sent, received)
    means = read_sums(tails(swaps, own.shape[0], head), 3, unknowns)
    start_norm, h11, h21, _, _, _ = arnoldi_one(*means)
    scale = 1.0 / start_norm
    inverse = 1.0 / h21
    sums = [jnp.zeros((R, LANES), f32) for _ in range(3)]

    def finish(j):
        held = rows_of(image, j) * scale
        first = rows_of(b, j) * scale
        second = (held - h11 * first) * inverse
        made = (0.5 * held + (rows_of(near, j) + rows_of(far, j)) * scale - h11 * held) * inverse
        sums[:] = [s + v * made for s, v in zip(sums, (first, second, made))]
        candidate[pl.ds(j * R, R), :] = made

    each = head + TAIL
    apply(
        per_group, each, slabs, places, ahead, blocks, swaps, high, low, target, near, far, window, table, finish, started
    )
    tile = sums_tile(sums).astype(bf16)
    for device in range(sums_out.shape[0]):
        sums_out[device] = tile


def ready_kernel(per_group, unknowns, b, image, sent, received, _, first, second, known):
    clusters = b.shape[0] // R
    means = read_sums(tails((sent, received), b.shape[0], clusters // per_group * R), 3, unknowns)
    values = arnoldi_one(*means)
    start_norm, h11, h21, _, _, _ = values
    lane = lane_ids()
    tile = jnp.zeros((R, LANES), f32)
    for n, value in enumerate(values):
        tile = jnp.where(lane == n, value, tile)
    known[...] = tile
    scale, inverse = 1.0 / start_norm, 1.0 / h21
    for j in range(clusters):
        span = pl.ds(j * R, R)
        one = b[span, :] * scale
        first[span, :] = one
        second[span, :] = (image[span, :] * scale - h11 * one) * inverse


def finish_kernel(unknowns, first, second, candidate, known, got, solution_out, next_out):
    clusters = first.shape[0] // R
    start_norm, h11, h21, v11, v22, v12 = [known[:, n : n + 1] for n in range(6)]
    h12, h22, ww = read_sums([got[device] for device in range(got.shape[0])], 3, unknowns)
    uu = ww - 2.0 * (h12 * h12 + h22 * h22) + h12 * h12 * v11 + h22 * h22 * v22 + 2.0 * h12 * h22 * v12
    h32 = jnp.sqrt(jnp.maximum(uu, 0.0) + epsilon)
    g11 = h11 * h11 + h21 * h21
    g12 = h11 * h12 + h21 * h22
    g22 = h12 * h12 + h22 * h22 + h32 * h32
    t1, t2 = start_norm * h11, start_norm * h12
    det = g11 * g22 - g12 * g12
    y1 = (g22 * t1 - g12 * t2) / det
    y2 = (g11 * t2 - g12 * t1) / det
    last = 1.0 / h32
    for j in range(clusters):
        span = slice(j * LANES, (j + 1) * LANES)
        one, two = rows_of(first, j), rows_of(second, j)
        solution_out[:, span] = y1 * one + y2 * two
        next_out[:, span] = (rows_of(candidate, j) - h12 * one - h22 * two) * last


def swapped(block, partner):
    return lax.ppermute(block, "rows", [(i, partner(i)) for i in range(lax.axis_size("rows"))])


def core_mate(i):
    return i ^ 1


def even_mate(i):
    return i ^ 2


def odd_mate(i):
    chip = i // 2
    other = chip + 1 if chip % 2 else chip - 1
    return 2 * (other % (lax.axis_size("rows") // 2)) + i % 2


def sends_of(block):
    return [block] + [swapped(block, partner) for partner in (core_mate, even_mate, odd_mate)]


def on_device(
    right_sides, near_blocks, near_cols, near_counts, basis_in, target_basis, coupling, far_cols
):
    width = right_sides.shape[1]
    clusters, slots = near_cols.shape
    rank = basis_in.shape[1]
    per_group = LANES // rank
    head = clusters // per_group * R
    size = lax.axis_size("rows")
    unknowns = float(width * size)
    rows = clusters * R

    def shape(*dims, dtype=f32):
        return jax.ShapeDtypeStruct(dims, dtype)

    def scratch(*dims, dtype=f32):
        return pltpu.VMEM(dims, dtype)

    def in_hbm(array):
        return pltpu.with_memory_space_constraint(array, pltpu.HBM)

    def call(kernel, name, out, ins, *args, scratch_shapes=()):
        return pl.pallas_call(
            kernel, out_shape=out, in_specs=ins, out_specs=jax.tree.map(lambda _: VMEM, out),
            scratch_shapes=scratch_shapes, compiler_params=PARAMS, name=name,
        )(*args)

    chips = size // 2
    middle = chips // 4
    order = [(middle + n) % chips for n in range(chips)]

    def gather(block):
        groups = [[2 * chip + core for chip in order] for core in range(2)]
        return lax.all_to_all(block, "rows", 0, 0, axis_index_groups=groups)

    def exchange(block):
        group = [2 * chip + core for chip in order for core in range(2)]
        return lax.all_to_all(block, "rows", 0, 0, axis_index_groups=[group])

    field, basis, lowered, payload = call(
        functools.partial(start_kernel, per_group), "start",
        (
            shape(rows, LANES), shape(clusters * rank, LANES, dtype=bf16), shape(rows, LANES, dtype=bf16),
            shape(size // 2, head, LANES, dtype=bf16),
        ),
        [HBM] * 2, in_hbm(right_sides), in_hbm(basis_in.reshape(clusters * rank, LANES)),
        scratch_shapes=[scratch(R, width), pltpu.SemaphoreType.DMA((2,))],
    )
    got = gather(payload)
    held = sends_of(lowered)

    blocks = in_hbm(near_blocks)
    early = 2

    def fetch(name, ranges, chunks, *behind):
        count = sum(count for _, count in ranges)
        here, token = call(
            functools.partial(fetch_kernel, ranges), name,
            (pltpu.VMEM((clusters, count, LANES, LANES), bf16), shape(R, LANES)),
            [HBM] + [ANY] * len(behind), blocks, *behind,
            scratch_shapes=[pltpu.SemaphoreType.DMA((len(ranges), chunks))],
        )
        return pltpu.with_memory_space_constraint(here, pltpu.VMEM), token

    def arrived(got, held, ranges, behind):
        rest, token = fetch("fetch", ranges, 4, got, behind)
        sent = call(
            functools.partial(relay_kernel, "rows"), "relay",
            shape(got.shape[0] * got.shape[1] + rows, LANES, dtype=bf16), [VMEM] * 3 + [ANY], got, *held[2:], token
        )
        return ahead, rest, sent, swapped(sent, core_mate)

    late = (1 + early, slots - 1 - early)
    places, ahead, token = call(
        functools.partial(ahead_kernel, "rows", size, middle, 1, rank), "ahead",
        (
            shape(3 * slots, clusters, dtype=jnp.int32), pltpu.VMEM((clusters, early, LANES, LANES), bf16),
            shape(R, LANES),
        ),
        [HBM] * 4 + [ANY], in_hbm(near_cols.T), in_hbm(near_counts.reshape(1, clusters)), in_hbm(far_cols.T), blocks,
        held[1],
        scratch_shapes=[
            scratch(slots, clusters, dtype=jnp.int32), scratch(1, clusters, dtype=jnp.int32),
            scratch(slots, clusters, dtype=jnp.int32), pltpu.SemaphoreType.DMA((5,)),
        ],
    )
    ahead = pltpu.with_memory_space_constraint(ahead, pltpu.VMEM)
    here = arrived(got, held, [(0, 1), late], token)
    made = call(
        prepare_kernel, "prepare",
        (
            shape(slots * rank, rank * clusters, dtype=bf16),
            shape(slots * rank, rank * clusters, dtype=bf16),
            shape(rank * clusters, LANES, dtype=bf16),
        ),
        [HBM] * 2 + [ANY],
        in_hbm(jnp.transpose(coupling, (1, 2, 3, 0))), in_hbm(target_basis.reshape(clusters * rank, LANES)), here[2],
        scratch_shapes=[
            scratch(slots, rank, rank, clusters), scratch(clusters * rank, LANES, dtype=bf16),
            pltpu.SemaphoreType.DMA((2,)),
        ],
    )
    kept = [scratch(rows, LANES), scratch(rows, LANES), scratch(5 * rows + R, LANES), scratch(size * head, LANES)]
    operands = [VMEM] * 4 + [SMEM] + [VMEM] * 9
    image, lowered, payload = call(
        functools.partial(first_kernel, per_group), "operator_one",
        (
            shape(rows, LANES), shape(rows, LANES, dtype=bf16),
            shape(size // 2, head + TAIL, LANES, dtype=bf16),
        ),
        operands, *held, places, *here, *made, field, basis, scratch_shapes=kept,
    )
    got = gather(payload)
    held = sends_of(lowered)
    started = call(
        own_kernel, "own", shape(rows, LANES), [HBM, VMEM, ANY], blocks, lowered, held[1],
        scratch_shapes=[scratch(clusters, 1, LANES, LANES, dtype=bf16), pltpu.SemaphoreType.DMA((4,))],
    )
    here = arrived(got, held, [late], started)
    candidate, sums = call(
        functools.partial(second_kernel, per_group, unknowns), "operator_two",
        (shape(rows, LANES), shape(size, R, LANES, dtype=bf16)),
        operands + [VMEM], *held, places, *here, *made, field, image, started, scratch_shapes=kept,
    )
    got = exchange(sums)
    first, second, known = call(
        functools.partial(ready_kernel, per_group, unknowns), "ready",
        (shape(rows, LANES), shape(rows, LANES), shape(R, LANES)),
        [VMEM] * 4 + [ANY], field, image, *here[2:], sums,
    )
    return call(
        functools.partial(finish_kernel, unknowns), "finish", (shape(R, width), shape(R, width)),
        [VMEM] * 5, first, second, candidate, known, got,
    )


def solution(mesh):
    return jax.shard_map(
        on_device,
        mesh=mesh,
        in_specs=(
            P("groups", "rows"),
            P("rows", None, None, None),
            P("rows", None),
            P("rows"),
            P("rows", None, None),
            P("rows", None, None),
            P("rows", None, None, None),
            P("rows", None),
        ),
        out_specs=(P("groups", "rows"), P("groups", "rows")),
        check_vma=False,
    )
```

```python
import functools

import jax
import jax.numpy as jnp
from jax import lax
from jax.experimental import pallas as pl
from jax.experimental.pallas import tpu as pltpu
from jax.sharding import PartitionSpec as P

epsilon = 1e-06
f32, bf16 = jnp.float32, jnp.bfloat16
VMEM = pl.BlockSpec(memory_space=pltpu.VMEM)
SMEM = pl.BlockSpec(memory_space=pltpu.SMEM)
HBM = pl.BlockSpec(memory_space=pltpu.HBM)
ANY = pl.BlockSpec(memory_space=pl.ANY)
R = 8
LANES = 128
SUM_SLOTS = 8
TAIL = 16
PARAMS = pltpu.CompilerParams(vmem_limit_bytes=24 * 1024 * 1024)


def lane_ids(rows=R):
    return lax.broadcasted_iota(jnp.int32, (rows, LANES), 1)


def rows_of(ref, j):
    return ref[pl.ds(j * R, R), :]


def dot(a, b, contract=(1, 0)):
    return lax.dot_general(a, b, (((contract[0],), (contract[1],)), ((), ())), preferred_element_type=f32)


def sums_tile(sums):
    lane = lane_ids()
    tile = jnp.zeros((R, LANES), f32)
    for t, partial in enumerate(sums):
        total = jnp.sum(partial, axis=1, keepdims=True)
        high = total.astype(bf16).astype(f32)
        middle = (total - high).astype(bf16).astype(f32)
        low = total - high - middle
        for part, value in enumerate((high, middle, low)):
            tile = jnp.where(lane == part * SUM_SLOTS + t, value, tile)
    return tile


def read_sums(parts, count, unknowns):
    total = jnp.zeros((R, LANES), f32)
    for part in parts:
        total = total + part.astype(f32)[:R]
    return [
        sum(total[:, p * SUM_SLOTS + t : p * SUM_SLOTS + t + 1] for p in range(3)) * (1.0 / unknowns)
        for t in range(count)
    ]


def tails(swaps, rows, head):
    each = head + TAIL
    return [
        values[pl.ds(device * each + head, TAIL), :]
        for values in swaps
        for device in range((values.shape[0] - rows) // each)
    ]


def compress(tiles, basis, group):
    stacked = jnp.concatenate(tiles, axis=0)
    high = stacked.astype(bf16)
    low = (stacked - high.astype(f32)).astype(bf16)
    return dot(jnp.concatenate([high, low], axis=0), basis[pl.ds(group * LANES, LANES), :], (1, 1))


def collect(products, per_group):
    rows = per_group * R
    both = products[:rows] + products[rows:]
    lane = lane_ids()
    tile = jnp.zeros((R, LANES), f32)
    for m in range(per_group):
        tile = jnp.where(lane // (LANES // per_group) == m, both[m * R : (m + 1) * R], tile)
    return tile


def write_payload(payload, parts, sums):
    if sums:
        parts = parts + [sums_tile(sums), jnp.zeros((TAIL - R, LANES), f32)]
    block = jnp.concatenate(parts, axis=0).astype(bf16)
    for device in range(payload.shape[0]):
        payload[device] = block


def start_kernel(per_group, b_hbm, basis_hbm, field, basis, lowered, payload, b, sems):
    copies = [
        pltpu.make_async_copy(b_hbm, b, sems.at[0]),
        pltpu.make_async_copy(basis_hbm, basis, sems.at[1]),
    ]
    for copy in copies:
        copy.start()
    for copy in copies:
        copy.wait()
    clusters = b.shape[1] // LANES
    tiles = [b[:, j * LANES : (j + 1) * LANES] for j in range(clusters)]
    field[...] = jnp.concatenate(tiles, axis=0)
    lowered[...] = jnp.concatenate(tiles, axis=0).astype(bf16)
    groups = [tiles[g : g + per_group] for g in range(0, clusters, per_group)]
    products = [compress(group, basis, g) for g, group in enumerate(groups)]
    write_payload(payload, [collect(product, per_group) for product in products], [])


def window_place(distance, clusters, me):
    core, chip = me % 2, me // 2
    before, after = 3 - chip % 2, 2 + chip % 2
    slot = [before, jnp.where(core == 0, 4, 1), 0, jnp.where(core == 0, 1, 4), after]
    slab = lax.div(distance, clusters)
    chosen = jnp.zeros_like(distance)
    for s, value in enumerate(slot):
        chosen = jnp.where(slab == s, value, chosen)
    return chosen * clusters + lax.rem(distance, clusters)


def prepare_kernel(
    axis, size, middle, near_cols_hbm, near_counts_hbm, far_cols_hbm, coupling_hbm, target_hbm, _,
    places, high_out, low_out, target_out, near_cols, near_counts, far_cols, coupling, target, sems,
):
    slots, rank, _, clusters = coupling.shape
    per_tile = LANES // clusters
    parts = [pl.ds(p, per_tile) for p in range(0, rank, per_tile)]
    pairs = (
        (near_cols_hbm, near_cols), (near_counts_hbm, near_counts), (far_cols_hbm, far_cols),
        (target_hbm, target), *((coupling_hbm.at[:, part], coupling.at[:, part]) for part in parts),
    )
    copies = [pltpu.make_async_copy(source, to, sems.at[n]) for n, (source, to) in enumerate(pairs)]
    for copy in copies:
        copy.start()
    for copy in copies[:3]:
        copy.wait()
    me = lax.axis_index(axis)
    every = clusters * size
    distance = near_cols[...] - me * clusters + 2 * clusters
    distance = jnp.where(distance < 0, distance + every, distance)
    distance = jnp.where(distance >= every, distance - every, distance)
    live = lax.broadcasted_iota(jnp.int32, (slots, clusters), 0) < near_counts[...]
    places[:slots, :] = jnp.where(live, window_place(distance, clusters, me), 5 * clusters) * R
    owner = lax.div(far_cols[...], clusters)
    other_core = (owner ^ me) & 1
    chips = size // 2
    chip = lax.rem(owner // 2 + (chips - middle), chips)
    per_group = LANES // rank
    inside = lax.rem(far_cols[...], clusters)
    tile = (other_core * chips + chip) * (clusters // per_group) + lax.div(inside, per_group)
    places[slots : 2 * slots, :] = tile * R
    slot = lax.broadcasted_iota(jnp.int32, (slots, clusters), 0)
    places[2 * slots :, :] = ((slot - inside) * rank) & (LANES - 1)
    size = rank * clusters
    row = lax.broadcasted_iota(jnp.int32, (size, 1), 0)
    column = lax.broadcasted_iota(jnp.int32, (size, size), 1)
    wanted = lax.rem(row, clusters) * rank + lax.div(row, clusters)
    copies[3].wait()
    target_out[...] = dot((column == wanted).astype(bf16), target[...]).astype(bf16)
    for s, copy in enumerate(copies[4:]):
        copy.wait()
        pieces = [
            coupling[:, s * per_tile + p].reshape(slots * rank, clusters) for p in range(per_tile)
        ]
        tile = jnp.concatenate(pieces, axis=1)
        high = tile.astype(bf16)
        high_out[:, s * LANES : (s + 1) * LANES] = high
        low_out[:, s * LANES : (s + 1) * LANES] = (tile - high.astype(f32)).astype(bf16)


def fetch_kernel(slots, blocks_hbm, *refs):
    *_, blocks, token, sems = refs
    chunks = sems.shape[1]
    each = blocks.shape[0] // chunks
    copies, at = [], 0
    for n, (first, count) in enumerate(slots):
        for c in range(chunks):
            clusters = pl.ds(c * each, each)
            copies.append(
                pltpu.make_async_copy(
                    blocks_hbm.at[clusters, pl.ds(first, count)], blocks.at[clusters, pl.ds(at, count)], sems.at[n, c]
                )
            )
        at += count
    for copy in copies:
        copy.start()
    token[...] = jnp.zeros_like(token)
    for copy in copies:
        copy.wait()


def own_kernel(blocks_hbm, own, _, near, blocks, sems):
    chunks = sems.shape[0]
    each = blocks.shape[0] // chunks
    copies = [
        pltpu.make_async_copy(
            blocks_hbm.at[pl.ds(c * each, each), pl.ds(0, 1)], blocks.at[pl.ds(c * each, each)], sems.at[c]
        )
        for c in range(chunks)
    ]
    for copy in copies:
        copy.start()
    for c, copy in enumerate(copies):
        copy.wait()
        for i in range(c * each, (c + 1) * each, 2):
            both = dot(own[pl.ds(i * R, 2 * R), :], jnp.concatenate([blocks[i, 0], blocks[i + 1, 0]], axis=0), (1, 1))
            near[pl.ds(i * R, R), :] = both[:R, :LANES]
            near[pl.ds((i + 1) * R, R), :] = both[R:, LANES:]


def relay_kernel(axis, got, even, odd, _, out):
    me = lax.axis_index(axis)
    devices, each, _ = got.shape
    for device in range(devices):
        out[pl.ds(device * each, each), :] = got[device]
    wants_even = (me // 2 + me) % 2 == 0
    span = pl.ds(devices * each, even.shape[0])

    @pl.when(wants_even)
    def _():
        out[span, :] = even[...]

    @pl.when(jnp.logical_not(wants_even))
    def _():
        out[span, :] = odd[...]


def apply(
    per_group, each, slabs, places, ahead, blocks, swaps, high, low, target, near, far, window, table, finish, started
):
    clusters = near.shape[0] // R
    early = ahead.shape[1]
    first = 0 if started is None else 1
    slots = early + blocks.shape[1] + first
    rank = LANES // per_group
    head = clusters // per_group * R
    rows = slabs[0].shape[0]
    devices = (swaps[0].shape[0] - rows) // each
    for at, slab in enumerate(slabs):
        window[pl.ds(at * rows, rows), :] = slab[...].astype(f32)
    window[pl.ds(len(slabs) * rows, rows), :] = swaps[1][pl.ds(devices * each, rows), :].astype(f32)
    window[pl.ds((len(slabs) + 1) * rows, R), :] = jnp.zeros((R, LANES), f32)
    for part, values in enumerate(swaps):
        for device in range(devices):
            at = (part * devices + device) * head
            table[pl.ds(at, head), :] = values[pl.ds(device * each, head), :].astype(f32)
    lane = lane_ids()

    def fetch(k, i):
        return window[pl.ds(pl.multiple_of(places[k, i], R), R), :]

    def block(k, i):
        if 0 < k <= early:
            return ahead[i, k - 1]
        return blocks[i, max(k - early - first, 0)]

    def pick(i):
        tile = jnp.zeros((R, LANES), f32)
        for k in range(slots):
            found = table[pl.ds(pl.multiple_of(places[slots + k, i], R), R), :]
            tile = jnp.where(lane // rank == k, pltpu.roll(found, places[2 * slots + k, i], 1), tile)
        return tile

    def product(i):
        sources = jnp.concatenate(
            [jnp.concatenate([fetch(k, i), fetch(k, i + 1)], axis=0) for k in range(first, slots)], axis=1
        )
        weights = jnp.concatenate(
            [jnp.concatenate([block(k, i), block(k, i + 1)], axis=0) for k in range(first, slots)], axis=1
        )
        return dot(sources.astype(bf16), weights, (1, 1))

    def settle(i, both):
        parts = [both[:R, :LANES], both[R:, LANES:]]
        if started is not None:
            parts = [part + rows_of(started, i + n) for n, part in enumerate(parts)]
        near[pl.ds(i * R, 2 * R), :] = jnp.concatenate(parts, axis=0)

    def expand(crossed):
        spread = []
        for s in range(rank * clusters // LANES):
            tile = jnp.zeros((R, LANES), f32)
            for n in range(clusters):
                part = crossed[n * R : (n + 1) * R, s * LANES : (s + 1) * LANES]
                tile = jnp.where(lane % clusters == n, part, tile)
            tile_high = tile.astype(bf16).astype(f32)
            for n, source in enumerate((tile_high, tile - tile_high)):
                held = [jnp.where(lane % clusters == c, source, 0.0) for c in range(clusters)]
                spread.append((n, jnp.concatenate(held, axis=0).astype(bf16)))
        return [jnp.concatenate([part for m, part in spread if m == n], axis=1) for n in range(2)]

    pairs = clusters // 2
    middle = pairs // 2
    picked, pending, done = [], None, 0
    for p in range(pairs):
        both = product(2 * p)
        if pending is not None:
            settle(2 * p - 2, pending)
        pending = both
        if p < middle:
            picked += [pick(n) for n in range(4 * p, 4 * p + 4)]
        if p == middle - 1:
            chosen = jnp.concatenate(picked, axis=0).astype(bf16)
            crossed = [dot(chosen, high[...]), dot(chosen, low[...])]
        if p == middle:
            spread = expand(crossed[0] + crossed[1])
            made = [dot(part, target[...]) for part in spread]
        if p == middle + 1:
            far[...] = made[0] + made[1]
        if p > middle + 1:
            ready = min(2 * p, done + 6)
            for n in range(done, ready):
                finish(n)
            done = ready
    settle(clusters - 2, pending)
    for n in range(done, clusters):
        finish(n)


def first_kernel(
    per_group, own, mate, even, odd, places, ahead, blocks, sent, received, high, low, target, b, basis,
    image, lowered, payload, near, far, window, table,
):
    clusters = near.shape[0] // R
    slabs, swaps = (own, mate, even, odd), (sent, received)
    each = clusters // per_group * R
    tiles, products, parts = [], [], []
    sums = [jnp.zeros((R, LANES), f32) for _ in range(3)]

    def finish(i):
        field = rows_of(b, i)
        made = 0.5 * field + (rows_of(near, i) + rows_of(far, i))
        sums[:] = [s + f * g for s, f, g in zip(sums, (field, field, made), (field, made, made))]
        tiles.append(made)
        if i % 2:
            both = jnp.concatenate(tiles[i - 1 :], axis=0)
            image[pl.ds((i - 1) * R, 2 * R), :] = both
            lowered[pl.ds((i - 1) * R, 2 * R), :] = both.astype(bf16)
        if i % per_group == per_group - 1:
            products.append(compress(tiles[-per_group:], basis, i // per_group))
            parts.extend(collect(product, per_group) for product in products[-2:-1])

    apply(
        per_group, each, slabs, places, ahead, blocks, swaps, high, low, target, near, far, window, table, finish, None
    )
    write_payload(payload, parts + [collect(products[-1], per_group)], sums)


def arnoldi_one(bb, bw, ww):
    whole = bb + epsilon
    start_norm = jnp.sqrt(whole)
    scale = 1.0 / start_norm
    v11 = bb / whole
    h11 = (bw * scale) * scale
    uu = jnp.maximum((ww * scale) * scale - 2.0 * h11 * h11 + h11 * h11 * v11, 0.0)
    h21 = jnp.sqrt(uu + epsilon)
    return start_norm, h11, h21, v11, uu / (uu + epsilon), h11 * (1.0 - v11) / h21


def second_kernel(
    per_group, unknowns, own, mate, even, odd, places, ahead, blocks, sent, received, high, low, target, b, image,
    started, candidate, sums_out, known, near, far, window, table,
):
    clusters = near.shape[0] // R
    head = clusters // per_group * R
    slabs, swaps = (own, mate, even, odd), (sent, received)
    means = read_sums(tails(swaps, own.shape[0], head), 3, unknowns)
    values = arnoldi_one(*means)
    start_norm, h11, h21, _, _, _ = values
    lane = lane_ids()
    tile = jnp.zeros((R, LANES), f32)
    for n, value in enumerate(values):
        tile = jnp.where(lane == n, value, tile)
    known[...] = tile
    scale = 1.0 / start_norm
    inverse = 1.0 / h21
    sums = [jnp.zeros((R, LANES), f32) for _ in range(3)]

    def finish(j):
        held = rows_of(image, j) * scale
        first = rows_of(b, j) * scale
        second = (held - h11 * first) * inverse
        made = (0.5 * held + (rows_of(near, j) + rows_of(far, j)) * scale - h11 * held) * inverse
        sums[:] = [s + v * made for s, v in zip(sums, (first, second, made))]
        candidate[pl.ds(j * R, R), :] = made

    each = head + TAIL
    apply(
        per_group, each, slabs, places, ahead, blocks, swaps, high, low, target, near, far, window, table, finish, started
    )
    tile = sums_tile(sums).astype(bf16)
    for device in range(sums_out.shape[0]):
        sums_out[device] = tile


def finish_kernel(unknowns, b, image, candidate, known, got, solution_out, next_out):
    clusters = b.shape[0] // R
    start_norm, h11, h21, v11, v22, v12 = [known[:, n : n + 1] for n in range(6)]
    h12, h22, ww = read_sums([got[device] for device in range(got.shape[0])], 3, unknowns)
    uu = ww - 2.0 * (h12 * h12 + h22 * h22) + h12 * h12 * v11 + h22 * h22 * v22 + 2.0 * h12 * h22 * v12
    h32 = jnp.sqrt(jnp.maximum(uu, 0.0) + epsilon)
    g11 = h11 * h11 + h21 * h21
    g12 = h11 * h12 + h21 * h22
    g22 = h12 * h12 + h22 * h22 + h32 * h32
    t1, t2 = start_norm * h11, start_norm * h12
    det = g11 * g22 - g12 * g12
    y1 = (g22 * t1 - g12 * t2) / det
    y2 = (g11 * t2 - g12 * t1) / det
    scale, inverse, last = 1.0 / start_norm, 1.0 / h21, 1.0 / h32
    for j in range(clusters):
        span = slice(j * LANES, (j + 1) * LANES)
        first = rows_of(b, j) * scale
        second = (rows_of(image, j) * scale - h11 * first) * inverse
        solution_out[:, span] = y1 * first + y2 * second
        next_out[:, span] = (rows_of(candidate, j) - h12 * first - h22 * second) * last


def swapped(block, partner):
    return lax.ppermute(block, "rows", [(i, partner(i)) for i in range(lax.axis_size("rows"))])


def core_mate(i):
    return i ^ 1


def even_mate(i):
    return i ^ 2


def odd_mate(i):
    chip = i // 2
    other = chip + 1 if chip % 2 else chip - 1
    return 2 * (other % (lax.axis_size("rows") // 2)) + i % 2


def sends_of(block):
    return [block] + [swapped(block, partner) for partner in (core_mate, even_mate, odd_mate)]


def on_device(
    right_sides, near_blocks, near_cols, near_counts, basis_in, target_basis, coupling, far_cols
):
    width = right_sides.shape[1]
    clusters, slots = near_cols.shape
    rank = basis_in.shape[1]
    per_group = LANES // rank
    head = clusters // per_group * R
    size = lax.axis_size("rows")
    unknowns = float(width * size)
    rows = clusters * R

    def shape(*dims, dtype=f32):
        return jax.ShapeDtypeStruct(dims, dtype)

    def scratch(*dims, dtype=f32):
        return pltpu.VMEM(dims, dtype)

    def in_hbm(array):
        return pltpu.with_memory_space_constraint(array, pltpu.HBM)

    def call(kernel, name, out, ins, *args, scratch_shapes=()):
        return pl.pallas_call(
            kernel, out_shape=out, in_specs=ins, out_specs=jax.tree.map(lambda _: VMEM, out),
            scratch_shapes=scratch_shapes, compiler_params=PARAMS, name=name,
        )(*args)

    chips = size // 2
    middle = chips // 4 + 1
    order = [(middle + n) % chips for n in range(chips)]

    def gather(block):
        groups = [[2 * chip + core for chip in order] for core in range(2)]
        return lax.all_to_all(block, "rows", 0, 0, axis_index_groups=groups)

    def exchange(block):
        group = [2 * chip + core for chip in order for core in range(2)]
        return lax.all_to_all(block, "rows", 0, 0, axis_index_groups=[group])

    field, basis, lowered, payload = call(
        functools.partial(start_kernel, per_group), "start",
        (
            shape(rows, LANES), shape(clusters * rank, LANES, dtype=bf16), shape(rows, LANES, dtype=bf16),
            shape(size // 2, head, LANES, dtype=bf16),
        ),
        [HBM] * 2, in_hbm(right_sides), in_hbm(basis_in.reshape(clusters * rank, LANES)),
        scratch_shapes=[scratch(R, width), pltpu.SemaphoreType.DMA((2,))],
    )
    got = gather(payload)
    held = sends_of(lowered)

    blocks = in_hbm(near_blocks)
    early = 2

    def fetch(name, ranges, chunks, *behind):
        count = sum(count for _, count in ranges)
        here, token = call(
            functools.partial(fetch_kernel, ranges), name,
            (pltpu.VMEM((clusters, count, LANES, LANES), bf16), shape(R, LANES)),
            [HBM] + [ANY] * len(behind), blocks, *behind,
            scratch_shapes=[pltpu.SemaphoreType.DMA((len(ranges), chunks))],
        )
        return pltpu.with_memory_space_constraint(here, pltpu.VMEM), token

    def arrived(got, held, ranges, behind):
        rest, token = fetch("fetch", ranges, 4, got, behind)
        sent = call(
            functools.partial(relay_kernel, "rows"), "relay",
            shape(got.shape[0] * got.shape[1] + rows, LANES, dtype=bf16), [VMEM] * 3 + [ANY], got, *held[2:], token
        )
        return ahead, rest, sent, swapped(sent, core_mate)

    late = (1 + early, slots - 1 - early)
    ahead, token = fetch("ahead", [(1, early)], 2, held[1])
    here = arrived(got, held, [(0, 1), late], token)
    prepared = call(
        functools.partial(prepare_kernel, "rows", size, middle), "prepare",
        (
            shape(3 * slots, clusters, dtype=jnp.int32),
            shape(slots * rank, rank * clusters, dtype=bf16),
            shape(slots * rank, rank * clusters, dtype=bf16),
            shape(rank * clusters, LANES, dtype=bf16),
        ),
        [HBM] * 5 + [ANY], in_hbm(near_cols.T), in_hbm(near_counts.reshape(1, clusters)), in_hbm(far_cols.T),
        in_hbm(jnp.transpose(coupling, (1, 2, 3, 0))), in_hbm(target_basis.reshape(clusters * rank, LANES)), here[2],
        scratch_shapes=[
            scratch(slots, clusters, dtype=jnp.int32), scratch(1, clusters, dtype=jnp.int32),
            scratch(slots, clusters, dtype=jnp.int32),
            scratch(slots, rank, rank, clusters), scratch(clusters * rank, LANES, dtype=bf16),
            pltpu.SemaphoreType.DMA((4 + rank * clusters // LANES,)),
        ],
    )
    places, *made = prepared
    kept = [scratch(rows, LANES), scratch(rows, LANES), scratch(5 * rows + R, LANES), scratch(size * head, LANES)]
    operands = [VMEM] * 4 + [SMEM] + [VMEM] * 9
    image, lowered, payload = call(
        functools.partial(first_kernel, per_group), "operator_one",
        (
            shape(rows, LANES), shape(rows, LANES, dtype=bf16),
            shape(size // 2, head + TAIL, LANES, dtype=bf16),
        ),
        operands, *held, places, *here, *made, field, basis, scratch_shapes=kept,
    )
    got = gather(payload)
    held = sends_of(lowered)
    started = call(
        own_kernel, "own", shape(rows, LANES), [HBM, VMEM, ANY], blocks, lowered, held[1],
        scratch_shapes=[scratch(clusters, 1, LANES, LANES, dtype=bf16), pltpu.SemaphoreType.DMA((4,))],
    )
    here = arrived(got, held, [late], started)
    candidate, sums, known = call(
        functools.partial(second_kernel, per_group, unknowns), "operator_two",
        (shape(rows, LANES), shape(size, R, LANES, dtype=bf16), shape(R, LANES)),
        operands + [VMEM], *held, places, *here, *made, field, image, started, scratch_shapes=kept,
    )
    return call(
        functools.partial(finish_kernel, unknowns), "finish", (shape(R, width), shape(R, width)),
        [VMEM] * 5, field, image, candidate, known, exchange(sums),
    )


def solution(mesh):
    return jax.shard_map(
        on_device,
        mesh=mesh,
        in_specs=(
            P("groups", "rows"),
            P("rows", None, None, None),
            P("rows", None),
            P("rows"),
            P("rows", None, None),
            P("rows", None, None),
            P("rows", None, None, None),
            P("rows", None),
        ),
        out_specs=(P("groups", "rows"), P("groups", "rows")),
        check_vma=False,
    )
```

```python
import functools

import jax
import jax.numpy as jnp
from jax import lax
from jax.experimental import pallas as pl
from jax.experimental.pallas import tpu as pltpu
from jax.sharding import PartitionSpec as P

epsilon = 1e-06
f32, bf16 = jnp.float32, jnp.bfloat16
VMEM = pl.BlockSpec(memory_space=pltpu.VMEM)
SMEM = pl.BlockSpec(memory_space=pltpu.SMEM)
HBM = pl.BlockSpec(memory_space=pltpu.HBM)
ANY = pl.BlockSpec(memory_space=pl.ANY)
R = 8
LANES = 128
SUM_SLOTS = 8
TAIL = 16
PARAMS = pltpu.CompilerParams(vmem_limit_bytes=24 * 1024 * 1024)


def lane_ids(rows=R):
    return lax.broadcasted_iota(jnp.int32, (rows, LANES), 1)


def rows_of(ref, j):
    return ref[pl.ds(j * R, R), :]


def dot(a, b, contract=(1, 0)):
    return lax.dot_general(a, b, (((contract[0],), (contract[1],)), ((), ())), preferred_element_type=f32)


def sums_tile(sums):
    lane = lane_ids()
    tile = jnp.zeros((R, LANES), f32)
    for t, partial in enumerate(sums):
        total = jnp.sum(partial, axis=1, keepdims=True)
        high = total.astype(bf16).astype(f32)
        middle = (total - high).astype(bf16).astype(f32)
        low = total - high - middle
        for part, value in enumerate((high, middle, low)):
            tile = jnp.where(lane == part * SUM_SLOTS + t, value, tile)
    return tile


def read_sums(parts, count, unknowns):
    total = jnp.zeros((R, LANES), f32)
    for part in parts:
        total = total + part.astype(f32)[:R]
    return [
        sum(total[:, p * SUM_SLOTS + t : p * SUM_SLOTS + t + 1] for p in range(3)) * (1.0 / unknowns)
        for t in range(count)
    ]


def tails(swaps, rows, head):
    each = head + TAIL
    return [
        values[pl.ds(device * each + head, TAIL), :]
        for values in swaps
        for device in range((values.shape[0] - rows) // each)
    ]


def compress(tiles, basis, group):
    stacked = jnp.concatenate(tiles, axis=0)
    high = stacked.astype(bf16)
    low = (stacked - high.astype(f32)).astype(bf16)
    return dot(jnp.concatenate([high, low], axis=0), basis[pl.ds(group * LANES, LANES), :], (1, 1))


def collect(products, per_group):
    rows = per_group * R
    both = products[:rows] + products[rows:]
    lane = lane_ids()
    tile = jnp.zeros((R, LANES), f32)
    for m in range(per_group):
        tile = jnp.where(lane // (LANES // per_group) == m, both[m * R : (m + 1) * R], tile)
    return tile


def write_payload(payload, parts, sums):
    if sums:
        parts = parts + [sums_tile(sums), jnp.zeros((TAIL - R, LANES), f32)]
    block = jnp.concatenate(parts, axis=0).astype(bf16)
    for device in range(payload.shape[0]):
        payload[device] = block


def start_kernel(per_group, b_hbm, basis_hbm, field, basis, lowered, payload, b, sems):
    copies = [
        pltpu.make_async_copy(b_hbm, b, sems.at[0]),
        pltpu.make_async_copy(basis_hbm, basis, sems.at[1]),
    ]
    for copy in copies:
        copy.start()
    for copy in copies:
        copy.wait()
    clusters = b.shape[1] // LANES
    tiles = [b[:, j * LANES : (j + 1) * LANES] for j in range(clusters)]
    field[...] = jnp.concatenate(tiles, axis=0)
    lowered[...] = jnp.concatenate(tiles, axis=0).astype(bf16)
    groups = [tiles[g : g + per_group] for g in range(0, clusters, per_group)]
    products = [compress(group, basis, g) for g, group in enumerate(groups)]
    write_payload(payload, [collect(product, per_group) for product in products], [])


def window_place(distance, clusters, me):
    core, chip = me % 2, me // 2
    before, after = 3 - chip % 2, 2 + chip % 2
    slot = [before, jnp.where(core == 0, 4, 1), 0, jnp.where(core == 0, 1, 4), after]
    slab = lax.div(distance, clusters)
    chosen = jnp.zeros_like(distance)
    for s, value in enumerate(slot):
        chosen = jnp.where(slab == s, value, chosen)
    return chosen * clusters + lax.rem(distance, clusters)


def prepare_kernel(
    axis, size, middle, near_cols_hbm, near_counts_hbm, far_cols_hbm, coupling_hbm, target_hbm, _,
    places, high_out, low_out, target_out, near_cols, near_counts, far_cols, coupling, target, sems,
):
    pairs = (
        (near_cols_hbm, near_cols), (near_counts_hbm, near_counts), (far_cols_hbm, far_cols),
        (coupling_hbm, coupling), (target_hbm, target),
    )
    copies = [pltpu.make_async_copy(source, to, sems.at[n]) for n, (source, to) in enumerate(pairs)]
    for copy in copies:
        copy.start()
    for copy in copies[:3]:
        copy.wait()
    slots, clusters = near_cols.shape
    me = lax.axis_index(axis)
    every = clusters * size
    distance = near_cols[...] - me * clusters + 2 * clusters
    distance = jnp.where(distance < 0, distance + every, distance)
    distance = jnp.where(distance >= every, distance - every, distance)
    live = lax.broadcasted_iota(jnp.int32, (slots, clusters), 0) < near_counts[...]
    places[:slots, :] = jnp.where(live, window_place(distance, clusters, me), 5 * clusters) * R
    owner = lax.div(far_cols[...], clusters)
    other_core = (owner ^ me) & 1
    chips = size // 2
    chip = lax.rem(owner // 2 + (chips - middle), chips)
    rank = coupling.shape[1]
    per_group = LANES // rank
    inside = lax.rem(far_cols[...], clusters)
    tile = (other_core * chips + chip) * (clusters // per_group) + lax.div(inside, per_group)
    places[slots : 2 * slots, :] = tile * R
    slot = lax.broadcasted_iota(jnp.int32, (slots, clusters), 0)
    places[2 * slots :, :] = ((slot - inside) * rank) & (LANES - 1)
    for copy in copies[3:5]:
        copy.wait()
    slots, rank, _, clusters = coupling.shape
    per_tile = LANES // clusters
    for s in range(rank // per_tile):
        pieces = [
            coupling[:, s * per_tile + p].reshape(slots * rank, clusters) for p in range(per_tile)
        ]
        tile = jnp.concatenate(pieces, axis=1)
        high = tile.astype(bf16)
        high_out[:, s * LANES : (s + 1) * LANES] = high
        low_out[:, s * LANES : (s + 1) * LANES] = (tile - high.astype(f32)).astype(bf16)
    size = rank * clusters
    row = lax.broadcasted_iota(jnp.int32, (size, 1), 0)
    column = lax.broadcasted_iota(jnp.int32, (size, size), 1)
    wanted = lax.rem(row, clusters) * rank + lax.div(row, clusters)
    target_out[...] = dot((column == wanted).astype(bf16), target[...]).astype(bf16)


def fetch_kernel(slots, blocks_hbm, *refs):
    *_, blocks, token, sems = refs
    chunks = sems.shape[1]
    each = blocks.shape[0] // chunks
    copies, at = [], 0
    for n, (first, count) in enumerate(slots):
        for c in range(chunks):
            clusters = pl.ds(c * each, each)
            copies.append(
                pltpu.make_async_copy(
                    blocks_hbm.at[clusters, pl.ds(first, count)], blocks.at[clusters, pl.ds(at, count)], sems.at[n, c]
                )
            )
        at += count
    for copy in copies:
        copy.start()
    token[...] = jnp.zeros_like(token)
    for copy in copies:
        copy.wait()


def own_kernel(blocks_hbm, own, _, near, blocks, sems):
    chunks = sems.shape[0]
    each = blocks.shape[0] // chunks
    copies = [
        pltpu.make_async_copy(
            blocks_hbm.at[pl.ds(c * each, each), pl.ds(0, 1)], blocks.at[pl.ds(c * each, each)], sems.at[c]
        )
        for c in range(chunks)
    ]
    for copy in copies:
        copy.start()
    for c, copy in enumerate(copies):
        copy.wait()
        for i in range(c * each, (c + 1) * each, 2):
            both = dot(own[pl.ds(i * R, 2 * R), :], jnp.concatenate([blocks[i, 0], blocks[i + 1, 0]], axis=0), (1, 1))
            near[pl.ds(i * R, R), :] = both[:R, :LANES]
            near[pl.ds((i + 1) * R, R), :] = both[R:, LANES:]


def relay_kernel(axis, got, even, odd, _, out):
    me = lax.axis_index(axis)
    devices, each, _ = got.shape
    for device in range(devices):
        out[pl.ds(device * each, each), :] = got[device]
    wants_even = (me // 2 + me) % 2 == 0
    span = pl.ds(devices * each, even.shape[0])

    @pl.when(wants_even)
    def _():
        out[span, :] = even[...]

    @pl.when(jnp.logical_not(wants_even))
    def _():
        out[span, :] = odd[...]


def apply(
    per_group, each, slabs, places, ahead, blocks, swaps, high, low, target, near, far, window, table, finish, started
):
    clusters = near.shape[0] // R
    early = ahead.shape[1]
    first = 0 if started is None else 1
    slots = early + blocks.shape[1] + first
    rank = LANES // per_group
    head = clusters // per_group * R
    rows = slabs[0].shape[0]
    devices = (swaps[0].shape[0] - rows) // each
    for at, slab in enumerate(slabs):
        window[pl.ds(at * rows, rows), :] = slab[...].astype(f32)
    window[pl.ds(len(slabs) * rows, rows), :] = swaps[1][pl.ds(devices * each, rows), :].astype(f32)
    window[pl.ds((len(slabs) + 1) * rows, R), :] = jnp.zeros((R, LANES), f32)
    for part, values in enumerate(swaps):
        for device in range(devices):
            at = (part * devices + device) * head
            table[pl.ds(at, head), :] = values[pl.ds(device * each, head), :].astype(f32)
    lane = lane_ids()

    def fetch(k, i):
        return window[pl.ds(pl.multiple_of(places[k, i], R), R), :]

    def block(k, i):
        if 0 < k <= early:
            return ahead[i, k - 1]
        return blocks[i, max(k - early - first, 0)]

    def pick(i):
        tile = jnp.zeros((R, LANES), f32)
        for k in range(slots):
            found = table[pl.ds(pl.multiple_of(places[slots + k, i], R), R), :]
            tile = jnp.where(lane // rank == k, pltpu.roll(found, places[2 * slots + k, i], 1), tile)
        return tile

    def product(i):
        sources = jnp.concatenate(
            [jnp.concatenate([fetch(k, i), fetch(k, i + 1)], axis=0) for k in range(first, slots)], axis=1
        )
        weights = jnp.concatenate(
            [jnp.concatenate([block(k, i), block(k, i + 1)], axis=0) for k in range(first, slots)], axis=1
        )
        return dot(sources.astype(bf16), weights, (1, 1))

    def settle(i, both):
        parts = [both[:R, :LANES], both[R:, LANES:]]
        if started is not None:
            parts = [part + rows_of(started, i + n) for n, part in enumerate(parts)]
        near[pl.ds(i * R, 2 * R), :] = jnp.concatenate(parts, axis=0)

    def expand(crossed):
        spread = []
        for s in range(rank * clusters // LANES):
            tile = jnp.zeros((R, LANES), f32)
            for n in range(clusters):
                part = crossed[n * R : (n + 1) * R, s * LANES : (s + 1) * LANES]
                tile = jnp.where(lane % clusters == n, part, tile)
            tile_high = tile.astype(bf16).astype(f32)
            for n, source in enumerate((tile_high, tile - tile_high)):
                held = [jnp.where(lane % clusters == c, source, 0.0) for c in range(clusters)]
                spread.append((n, jnp.concatenate(held, axis=0).astype(bf16)))
        return [jnp.concatenate([part for m, part in spread if m == n], axis=1) for n in range(2)]

    pairs = clusters // 2
    middle = pairs // 2
    picked, pending, done = [], None, 0
    for p in range(pairs):
        both = product(2 * p)
        if pending is not None:
            settle(2 * p - 2, pending)
        pending = both
        if p < middle:
            picked += [pick(n) for n in range(4 * p, 4 * p + 4)]
        if p == middle - 1:
            chosen = jnp.concatenate(picked, axis=0).astype(bf16)
            crossed = [dot(chosen, high[...]), dot(chosen, low[...])]
        if p == middle:
            spread = expand(crossed[0] + crossed[1])
            made = [dot(part, target[...]) for part in spread]
        if p == middle + 1:
            far[...] = made[0] + made[1]
        if p > middle + 1:
            ready = min(2 * p, done + 6)
            for n in range(done, ready):
                finish(n)
            done = ready
    settle(clusters - 2, pending)
    for n in range(done, clusters):
        finish(n)


def first_kernel(
    per_group, own, mate, even, odd, places, ahead, blocks, sent, received, high, low, target, b, basis,
    image, lowered, payload, near, far, window, table,
):
    clusters = near.shape[0] // R
    slabs, swaps = (own, mate, even, odd), (sent, received)
    each = clusters // per_group * R
    tiles, products, parts = [], [], []
    sums = [jnp.zeros((R, LANES), f32) for _ in range(3)]

    def finish(i):
        field = rows_of(b, i)
        made = 0.5 * field + (rows_of(near, i) + rows_of(far, i))
        sums[:] = [s + f * g for s, f, g in zip(sums, (field, field, made), (field, made, made))]
        tiles.append(made)
        if i % 2:
            both = jnp.concatenate(tiles[i - 1 :], axis=0)
            image[pl.ds((i - 1) * R, 2 * R), :] = both
            lowered[pl.ds((i - 1) * R, 2 * R), :] = both.astype(bf16)
        if i % per_group == per_group - 1:
            products.append(compress(tiles[-per_group:], basis, i // per_group))
            parts.extend(collect(product, per_group) for product in products[-2:-1])

    apply(
        per_group, each, slabs, places, ahead, blocks, swaps, high, low, target, near, far, window, table, finish, None
    )
    write_payload(payload, parts + [collect(products[-1], per_group)], sums)


def arnoldi_one(bb, bw, ww):
    whole = bb + epsilon
    start_norm = jnp.sqrt(whole)
    scale = 1.0 / start_norm
    v11 = bb / whole
    h11 = (bw * scale) * scale
    uu = jnp.maximum((ww * scale) * scale - 2.0 * h11 * h11 + h11 * h11 * v11, 0.0)
    h21 = jnp.sqrt(uu + epsilon)
    return start_norm, h11, h21, v11, uu / (uu + epsilon), h11 * (1.0 - v11) / h21


def second_kernel(
    per_group, unknowns, own, mate, even, odd, places, ahead, blocks, sent, received, high, low, target, b, image,
    started, candidate, sums_out, known, near, far, window, table,
):
    clusters = near.shape[0] // R
    head = clusters // per_group * R
    slabs, swaps = (own, mate, even, odd), (sent, received)
    means = read_sums(tails(swaps, own.shape[0], head), 3, unknowns)
    values = arnoldi_one(*means)
    start_norm, h11, h21, _, _, _ = values
    lane = lane_ids()
    tile = jnp.zeros((R, LANES), f32)
    for n, value in enumerate(values):
        tile = jnp.where(lane == n, value, tile)
    known[...] = tile
    scale = 1.0 / start_norm
    inverse = 1.0 / h21
    sums = [jnp.zeros((R, LANES), f32) for _ in range(3)]

    def finish(j):
        held = rows_of(image, j) * scale
        first = rows_of(b, j) * scale
        second = (held - h11 * first) * inverse
        made = (0.5 * held + (rows_of(near, j) + rows_of(far, j)) * scale - h11 * held) * inverse
        sums[:] = [s + v * made for s, v in zip(sums, (first, second, made))]
        candidate[pl.ds(j * R, R), :] = made

    each = head + TAIL
    apply(
        per_group, each, slabs, places, ahead, blocks, swaps, high, low, target, near, far, window, table, finish, started
    )
    tile = sums_tile(sums).astype(bf16)
    for device in range(sums_out.shape[0]):
        sums_out[device] = tile


def finish_kernel(unknowns, b, image, candidate, known, got, solution_out, next_out):
    clusters = b.shape[0] // R
    start_norm, h11, h21, v11, v22, v12 = [known[:, n : n + 1] for n in range(6)]
    h12, h22, ww = read_sums([got[device] for device in range(got.shape[0])], 3, unknowns)
    uu = ww - 2.0 * (h12 * h12 + h22 * h22) + h12 * h12 * v11 + h22 * h22 * v22 + 2.0 * h12 * h22 * v12
    h32 = jnp.sqrt(jnp.maximum(uu, 0.0) + epsilon)
    g11 = h11 * h11 + h21 * h21
    g12 = h11 * h12 + h21 * h22
    g22 = h12 * h12 + h22 * h22 + h32 * h32
    t1, t2 = start_norm * h11, start_norm * h12
    det = g11 * g22 - g12 * g12
    y1 = (g22 * t1 - g12 * t2) / det
    y2 = (g11 * t2 - g12 * t1) / det
    scale, inverse, last = 1.0 / start_norm, 1.0 / h21, 1.0 / h32
    for j in range(clusters):
        span = slice(j * LANES, (j + 1) * LANES)
        first = rows_of(b, j) * scale
        second = (rows_of(image, j) * scale - h11 * first) * inverse
        solution_out[:, span] = y1 * first + y2 * second
        next_out[:, span] = (rows_of(candidate, j) - h12 * first - h22 * second) * last


def swapped(block, partner):
    return lax.ppermute(block, "rows", [(i, partner(i)) for i in range(lax.axis_size("rows"))])


def core_mate(i):
    return i ^ 1


def even_mate(i):
    return i ^ 2


def odd_mate(i):
    chip = i // 2
    other = chip + 1 if chip % 2 else chip - 1
    return 2 * (other % (lax.axis_size("rows") // 2)) + i % 2


def sends_of(block):
    mate, odd, even = [swapped(block, partner) for partner in (core_mate, odd_mate, even_mate)]
    return [block, mate, even, odd]


def on_device(
    right_sides, near_blocks, near_cols, near_counts, basis_in, target_basis, coupling, far_cols
):
    width = right_sides.shape[1]
    clusters, slots = near_cols.shape
    rank = basis_in.shape[1]
    per_group = LANES // rank
    head = clusters // per_group * R
    size = lax.axis_size("rows")
    unknowns = float(width * size)
    rows = clusters * R

    def shape(*dims, dtype=f32):
        return jax.ShapeDtypeStruct(dims, dtype)

    def scratch(*dims, dtype=f32):
        return pltpu.VMEM(dims, dtype)

    def in_hbm(array):
        return pltpu.with_memory_space_constraint(array, pltpu.HBM)

    def call(kernel, name, out, ins, *args, scratch_shapes=()):
        return pl.pallas_call(
            kernel, out_shape=out, in_specs=ins, out_specs=jax.tree.map(lambda _: VMEM, out),
            scratch_shapes=scratch_shapes, compiler_params=PARAMS, name=name,
        )(*args)

    chips = size // 2
    middle = chips // 4 + 1
    order = [(middle + n) % chips for n in range(chips)]

    def gather(block):
        groups = [[2 * chip + core for chip in order] for core in range(2)]
        return lax.all_to_all(block, "rows", 0, 0, axis_index_groups=groups)

    def exchange(block):
        group = [2 * chip + core for chip in order for core in range(2)]
        return lax.all_to_all(block, "rows", 0, 0, axis_index_groups=[group])

    field, basis, lowered, payload = call(
        functools.partial(start_kernel, per_group), "start",
        (
            shape(rows, LANES), shape(clusters * rank, LANES, dtype=bf16), shape(rows, LANES, dtype=bf16),
            shape(size // 2, head, LANES, dtype=bf16),
        ),
        [HBM] * 2, in_hbm(right_sides), in_hbm(basis_in.reshape(clusters * rank, LANES)),
        scratch_shapes=[scratch(R, width), pltpu.SemaphoreType.DMA((2,))],
    )
    got = gather(payload)
    held = sends_of(lowered)

    blocks = in_hbm(near_blocks)
    early = 2

    def fetch(name, ranges, chunks, *behind):
        count = sum(count for _, count in ranges)
        here, token = call(
            functools.partial(fetch_kernel, ranges), name,
            (pltpu.VMEM((clusters, count, LANES, LANES), bf16), shape(R, LANES)),
            [HBM] + [ANY] * len(behind), blocks, *behind,
            scratch_shapes=[pltpu.SemaphoreType.DMA((len(ranges), chunks))],
        )
        return pltpu.with_memory_space_constraint(here, pltpu.VMEM), token

    def arrived(got, held, ranges, behind):
        rest, token = fetch("fetch", ranges, 4, got, behind)
        sent = call(
            functools.partial(relay_kernel, "rows"), "relay",
            shape(got.shape[0] * got.shape[1] + rows, LANES, dtype=bf16), [VMEM] * 3 + [ANY], got, *held[2:], token
        )
        return ahead, rest, sent, swapped(sent, core_mate)

    late = (1 + early, slots - 1 - early)
    ahead, token = fetch("ahead", [(1, early)], 2, held[1])
    here = arrived(got, held, [(0, 1), late], token)
    prepared = call(
        functools.partial(prepare_kernel, "rows", size, middle), "prepare",
        (
            shape(3 * slots, clusters, dtype=jnp.int32),
            shape(slots * rank, rank * clusters, dtype=bf16),
            shape(slots * rank, rank * clusters, dtype=bf16),
            shape(rank * clusters, LANES, dtype=bf16),
        ),
        [HBM] * 5 + [ANY], in_hbm(near_cols.T), in_hbm(near_counts.reshape(1, clusters)), in_hbm(far_cols.T),
        in_hbm(jnp.transpose(coupling, (1, 2, 3, 0))), in_hbm(target_basis.reshape(clusters * rank, LANES)), here[2],
        scratch_shapes=[
            scratch(slots, clusters, dtype=jnp.int32), scratch(1, clusters, dtype=jnp.int32),
            scratch(slots, clusters, dtype=jnp.int32),
            scratch(slots, rank, rank, clusters), scratch(clusters * rank, LANES, dtype=bf16),
            pltpu.SemaphoreType.DMA((5,)),
        ],
    )
    places, *made = prepared
    kept = [scratch(rows, LANES), scratch(rows, LANES), scratch(5 * rows + R, LANES), scratch(size * head, LANES)]
    operands = [VMEM] * 4 + [SMEM] + [VMEM] * 9
    image, lowered, payload = call(
        functools.partial(first_kernel, per_group), "operator_one",
        (
            shape(rows, LANES), shape(rows, LANES, dtype=bf16),
            shape(size // 2, head + TAIL, LANES, dtype=bf16),
        ),
        operands, *held, places, *here, *made, field, basis, scratch_shapes=kept,
    )
    got = gather(payload)
    held = sends_of(lowered)
    started = call(
        own_kernel, "own", shape(rows, LANES), [HBM, VMEM, ANY], blocks, lowered, held[1],
        scratch_shapes=[scratch(clusters, 1, LANES, LANES, dtype=bf16), pltpu.SemaphoreType.DMA((4,))],
    )
    here = arrived(got, held, [late], started)
    candidate, sums, known = call(
        functools.partial(second_kernel, per_group, unknowns), "operator_two",
        (shape(rows, LANES), shape(size, R, LANES, dtype=bf16), shape(R, LANES)),
        operands + [VMEM], *held, places, *here, *made, field, image, started, scratch_shapes=kept,
    )
    return call(
        functools.partial(finish_kernel, unknowns), "finish", (shape(R, width), shape(R, width)),
        [VMEM] * 5, field, image, candidate, known, exchange(sums),
    )


def solution(mesh):
    return jax.shard_map(
        on_device,
        mesh=mesh,
        in_specs=(
            P("groups", "rows"),
            P("rows", None, None, None),
            P("rows", None),
            P("rows"),
            P("rows", None, None),
            P("rows", None, None),
            P("rows", None, None, None),
            P("rows", None),
        ),
        out_specs=(P("groups", "rows"), P("groups", "rows")),
        check_vma=False,
    )
```

```python
import functools

import jax
import jax.numpy as jnp
from jax import lax
from jax.experimental import pallas as pl
from jax.experimental.pallas import tpu as pltpu
from jax.sharding import PartitionSpec as P

epsilon = 1e-06
f32, bf16 = jnp.float32, jnp.bfloat16
VMEM = pl.BlockSpec(memory_space=pltpu.VMEM)
SMEM = pl.BlockSpec(memory_space=pltpu.SMEM)
HBM = pl.BlockSpec(memory_space=pltpu.HBM)
ANY = pl.BlockSpec(memory_space=pl.ANY)
R = 8
LANES = 128
SUM_SLOTS = 8
TAIL = 16
PARAMS = pltpu.CompilerParams(vmem_limit_bytes=24 * 1024 * 1024)


def lane_ids(rows=R):
    return lax.broadcasted_iota(jnp.int32, (rows, LANES), 1)


def rows_of(ref, j):
    return ref[pl.ds(j * R, R), :]


def dot(a, b, contract=(1, 0)):
    return lax.dot_general(a, b, (((contract[0],), (contract[1],)), ((), ())), preferred_element_type=f32)


def sums_tile(sums):
    lane = lane_ids()
    tile = jnp.zeros((R, LANES), f32)
    for t, partial in enumerate(sums):
        total = jnp.sum(partial, axis=1, keepdims=True)
        high = total.astype(bf16).astype(f32)
        middle = (total - high).astype(bf16).astype(f32)
        low = total - high - middle
        for part, value in enumerate((high, middle, low)):
            tile = jnp.where(lane == part * SUM_SLOTS + t, value, tile)
    return tile


def read_sums(parts, count, unknowns):
    total = jnp.zeros((R, LANES), f32)
    for part in parts:
        total = total + part.astype(f32)[:R]
    return [
        sum(total[:, p * SUM_SLOTS + t : p * SUM_SLOTS + t + 1] for p in range(3)) * (1.0 / unknowns)
        for t in range(count)
    ]


def tails(swaps, rows, head):
    each = head + TAIL
    return [
        values[pl.ds(device * each + head, TAIL), :]
        for values in swaps
        for device in range((values.shape[0] - rows) // each)
    ]


def compress(tiles, basis, group):
    stacked = jnp.concatenate(tiles, axis=0)
    high = stacked.astype(bf16)
    low = (stacked - high.astype(f32)).astype(bf16)
    return dot(jnp.concatenate([high, low], axis=0), basis[pl.ds(group * LANES, LANES), :], (1, 1))


def collect(products, per_group):
    rows = per_group * R
    both = products[:rows] + products[rows:]
    lane = lane_ids()
    tile = jnp.zeros((R, LANES), f32)
    for m in range(per_group):
        tile = jnp.where(lane // (LANES // per_group) == m, both[m * R : (m + 1) * R], tile)
    return tile


def write_payload(payload, parts, sums):
    if sums:
        parts = parts + [sums_tile(sums), jnp.zeros((TAIL - R, LANES), f32)]
    block = jnp.concatenate(parts, axis=0).astype(bf16)
    for device in range(payload.shape[0]):
        payload[device] = block


def start_kernel(per_group, b_hbm, basis_hbm, field, basis, lowered, payload, b, sems):
    copies = [
        pltpu.make_async_copy(b_hbm, b, sems.at[0]),
        pltpu.make_async_copy(basis_hbm, basis, sems.at[1]),
    ]
    for copy in copies:
        copy.start()
    for copy in copies:
        copy.wait()
    clusters = b.shape[1] // LANES
    tiles = [b[:, j * LANES : (j + 1) * LANES] for j in range(clusters)]
    field[...] = jnp.concatenate(tiles, axis=0)
    lowered[...] = jnp.concatenate(tiles, axis=0).astype(bf16)
    groups = [tiles[g : g + per_group] for g in range(0, clusters, per_group)]
    products = [compress(group, basis, g) for g, group in enumerate(groups)]
    write_payload(payload, [collect(product, per_group) for product in products], [])


def window_place(distance, clusters, me):
    core, chip = me % 2, me // 2
    before, after = 3 - chip % 2, 2 + chip % 2
    slot = [before, jnp.where(core == 0, 4, 1), 0, jnp.where(core == 0, 1, 4), after]
    slab = lax.div(distance, clusters)
    chosen = jnp.zeros_like(distance)
    for s, value in enumerate(slot):
        chosen = jnp.where(slab == s, value, chosen)
    return chosen * clusters + lax.rem(distance, clusters)


def prepare_kernel(
    axis, size, middle, near_cols_hbm, near_counts_hbm, far_cols_hbm, coupling_hbm, target_hbm, _,
    places, high_out, low_out, target_out, near_cols, near_counts, far_cols, coupling, target, sems,
):
    pairs = (
        (near_cols_hbm, near_cols), (near_counts_hbm, near_counts), (far_cols_hbm, far_cols),
        (coupling_hbm, coupling), (target_hbm, target),
    )
    copies = [pltpu.make_async_copy(source, to, sems.at[n]) for n, (source, to) in enumerate(pairs)]
    for copy in copies:
        copy.start()
    for copy in copies[:3]:
        copy.wait()
    slots, clusters = near_cols.shape
    me = lax.axis_index(axis)
    every = clusters * size
    distance = near_cols[...] - me * clusters + 2 * clusters
    distance = jnp.where(distance < 0, distance + every, distance)
    distance = jnp.where(distance >= every, distance - every, distance)
    live = lax.broadcasted_iota(jnp.int32, (slots, clusters), 0) < near_counts[...]
    places[:slots, :] = jnp.where(live, window_place(distance, clusters, me), 5 * clusters) * R
    owner = lax.div(far_cols[...], clusters)
    other_core = (owner ^ me) & 1
    chips = size // 2
    chip = lax.rem(owner // 2 + (chips - middle), chips)
    rank = coupling.shape[1]
    per_group = LANES // rank
    inside = lax.rem(far_cols[...], clusters)
    tile = (other_core * chips + chip) * (clusters // per_group) + lax.div(inside, per_group)
    places[slots : 2 * slots, :] = tile * R
    slot = lax.broadcasted_iota(jnp.int32, (slots, clusters), 0)
    places[2 * slots :, :] = ((slot - inside) * rank) & (LANES - 1)
    for copy in copies[3:5]:
        copy.wait()
    slots, rank, _, clusters = coupling.shape
    per_tile = LANES // clusters
    for s in range(rank // per_tile):
        pieces = [
            coupling[:, s * per_tile + p].reshape(slots * rank, clusters) for p in range(per_tile)
        ]
        tile = jnp.concatenate(pieces, axis=1)
        high = tile.astype(bf16)
        high_out[:, s * LANES : (s + 1) * LANES] = high
        low_out[:, s * LANES : (s + 1) * LANES] = (tile - high.astype(f32)).astype(bf16)
    size = rank * clusters
    row = lax.broadcasted_iota(jnp.int32, (size, 1), 0)
    column = lax.broadcasted_iota(jnp.int32, (size, size), 1)
    wanted = lax.rem(row, clusters) * rank + lax.div(row, clusters)
    target_out[...] = dot((column == wanted).astype(bf16), target[...]).astype(bf16)


def fetch_kernel(slots, blocks_hbm, *refs):
    *_, blocks, token, sems = refs
    chunks = sems.shape[1]
    each = blocks.shape[0] // chunks
    copies, at = [], 0
    for n, (first, count) in enumerate(slots):
        for c in range(chunks):
            clusters = pl.ds(c * each, each)
            copies.append(
                pltpu.make_async_copy(
                    blocks_hbm.at[clusters, pl.ds(first, count)], blocks.at[clusters, pl.ds(at, count)], sems.at[n, c]
                )
            )
        at += count
    for copy in copies:
        copy.start()
    token[...] = jnp.zeros_like(token)
    for copy in copies:
        copy.wait()


def own_kernel(blocks_hbm, own, _, near, blocks, sems):
    chunks = sems.shape[0]
    each = blocks.shape[0] // chunks
    copies = [
        pltpu.make_async_copy(
            blocks_hbm.at[pl.ds(c * each, each), pl.ds(0, 1)], blocks.at[pl.ds(c * each, each)], sems.at[c]
        )
        for c in range(chunks)
    ]
    for copy in copies:
        copy.start()
    products = []
    for c, copy in enumerate(copies):
        copy.wait()
        for i in range(c * each, (c + 1) * each, 2):
            weights = jnp.concatenate([blocks[i, 0], blocks[i + 1, 0]], axis=0)
            products.append(dot(own[pl.ds(i * R, 2 * R), :], weights, (1, 1)))
    for n, both in enumerate(products):
        near[pl.ds(2 * n * R, 2 * R), :] = jnp.concatenate([both[:R, :LANES], both[R:, LANES:]], axis=0)


def relay_kernel(axis, got, even, odd, _, out):
    me = lax.axis_index(axis)
    devices, each, _ = got.shape
    for device in range(devices):
        out[pl.ds(device * each, each), :] = got[device]
    wants_even = (me // 2 + me) % 2 == 0
    span = pl.ds(devices * each, even.shape[0])

    @pl.when(wants_even)
    def _():
        out[span, :] = even[...]

    @pl.when(jnp.logical_not(wants_even))
    def _():
        out[span, :] = odd[...]


def apply(
    per_group, each, slabs, places, ahead, blocks, swaps, high, low, target, near, far, window, table, finish, started
):
    clusters = near.shape[0] // R
    early = ahead.shape[1]
    first = 0 if started is None else 1
    slots = early + blocks.shape[1] + first
    rank = LANES // per_group
    head = clusters // per_group * R
    rows = slabs[0].shape[0]
    devices = (swaps[0].shape[0] - rows) // each
    for at, slab in enumerate(slabs):
        window[pl.ds(at * rows, rows), :] = slab[...].astype(f32)
    window[pl.ds(len(slabs) * rows, rows), :] = swaps[1][pl.ds(devices * each, rows), :].astype(f32)
    window[pl.ds((len(slabs) + 1) * rows, R), :] = jnp.zeros((R, LANES), f32)
    for part, values in enumerate(swaps):
        for device in range(devices):
            at = (part * devices + device) * head
            table[pl.ds(at, head), :] = values[pl.ds(device * each, head), :].astype(f32)
    lane = lane_ids()

    def fetch(k, i):
        return window[pl.ds(pl.multiple_of(places[k, i], R), R), :]

    def block(k, i):
        if 0 < k <= early:
            return ahead[i, k - 1]
        return blocks[i, max(k - early - first, 0)]

    def pick(i):
        tile = jnp.zeros((R, LANES), f32)
        for k in range(slots):
            found = table[pl.ds(pl.multiple_of(places[slots + k, i], R), R), :]
            tile = jnp.where(lane // rank == k, pltpu.roll(found, places[2 * slots + k, i], 1), tile)
        return tile

    def product(i):
        sources = jnp.concatenate(
            [jnp.concatenate([fetch(k, i), fetch(k, i + 1)], axis=0) for k in range(first, slots)], axis=1
        )
        weights = jnp.concatenate(
            [jnp.concatenate([block(k, i), block(k, i + 1)], axis=0) for k in range(first, slots)], axis=1
        )
        return dot(sources.astype(bf16), weights, (1, 1))

    def settle(i, both):
        parts = [both[:R, :LANES], both[R:, LANES:]]
        if started is not None:
            parts = [part + rows_of(started, i + n) for n, part in enumerate(parts)]
        near[pl.ds(i * R, 2 * R), :] = jnp.concatenate(parts, axis=0)

    def expand(crossed):
        spread = []
        for s in range(rank * clusters // LANES):
            tile = jnp.zeros((R, LANES), f32)
            for n in range(clusters):
                part = crossed[n * R : (n + 1) * R, s * LANES : (s + 1) * LANES]
                tile = jnp.where(lane % clusters == n, part, tile)
            tile_high = tile.astype(bf16).astype(f32)
            for n, source in enumerate((tile_high, tile - tile_high)):
                held = [jnp.where(lane % clusters == c, source, 0.0) for c in range(clusters)]
                spread.append((n, jnp.concatenate(held, axis=0).astype(bf16)))
        return [jnp.concatenate([part for m, part in spread if m == n], axis=1) for n in range(2)]

    pairs = clusters // 2
    middle = pairs // 2
    picked, pending, done = [], None, 0
    for p in range(pairs):
        both = product(2 * p)
        if pending is not None:
            settle(2 * p - 2, pending)
        pending = both
        if p < middle:
            picked += [pick(n) for n in range(4 * p, 4 * p + 4)]
        if p == middle - 1:
            chosen = jnp.concatenate(picked, axis=0).astype(bf16)
            crossed = [dot(chosen, high[...]), dot(chosen, low[...])]
        if p == middle:
            spread = expand(crossed[0] + crossed[1])
            made = [dot(part, target[...]) for part in spread]
        if p == middle + 1:
            far[...] = made[0] + made[1]
        if p > middle + 1:
            ready = min(2 * p, done + 6)
            for n in range(done, ready):
                finish(n)
            done = ready
    settle(clusters - 2, pending)
    for n in range(done, clusters):
        finish(n)


def first_kernel(
    per_group, own, mate, even, odd, places, ahead, blocks, sent, received, high, low, target, b, basis,
    image, lowered, payload, near, far, window, table,
):
    clusters = near.shape[0] // R
    slabs, swaps = (own, mate, even, odd), (sent, received)
    each = clusters // per_group * R
    tiles, products, parts = [], [], []
    sums = [jnp.zeros((R, LANES), f32) for _ in range(3)]

    def finish(i):
        field = rows_of(b, i)
        made = 0.5 * field + (rows_of(near, i) + rows_of(far, i))
        sums[:] = [s + f * g for s, f, g in zip(sums, (field, field, made), (field, made, made))]
        tiles.append(made)
        if i % 2:
            both = jnp.concatenate(tiles[i - 1 :], axis=0)
            image[pl.ds((i - 1) * R, 2 * R), :] = both
            lowered[pl.ds((i - 1) * R, 2 * R), :] = both.astype(bf16)
        if i % per_group == per_group - 1:
            products.append(compress(tiles[-per_group:], basis, i // per_group))
            parts.extend(collect(product, per_group) for product in products[-2:-1])

    apply(
        per_group, each, slabs, places, ahead, blocks, swaps, high, low, target, near, far, window, table, finish, None
    )
    write_payload(payload, parts + [collect(products[-1], per_group)], sums)


def arnoldi_one(bb, bw, ww):
    whole = bb + epsilon
    start_norm = jnp.sqrt(whole)
    scale = 1.0 / start_norm
    v11 = bb / whole
    h11 = (bw * scale) * scale
    uu = jnp.maximum((ww * scale) * scale - 2.0 * h11 * h11 + h11 * h11 * v11, 0.0)
    h21 = jnp.sqrt(uu + epsilon)
    return start_norm, h11, h21, v11, uu / (uu + epsilon), h11 * (1.0 - v11) / h21


def second_kernel(
    per_group, unknowns, own, mate, even, odd, places, ahead, blocks, sent, received, high, low, target, b, image,
    started, candidate, sums_out, known, near, far, window, table,
):
    clusters = near.shape[0] // R
    head = clusters // per_group * R
    slabs, swaps = (own, mate, even, odd), (sent, received)
    means = read_sums(tails(swaps, own.shape[0], head), 3, unknowns)
    values = arnoldi_one(*means)
    start_norm, h11, h21, _, _, _ = values
    lane = lane_ids()
    tile = jnp.zeros((R, LANES), f32)
    for n, value in enumerate(values):
        tile = jnp.where(lane == n, value, tile)
    known[...] = tile
    scale = 1.0 / start_norm
    inverse = 1.0 / h21
    sums = [jnp.zeros((R, LANES), f32) for _ in range(3)]

    def finish(j):
        held = rows_of(image, j) * scale
        first = rows_of(b, j) * scale
        second = (held - h11 * first) * inverse
        made = (0.5 * held + (rows_of(near, j) + rows_of(far, j)) * scale - h11 * held) * inverse
        sums[:] = [s + v * made for s, v in zip(sums, (first, second, made))]
        candidate[pl.ds(j * R, R), :] = made

    each = head + TAIL
    apply(
        per_group, each, slabs, places, ahead, blocks, swaps, high, low, target, near, far, window, table, finish, started
    )
    tile = sums_tile(sums).astype(bf16)
    for device in range(sums_out.shape[0]):
        sums_out[device] = tile


def finish_kernel(unknowns, b, image, candidate, known, got, solution_out, next_out):
    clusters = b.shape[0] // R
    start_norm, h11, h21, v11, v22, v12 = [known[:, n : n + 1] for n in range(6)]
    h12, h22, ww = read_sums([got[device] for device in range(got.shape[0])], 3, unknowns)
    uu = ww - 2.0 * (h12 * h12 + h22 * h22) + h12 * h12 * v11 + h22 * h22 * v22 + 2.0 * h12 * h22 * v12
    h32 = jnp.sqrt(jnp.maximum(uu, 0.0) + epsilon)
    g11 = h11 * h11 + h21 * h21
    g12 = h11 * h12 + h21 * h22
    g22 = h12 * h12 + h22 * h22 + h32 * h32
    t1, t2 = start_norm * h11, start_norm * h12
    det = g11 * g22 - g12 * g12
    y1 = (g22 * t1 - g12 * t2) / det
    y2 = (g11 * t2 - g12 * t1) / det
    scale, inverse, last = 1.0 / start_norm, 1.0 / h21, 1.0 / h32
    for j in range(clusters):
        span = slice(j * LANES, (j + 1) * LANES)
        first = rows_of(b, j) * scale
        second = (rows_of(image, j) * scale - h11 * first) * inverse
        solution_out[:, span] = y1 * first + y2 * second
        next_out[:, span] = (rows_of(candidate, j) - h12 * first - h22 * second) * last


def swapped(block, partner):
    return lax.ppermute(block, "rows", [(i, partner(i)) for i in range(lax.axis_size("rows"))])


def core_mate(i):
    return i ^ 1


def even_mate(i):
    return i ^ 2


def odd_mate(i):
    chip = i // 2
    other = chip + 1 if chip % 2 else chip - 1
    return 2 * (other % (lax.axis_size("rows") // 2)) + i % 2


def sends_of(block):
    mate, odd, even = [swapped(block, partner) for partner in (core_mate, odd_mate, even_mate)]
    return [block, mate, even, odd]


def on_device(
    right_sides, near_blocks, near_cols, near_counts, basis_in, target_basis, coupling, far_cols
):
    width = right_sides.shape[1]
    clusters, slots = near_cols.shape
    rank = basis_in.shape[1]
    per_group = LANES // rank
    head = clusters // per_group * R
    size = lax.axis_size("rows")
    unknowns = float(width * size)
    rows = clusters * R

    def shape(*dims, dtype=f32):
        return jax.ShapeDtypeStruct(dims, dtype)

    def scratch(*dims, dtype=f32):
        return pltpu.VMEM(dims, dtype)

    def in_hbm(array):
        return pltpu.with_memory_space_constraint(array, pltpu.HBM)

    def call(kernel, name, out, ins, *args, scratch_shapes=()):
        return pl.pallas_call(
            kernel, out_shape=out, in_specs=ins, out_specs=jax.tree.map(lambda _: VMEM, out),
            scratch_shapes=scratch_shapes, compiler_params=PARAMS, name=name,
        )(*args)

    chips = size // 2
    middle = chips // 4 + 1
    order = [(middle + n) % chips for n in range(chips)]

    def gather(block):
        groups = [[2 * chip + core for chip in order] for core in range(2)]
        return lax.all_to_all(block, "rows", 0, 0, axis_index_groups=groups)

    def exchange(block):
        group = [2 * chip + core for chip in order for core in range(2)]
        return lax.all_to_all(block, "rows", 0, 0, axis_index_groups=[group])

    field, basis, lowered, payload = call(
        functools.partial(start_kernel, per_group), "start",
        (
            shape(rows, LANES), shape(clusters * rank, LANES, dtype=bf16), shape(rows, LANES, dtype=bf16),
            shape(size // 2, head, LANES, dtype=bf16),
        ),
        [HBM] * 2, in_hbm(right_sides), in_hbm(basis_in.reshape(clusters * rank, LANES)),
        scratch_shapes=[scratch(R, width), pltpu.SemaphoreType.DMA((2,))],
    )
    got = gather(payload)
    held = sends_of(lowered)

    blocks = in_hbm(near_blocks)
    early = 2

    def fetch(name, ranges, chunks, *behind):
        count = sum(count for _, count in ranges)
        here, token = call(
            functools.partial(fetch_kernel, ranges), name,
            (pltpu.VMEM((clusters, count, LANES, LANES), bf16), shape(R, LANES)),
            [HBM] + [ANY] * len(behind), blocks, *behind,
            scratch_shapes=[pltpu.SemaphoreType.DMA((len(ranges), chunks))],
        )
        return pltpu.with_memory_space_constraint(here, pltpu.VMEM), token

    def arrived(got, held, ranges, behind):
        rest, token = fetch("fetch", ranges, 4, got, behind)
        sent = call(
            functools.partial(relay_kernel, "rows"), "relay",
            shape(got.shape[0] * got.shape[1] + rows, LANES, dtype=bf16), [VMEM] * 3 + [ANY], got, *held[2:], token
        )
        return ahead, rest, sent, swapped(sent, core_mate)

    late = (1 + early, slots - 1 - early)
    ahead, token = fetch("ahead", [(1, early)], 2, held[1])
    here = arrived(got, held, [(0, 1), late], token)
    prepared = call(
        functools.partial(prepare_kernel, "rows", size, middle), "prepare",
        (
            shape(3 * slots, clusters, dtype=jnp.int32),
            shape(slots * rank, rank * clusters, dtype=bf16),
            shape(slots * rank, rank * clusters, dtype=bf16),
            shape(rank * clusters, LANES, dtype=bf16),
        ),
        [HBM] * 5 + [ANY], in_hbm(near_cols.T), in_hbm(near_counts.reshape(1, clusters)), in_hbm(far_cols.T),
        in_hbm(jnp.transpose(coupling, (1, 2, 3, 0))), in_hbm(target_basis.reshape(clusters * rank, LANES)), here[2],
        scratch_shapes=[
            scratch(slots, clusters, dtype=jnp.int32), scratch(1, clusters, dtype=jnp.int32),
            scratch(slots, clusters, dtype=jnp.int32),
            scratch(slots, rank, rank, clusters), scratch(clusters * rank, LANES, dtype=bf16),
            pltpu.SemaphoreType.DMA((5,)),
        ],
    )
    places, *made = prepared
    kept = [scratch(rows, LANES), scratch(rows, LANES), scratch(5 * rows + R, LANES), scratch(size * head, LANES)]
    operands = [VMEM] * 4 + [SMEM] + [VMEM] * 9
    image, lowered, payload = call(
        functools.partial(first_kernel, per_group), "operator_one",
        (
            shape(rows, LANES), shape(rows, LANES, dtype=bf16),
            shape(size // 2, head + TAIL, LANES, dtype=bf16),
        ),
        operands, *held, places, *here, *made, field, basis, scratch_shapes=kept,
    )
    got = gather(payload)
    held = sends_of(lowered)
    started = call(
        own_kernel, "own", shape(rows, LANES), [HBM, VMEM, ANY], blocks, lowered, held[1],
        scratch_shapes=[scratch(clusters, 1, LANES, LANES, dtype=bf16), pltpu.SemaphoreType.DMA((8,))],
    )
    here = arrived(got, held, [late], started)
    candidate, sums, known = call(
        functools.partial(second_kernel, per_group, unknowns), "operator_two",
        (shape(rows, LANES), shape(size, R, LANES, dtype=bf16), shape(R, LANES)),
        operands + [VMEM], *held, places, *here, *made, field, image, started, scratch_shapes=kept,
    )
    return call(
        functools.partial(finish_kernel, unknowns), "finish", (shape(R, width), shape(R, width)),
        [VMEM] * 5, field, image, candidate, known, exchange(sums),
    )


def solution(mesh):
    return jax.shard_map(
        on_device,
        mesh=mesh,
        in_specs=(
            P("groups", "rows"),
            P("rows", None, None, None),
            P("rows", None),
            P("rows"),
            P("rows", None, None),
            P("rows", None, None),
            P("rows", None, None, None),
            P("rows", None),
        ),
        out_specs=(P("groups", "rows"), P("groups", "rows")),
        check_vma=False,
    )
```

```python
import functools

import jax
import jax.numpy as jnp
from jax import lax
from jax.experimental import pallas as pl
from jax.experimental.pallas import tpu as pltpu
from jax.sharding import PartitionSpec as P

epsilon = 1e-06
f32, bf16 = jnp.float32, jnp.bfloat16
VMEM = pl.BlockSpec(memory_space=pltpu.VMEM)
SMEM = pl.BlockSpec(memory_space=pltpu.SMEM)
HBM = pl.BlockSpec(memory_space=pltpu.HBM)
ANY = pl.BlockSpec(memory_space=pl.ANY)
R = 8
LANES = 128
SUM_SLOTS = 8
TAIL = 16
PARAMS = pltpu.CompilerParams(vmem_limit_bytes=24 * 1024 * 1024)


def lane_ids(rows=R):
    return lax.broadcasted_iota(jnp.int32, (rows, LANES), 1)


def rows_of(ref, j):
    return ref[pl.ds(j * R, R), :]


def dot(a, b, contract=(1, 0)):
    return lax.dot_general(a, b, (((contract[0],), (contract[1],)), ((), ())), preferred_element_type=f32)


def sums_tile(sums):
    lane = lane_ids()
    tile = jnp.zeros((R, LANES), f32)
    for t, partial in enumerate(sums):
        total = jnp.sum(partial, axis=1, keepdims=True)
        high = total.astype(bf16).astype(f32)
        middle = (total - high).astype(bf16).astype(f32)
        low = total - high - middle
        for part, value in enumerate((high, middle, low)):
            tile = jnp.where(lane == part * SUM_SLOTS + t, value, tile)
    return tile


def read_sums(parts, count, unknowns):
    total = jnp.zeros((R, LANES), f32)
    for part in parts:
        total = total + part.astype(f32)[:R]
    return [
        sum(total[:, p * SUM_SLOTS + t : p * SUM_SLOTS + t + 1] for p in range(3)) * (1.0 / unknowns)
        for t in range(count)
    ]


def tails(swaps, rows, head):
    each = head + TAIL
    return [
        values[pl.ds(device * each + head, TAIL), :]
        for values in swaps
        for device in range((values.shape[0] - rows) // each)
    ]


def compress(tiles, basis, group):
    stacked = jnp.concatenate(tiles, axis=0)
    high = stacked.astype(bf16)
    low = (stacked - high.astype(f32)).astype(bf16)
    return dot(jnp.concatenate([high, low], axis=0), basis[pl.ds(group * LANES, LANES), :], (1, 1))


def collect(products, per_group):
    rows = per_group * R
    both = products[:rows] + products[rows:]
    lane = lane_ids()
    tile = jnp.zeros((R, LANES), f32)
    for m in range(per_group):
        tile = jnp.where(lane // (LANES // per_group) == m, both[m * R : (m + 1) * R], tile)
    return tile


def write_payload(payload, parts, sums):
    if sums:
        parts = parts + [sums_tile(sums), jnp.zeros((TAIL - R, LANES), f32)]
    block = jnp.concatenate(parts, axis=0).astype(bf16)
    for device in range(payload.shape[0]):
        payload[device] = block


def start_kernel(per_group, b_hbm, basis_hbm, field, basis, lowered, payload, b, sems):
    copies = [
        pltpu.make_async_copy(b_hbm, b, sems.at[0]),
        pltpu.make_async_copy(basis_hbm, basis, sems.at[1]),
    ]
    for copy in copies:
        copy.start()
    for copy in copies:
        copy.wait()
    clusters = b.shape[1] // LANES
    tiles = [b[:, j * LANES : (j + 1) * LANES] for j in range(clusters)]
    field[...] = jnp.concatenate(tiles, axis=0)
    lowered[...] = jnp.concatenate(tiles, axis=0).astype(bf16)
    groups = [tiles[g : g + per_group] for g in range(0, clusters, per_group)]
    products = [compress(group, basis, g) for g, group in enumerate(groups)]
    write_payload(payload, [collect(product, per_group) for product in products], [])


def window_place(distance, clusters, me):
    core, chip = me % 2, me // 2
    before, after = 3 - chip % 2, 2 + chip % 2
    slot = [before, jnp.where(core == 0, 4, 1), 0, jnp.where(core == 0, 1, 4), after]
    slab = lax.div(distance, clusters)
    chosen = jnp.zeros_like(distance)
    for s, value in enumerate(slot):
        chosen = jnp.where(slab == s, value, chosen)
    return chosen * clusters + lax.rem(distance, clusters)


def prepare_kernel(
    axis, size, middle, near_cols_hbm, near_counts_hbm, far_cols_hbm, coupling_hbm, target_hbm, _,
    places, high_out, low_out, target_out, near_cols, near_counts, far_cols, coupling, target, sems,
):
    pairs = (
        (near_cols_hbm, near_cols), (near_counts_hbm, near_counts), (far_cols_hbm, far_cols),
        (coupling_hbm, coupling), (target_hbm, target),
    )
    copies = [pltpu.make_async_copy(source, to, sems.at[n]) for n, (source, to) in enumerate(pairs)]
    for copy in copies:
        copy.start()
    for copy in copies[:3]:
        copy.wait()
    slots, clusters = near_cols.shape
    me = lax.axis_index(axis)
    every = clusters * size
    distance = near_cols[...] - me * clusters + 2 * clusters
    distance = jnp.where(distance < 0, distance + every, distance)
    distance = jnp.where(distance >= every, distance - every, distance)
    live = lax.broadcasted_iota(jnp.int32, (slots, clusters), 0) < near_counts[...]
    places[:slots, :] = jnp.where(live, window_place(distance, clusters, me), 5 * clusters) * R
    owner = lax.div(far_cols[...], clusters)
    other_core = (owner ^ me) & 1
    chips = size // 2
    chip = lax.rem(owner // 2 + (chips - middle), chips)
    rank = coupling.shape[1]
    per_group = LANES // rank
    inside = lax.rem(far_cols[...], clusters)
    tile = (other_core * chips + chip) * (clusters // per_group) + lax.div(inside, per_group)
    places[slots : 2 * slots, :] = tile * R
    slot = lax.broadcasted_iota(jnp.int32, (slots, clusters), 0)
    places[2 * slots :, :] = ((slot - inside) * rank) & (LANES - 1)
    for copy in copies[3:5]:
        copy.wait()
    slots, rank, _, clusters = coupling.shape
    per_tile = LANES // clusters
    for s in range(rank // per_tile):
        pieces = [
            coupling[:, s * per_tile + p].reshape(slots * rank, clusters) for p in range(per_tile)
        ]
        tile = jnp.concatenate(pieces, axis=1)
        high = tile.astype(bf16)
        high_out[:, s * LANES : (s + 1) * LANES] = high
        low_out[:, s * LANES : (s + 1) * LANES] = (tile - high.astype(f32)).astype(bf16)
    size = rank * clusters
    row = lax.broadcasted_iota(jnp.int32, (size, 1), 0)
    column = lax.broadcasted_iota(jnp.int32, (size, size), 1)
    wanted = lax.rem(row, clusters) * rank + lax.div(row, clusters)
    target_out[...] = dot((column == wanted).astype(bf16), target[...]).astype(bf16)


def fetch_kernel(slots, blocks_hbm, *refs):
    *_, blocks, token, sems = refs
    chunks = sems.shape[1]
    each = blocks.shape[0] // chunks
    copies, at = [], 0
    for n, (first, count) in enumerate(slots):
        for c in range(chunks):
            clusters = pl.ds(c * each, each)
            copies.append(
                pltpu.make_async_copy(
                    blocks_hbm.at[clusters, pl.ds(first, count)], blocks.at[clusters, pl.ds(at, count)], sems.at[n, c]
                )
            )
        at += count
    for copy in copies:
        copy.start()
    token[...] = jnp.zeros_like(token)
    for copy in copies:
        copy.wait()


def own_kernel(blocks_hbm, own, _, near, blocks, sems):
    chunks = sems.shape[0]
    each = blocks.shape[0] // chunks
    copies = [
        pltpu.make_async_copy(
            blocks_hbm.at[pl.ds(c * each, each), pl.ds(0, 1)], blocks.at[pl.ds(c * each, each)], sems.at[c]
        )
        for c in range(chunks)
    ]
    for copy in copies:
        copy.start()
    products = []
    for c, copy in enumerate(copies):
        copy.wait()
        for i in range(c * each, (c + 1) * each, 2):
            weights = jnp.concatenate([blocks[i, 0], blocks[i + 1, 0]], axis=0)
            products.append(dot(own[pl.ds(i * R, 2 * R), :], weights, (1, 1)))
    for n, both in enumerate(products):
        near[pl.ds(2 * n * R, 2 * R), :] = jnp.concatenate([both[:R, :LANES], both[R:, LANES:]], axis=0)


def relay_kernel(axis, got, even, odd, _, out):
    me = lax.axis_index(axis)
    devices, each, _ = got.shape
    for device in range(devices):
        out[pl.ds(device * each, each), :] = got[device]
    wants_even = (me // 2 + me) % 2 == 0
    span = pl.ds(devices * each, even.shape[0])

    @pl.when(wants_even)
    def _():
        out[span, :] = even[...]

    @pl.when(jnp.logical_not(wants_even))
    def _():
        out[span, :] = odd[...]


def apply(
    per_group, each, slabs, places, ahead, blocks, swaps, high, low, target, near, far, window, table, finish, started
):
    clusters = near.shape[0] // R
    early = ahead.shape[1]
    first = 0 if started is None else 1
    slots = early + blocks.shape[1] + first
    rank = LANES // per_group
    head = clusters // per_group * R
    rows = slabs[0].shape[0]
    devices = (swaps[0].shape[0] - rows) // each
    for at, slab in enumerate(slabs):
        window[pl.ds(at * rows, rows), :] = slab[...].astype(f32)
    window[pl.ds(len(slabs) * rows, rows), :] = swaps[1][pl.ds(devices * each, rows), :].astype(f32)
    window[pl.ds((len(slabs) + 1) * rows, R), :] = jnp.zeros((R, LANES), f32)
    for part, values in enumerate(swaps):
        for device in range(devices):
            at = (part * devices + device) * head
            table[pl.ds(at, head), :] = values[pl.ds(device * each, head), :].astype(f32)
    lane = lane_ids()

    def fetch(k, i):
        return window[pl.ds(pl.multiple_of(places[k, i], R), R), :]

    def block(k, i):
        if 0 < k <= early:
            return ahead[i, k - 1]
        return blocks[i, max(k - early - first, 0)]

    def pick(i):
        tile = jnp.zeros((R, LANES), f32)
        for k in range(slots):
            found = table[pl.ds(pl.multiple_of(places[slots + k, i], R), R), :]
            tile = jnp.where(lane // rank == k, pltpu.roll(found, places[2 * slots + k, i], 1), tile)
        return tile

    def product(i):
        sources = jnp.concatenate(
            [jnp.concatenate([fetch(k, i), fetch(k, i + 1)], axis=0) for k in range(first, slots)], axis=1
        )
        weights = jnp.concatenate(
            [jnp.concatenate([block(k, i), block(k, i + 1)], axis=0) for k in range(first, slots)], axis=1
        )
        return dot(sources.astype(bf16), weights, (1, 1))

    def settle(i, both):
        parts = [both[:R, :LANES], both[R:, LANES:]]
        if started is not None:
            parts = [part + rows_of(started, i + n) for n, part in enumerate(parts)]
        near[pl.ds(i * R, 2 * R), :] = jnp.concatenate(parts, axis=0)

    def expand(crossed):
        spread = []
        for s in range(rank * clusters // LANES):
            tile = jnp.zeros((R, LANES), f32)
            for n in range(clusters):
                part = crossed[n * R : (n + 1) * R, s * LANES : (s + 1) * LANES]
                tile = jnp.where(lane % clusters == n, part, tile)
            tile_high = tile.astype(bf16).astype(f32)
            for n, source in enumerate((tile_high, tile - tile_high)):
                held = [jnp.where(lane % clusters == c, source, 0.0) for c in range(clusters)]
                spread.append((n, jnp.concatenate(held, axis=0).astype(bf16)))
        return [jnp.concatenate([part for m, part in spread if m == n], axis=1) for n in range(2)]

    pairs = clusters // 2
    middle = pairs // 2
    picked, pending, done = [], None, 0
    for p in range(pairs):
        both = product(2 * p)
        if pending is not None:
            settle(2 * p - 2, pending)
        pending = both
        if p < middle:
            picked += [pick(n) for n in range(4 * p, 4 * p + 4)]
        if p == middle - 1:
            chosen = jnp.concatenate(picked, axis=0).astype(bf16)
            crossed = [dot(chosen, high[...]), dot(chosen, low[...])]
        if p == middle:
            spread = expand(crossed[0] + crossed[1])
            made = [dot(part, target[...]) for part in spread]
        if p == middle + 1:
            far[...] = made[0] + made[1]
        if p > middle + 1:
            ready = min(2 * p, done + 6)
            for n in range(done, ready):
                finish(n)
            done = ready
    settle(clusters - 2, pending)
    for n in range(done, clusters):
        finish(n)


def first_kernel(
    per_group, own, mate, even, odd, places, ahead, blocks, sent, received, high, low, target, b, basis,
    image, lowered, payload, near, far, window, table,
):
    clusters = near.shape[0] // R
    slabs, swaps = (own, mate, even, odd), (sent, received)
    each = clusters // per_group * R
    tiles, products, parts = [], [], []
    sums = [jnp.zeros((R, LANES), f32) for _ in range(3)]

    def finish(i):
        field = rows_of(b, i)
        made = 0.5 * field + (rows_of(near, i) + rows_of(far, i))
        sums[:] = [s + f * g for s, f, g in zip(sums, (field, field, made), (field, made, made))]
        tiles.append(made)
        if i % 2:
            both = jnp.concatenate(tiles[i - 1 :], axis=0)
            image[pl.ds((i - 1) * R, 2 * R), :] = both
            lowered[pl.ds((i - 1) * R, 2 * R), :] = both.astype(bf16)
        if i % per_group == per_group - 1:
            products.append(compress(tiles[-per_group:], basis, i // per_group))
            parts.extend(collect(product, per_group) for product in products[-2:-1])

    apply(
        per_group, each, slabs, places, ahead, blocks, swaps, high, low, target, near, far, window, table, finish, None
    )
    write_payload(payload, parts + [collect(products[-1], per_group)], sums)


def arnoldi_one(bb, bw, ww):
    whole = bb + epsilon
    start_norm = jnp.sqrt(whole)
    scale = 1.0 / start_norm
    v11 = bb / whole
    h11 = (bw * scale) * scale
    uu = jnp.maximum((ww * scale) * scale - 2.0 * h11 * h11 + h11 * h11 * v11, 0.0)
    h21 = jnp.sqrt(uu + epsilon)
    return start_norm, h11, h21, v11, uu / (uu + epsilon), h11 * (1.0 - v11) / h21


def second_kernel(
    per_group, unknowns, own, mate, even, odd, places, ahead, blocks, sent, received, high, low, target, b, image,
    started, candidate, sums_out, known, near, far, window, table,
):
    clusters = near.shape[0] // R
    head = clusters // per_group * R
    slabs, swaps = (own, mate, even, odd), (sent, received)
    means = read_sums(tails(swaps, own.shape[0], head), 3, unknowns)
    values = arnoldi_one(*means)
    start_norm, h11, h21, _, _, _ = values
    lane = lane_ids()
    tile = jnp.zeros((R, LANES), f32)
    for n, value in enumerate(values):
        tile = jnp.where(lane == n, value, tile)
    known[...] = tile
    scale = 1.0 / start_norm
    inverse = 1.0 / h21
    sums = [jnp.zeros((R, LANES), f32) for _ in range(3)]

    def finish(j):
        held = rows_of(image, j) * scale
        first = rows_of(b, j) * scale
        second = (held - h11 * first) * inverse
        made = (0.5 * held + (rows_of(near, j) + rows_of(far, j)) * scale - h11 * held) * inverse
        sums[:] = [s + v * made for s, v in zip(sums, (first, second, made))]
        candidate[pl.ds(j * R, R), :] = made

    each = head + TAIL
    apply(
        per_group, each, slabs, places, ahead, blocks, swaps, high, low, target, near, far, window, table, finish, started
    )
    tile = sums_tile(sums).astype(bf16)
    for device in range(sums_out.shape[0]):
        sums_out[device] = tile


def finish_kernel(unknowns, b, image, candidate, known, got, solution_out, next_out):
    clusters = b.shape[0] // R
    start_norm, h11, h21, v11, v22, v12 = [known[:, n : n + 1] for n in range(6)]
    h12, h22, ww = read_sums([got[device] for device in range(got.shape[0])], 3, unknowns)
    uu = ww - 2.0 * (h12 * h12 + h22 * h22) + h12 * h12 * v11 + h22 * h22 * v22 + 2.0 * h12 * h22 * v12
    h32 = jnp.sqrt(jnp.maximum(uu, 0.0) + epsilon)
    g11 = h11 * h11 + h21 * h21
    g12 = h11 * h12 + h21 * h22
    g22 = h12 * h12 + h22 * h22 + h32 * h32
    t1, t2 = start_norm * h11, start_norm * h12
    det = g11 * g22 - g12 * g12
    y1 = (g22 * t1 - g12 * t2) / det
    y2 = (g11 * t2 - g12 * t1) / det
    scale, inverse, last = 1.0 / start_norm, 1.0 / h21, 1.0 / h32
    for j in range(clusters):
        span = slice(j * LANES, (j + 1) * LANES)
        first = rows_of(b, j) * scale
        second = (rows_of(image, j) * scale - h11 * first) * inverse
        solution_out[:, span] = y1 * first + y2 * second
        next_out[:, span] = (rows_of(candidate, j) - h12 * first - h22 * second) * last


def swapped(block, partner):
    return lax.ppermute(block, "rows", [(i, partner(i)) for i in range(lax.axis_size("rows"))])


def core_mate(i):
    return i ^ 1


def even_mate(i):
    return i ^ 2


def odd_mate(i):
    chip = i // 2
    other = chip + 1 if chip % 2 else chip - 1
    return 2 * (other % (lax.axis_size("rows") // 2)) + i % 2


def sends_of(block):
    mate, odd, even = [swapped(block, partner) for partner in (core_mate, odd_mate, even_mate)]
    return [block, mate, even, odd]


def on_device(
    right_sides, near_blocks, near_cols, near_counts, basis_in, target_basis, coupling, far_cols
):
    width = right_sides.shape[1]
    clusters, slots = near_cols.shape
    rank = basis_in.shape[1]
    per_group = LANES // rank
    head = clusters // per_group * R
    size = lax.axis_size("rows")
    unknowns = float(width * size)
    rows = clusters * R

    def shape(*dims, dtype=f32):
        return jax.ShapeDtypeStruct(dims, dtype)

    def scratch(*dims, dtype=f32):
        return pltpu.VMEM(dims, dtype)

    def in_hbm(array):
        return pltpu.with_memory_space_constraint(array, pltpu.HBM)

    def call(kernel, name, out, ins, *args, scratch_shapes=()):
        return pl.pallas_call(
            kernel, out_shape=out, in_specs=ins, out_specs=jax.tree.map(lambda _: VMEM, out),
            scratch_shapes=scratch_shapes, compiler_params=PARAMS, name=name,
        )(*args)

    chips = size // 2
    middle = chips // 4 + 1
    order = [(middle + n) % chips for n in range(chips)]

    def gather(block):
        groups = [[2 * chip + core for chip in order] for core in range(2)]
        return lax.all_to_all(block, "rows", 0, 0, axis_index_groups=groups)

    def exchange(block):
        group = [2 * chip + core for chip in order for core in range(2)]
        return lax.all_to_all(block, "rows", 0, 0, axis_index_groups=[group])

    field, basis, lowered, payload = call(
        functools.partial(start_kernel, per_group), "start",
        (
            shape(rows, LANES), shape(clusters * rank, LANES, dtype=bf16), shape(rows, LANES, dtype=bf16),
            shape(size // 2, head, LANES, dtype=bf16),
        ),
        [HBM] * 2, in_hbm(right_sides), in_hbm(basis_in.reshape(clusters * rank, LANES)),
        scratch_shapes=[scratch(R, width), pltpu.SemaphoreType.DMA((2,))],
    )
    got = gather(payload)
    held = sends_of(lowered)

    blocks = in_hbm(near_blocks)
    early = 2

    def fetch(name, ranges, chunks, *behind):
        count = sum(count for _, count in ranges)
        here, token = call(
            functools.partial(fetch_kernel, ranges), name,
            (pltpu.VMEM((clusters, count, LANES, LANES), bf16), shape(R, LANES)),
            [HBM] + [ANY] * len(behind), blocks, *behind,
            scratch_shapes=[pltpu.SemaphoreType.DMA((len(ranges), chunks))],
        )
        return pltpu.with_memory_space_constraint(here, pltpu.VMEM), token

    def arrived(got, held, ranges, behind):
        rest, token = fetch("fetch", ranges, 1, got, behind)
        sent = call(
            functools.partial(relay_kernel, "rows"), "relay",
            shape(got.shape[0] * got.shape[1] + rows, LANES, dtype=bf16), [VMEM] * 3 + [ANY], got, *held[2:], token
        )
        return ahead, rest, sent, swapped(sent, core_mate)

    late = (1 + early, slots - 1 - early)
    ahead, token = fetch("ahead", [(1, early)], 1, held[1])
    here = arrived(got, held, [(0, 1), late], token)
    prepared = call(
        functools.partial(prepare_kernel, "rows", size, middle), "prepare",
        (
            shape(3 * slots, clusters, dtype=jnp.int32),
            shape(slots * rank, rank * clusters, dtype=bf16),
            shape(slots * rank, rank * clusters, dtype=bf16),
            shape(rank * clusters, LANES, dtype=bf16),
        ),
        [HBM] * 5 + [ANY], in_hbm(near_cols.T), in_hbm(near_counts.reshape(1, clusters)), in_hbm(far_cols.T),
        in_hbm(jnp.transpose(coupling, (1, 2, 3, 0))), in_hbm(target_basis.reshape(clusters * rank, LANES)), here[2],
        scratch_shapes=[
            scratch(slots, clusters, dtype=jnp.int32), scratch(1, clusters, dtype=jnp.int32),
            scratch(slots, clusters, dtype=jnp.int32),
            scratch(slots, rank, rank, clusters), scratch(clusters * rank, LANES, dtype=bf16),
            pltpu.SemaphoreType.DMA((5,)),
        ],
    )
    places, *made = prepared
    kept = [scratch(rows, LANES), scratch(rows, LANES), scratch(5 * rows + R, LANES), scratch(size * head, LANES)]
    operands = [VMEM] * 4 + [SMEM] + [VMEM] * 9
    image, lowered, payload = call(
        functools.partial(first_kernel, per_group), "operator_one",
        (
            shape(rows, LANES), shape(rows, LANES, dtype=bf16),
            shape(size // 2, head + TAIL, LANES, dtype=bf16),
        ),
        operands, *held, places, *here, *made, field, basis, scratch_shapes=kept,
    )
    got = gather(payload)
    held = sends_of(lowered)
    started = call(
        own_kernel, "own", shape(rows, LANES), [HBM, VMEM, ANY], blocks, lowered, held[1],
        scratch_shapes=[scratch(clusters, 1, LANES, LANES, dtype=bf16), pltpu.SemaphoreType.DMA((1,))],
    )
    here = arrived(got, held, [late], started)
    candidate, sums, known = call(
        functools.partial(second_kernel, per_group, unknowns), "operator_two",
        (shape(rows, LANES), shape(size, R, LANES, dtype=bf16), shape(R, LANES)),
        operands + [VMEM], *held, places, *here, *made, field, image, started, scratch_shapes=kept,
    )
    return call(
        functools.partial(finish_kernel, unknowns), "finish", (shape(R, width), shape(R, width)),
        [VMEM] * 5, field, image, candidate, known, exchange(sums),
    )


def solution(mesh):
    return jax.shard_map(
        on_device,
        mesh=mesh,
        in_specs=(
            P("groups", "rows"),
            P("rows", None, None, None),
            P("rows", None),
            P("rows"),
            P("rows", None, None),
            P("rows", None, None),
            P("rows", None, None, None),
            P("rows", None),
        ),
        out_specs=(P("groups", "rows"), P("groups", "rows")),
        check_vma=False,
    )
```

```python
import functools

import jax
import jax.numpy as jnp
from jax import lax
from jax.experimental import pallas as pl
from jax.experimental.pallas import tpu as pltpu
from jax.sharding import PartitionSpec as P

epsilon = 1e-06
f32, bf16 = jnp.float32, jnp.bfloat16
VMEM = pl.BlockSpec(memory_space=pltpu.VMEM)
SMEM = pl.BlockSpec(memory_space=pltpu.SMEM)
HBM = pl.BlockSpec(memory_space=pltpu.HBM)
ANY = pl.BlockSpec(memory_space=pl.ANY)
R = 8
LANES = 128
SUM_SLOTS = 8
TAIL = 16
PARAMS = pltpu.CompilerParams(vmem_limit_bytes=24 * 1024 * 1024)


def lane_ids(rows=R):
    return lax.broadcasted_iota(jnp.int32, (rows, LANES), 1)


def rows_of(ref, j):
    return ref[pl.ds(j * R, R), :]


def dot(a, b, contract=(1, 0)):
    return lax.dot_general(a, b, (((contract[0],), (contract[1],)), ((), ())), preferred_element_type=f32)


def sums_tile(sums):
    lane = lane_ids()
    tile = jnp.zeros((R, LANES), f32)
    for t, partial in enumerate(sums):
        total = jnp.sum(partial, axis=1, keepdims=True)
        high = total.astype(bf16).astype(f32)
        middle = (total - high).astype(bf16).astype(f32)
        low = total - high - middle
        for part, value in enumerate((high, middle, low)):
            tile = jnp.where(lane == part * SUM_SLOTS + t, value, tile)
    return tile


def read_sums(parts, count, unknowns):
    total = jnp.zeros((R, LANES), f32)
    for part in parts:
        total = total + part.astype(f32)[:R]
    return [
        sum(total[:, p * SUM_SLOTS + t : p * SUM_SLOTS + t + 1] for p in range(3)) * (1.0 / unknowns)
        for t in range(count)
    ]


def tails(swaps, rows, head):
    each = head + TAIL
    return [
        values[pl.ds(device * each + head, TAIL), :]
        for values in swaps
        for device in range((values.shape[0] - rows) // each)
    ]


def compress(tiles, basis, group):
    stacked = jnp.concatenate(tiles, axis=0)
    high = stacked.astype(bf16)
    low = (stacked - high.astype(f32)).astype(bf16)
    return dot(jnp.concatenate([high, low], axis=0), basis[pl.ds(group * LANES, LANES), :], (1, 1))


def collect(products, per_group):
    rows = per_group * R
    both = products[:rows] + products[rows:]
    lane = lane_ids()
    tile = jnp.zeros((R, LANES), f32)
    for m in range(per_group):
        tile = jnp.where(lane // (LANES // per_group) == m, both[m * R : (m + 1) * R], tile)
    return tile


def write_payload(payload, parts, sums):
    if sums:
        parts = parts + [sums_tile(sums), jnp.zeros((TAIL - R, LANES), f32)]
    block = jnp.concatenate(parts, axis=0).astype(bf16)
    for device in range(payload.shape[0]):
        payload[device] = block


def start_kernel(per_group, b_hbm, basis_hbm, field, basis, lowered, payload, b, sems):
    copies = [
        pltpu.make_async_copy(b_hbm, b, sems.at[0]),
        pltpu.make_async_copy(basis_hbm, basis, sems.at[1]),
    ]
    for copy in copies:
        copy.start()
    for copy in copies:
        copy.wait()
    clusters = b.shape[1] // LANES
    tiles = [b[:, j * LANES : (j + 1) * LANES] for j in range(clusters)]
    field[...] = jnp.concatenate(tiles, axis=0)
    lowered[...] = jnp.concatenate(tiles, axis=0).astype(bf16)
    groups = [tiles[g : g + per_group] for g in range(0, clusters, per_group)]
    products = [compress(group, basis, g) for g, group in enumerate(groups)]
    write_payload(payload, [collect(product, per_group) for product in products], [])


def window_place(distance, clusters, me):
    core, chip = me % 2, me // 2
    before, after = 3 - chip % 2, 2 + chip % 2
    slot = [before, jnp.where(core == 0, 4, 1), 0, jnp.where(core == 0, 1, 4), after]
    slab = lax.div(distance, clusters)
    chosen = jnp.zeros_like(distance)
    for s, value in enumerate(slot):
        chosen = jnp.where(slab == s, value, chosen)
    return chosen * clusters + lax.rem(distance, clusters)


def prepare_kernel(
    axis, size, middle, near_cols_hbm, near_counts_hbm, far_cols_hbm, coupling_hbm, target_hbm, _,
    places, high_out, low_out, target_out, near_cols, near_counts, far_cols, coupling, target, sems,
):
    pairs = (
        (near_cols_hbm, near_cols), (near_counts_hbm, near_counts), (far_cols_hbm, far_cols),
        (coupling_hbm, coupling), (target_hbm, target),
    )
    copies = [pltpu.make_async_copy(source, to, sems.at[n]) for n, (source, to) in enumerate(pairs)]
    for copy in copies:
        copy.start()
    for copy in copies[:3]:
        copy.wait()
    slots, clusters = near_cols.shape
    me = lax.axis_index(axis)
    every = clusters * size
    distance = near_cols[...] - me * clusters + 2 * clusters
    distance = jnp.where(distance < 0, distance + every, distance)
    distance = jnp.where(distance >= every, distance - every, distance)
    live = lax.broadcasted_iota(jnp.int32, (slots, clusters), 0) < near_counts[...]
    places[:slots, :] = jnp.where(live, window_place(distance, clusters, me), 5 * clusters) * R
    owner = lax.div(far_cols[...], clusters)
    other_core = (owner ^ me) & 1
    chips = size // 2
    chip = lax.rem(middle + chips - owner // 2, chips)
    rank = coupling.shape[1]
    per_group = LANES // rank
    inside = lax.rem(far_cols[...], clusters)
    tile = (other_core * chips + chip) * (clusters // per_group) + lax.div(inside, per_group)
    places[slots : 2 * slots, :] = tile * R
    slot = lax.broadcasted_iota(jnp.int32, (slots, clusters), 0)
    places[2 * slots :, :] = ((slot - inside) * rank) & (LANES - 1)
    for copy in copies[3:5]:
        copy.wait()
    slots, rank, _, clusters = coupling.shape
    per_tile = LANES // clusters
    for s in range(rank // per_tile):
        pieces = [
            coupling[:, s * per_tile + p].reshape(slots * rank, clusters) for p in range(per_tile)
        ]
        tile = jnp.concatenate(pieces, axis=1)
        high = tile.astype(bf16)
        high_out[:, s * LANES : (s + 1) * LANES] = high
        low_out[:, s * LANES : (s + 1) * LANES] = (tile - high.astype(f32)).astype(bf16)
    size = rank * clusters
    row = lax.broadcasted_iota(jnp.int32, (size, 1), 0)
    column = lax.broadcasted_iota(jnp.int32, (size, size), 1)
    wanted = lax.rem(row, clusters) * rank + lax.div(row, clusters)
    target_out[...] = dot((column == wanted).astype(bf16), target[...]).astype(bf16)


def fetch_kernel(slots, blocks_hbm, *refs):
    *_, blocks, token, sems = refs
    chunks = sems.shape[1]
    each = blocks.shape[0] // chunks
    copies, at = [], 0
    for n, (first, count) in enumerate(slots):
        for c in range(chunks):
            clusters = pl.ds(c * each, each)
            copies.append(
                pltpu.make_async_copy(
                    blocks_hbm.at[clusters, pl.ds(first, count)], blocks.at[clusters, pl.ds(at, count)], sems.at[n, c]
                )
            )
        at += count
    for copy in copies:
        copy.start()
    token[...] = jnp.zeros_like(token)
    for copy in copies:
        copy.wait()


def own_kernel(blocks_hbm, own, _, near, blocks, sems):
    chunks = sems.shape[0]
    each = blocks.shape[0] // chunks
    copies = [
        pltpu.make_async_copy(
            blocks_hbm.at[pl.ds(c * each, each), pl.ds(0, 1)], blocks.at[pl.ds(c * each, each)], sems.at[c]
        )
        for c in range(chunks)
    ]
    for copy in copies:
        copy.start()
    products = []
    for c, copy in enumerate(copies):
        copy.wait()
        for i in range(c * each, (c + 1) * each, 2):
            weights = jnp.concatenate([blocks[i, 0], blocks[i + 1, 0]], axis=0)
            products.append(dot(own[pl.ds(i * R, 2 * R), :], weights, (1, 1)))
    for n, both in enumerate(products):
        near[pl.ds(2 * n * R, 2 * R), :] = jnp.concatenate([both[:R, :LANES], both[R:, LANES:]], axis=0)


def relay_kernel(axis, got, even, odd, _, out):
    me = lax.axis_index(axis)
    devices, each, _ = got.shape
    for device in range(devices):
        out[pl.ds(device * each, each), :] = got[device]
    wants_even = (me // 2 + me) % 2 == 0
    span = pl.ds(devices * each, even.shape[0])

    @pl.when(wants_even)
    def _():
        out[span, :] = even[...]

    @pl.when(jnp.logical_not(wants_even))
    def _():
        out[span, :] = odd[...]


def apply(
    per_group, each, slabs, places, ahead, blocks, swaps, high, low, target, near, far, window, table, finish, started
):
    clusters = near.shape[0] // R
    early = ahead.shape[1]
    first = 0 if started is None else 1
    slots = early + blocks.shape[1] + first
    rank = LANES // per_group
    head = clusters // per_group * R
    rows = slabs[0].shape[0]
    devices = (swaps[0].shape[0] - rows) // each
    for at, slab in enumerate(slabs):
        window[pl.ds(at * rows, rows), :] = slab[...].astype(f32)
    window[pl.ds(len(slabs) * rows, rows), :] = swaps[1][pl.ds(devices * each, rows), :].astype(f32)
    window[pl.ds((len(slabs) + 1) * rows, R), :] = jnp.zeros((R, LANES), f32)
    for part, values in enumerate(swaps):
        for device in range(devices):
            at = (part * devices + device) * head
            table[pl.ds(at, head), :] = values[pl.ds(device * each, head), :].astype(f32)
    lane = lane_ids()

    def fetch(k, i):
        return window[pl.ds(pl.multiple_of(places[k, i], R), R), :]

    def block(k, i):
        if 0 < k <= early:
            return ahead[i, k - 1]
        return blocks[i, max(k - early - first, 0)]

    def pick(i):
        tile = jnp.zeros((R, LANES), f32)
        for k in range(slots):
            found = table[pl.ds(pl.multiple_of(places[slots + k, i], R), R), :]
            tile = jnp.where(lane // rank == k, pltpu.roll(found, places[2 * slots + k, i], 1), tile)
        return tile

    def product(i):
        sources = jnp.concatenate(
            [jnp.concatenate([fetch(k, i), fetch(k, i + 1)], axis=0) for k in range(first, slots)], axis=1
        )
        weights = jnp.concatenate(
            [jnp.concatenate([block(k, i), block(k, i + 1)], axis=0) for k in range(first, slots)], axis=1
        )
        return dot(sources.astype(bf16), weights, (1, 1))

    def settle(i, both):
        parts = [both[:R, :LANES], both[R:, LANES:]]
        if started is not None:
            parts = [part + rows_of(started, i + n) for n, part in enumerate(parts)]
        near[pl.ds(i * R, 2 * R), :] = jnp.concatenate(parts, axis=0)

    def expand(crossed):
        spread = []
        for s in range(rank * clusters // LANES):
            tile = jnp.zeros((R, LANES), f32)
            for n in range(clusters):
                part = crossed[n * R : (n + 1) * R, s * LANES : (s + 1) * LANES]
                tile = jnp.where(lane % clusters == n, part, tile)
            tile_high = tile.astype(bf16).astype(f32)
            for n, source in enumerate((tile_high, tile - tile_high)):
                held = [jnp.where(lane % clusters == c, source, 0.0) for c in range(clusters)]
                spread.append((n, jnp.concatenate(held, axis=0).astype(bf16)))
        return [jnp.concatenate([part for m, part in spread if m == n], axis=1) for n in range(2)]

    pairs = clusters // 2
    middle = pairs // 2
    picked, pending, done = [], None, 0
    for p in range(pairs):
        both = product(2 * p)
        if pending is not None:
            settle(2 * p - 2, pending)
        pending = both
        if p < middle:
            picked += [pick(n) for n in range(4 * p, 4 * p + 4)]
        if p == middle - 1:
            chosen = jnp.concatenate(picked, axis=0).astype(bf16)
            crossed = [dot(chosen, high[...]), dot(chosen, low[...])]
        if p == middle:
            spread = expand(crossed[0] + crossed[1])
            made = [dot(part, target[...]) for part in spread]
        if p == middle + 1:
            far[...] = made[0] + made[1]
        if p > middle + 1:
            ready = min(2 * p, done + 6)
            for n in range(done, ready):
                finish(n)
            done = ready
    settle(clusters - 2, pending)
    for n in range(done, clusters):
        finish(n)


def first_kernel(
    per_group, own, mate, even, odd, places, ahead, blocks, sent, received, high, low, target, b, basis,
    image, lowered, payload, near, far, window, table,
):
    clusters = near.shape[0] // R
    slabs, swaps = (own, mate, even, odd), (sent, received)
    each = clusters // per_group * R
    tiles, products, parts = [], [], []
    sums = [jnp.zeros((R, LANES), f32) for _ in range(3)]

    def finish(i):
        field = rows_of(b, i)
        made = 0.5 * field + (rows_of(near, i) + rows_of(far, i))
        sums[:] = [s + f * g for s, f, g in zip(sums, (field, field, made), (field, made, made))]
        tiles.append(made)
        if i % 2:
            both = jnp.concatenate(tiles[i - 1 :], axis=0)
            image[pl.ds((i - 1) * R, 2 * R), :] = both
            lowered[pl.ds((i - 1) * R, 2 * R), :] = both.astype(bf16)
        if i % per_group == per_group - 1:
            products.append(compress(tiles[-per_group:], basis, i // per_group))
            parts.extend(collect(product, per_group) for product in products[-2:-1])

    apply(
        per_group, each, slabs, places, ahead, blocks, swaps, high, low, target, near, far, window, table, finish, None
    )
    write_payload(payload, parts + [collect(products[-1], per_group)], sums)


def arnoldi_one(bb, bw, ww):
    whole = bb + epsilon
    start_norm = jnp.sqrt(whole)
    scale = 1.0 / start_norm
    v11 = bb / whole
    h11 = (bw * scale) * scale
    uu = jnp.maximum((ww * scale) * scale - 2.0 * h11 * h11 + h11 * h11 * v11, 0.0)
    h21 = jnp.sqrt(uu + epsilon)
    return start_norm, h11, h21, v11, uu / (uu + epsilon), h11 * (1.0 - v11) / h21


def second_kernel(
    per_group, unknowns, own, mate, even, odd, places, ahead, blocks, sent, received, high, low, target, b, image,
    started, candidate, sums_out, known, near, far, window, table,
):
    clusters = near.shape[0] // R
    head = clusters // per_group * R
    slabs, swaps = (own, mate, even, odd), (sent, received)
    means = read_sums(tails(swaps, own.shape[0], head), 3, unknowns)
    values = arnoldi_one(*means)
    start_norm, h11, h21, _, _, _ = values
    lane = lane_ids()
    tile = jnp.zeros((R, LANES), f32)
    for n, value in enumerate(values):
        tile = jnp.where(lane == n, value, tile)
    known[...] = tile
    scale = 1.0 / start_norm
    inverse = 1.0 / h21
    sums = [jnp.zeros((R, LANES), f32) for _ in range(3)]

    def finish(j):
        held = rows_of(image, j) * scale
        first = rows_of(b, j) * scale
        second = (held - h11 * first) * inverse
        made = (0.5 * held + (rows_of(near, j) + rows_of(far, j)) * scale - h11 * held) * inverse
        sums[:] = [s + v * made for s, v in zip(sums, (first, second, made))]
        candidate[pl.ds(j * R, R), :] = made

    each = head + TAIL
    apply(
        per_group, each, slabs, places, ahead, blocks, swaps, high, low, target, near, far, window, table, finish, started
    )
    tile = sums_tile(sums).astype(bf16)
    for device in range(sums_out.shape[0]):
        sums_out[device] = tile


def finish_kernel(unknowns, b, image, candidate, known, got, solution_out, next_out):
    clusters = b.shape[0] // R
    start_norm, h11, h21, v11, v22, v12 = [known[:, n : n + 1] for n in range(6)]
    h12, h22, ww = read_sums([got[device] for device in range(got.shape[0])], 3, unknowns)
    uu = ww - 2.0 * (h12 * h12 + h22 * h22) + h12 * h12 * v11 + h22 * h22 * v22 + 2.0 * h12 * h22 * v12
    h32 = jnp.sqrt(jnp.maximum(uu, 0.0) + epsilon)
    g11 = h11 * h11 + h21 * h21
    g12 = h11 * h12 + h21 * h22
    g22 = h12 * h12 + h22 * h22 + h32 * h32
    t1, t2 = start_norm * h11, start_norm * h12
    det = g11 * g22 - g12 * g12
    y1 = (g22 * t1 - g12 * t2) / det
    y2 = (g11 * t2 - g12 * t1) / det
    scale, inverse, last = 1.0 / start_norm, 1.0 / h21, 1.0 / h32
    for j in range(clusters):
        span = slice(j * LANES, (j + 1) * LANES)
        first = rows_of(b, j) * scale
        second = (rows_of(image, j) * scale - h11 * first) * inverse
        solution_out[:, span] = y1 * first + y2 * second
        next_out[:, span] = (rows_of(candidate, j) - h12 * first - h22 * second) * last


def swapped(block, partner):
    return lax.ppermute(block, "rows", [(i, partner(i)) for i in range(lax.axis_size("rows"))])


def core_mate(i):
    return i ^ 1


def even_mate(i):
    return i ^ 2


def odd_mate(i):
    chip = i // 2
    other = chip + 1 if chip % 2 else chip - 1
    return 2 * (other % (lax.axis_size("rows") // 2)) + i % 2


def sends_of(block):
    mate, odd, even = [swapped(block, partner) for partner in (core_mate, odd_mate, even_mate)]
    return [block, mate, even, odd]


def on_device(
    right_sides, near_blocks, near_cols, near_counts, basis_in, target_basis, coupling, far_cols
):
    width = right_sides.shape[1]
    clusters, slots = near_cols.shape
    rank = basis_in.shape[1]
    per_group = LANES // rank
    head = clusters // per_group * R
    size = lax.axis_size("rows")
    unknowns = float(width * size)
    rows = clusters * R

    def shape(*dims, dtype=f32):
        return jax.ShapeDtypeStruct(dims, dtype)

    def scratch(*dims, dtype=f32):
        return pltpu.VMEM(dims, dtype)

    def in_hbm(array):
        return pltpu.with_memory_space_constraint(array, pltpu.HBM)

    def call(kernel, name, out, ins, *args, scratch_shapes=()):
        return pl.pallas_call(
            kernel, out_shape=out, in_specs=ins, out_specs=jax.tree.map(lambda _: VMEM, out),
            scratch_shapes=scratch_shapes, compiler_params=PARAMS, name=name,
        )(*args)

    chips = size // 2
    middle = chips // 4 + 1
    order = [(middle - n) % chips for n in range(chips)]

    def gather(block):
        groups = [[2 * chip + core for chip in order] for core in range(2)]
        return lax.all_to_all(block, "rows", 0, 0, axis_index_groups=groups)

    def exchange(block):
        group = [2 * chip + core for chip in order for core in range(2)]
        return lax.all_to_all(block, "rows", 0, 0, axis_index_groups=[group])

    field, basis, lowered, payload = call(
        functools.partial(start_kernel, per_group), "start",
        (
            shape(rows, LANES), shape(clusters * rank, LANES, dtype=bf16), shape(rows, LANES, dtype=bf16),
            shape(size // 2, head, LANES, dtype=bf16),
        ),
        [HBM] * 2, in_hbm(right_sides), in_hbm(basis_in.reshape(clusters * rank, LANES)),
        scratch_shapes=[scratch(R, width), pltpu.SemaphoreType.DMA((2,))],
    )
    got = gather(payload)
    held = sends_of(lowered)

    blocks = in_hbm(near_blocks)
    early = 2

    def fetch(name, ranges, chunks, *behind):
        count = sum(count for _, count in ranges)
        here, token = call(
            functools.partial(fetch_kernel, ranges), name,
            (pltpu.VMEM((clusters, count, LANES, LANES), bf16), shape(R, LANES)),
            [HBM] + [ANY] * len(behind), blocks, *behind,
            scratch_shapes=[pltpu.SemaphoreType.DMA((len(ranges), chunks))],
        )
        return pltpu.with_memory_space_constraint(here, pltpu.VMEM), token

    def arrived(got, held, ranges, behind):
        rest, token = fetch("fetch", ranges, 1, got, behind)
        sent = call(
            functools.partial(relay_kernel, "rows"), "relay",
            shape(got.shape[0] * got.shape[1] + rows, LANES, dtype=bf16), [VMEM] * 3 + [ANY], got, *held[2:], token
        )
        return ahead, rest, sent, swapped(sent, core_mate)

    late = (1 + early, slots - 1 - early)
    ahead, token = fetch("ahead", [(1, early)], 1, held[1])
    here = arrived(got, held, [(0, 1), late], token)
    prepared = call(
        functools.partial(prepare_kernel, "rows", size, middle), "prepare",
        (
            shape(3 * slots, clusters, dtype=jnp.int32),
            shape(slots * rank, rank * clusters, dtype=bf16),
            shape(slots * rank, rank * clusters, dtype=bf16),
            shape(rank * clusters, LANES, dtype=bf16),
        ),
        [HBM] * 5 + [ANY], in_hbm(near_cols.T), in_hbm(near_counts.reshape(1, clusters)), in_hbm(far_cols.T),
        in_hbm(jnp.transpose(coupling, (1, 2, 3, 0))), in_hbm(target_basis.reshape(clusters * rank, LANES)), here[2],
        scratch_shapes=[
            scratch(slots, clusters, dtype=jnp.int32), scratch(1, clusters, dtype=jnp.int32),
            scratch(slots, clusters, dtype=jnp.int32),
            scratch(slots, rank, rank, clusters), scratch(clusters * rank, LANES, dtype=bf16),
            pltpu.SemaphoreType.DMA((5,)),
        ],
    )
    places, *made = prepared
    kept = [scratch(rows, LANES), scratch(rows, LANES), scratch(5 * rows + R, LANES), scratch(size * head, LANES)]
    operands = [VMEM] * 4 + [SMEM] + [VMEM] * 9
    image, lowered, payload = call(
        functools.partial(first_kernel, per_group), "operator_one",
        (
            shape(rows, LANES), shape(rows, LANES, dtype=bf16),
            shape(size // 2, head + TAIL, LANES, dtype=bf16),
        ),
        operands, *held, places, *here, *made, field, basis, scratch_shapes=kept,
    )
    got = gather(payload)
    held = sends_of(lowered)
    started = call(
        own_kernel, "own", shape(rows, LANES), [HBM, VMEM, ANY], blocks, lowered, held[1],
        scratch_shapes=[scratch(clusters, 1, LANES, LANES, dtype=bf16), pltpu.SemaphoreType.DMA((1,))],
    )
    here = arrived(got, held, [late], started)
    candidate, sums, known = call(
        functools.partial(second_kernel, per_group, unknowns), "operator_two",
        (shape(rows, LANES), shape(size, R, LANES, dtype=bf16), shape(R, LANES)),
        operands + [VMEM], *held, places, *here, *made, field, image, started, scratch_shapes=kept,
    )
    return call(
        functools.partial(finish_kernel, unknowns), "finish", (shape(R, width), shape(R, width)),
        [VMEM] * 5, field, image, candidate, known, exchange(sums),
    )


def solution(mesh):
    return jax.shard_map(
        on_device,
        mesh=mesh,
        in_specs=(
            P("groups", "rows"),
            P("rows", None, None, None),
            P("rows", None),
            P("rows"),
            P("rows", None, None),
            P("rows", None, None),
            P("rows", None, None, None),
            P("rows", None),
        ),
        out_specs=(P("groups", "rows"), P("groups", "rows")),
        check_vma=False,
    )
```

```python
import functools

import jax
import jax.numpy as jnp
from jax import lax
from jax.experimental import pallas as pl
from jax.experimental.pallas import tpu as pltpu
from jax.sharding import PartitionSpec as P

epsilon = 1e-06
f32, bf16 = jnp.float32, jnp.bfloat16
VMEM = pl.BlockSpec(memory_space=pltpu.VMEM)
SMEM = pl.BlockSpec(memory_space=pltpu.SMEM)
HBM = pl.BlockSpec(memory_space=pltpu.HBM)
ANY = pl.BlockSpec(memory_space=pl.ANY)
R = 8
LANES = 128
SUM_SLOTS = 8
TAIL = 16
PARAMS = pltpu.CompilerParams(vmem_limit_bytes=24 * 1024 * 1024)


def lane_ids(rows=R):
    return lax.broadcasted_iota(jnp.int32, (rows, LANES), 1)


def rows_of(ref, j):
    return ref[pl.ds(j * R, R), :]


def dot(a, b, contract=(1, 0)):
    return lax.dot_general(a, b, (((contract[0],), (contract[1],)), ((), ())), preferred_element_type=f32)


def sums_tile(sums):
    lane = lane_ids()
    tile = jnp.zeros((R, LANES), f32)
    for t, partial in enumerate(sums):
        total = jnp.sum(partial, axis=1, keepdims=True)
        high = total.astype(bf16).astype(f32)
        middle = (total - high).astype(bf16).astype(f32)
        low = total - high - middle
        for part, value in enumerate((high, middle, low)):
            tile = jnp.where(lane == part * SUM_SLOTS + t, value, tile)
    return tile


def read_sums(parts, count, unknowns):
    total = jnp.zeros((R, LANES), f32)
    for part in parts:
        total = total + part.astype(f32)[:R]
    return [
        sum(total[:, p * SUM_SLOTS + t : p * SUM_SLOTS + t + 1] for p in range(3)) * (1.0 / unknowns)
        for t in range(count)
    ]


def tails(swaps, rows, head):
    each = head + TAIL
    return [
        values[pl.ds(device * each + head, TAIL), :]
        for values in swaps
        for device in range((values.shape[0] - rows) // each)
    ]


def compress(tiles, basis, group):
    stacked = jnp.concatenate(tiles, axis=0)
    high = stacked.astype(bf16)
    low = (stacked - high.astype(f32)).astype(bf16)
    return dot(jnp.concatenate([high, low], axis=0), basis[pl.ds(group * LANES, LANES), :], (1, 1))


def collect(products, per_group):
    rows = per_group * R
    both = products[:rows] + products[rows:]
    lane = lane_ids()
    tile = jnp.zeros((R, LANES), f32)
    for m in range(per_group):
        tile = jnp.where(lane // (LANES // per_group) == m, both[m * R : (m + 1) * R], tile)
    return tile


def write_payload(payload, parts, sums):
    if sums:
        parts = parts + [sums_tile(sums), jnp.zeros((TAIL - R, LANES), f32)]
    block = jnp.concatenate(parts, axis=0).astype(bf16)
    for device in range(payload.shape[0]):
        payload[device] = block


def start_kernel(per_group, b_hbm, basis_hbm, field, basis, lowered, payload, b, sems):
    copies = [
        pltpu.make_async_copy(b_hbm, b, sems.at[0]),
        pltpu.make_async_copy(basis_hbm, basis, sems.at[1]),
    ]
    for copy in copies:
        copy.start()
    for copy in copies:
        copy.wait()
    clusters = b.shape[1] // LANES
    tiles = [b[:, j * LANES : (j + 1) * LANES] for j in range(clusters)]
    field[...] = jnp.concatenate(tiles, axis=0)
    lowered[...] = jnp.concatenate(tiles, axis=0).astype(bf16)
    groups = [tiles[g : g + per_group] for g in range(0, clusters, per_group)]
    products = [compress(group, basis, g) for g, group in enumerate(groups)]
    write_payload(payload, [collect(product, per_group) for product in products], [])


def window_place(distance, clusters, me):
    core, chip = me % 2, me // 2
    before, after = 3 - chip % 2, 2 + chip % 2
    slot = [before, jnp.where(core == 0, 4, 1), 0, jnp.where(core == 0, 1, 4), after]
    slab = lax.div(distance, clusters)
    chosen = jnp.zeros_like(distance)
    for s, value in enumerate(slot):
        chosen = jnp.where(slab == s, value, chosen)
    return chosen * clusters + lax.rem(distance, clusters)


def prepare_kernel(
    axis, size, middle, near_cols_hbm, near_counts_hbm, far_cols_hbm, coupling_hbm, target_hbm, _,
    places, high_out, low_out, target_out, near_cols, near_counts, far_cols, coupling, target, sems,
):
    pairs = (
        (coupling_hbm, coupling), (near_cols_hbm, near_cols), (near_counts_hbm, near_counts),
        (far_cols_hbm, far_cols), (target_hbm, target),
    )
    copies = [pltpu.make_async_copy(source, to, sems.at[n]) for n, (source, to) in enumerate(pairs)]
    for copy in copies:
        copy.start()
    for copy in copies[1:4]:
        copy.wait()
    slots, clusters = near_cols.shape
    me = lax.axis_index(axis)
    every = clusters * size
    distance = near_cols[...] - me * clusters + 2 * clusters
    distance = jnp.where(distance < 0, distance + every, distance)
    distance = jnp.where(distance >= every, distance - every, distance)
    live = lax.broadcasted_iota(jnp.int32, (slots, clusters), 0) < near_counts[...]
    places[:slots, :] = jnp.where(live, window_place(distance, clusters, me), 5 * clusters) * R
    owner = lax.div(far_cols[...], clusters)
    other_core = (owner ^ me) & 1
    chips = size // 2
    chip = lax.rem(middle + chips - owner // 2, chips)
    rank = coupling.shape[1]
    per_group = LANES // rank
    inside = lax.rem(far_cols[...], clusters)
    tile = (other_core * chips + chip) * (clusters // per_group) + lax.div(inside, per_group)
    places[slots : 2 * slots, :] = tile * R
    slot = lax.broadcasted_iota(jnp.int32, (slots, clusters), 0)
    places[2 * slots :, :] = ((slot - inside) * rank) & (LANES - 1)
    _, rank, _, clusters = coupling.shape
    size = rank * clusters
    row = lax.broadcasted_iota(jnp.int32, (size, 1), 0)
    column = lax.broadcasted_iota(jnp.int32, (size, size), 1)
    wanted = lax.rem(row, clusters) * rank + lax.div(row, clusters)
    picks = (column == wanted).astype(bf16)
    copies[4].wait()
    target_out[...] = dot(picks, target[...]).astype(bf16)
    copies[0].wait()
    per_tile = LANES // clusters
    for s in range(rank // per_tile):
        pieces = [
            coupling[:, s * per_tile + p].reshape(slots * rank, clusters) for p in range(per_tile)
        ]
        tile = jnp.concatenate(pieces, axis=1)
        high = tile.astype(bf16)
        high_out[:, s * LANES : (s + 1) * LANES] = high
        low_out[:, s * LANES : (s + 1) * LANES] = (tile - high.astype(f32)).astype(bf16)


def fetch_kernel(slots, blocks_hbm, *refs):
    *_, blocks, token, sems = refs
    chunks = sems.shape[1]
    each = blocks.shape[0] // chunks
    copies, at = [], 0
    for n, (first, count) in enumerate(slots):
        for c in range(chunks):
            clusters = pl.ds(c * each, each)
            copies.append(
                pltpu.make_async_copy(
                    blocks_hbm.at[clusters, pl.ds(first, count)], blocks.at[clusters, pl.ds(at, count)], sems.at[n, c]
                )
            )
        at += count
    for copy in copies:
        copy.start()
    token[...] = jnp.zeros_like(token)
    for copy in copies:
        copy.wait()


def own_kernel(blocks_hbm, own, _, near, blocks, sems):
    chunks = sems.shape[0]
    each = blocks.shape[0] // chunks
    copies = [
        pltpu.make_async_copy(
            blocks_hbm.at[pl.ds(c * each, each), pl.ds(0, 1)], blocks.at[pl.ds(c * each, each)], sems.at[c]
        )
        for c in range(chunks)
    ]
    for copy in copies:
        copy.start()
    products = []
    for c, copy in enumerate(copies):
        copy.wait()
        for i in range(c * each, (c + 1) * each, 2):
            weights = jnp.concatenate([blocks[i, 0], blocks[i + 1, 0]], axis=0)
            products.append(dot(own[pl.ds(i * R, 2 * R), :], weights, (1, 1)))
    for n, both in enumerate(products):
        near[pl.ds(2 * n * R, 2 * R), :] = jnp.concatenate([both[:R, :LANES], both[R:, LANES:]], axis=0)


def relay_kernel(axis, got, even, odd, _, out):
    me = lax.axis_index(axis)
    devices, each, _ = got.shape
    for device in range(devices):
        out[pl.ds(device * each, each), :] = got[device]
    wants_even = (me // 2 + me) % 2 == 0
    span = pl.ds(devices * each, even.shape[0])

    @pl.when(wants_even)
    def _():
        out[span, :] = even[...]

    @pl.when(jnp.logical_not(wants_even))
    def _():
        out[span, :] = odd[...]


def apply(
    per_group, each, slabs, places, ahead, blocks, swaps, high, low, target, near, far, window, table, finish, started
):
    clusters = near.shape[0] // R
    early = ahead.shape[1]
    first = 0 if started is None else 1
    slots = early + blocks.shape[1] + first
    rank = LANES // per_group
    head = clusters // per_group * R
    rows = slabs[0].shape[0]
    devices = (swaps[0].shape[0] - rows) // each
    for at, slab in enumerate(slabs):
        window[pl.ds(at * rows, rows), :] = slab[...].astype(f32)
    window[pl.ds(len(slabs) * rows, rows), :] = swaps[1][pl.ds(devices * each, rows), :].astype(f32)
    window[pl.ds((len(slabs) + 1) * rows, R), :] = jnp.zeros((R, LANES), f32)
    for part, values in enumerate(swaps):
        for device in range(devices):
            at = (part * devices + device) * head
            table[pl.ds(at, head), :] = values[pl.ds(device * each, head), :].astype(f32)
    lane = lane_ids()

    def fetch(k, i):
        return window[pl.ds(pl.multiple_of(places[k, i], R), R), :]

    def block(k, i):
        if 0 < k <= early:
            return ahead[i, k - 1]
        return blocks[i, max(k - early - first, 0)]

    def pick(i):
        tile = jnp.zeros((R, LANES), f32)
        for k in range(slots):
            found = table[pl.ds(pl.multiple_of(places[slots + k, i], R), R), :]
            tile = jnp.where(lane // rank == k, pltpu.roll(found, places[2 * slots + k, i], 1), tile)
        return tile

    def product(i):
        sources = jnp.concatenate(
            [jnp.concatenate([fetch(k, i), fetch(k, i + 1)], axis=0) for k in range(first, slots)], axis=1
        )
        weights = jnp.concatenate(
            [jnp.concatenate([block(k, i), block(k, i + 1)], axis=0) for k in range(first, slots)], axis=1
        )
        return dot(sources.astype(bf16), weights, (1, 1))

    def settle(i, both):
        parts = [both[:R, :LANES], both[R:, LANES:]]
        if started is not None:
            parts = [part + rows_of(started, i + n) for n, part in enumerate(parts)]
        near[pl.ds(i * R, 2 * R), :] = jnp.concatenate(parts, axis=0)

    def expand(crossed):
        spread = []
        for s in range(rank * clusters // LANES):
            tile = jnp.zeros((R, LANES), f32)
            for n in range(clusters):
                part = crossed[n * R : (n + 1) * R, s * LANES : (s + 1) * LANES]
                tile = jnp.where(lane % clusters == n, part, tile)
            tile_high = tile.astype(bf16).astype(f32)
            for n, source in enumerate((tile_high, tile - tile_high)):
                held = [jnp.where(lane % clusters == c, source, 0.0) for c in range(clusters)]
                spread.append((n, jnp.concatenate(held, axis=0).astype(bf16)))
        return [jnp.concatenate([part for m, part in spread if m == n], axis=1) for n in range(2)]

    pairs = clusters // 2
    middle = pairs // 2
    picked, pending, done = [], None, 0
    for p in range(pairs):
        both = product(2 * p)
        if pending is not None:
            settle(2 * p - 2, pending)
        pending = both
        if p < middle:
            picked += [pick(n) for n in range(4 * p, 4 * p + 4)]
        if p == middle - 1:
            chosen = jnp.concatenate(picked, axis=0).astype(bf16)
            crossed = [dot(chosen, high[...]), dot(chosen, low[...])]
        if p == middle:
            spread = expand(crossed[0] + crossed[1])
            made = [dot(part, target[...]) for part in spread]
        if p == middle + 1:
            far[...] = made[0] + made[1]
        if p > middle + 1:
            ready = min(2 * p, done + 6)
            for n in range(done, ready):
                finish(n)
            done = ready
    settle(clusters - 2, pending)
    for n in range(done, clusters):
        finish(n)


def first_kernel(
    per_group, own, mate, even, odd, places, ahead, blocks, sent, received, high, low, target, b, basis,
    image, lowered, payload, near, far, window, table,
):
    clusters = near.shape[0] // R
    slabs, swaps = (own, mate, even, odd), (sent, received)
    each = clusters // per_group * R
    tiles, products, parts = [], [], []
    sums = [jnp.zeros((R, LANES), f32) for _ in range(3)]

    def finish(i):
        field = rows_of(b, i)
        made = 0.5 * field + (rows_of(near, i) + rows_of(far, i))
        sums[:] = [s + f * g for s, f, g in zip(sums, (field, field, made), (field, made, made))]
        tiles.append(made)
        if i % 2:
            both = jnp.concatenate(tiles[i - 1 :], axis=0)
            image[pl.ds((i - 1) * R, 2 * R), :] = both
            lowered[pl.ds((i - 1) * R, 2 * R), :] = both.astype(bf16)
        if i % per_group == per_group - 1:
            products.append(compress(tiles[-per_group:], basis, i // per_group))
            parts.extend(collect(product, per_group) for product in products[-2:-1])

    apply(
        per_group, each, slabs, places, ahead, blocks, swaps, high, low, target, near, far, window, table, finish, None
    )
    write_payload(payload, parts + [collect(products[-1], per_group)], sums)


def arnoldi_one(bb, bw, ww):
    whole = bb + epsilon
    start_norm = jnp.sqrt(whole)
    scale = 1.0 / start_norm
    v11 = bb / whole
    h11 = (bw * scale) * scale
    uu = jnp.maximum((ww * scale) * scale - 2.0 * h11 * h11 + h11 * h11 * v11, 0.0)
    h21 = jnp.sqrt(uu + epsilon)
    return start_norm, h11, h21, v11, uu / (uu + epsilon), h11 * (1.0 - v11) / h21


def second_kernel(
    per_group, unknowns, own, mate, even, odd, places, ahead, blocks, sent, received, high, low, target, b, image,
    started, candidate, sums_out, known, near, far, window, table,
):
    clusters = near.shape[0] // R
    head = clusters // per_group * R
    slabs, swaps = (own, mate, even, odd), (sent, received)
    means = read_sums(tails(swaps, own.shape[0], head), 3, unknowns)
    values = arnoldi_one(*means)
    start_norm, h11, h21, _, _, _ = values
    lane = lane_ids()
    tile = jnp.zeros((R, LANES), f32)
    for n, value in enumerate(values):
        tile = jnp.where(lane == n, value, tile)
    known[...] = tile
    scale = 1.0 / start_norm
    inverse = 1.0 / h21
    sums = [jnp.zeros((R, LANES), f32) for _ in range(3)]

    def finish(j):
        held = rows_of(image, j) * scale
        first = rows_of(b, j) * scale
        second = (held - h11 * first) * inverse
        made = (0.5 * held + (rows_of(near, j) + rows_of(far, j)) * scale - h11 * held) * inverse
        sums[:] = [s + v * made for s, v in zip(sums, (first, second, made))]
        candidate[pl.ds(j * R, R), :] = made

    each = head + TAIL
    apply(
        per_group, each, slabs, places, ahead, blocks, swaps, high, low, target, near, far, window, table, finish, started
    )
    tile = sums_tile(sums).astype(bf16)
    for device in range(sums_out.shape[0]):
        sums_out[device] = tile


def finish_kernel(unknowns, b, image, candidate, known, got, solution_out, next_out):
    clusters = b.shape[0] // R
    start_norm, h11, h21, v11, v22, v12 = [known[:, n : n + 1] for n in range(6)]
    h12, h22, ww = read_sums([got[device] for device in range(got.shape[0])], 3, unknowns)
    uu = ww - 2.0 * (h12 * h12 + h22 * h22) + h12 * h12 * v11 + h22 * h22 * v22 + 2.0 * h12 * h22 * v12
    h32 = jnp.sqrt(jnp.maximum(uu, 0.0) + epsilon)
    g11 = h11 * h11 + h21 * h21
    g12 = h11 * h12 + h21 * h22
    g22 = h12 * h12 + h22 * h22 + h32 * h32
    t1, t2 = start_norm * h11, start_norm * h12
    det = g11 * g22 - g12 * g12
    y1 = (g22 * t1 - g12 * t2) / det
    y2 = (g11 * t2 - g12 * t1) / det
    scale, inverse, last = 1.0 / start_norm, 1.0 / h21, 1.0 / h32
    for j in range(clusters):
        span = slice(j * LANES, (j + 1) * LANES)
        first = rows_of(b, j) * scale
        second = (rows_of(image, j) * scale - h11 * first) * inverse
        solution_out[:, span] = y1 * first + y2 * second
        next_out[:, span] = (rows_of(candidate, j) - h12 * first - h22 * second) * last


def swapped(block, partner):
    return lax.ppermute(block, "rows", [(i, partner(i)) for i in range(lax.axis_size("rows"))])


def core_mate(i):
    return i ^ 1


def even_mate(i):
    return i ^ 2


def odd_mate(i):
    chip = i // 2
    other = chip + 1 if chip % 2 else chip - 1
    return 2 * (other % (lax.axis_size("rows") // 2)) + i % 2


def sends_of(block):
    mate, odd, even = [swapped(block, partner) for partner in (core_mate, odd_mate, even_mate)]
    return [block, mate, even, odd]


def on_device(
    right_sides, near_blocks, near_cols, near_counts, basis_in, target_basis, coupling, far_cols
):
    width = right_sides.shape[1]
    clusters, slots = near_cols.shape
    rank = basis_in.shape[1]
    per_group = LANES // rank
    head = clusters // per_group * R
    size = lax.axis_size("rows")
    unknowns = float(width * size)
    rows = clusters * R

    def shape(*dims, dtype=f32):
        return jax.ShapeDtypeStruct(dims, dtype)

    def scratch(*dims, dtype=f32):
        return pltpu.VMEM(dims, dtype)

    def in_hbm(array):
        return pltpu.with_memory_space_constraint(array, pltpu.HBM)

    def call(kernel, name, out, ins, *args, scratch_shapes=()):
        return pl.pallas_call(
            kernel, out_shape=out, in_specs=ins, out_specs=jax.tree.map(lambda _: VMEM, out),
            scratch_shapes=scratch_shapes, compiler_params=PARAMS, name=name,
        )(*args)

    chips = size // 2
    middle = chips // 4 + 1
    order = [(middle - n) % chips for n in range(chips)]

    def gather(block):
        groups = [[2 * chip + core for chip in order] for core in range(2)]
        return lax.all_to_all(block, "rows", 0, 0, axis_index_groups=groups)

    def exchange(block):
        group = [2 * chip + core for chip in order for core in range(2)]
        return lax.all_to_all(block, "rows", 0, 0, axis_index_groups=[group])

    field, basis, lowered, payload = call(
        functools.partial(start_kernel, per_group), "start",
        (
            shape(rows, LANES), shape(clusters * rank, LANES, dtype=bf16), shape(rows, LANES, dtype=bf16),
            shape(size // 2, head, LANES, dtype=bf16),
        ),
        [HBM] * 2, in_hbm(right_sides), in_hbm(basis_in.reshape(clusters * rank, LANES)),
        scratch_shapes=[scratch(R, width), pltpu.SemaphoreType.DMA((2,))],
    )
    got = gather(payload)
    held = sends_of(lowered)

    blocks = in_hbm(near_blocks)
    early = 2

    def fetch(name, ranges, chunks, *behind):
        count = sum(count for _, count in ranges)
        here, token = call(
            functools.partial(fetch_kernel, ranges), name,
            (pltpu.VMEM((clusters, count, LANES, LANES), bf16), shape(R, LANES)),
            [HBM] + [ANY] * len(behind), blocks, *behind,
            scratch_shapes=[pltpu.SemaphoreType.DMA((len(ranges), chunks))],
        )
        return pltpu.with_memory_space_constraint(here, pltpu.VMEM), token

    def arrived(got, held, ranges, behind):
        rest, token = fetch("fetch", ranges, 1, got, behind)
        sent = call(
            functools.partial(relay_kernel, "rows"), "relay",
            shape(got.shape[0] * got.shape[1] + rows, LANES, dtype=bf16), [VMEM] * 3 + [ANY], got, *held[2:], token
        )
        return ahead, rest, sent, swapped(sent, core_mate)

    late = (1 + early, slots - 1 - early)
    ahead, token = fetch("ahead", [(1, early)], 1, held[1])
    here = arrived(got, held, [(0, 1), late], token)
    prepared = call(
        functools.partial(prepare_kernel, "rows", size, middle), "prepare",
        (
            shape(3 * slots, clusters, dtype=jnp.int32),
            shape(slots * rank, rank * clusters, dtype=bf16),
            shape(slots * rank, rank * clusters, dtype=bf16),
            shape(rank * clusters, LANES, dtype=bf16),
        ),
        [HBM] * 5 + [ANY], in_hbm(near_cols.T), in_hbm(near_counts.reshape(1, clusters)), in_hbm(far_cols.T),
        in_hbm(jnp.transpose(coupling, (1, 2, 3, 0))), in_hbm(target_basis.reshape(clusters * rank, LANES)), here[2],
        scratch_shapes=[
            scratch(slots, clusters, dtype=jnp.int32), scratch(1, clusters, dtype=jnp.int32),
            scratch(slots, clusters, dtype=jnp.int32),
            scratch(slots, rank, rank, clusters), scratch(clusters * rank, LANES, dtype=bf16),
            pltpu.SemaphoreType.DMA((5,)),
        ],
    )
    places, *made = prepared
    kept = [scratch(rows, LANES), scratch(rows, LANES), scratch(5 * rows + R, LANES), scratch(size * head, LANES)]
    operands = [VMEM] * 4 + [SMEM] + [VMEM] * 9
    image, lowered, payload = call(
        functools.partial(first_kernel, per_group), "operator_one",
        (
            shape(rows, LANES), shape(rows, LANES, dtype=bf16),
            shape(size // 2, head + TAIL, LANES, dtype=bf16),
        ),
        operands, *held, places, *here, *made, field, basis, scratch_shapes=kept,
    )
    got = gather(payload)
    held = sends_of(lowered)
    started = call(
        own_kernel, "own", shape(rows, LANES), [HBM, VMEM, ANY], blocks, lowered, held[1],
        scratch_shapes=[scratch(clusters, 1, LANES, LANES, dtype=bf16), pltpu.SemaphoreType.DMA((1,))],
    )
    here = arrived(got, held, [late], started)
    candidate, sums, known = call(
        functools.partial(second_kernel, per_group, unknowns), "operator_two",
        (shape(rows, LANES), shape(size, R, LANES, dtype=bf16), shape(R, LANES)),
        operands + [VMEM], *held, places, *here, *made, field, image, started, scratch_shapes=kept,
    )
    return call(
        functools.partial(finish_kernel, unknowns), "finish", (shape(R, width), shape(R, width)),
        [VMEM] * 5, field, image, candidate, known, exchange(sums),
    )


def solution(mesh):
    return jax.shard_map(
        on_device,
        mesh=mesh,
        in_specs=(
            P("groups", "rows"),
            P("rows", None, None, None),
            P("rows", None),
            P("rows"),
            P("rows", None, None),
            P("rows", None, None),
            P("rows", None, None, None),
            P("rows", None),
        ),
        out_specs=(P("groups", "rows"), P("groups", "rows")),
        check_vma=False,
    )
```

```python
import functools

import jax
import jax.numpy as jnp
from jax import lax
from jax.experimental import pallas as pl
from jax.experimental.pallas import tpu as pltpu
from jax.sharding import PartitionSpec as P

epsilon = 1e-06
f32, bf16 = jnp.float32, jnp.bfloat16
VMEM = pl.BlockSpec(memory_space=pltpu.VMEM)
SMEM = pl.BlockSpec(memory_space=pltpu.SMEM)
HBM = pl.BlockSpec(memory_space=pltpu.HBM)
ANY = pl.BlockSpec(memory_space=pl.ANY)
R = 8
LANES = 128
SUM_SLOTS = 8
TAIL = 16
PARAMS = pltpu.CompilerParams(vmem_limit_bytes=24 * 1024 * 1024)


def lane_ids(rows=R):
    return lax.broadcasted_iota(jnp.int32, (rows, LANES), 1)


def rows_of(ref, j):
    return ref[pl.ds(j * R, R), :]


def dot(a, b, contract=(1, 0)):
    return lax.dot_general(a, b, (((contract[0],), (contract[1],)), ((), ())), preferred_element_type=f32)


def sums_tile(sums):
    lane = lane_ids()
    tile = jnp.zeros((R, LANES), f32)
    for t, partial in enumerate(sums):
        total = jnp.sum(partial, axis=1, keepdims=True)
        high = total.astype(bf16).astype(f32)
        middle = (total - high).astype(bf16).astype(f32)
        low = total - high - middle
        for part, value in enumerate((high, middle, low)):
            tile = jnp.where(lane == part * SUM_SLOTS + t, value, tile)
    return tile


def read_sums(parts, count, unknowns):
    total = jnp.zeros((R, LANES), f32)
    for part in parts:
        total = total + part.astype(f32)[:R]
    return [
        sum(total[:, p * SUM_SLOTS + t : p * SUM_SLOTS + t + 1] for p in range(3)) * (1.0 / unknowns)
        for t in range(count)
    ]


def tails(swaps, rows, head):
    each = head + TAIL
    return [
        values[pl.ds(device * each + head, TAIL), :]
        for values in swaps
        for device in range((values.shape[0] - rows) // each)
    ]


def compress(tiles, basis, group):
    stacked = jnp.concatenate(tiles, axis=0)
    high = stacked.astype(bf16)
    low = (stacked - high.astype(f32)).astype(bf16)
    return dot(jnp.concatenate([high, low], axis=0), basis[pl.ds(group * LANES, LANES), :], (1, 1))


def collect(products, per_group):
    rows = per_group * R
    both = products[:rows] + products[rows:]
    lane = lane_ids()
    tile = jnp.zeros((R, LANES), f32)
    for m in range(per_group):
        tile = jnp.where(lane // (LANES // per_group) == m, both[m * R : (m + 1) * R], tile)
    return tile


def write_payload(payload, parts, sums):
    if sums:
        parts = parts + [sums_tile(sums), jnp.zeros((TAIL - R, LANES), f32)]
    block = jnp.concatenate(parts, axis=0).astype(bf16)
    for device in range(payload.shape[0]):
        payload[device] = block


def start_kernel(per_group, b_hbm, basis_hbm, field, basis, lowered, payload, b, sems):
    copies = [
        pltpu.make_async_copy(b_hbm, b, sems.at[0]),
        pltpu.make_async_copy(basis_hbm, basis, sems.at[1]),
    ]
    for copy in copies:
        copy.start()
    for copy in copies:
        copy.wait()
    clusters = b.shape[1] // LANES
    tiles = [b[:, j * LANES : (j + 1) * LANES] for j in range(clusters)]
    field[...] = jnp.concatenate(tiles, axis=0)
    lowered[...] = jnp.concatenate(tiles, axis=0).astype(bf16)
    groups = [tiles[g : g + per_group] for g in range(0, clusters, per_group)]
    products = [compress(group, basis, g) for g, group in enumerate(groups)]
    write_payload(payload, [collect(product, per_group) for product in products], [])


def window_place(distance, clusters, me):
    core, chip = me % 2, me // 2
    before, after = 3 - chip % 2, 2 + chip % 2
    slot = [before, jnp.where(core == 0, 4, 1), 0, jnp.where(core == 0, 1, 4), after]
    slab = lax.div(distance, clusters)
    chosen = jnp.zeros_like(distance)
    for s, value in enumerate(slot):
        chosen = jnp.where(slab == s, value, chosen)
    return chosen * clusters + lax.rem(distance, clusters)


def prepare_kernel(
    axis, size, middle, near_cols_hbm, near_counts_hbm, far_cols_hbm, coupling_hbm, target_hbm, _,
    places, high_out, low_out, target_out, near_cols, near_counts, far_cols, coupling, target, sems,
):
    pairs = (
        (near_cols_hbm, near_cols), (near_counts_hbm, near_counts), (far_cols_hbm, far_cols),
        (coupling_hbm, coupling), (target_hbm, target),
    )
    copies = [pltpu.make_async_copy(source, to, sems.at[n]) for n, (source, to) in enumerate(pairs)]
    for copy in copies:
        copy.start()
    for copy in copies[:3]:
        copy.wait()
    slots, clusters = near_cols.shape
    me = lax.axis_index(axis)
    every = clusters * size
    distance = near_cols[...] - me * clusters + 2 * clusters
    distance = jnp.where(distance < 0, distance + every, distance)
    distance = jnp.where(distance >= every, distance - every, distance)
    live = lax.broadcasted_iota(jnp.int32, (slots, clusters), 0) < near_counts[...]
    places[:slots, :] = jnp.where(live, window_place(distance, clusters, me), 5 * clusters) * R
    owner = lax.div(far_cols[...], clusters)
    other_core = (owner ^ me) & 1
    chips = size // 2
    chip = lax.rem(middle + chips - owner // 2, chips)
    rank = coupling.shape[1]
    per_group = LANES // rank
    inside = lax.rem(far_cols[...], clusters)
    tile = (other_core * chips + chip) * (clusters // per_group) + lax.div(inside, per_group)
    places[slots : 2 * slots, :] = tile * R
    slot = lax.broadcasted_iota(jnp.int32, (slots, clusters), 0)
    places[2 * slots :, :] = ((slot - inside) * rank) & (LANES - 1)
    for copy in copies[3:5]:
        copy.wait()
    slots, rank, _, clusters = coupling.shape
    per_tile = LANES // clusters
    for s in range(rank // per_tile):
        pieces = [
            coupling[:, s * per_tile + p].reshape(slots * rank, clusters) for p in range(per_tile)
        ]
        tile = jnp.concatenate(pieces, axis=1)
        high = tile.astype(bf16)
        high_out[:, s * LANES : (s + 1) * LANES] = high
        low_out[:, s * LANES : (s + 1) * LANES] = (tile - high.astype(f32)).astype(bf16)
    size = rank * clusters
    row = lax.broadcasted_iota(jnp.int32, (size, 1), 0)
    column = lax.broadcasted_iota(jnp.int32, (size, size), 1)
    wanted = lax.rem(row, clusters) * rank + lax.div(row, clusters)
    target_out[...] = dot((column == wanted).astype(bf16), target[...]).astype(bf16)


def fetch_kernel(slots, blocks_hbm, *refs):
    *_, blocks, token, sems = refs
    chunks = sems.shape[1]
    each = blocks.shape[0] // chunks
    copies, at = [], 0
    for n, (first, count) in enumerate(slots):
        for c in range(chunks):
            clusters = pl.ds(c * each, each)
            copies.append(
                pltpu.make_async_copy(
                    blocks_hbm.at[clusters, pl.ds(first, count)], blocks.at[clusters, pl.ds(at, count)], sems.at[n, c]
                )
            )
        at += count
    for copy in copies:
        copy.start()
    token[...] = jnp.zeros_like(token)
    for copy in copies:
        copy.wait()


def own_kernel(blocks_hbm, own, _, near, blocks, sems):
    chunks = sems.shape[0]
    each = blocks.shape[0] // chunks
    copies = [
        pltpu.make_async_copy(
            blocks_hbm.at[pl.ds(c * each, each), pl.ds(0, 1)], blocks.at[pl.ds(c * each, each)], sems.at[c]
        )
        for c in range(chunks)
    ]
    for copy in copies:
        copy.start()
    products = []
    for c, copy in enumerate(copies):
        copy.wait()
        for i in range(c * each, (c + 1) * each, 2):
            weights = jnp.concatenate([blocks[i, 0], blocks[i + 1, 0]], axis=0)
            products.append(dot(own[pl.ds(i * R, 2 * R), :], weights, (1, 1)))
    for n, both in enumerate(products):
        near[pl.ds(2 * n * R, 2 * R), :] = jnp.concatenate([both[:R, :LANES], both[R:, LANES:]], axis=0)


def relay_kernel(axis, got, even, odd, _, out):
    me = lax.axis_index(axis)
    devices, each, _ = got.shape
    for device in range(devices):
        out[pl.ds(device * each, each), :] = got[device]
    wants_even = (me // 2 + me) % 2 == 0
    span = pl.ds(devices * each, even.shape[0])

    @pl.when(wants_even)
    def _():
        out[span, :] = even[...]

    @pl.when(jnp.logical_not(wants_even))
    def _():
        out[span, :] = odd[...]


def apply(
    per_group, each, slabs, places, ahead, blocks, swaps, high, low, target, near, far, window, table, finish, started
):
    clusters = near.shape[0] // R
    early = ahead.shape[1]
    first = 0 if started is None else 1
    slots = early + blocks.shape[1] + first
    rank = LANES // per_group
    head = clusters // per_group * R
    rows = slabs[0].shape[0]
    devices = (swaps[0].shape[0] - rows) // each
    for at, slab in enumerate(slabs):
        window[pl.ds(at * rows, rows), :] = slab[...].astype(f32)
    window[pl.ds(len(slabs) * rows, rows), :] = swaps[1][pl.ds(devices * each, rows), :].astype(f32)
    window[pl.ds((len(slabs) + 1) * rows, R), :] = jnp.zeros((R, LANES), f32)
    for part, values in enumerate(swaps):
        for device in range(devices):
            at = (part * devices + device) * head
            table[pl.ds(at, head), :] = values[pl.ds(device * each, head), :].astype(f32)
    lane = lane_ids()

    def fetch(k, i):
        return window[pl.ds(pl.multiple_of(places[k, i], R), R), :]

    def block(k, i):
        if 0 < k <= early:
            return ahead[i, k - 1]
        return blocks[i, max(k - early - first, 0)]

    def pick(i):
        tile = jnp.zeros((R, LANES), f32)
        for k in range(slots):
            found = table[pl.ds(pl.multiple_of(places[slots + k, i], R), R), :]
            tile = jnp.where(lane // rank == k, pltpu.roll(found, places[2 * slots + k, i], 1), tile)
        return tile

    def product(i):
        sources = jnp.concatenate(
            [jnp.concatenate([fetch(k, i), fetch(k, i + 1)], axis=0) for k in range(first, slots)], axis=1
        )
        weights = jnp.concatenate(
            [jnp.concatenate([block(k, i), block(k, i + 1)], axis=0) for k in range(first, slots)], axis=1
        )
        return dot(sources.astype(bf16), weights, (1, 1))

    def settle(i, both):
        parts = [both[:R, :LANES], both[R:, LANES:]]
        if started is not None:
            parts = [part + rows_of(started, i + n) for n, part in enumerate(parts)]
        near[pl.ds(i * R, 2 * R), :] = jnp.concatenate(parts, axis=0)

    def expand(crossed):
        spread = []
        for s in range(rank * clusters // LANES):
            tile = jnp.zeros((R, LANES), f32)
            for n in range(clusters):
                part = crossed[n * R : (n + 1) * R, s * LANES : (s + 1) * LANES]
                tile = jnp.where(lane % clusters == n, part, tile)
            tile_high = tile.astype(bf16).astype(f32)
            for n, source in enumerate((tile_high, tile - tile_high)):
                held = [jnp.where(lane % clusters == c, source, 0.0) for c in range(clusters)]
                spread.append((n, jnp.concatenate(held, axis=0).astype(bf16)))
        return [jnp.concatenate([part for m, part in spread if m == n], axis=1) for n in range(2)]

    pairs = clusters // 2
    middle = pairs // 2
    picked, pending, done = [], None, 0
    for p in range(pairs):
        both = product(2 * p)
        if pending is not None:
            settle(2 * p - 2, pending)
        pending = both
        if p < middle:
            picked += [pick(n) for n in range(4 * p, 4 * p + 4)]
        if p == middle - 1:
            chosen = jnp.concatenate(picked, axis=0).astype(bf16)
            crossed = [dot(chosen, high[...]), dot(chosen, low[...])]
        if p == middle:
            spread = expand(crossed[0] + crossed[1])
            made = [dot(part, target[...]) for part in spread]
        if p == middle + 1:
            far[...] = made[0] + made[1]
        if p > middle + 1:
            ready = min(2 * p, done + 6)
            for n in range(done, ready):
                finish(n)
            done = ready
    settle(clusters - 2, pending)
    for n in range(done, clusters):
        finish(n)


def first_kernel(
    per_group, own, mate, even, odd, places, ahead, blocks, sent, received, high, low, target, b, basis,
    image, lowered, payload, near, far, window, table,
):
    clusters = near.shape[0] // R
    slabs, swaps = (own, mate, even, odd), (sent, received)
    each = clusters // per_group * R
    tiles, products, parts = [], [], []
    sums = [jnp.zeros((R, LANES), f32) for _ in range(3)]

    def finish(i):
        field = rows_of(b, i)
        made = 0.5 * field + (rows_of(near, i) + rows_of(far, i))
        sums[:] = [s + f * g for s, f, g in zip(sums, (field, field, made), (field, made, made))]
        tiles.append(made)
        if i % 2:
            both = jnp.concatenate(tiles[i - 1 :], axis=0)
            image[pl.ds((i - 1) * R, 2 * R), :] = both
            lowered[pl.ds((i - 1) * R, 2 * R), :] = both.astype(bf16)
        if i % per_group == per_group - 1:
            products.append(compress(tiles[-per_group:], basis, i // per_group))
            parts.extend(collect(product, per_group) for product in products[-2:-1])

    apply(
        per_group, each, slabs, places, ahead, blocks, swaps, high, low, target, near, far, window, table, finish, None
    )
    write_payload(payload, parts + [collect(products[-1], per_group)], sums)


def arnoldi_one(bb, bw, ww):
    whole = bb + epsilon
    start_norm = jnp.sqrt(whole)
    scale = 1.0 / start_norm
    v11 = bb / whole
    h11 = (bw * scale) * scale
    uu = jnp.maximum((ww * scale) * scale - 2.0 * h11 * h11 + h11 * h11 * v11, 0.0)
    h21 = jnp.sqrt(uu + epsilon)
    return start_norm, h11, h21, v11, uu / (uu + epsilon), h11 * (1.0 - v11) / h21


def second_kernel(
    per_group, unknowns, own, mate, even, odd, places, ahead, blocks, sent, received, high, low, target, b, image,
    started, candidate, sums_out, known, near, far, window, table,
):
    clusters = near.shape[0] // R
    head = clusters // per_group * R
    slabs, swaps = (own, mate, even, odd), (sent, received)
    means = read_sums(tails(swaps, own.shape[0], head), 3, unknowns)
    values = arnoldi_one(*means)
    start_norm, h11, h21, _, _, _ = values
    lane = lane_ids()
    tile = jnp.zeros((R, LANES), f32)
    for n, value in enumerate(values):
        tile = jnp.where(lane == n, value, tile)
    known[...] = tile
    scale = 1.0 / start_norm
    inverse = 1.0 / h21
    sums = [jnp.zeros((R, LANES), f32) for _ in range(3)]

    def finish(j):
        held = rows_of(image, j) * scale
        first = rows_of(b, j) * scale
        second = (held - h11 * first) * inverse
        made = (0.5 * held + (rows_of(near, j) + rows_of(far, j)) * scale - h11 * held) * inverse
        sums[:] = [s + v * made for s, v in zip(sums, (first, second, made))]
        candidate[pl.ds(j * R, R), :] = made

    each = head + TAIL
    apply(
        per_group, each, slabs, places, ahead, blocks, swaps, high, low, target, near, far, window, table, finish, started
    )
    tile = sums_tile(sums).astype(bf16)
    for device in range(sums_out.shape[0]):
        sums_out[device] = tile


def finish_kernel(unknowns, b, image, candidate, known, got, solution_out, next_out):
    clusters = b.shape[0] // R
    start_norm, h11, h21, v11, v22, v12 = [known[:, n : n + 1] for n in range(6)]
    h12, h22, ww = read_sums([got[device] for device in range(got.shape[0])], 3, unknowns)
    uu = ww - 2.0 * (h12 * h12 + h22 * h22) + h12 * h12 * v11 + h22 * h22 * v22 + 2.0 * h12 * h22 * v12
    h32 = jnp.sqrt(jnp.maximum(uu, 0.0) + epsilon)
    g11 = h11 * h11 + h21 * h21
    g12 = h11 * h12 + h21 * h22
    g22 = h12 * h12 + h22 * h22 + h32 * h32
    t1, t2 = start_norm * h11, start_norm * h12
    det = g11 * g22 - g12 * g12
    y1 = (g22 * t1 - g12 * t2) / det
    y2 = (g11 * t2 - g12 * t1) / det
    scale, inverse, last = 1.0 / start_norm, 1.0 / h21, 1.0 / h32
    for j in range(clusters):
        span = slice(j * LANES, (j + 1) * LANES)
        first = rows_of(b, j) * scale
        second = (rows_of(image, j) * scale - h11 * first) * inverse
        solution_out[:, span] = y1 * first + y2 * second
        next_out[:, span] = (rows_of(candidate, j) - h12 * first - h22 * second) * last


def swapped(block, partner):
    return lax.ppermute(block, "rows", [(i, partner(i)) for i in range(lax.axis_size("rows"))])


def core_mate(i):
    return i ^ 1


def even_mate(i):
    return i ^ 2


def odd_mate(i):
    chip = i // 2
    other = chip + 1 if chip % 2 else chip - 1
    return 2 * (other % (lax.axis_size("rows") // 2)) + i % 2


def sends_of(block):
    mate, odd, even = [swapped(block, partner) for partner in (core_mate, odd_mate, even_mate)]
    return [block, mate, even, odd]


def on_device(
    right_sides, near_blocks, near_cols, near_counts, basis_in, target_basis, coupling, far_cols
):
    width = right_sides.shape[1]
    clusters, slots = near_cols.shape
    rank = basis_in.shape[1]
    per_group = LANES // rank
    head = clusters // per_group * R
    size = lax.axis_size("rows")
    unknowns = float(width * size)
    rows = clusters * R

    def shape(*dims, dtype=f32):
        return jax.ShapeDtypeStruct(dims, dtype)

    def scratch(*dims, dtype=f32):
        return pltpu.VMEM(dims, dtype)

    def in_hbm(array):
        return pltpu.with_memory_space_constraint(array, pltpu.HBM)

    def call(kernel, name, out, ins, *args, scratch_shapes=()):
        return pl.pallas_call(
            kernel, out_shape=out, in_specs=ins, out_specs=jax.tree.map(lambda _: VMEM, out),
            scratch_shapes=scratch_shapes, compiler_params=PARAMS, name=name,
        )(*args)

    chips = size // 2
    middle = chips // 4 + 1
    order = [(middle - n) % chips for n in range(chips)]

    def gather(block):
        groups = [[2 * chip + core for chip in order] for core in range(2)]
        return lax.all_to_all(block, "rows", 0, 0, axis_index_groups=groups)

    def exchange(block):
        group = [2 * chip + core for chip in order for core in range(2)]
        return lax.all_to_all(block, "rows", 0, 0, axis_index_groups=[group])

    field, basis, lowered, payload = call(
        functools.partial(start_kernel, per_group), "start",
        (
            shape(rows, LANES), shape(clusters * rank, LANES, dtype=bf16), shape(rows, LANES, dtype=bf16),
            shape(size // 2, head, LANES, dtype=bf16),
        ),
        [HBM] * 2, in_hbm(right_sides), in_hbm(basis_in.reshape(clusters * rank, LANES)),
        scratch_shapes=[scratch(R, width), pltpu.SemaphoreType.DMA((2,))],
    )
    got = gather(payload)
    held = sends_of(lowered)

    blocks = in_hbm(near_blocks)
    early = 2

    def fetch(name, ranges, chunks, *behind):
        count = sum(count for _, count in ranges)
        here, token = call(
            functools.partial(fetch_kernel, ranges), name,
            (pltpu.VMEM((clusters, count, LANES, LANES), bf16), shape(R, LANES)),
            [HBM] + [ANY] * len(behind), blocks, *behind,
            scratch_shapes=[pltpu.SemaphoreType.DMA((len(ranges), chunks))],
        )
        return pltpu.with_memory_space_constraint(here, pltpu.VMEM), token

    def arrived(got, held, ranges, behind):
        rest, token = fetch("fetch", ranges, 1, got, behind)
        sent = call(
            functools.partial(relay_kernel, "rows"), "relay",
            shape(got.shape[0] * got.shape[1] + rows, LANES, dtype=bf16), [VMEM] * 3 + [ANY], got, *held[2:], token
        )
        return ahead, rest, sent, swapped(sent, core_mate)

    late = (1 + early, slots - 1 - early)
    ahead, token = fetch("ahead", [(1, early)], 1, held[1])
    here = arrived(got, held, [(0, 1), late], token)
    prepared = call(
        functools.partial(prepare_kernel, "rows", size, middle), "prepare",
        (
            shape(3 * slots, clusters, dtype=jnp.int32),
            shape(slots * rank, rank * clusters, dtype=bf16),
            shape(slots * rank, rank * clusters, dtype=bf16),
            shape(rank * clusters, LANES, dtype=bf16),
        ),
        [HBM] * 5 + [ANY], in_hbm(near_cols.T), in_hbm(near_counts.reshape(1, clusters)), in_hbm(far_cols.T),
        in_hbm(jnp.transpose(coupling, (1, 2, 3, 0))), in_hbm(target_basis.reshape(clusters * rank, LANES)), here[2],
        scratch_shapes=[
            scratch(slots, clusters, dtype=jnp.int32), scratch(1, clusters, dtype=jnp.int32),
            scratch(slots, clusters, dtype=jnp.int32),
            scratch(slots, rank, rank, clusters), scratch(clusters * rank, LANES, dtype=bf16),
            pltpu.SemaphoreType.DMA((5,)),
        ],
    )
    places, *made = prepared
    kept = [scratch(rows, LANES), scratch(rows, LANES), scratch(5 * rows + R, LANES), scratch(size * head, LANES)]
    operands = [VMEM] * 4 + [SMEM] + [VMEM] * 9
    image, lowered, payload = call(
        functools.partial(first_kernel, per_group), "operator_one",
        (
            shape(rows, LANES), shape(rows, LANES, dtype=bf16),
            shape(size // 2, head + TAIL, LANES, dtype=bf16),
        ),
        operands, *held, places, *here, *made, field, basis, scratch_shapes=kept,
    )
    got = gather(payload)
    held = sends_of(lowered)
    started = call(
        own_kernel, "own", shape(rows, LANES), [HBM, VMEM, ANY], blocks, lowered, held[1],
        scratch_shapes=[scratch(clusters, 1, LANES, LANES, dtype=bf16), pltpu.SemaphoreType.DMA((2,))],
    )
    here = arrived(got, held, [late], started)
    candidate, sums, known = call(
        functools.partial(second_kernel, per_group, unknowns), "operator_two",
        (shape(rows, LANES), shape(size, R, LANES, dtype=bf16), shape(R, LANES)),
        operands + [VMEM], *held, places, *here, *made, field, image, started, scratch_shapes=kept,
    )
    return call(
        functools.partial(finish_kernel, unknowns), "finish", (shape(R, width), shape(R, width)),
        [VMEM] * 5, field, image, candidate, known, exchange(sums),
    )


def solution(mesh):
    return jax.shard_map(
        on_device,
        mesh=mesh,
        in_specs=(
            P("groups", "rows"),
            P("rows", None, None, None),
            P("rows", None),
            P("rows"),
            P("rows", None, None),
            P("rows", None, None),
            P("rows", None, None, None),
            P("rows", None),
        ),
        out_specs=(P("groups", "rows"), P("groups", "rows")),
        check_vma=False,
    )
```
